32 devices in a mesh: dp: 8 (over z, x), grp: 4 (over y, core).
Axes of the slice: x: 2, y: 2, z: 4, core: 2. Of those that a mesh axis runs over, the one named last changes fastest.
Arguments:
- doc_tokens: bfloat16 [32, 512, 768], P(('dp', 'grp')), may hold values from -6 to 6
- doc_lengths: int32 [32, 4], P(('dp', 'grp')), may hold values from 1 to 256, 480 in all within a row
- query_tokens: bfloat16 [64, 32, 768], P(('dp', 'grp')), may hold values from -6 to 6
- query_lengths: int32 [64], P(('dp', 'grp')), may hold values from 8 to 32
- candidates: int32 [64, 32], P(('dp', 'grp')), may hold values from 0 to 31
- labels: int32 [64], P(('dp', 'grp')), may hold values from 0 to 31
- gain_attn: bfloat16 [768], replicated, may hold values from 0.5 to 1.5
- w_query: bfloat16 [768, 768], replicated, may hold values from -0.02734375 to 0.02734375
- w_key: bfloat16 [768, 768], replicated, may hold values from -0.21875 to 0.21875
- w_value: bfloat16 [768, 768], replicated, may hold values from -0.21875 to 0.21875
- w_out: bfloat16 [768, 768], replicated, may hold values from -0.875 to 0.875
- bias_table: bfloat16 [32, 12], replicated, may hold values from -4 to 4
- gain_ffn: bfloat16 [768], replicated, may hold values from 0.5 to 1.5
- w_gate: bfloat16 [768, 2048], replicated, may hold values from -0.21875 to 0.21875
- w_up: bfloat16 [768, 2048], replicated, may hold values from -0.21875 to 0.21875
- w_down: bfloat16 [2048, 768], replicated, may hold values from -0.125 to 0.125
- gain_final: bfloat16 [768], replicated, may hold values from 0.5 to 1.5
- w_proj: bfloat16 [768, 128], replicated, may hold values from -0.21875 to 0.21875
Outputs:
- loss: float32 [], replicated
- doc_grad: float32 [32, 512, 768], P(('dp', 'grp'))
- query_grad: float32 [64, 32, 768], P(('dp', 'grp'))
- gain_attn_grad: float32 [768], P(('dp', 'grp'))
- w_query_grad: float32 [768, 768], P(('dp', 'grp'))
- w_key_grad: float32 [768, 768], P(('dp', 'grp'))
- w_value_grad: float32 [768, 768], P(('dp', 'grp'))
- w_out_grad: float32 [768, 768], P(('dp', 'grp'))
- bias_table_grad: float32 [32, 12], replicated
- gain_ffn_grad: float32 [768], P(('dp', 'grp'))
- w_gate_grad: float32 [768, 2048], P(('dp', 'grp'))
- w_up_grad: float32 [768, 2048], P(('dp', 'grp'))
- w_down_grad: float32 [2048, 768], P(('dp', 'grp'))
- gain_final_grad: float32 [768], P(('dp', 'grp'))
- w_proj_grad: float32 [768, 128], P(('dp', 'grp'))
The draws below stay inside these ranges and needn't reach their ends.
Inputs may be any that keep to these rules, and one draw needn't show every extreme that they name: `doc_lengths`: the lengths of each row's 4 documents sum to 480, and in every row the longest is 256. `candidates`: numbers of blocks of the query's own group.
All inputs are finite; a program needn't handle non-finite values.
Results may differ from the reference program's by a relative error of at most 0.017.
Values may be sent and summed in bfloat16 or wider, within the bound.
No kernel may reach another device: no remote copies, remote signals or barrier semaphores. Data moves between devices by JAX's collectives and lax.ppermute only.
A program may use at most 192 MiB of HBM per device.

```python
import math
import jax
import jax.numpy as jnp
import numpy as np
from jax import lax

D = 768
H = 12
HD = 64
FF = 2048
PROJ = 128
BUCKETS = 32
DIST = 128
DLEN = 512
QLEN = 32
BLK = 128
C = 32
DOCS_ROW = 4
ROW_FILL = 480
MOST_DOC = 256
DOC_DEV = 1
QRY_DEV = 2
DOCS = 32
NQ = 64
NBLK = 32
N_DP = 8
N_GRP = 4


def place_ends(result, rng, smallest, high):
    extent = result.shape
    place = [jax.random.randint(jax.random.fold_in(rng, axis), (), 0, extent[axis]) for axis in range(len(extent))]
    result = result.at[tuple(place)].set(smallest)
    longest = extent.index(max(extent))
    place[longest] = (place[longest] + 1) % extent[longest]
    return result.at[tuple(place)].set(high)


def block_levels(key, dims, shards, low, top_value):
    gain = 1.0
    for position, blocks in shards:
        steps = jax.random.uniform(jax.random.fold_in(jax.random.fold_in(key, 6), position), (blocks,), jnp.float32, low / len(shards), top_value / len(shards))
        gain = gain * jnp.repeat(jnp.exp(steps), dims[position] // blocks).reshape((-1,) + (1,) * (len(dims) - 1 - position))
    return gain


def length_profile(count, total, limit, skew):
    portions = [(1 << 20) // math.isqrt(standing ** skew) + 1 for standing in range(2, count + 1)]
    surplus, counts = total - limit - (count - 1), [1] * (count - 1)
    while surplus > 0:
        movable = [i for i in range(count - 1) if counts[i] < limit]
        pool, remaining = sum([portions[i] for i in movable]), surplus
        for i in movable:
            more = min(limit - counts[i], max(1, remaining * portions[i] // pool), surplus)
            counts[i] = counts[i] + more
            surplus = surplus - more
    return np.array([limit] + counts)


def uneven(key, count, total, bound, skew):
    if count == 2:
        one = jax.random.randint(key, (), max(1, total - bound), min(bound, total - 1) + 1)
        return jnp.stack([one, total - one])
    lengths = jnp.asarray(length_profile(count, total, bound, skew), jnp.int32)
    couples = (count - 1) // 2
    donor, taker = lengths[1:1 + 2 * couples:2], lengths[2:2 + 2 * couples:2]
    room = jnp.minimum(donor - 1, bound - taker)
    moved = jax.random.randint(jax.random.fold_in(key, 1), (couples,), 0, 1 << 20) % (room + 1)
    lengths = lengths.at[1:1 + 2 * couples:2].set(donor - moved).at[2:2 + 2 * couples:2].set(taker + moved)
    return lengths[jax.random.permutation(jax.random.fold_in(key, 2), count)]


def normal_values(key, shape, spread, limit, cuts=(), kind=jnp.bfloat16):
    loudness = block_levels(key, shape, cuts, -0.22, 0.18) if cuts else 1.0
    entries = jax.random.normal(key, shape, jnp.float32) * spread * loudness
    return jnp.minimum(jnp.maximum(entries, -limit), limit).astype(kind)


def setup_inputs(seed: int = 0) -> dict:
    seeds = jax.random.split(jax.random.key(seed), 19)
    doc_tokens = normal_values(seeds[0], (DOCS, DLEN, D), 1.0, 6.0, ((0, 32),))
    doc_lengths = jax.vmap(lambda own: uneven(own, DOCS_ROW, ROW_FILL, MOST_DOC, 1))(jax.random.split(seeds[1], DOCS)).reshape((DOCS, DOCS_ROW)).astype(jnp.int32)
    query_tokens = normal_values(seeds[2], (NQ, QLEN, D), 1.0, 6.0, ((0, 32),))
    query_lengths = place_ends(jax.random.randint(seeds[3], (NQ,), QLEN // 4, QLEN + 1), jax.random.fold_in(seeds[3], 1), QLEN // 4, QLEN).astype(jnp.int32)
    candidates = place_ends(jax.random.randint(seeds[4], (NQ, C), 0, NBLK), jax.random.fold_in(seeds[4], 1), 0, NBLK - 1).astype(jnp.int32)
    labels = place_ends(jax.random.randint(seeds[5], (NQ,), 0, C), jax.random.fold_in(seeds[5], 1), 0, C - 1).astype(jnp.int32)
    gain_attn = jnp.clip(1.0 + 0.1 * jax.random.normal(seeds[6], (D,), jnp.float32), 0.5, 1.5).astype(jnp.bfloat16)
    w_query = normal_values(seeds[7], (D, H * HD), (D * HD) ** -0.5, 0.02734375)
    w_key = normal_values(seeds[8], (D, H * HD), D ** -0.5, 0.21875)
    w_value = normal_values(seeds[9], (D, H * HD), D ** -0.5, 0.21875)
    w_out = normal_values(seeds[10], (H * HD, D), (H * HD // 16) ** -0.5, 0.875)
    bias_table = normal_values(seeds[11], (BUCKETS, H), 1.0, 4.0)
    gain_ffn = jnp.clip(1.0 + 0.1 * jax.random.normal(seeds[12], (D,), jnp.float32), 0.5, 1.5).astype(jnp.bfloat16)
    w_gate = normal_values(seeds[13], (D, FF), D ** -0.5, 0.21875)
    w_up = normal_values(seeds[14], (D, FF), D ** -0.5, 0.21875)
    w_down = normal_values(seeds[15], (FF, D), FF ** -0.5, 0.125)
    gain_final = jnp.clip(1.0 + 0.1 * jax.random.normal(seeds[16], (D,), jnp.float32), 0.5, 1.5).astype(jnp.bfloat16)
    w_proj = normal_values(seeds[17], (D, PROJ), D ** -0.5, 0.21875)
    return dict(doc_tokens=doc_tokens, doc_lengths=doc_lengths, query_tokens=query_tokens, query_lengths=query_lengths, candidates=candidates, labels=labels, gain_attn=gain_attn, w_query=w_query, w_key=w_key, w_value=w_value, w_out=w_out, bias_table=bias_table, gain_ffn=gain_ffn, w_gate=w_gate, w_up=w_up, w_down=w_down, gain_final=gain_final, w_proj=w_proj)


eps_norm = 1e-06
normalizer_sharpness = 0.25
logit_scale = 16.0
excluded_entry_default = -1e+30
highest = lax.Precision.HIGHEST

@jax.custom_vjp
def low(v):
    return lax.optimization_barrier(v.astype(jnp.bfloat16)).astype(jnp.float32)

@jax.custom_vjp
def low_back(v):
    return v

def low_keep(v):
    return (low(v), None)

def low_pass(kept, grad):
    return (grad,)

def back_keep(v):
    return (v, None)

def back_low(kept, grad):
    return (low(grad),)
low.defvjp(low_keep, low_pass)
low_back.defvjp(back_keep, back_low)

def bucket_tables(length):
    offsets = np.arange(-(length - 1), length)
    half_count = BUCKETS // 2
    exact_count = half_count // 2
    distance = np.abs(offsets)
    scaled = np.log(np.maximum(distance, 1) / exact_count) / np.log(DIST / exact_count) * (half_count - exact_count)
    far_bucket = np.minimum(exact_count + np.maximum(scaled, 0).astype(np.int64), half_count - 1)
    bucket = (offsets > 0) * half_count + np.where(distance < exact_count, distance, far_bucket)
    onehot = (bucket[:, None] == np.arange(BUCKETS)[None, :]).astype(np.float32)
    positions = np.arange(length)
    lookup = (positions[None, :] - positions[:, None] + length - 1).astype(np.int32)
    return (onehot, lookup)

def relative_bias(bias_table, length):
    onehot, lookup = bucket_tables(length)
    per_offset = jnp.dot(jnp.asarray(onehot, bias_table.dtype), bias_table, precision=highest)
    return jnp.transpose(jnp.take(per_offset, jnp.asarray(lookup), axis=0), (2, 0, 1))

def rms_norm(values, gain_vec):
    return values * lax.rsqrt(lax.optimization_barrier(jnp.mean(values * values, axis=-1, keepdims=True)) + eps_norm) * gain_vec

def document_mask(lengths_rows, length):
    doc_ends = jnp.cumsum(lengths_rows, axis=-1)
    positions = jnp.arange(length, dtype=jnp.int32)
    segment = lax.optimization_barrier(jnp.sum((positions[None, :, None] >= doc_ends[:, None, :]).astype(jnp.int32), axis=-1))
    allowed = segment[:, :, None] == segment[:, None, :]
    word_present_flag = positions[None, :] < doc_ends[:, -1:]
    return (allowed, word_present_flag)

def query_mask(query_lens, length):
    positions = jnp.arange(length, dtype=jnp.int32)
    keys_ok = positions[None, :] < query_lens[:, None]
    allowed = jnp.broadcast_to(keys_ok[:, None, :], (keys_ok.shape[0], length, length))
    return (allowed, keys_ok)

def attend_row(normed, allowed, pos_bias, w_query, w_key, w_value, w_out):
    length = normed.shape[0]
    queries = low_back(low(jnp.dot(normed, w_query, precision=highest))).reshape(length, H, HD)
    key_rows = low_back(low(jnp.dot(normed, w_key, precision=highest))).reshape(length, H, HD)
    value_rows = low_back(low(jnp.dot(normed, w_value, precision=highest))).reshape(length, H, HD)
    scores = low_back(jnp.einsum('qhd,khd->hqk', queries, key_rows, precision=highest) + pos_bias)
    scores = jnp.where(allowed[None], scores, excluded_entry_default)
    aggregation_factors = low(jax.nn.softmax(scores, axis=-1))
    mixed = jnp.einsum('hqk,khd->qhd', aggregation_factors, value_rows, precision=highest).reshape(length, H * HD)
    mixed = low_back(low(mixed))
    return low_back(jnp.dot(mixed, w_out, precision=highest))

def encode(rows_x, allowed, params):
    gain_attn, w_query, w_key, w_value, w_out, bias_table, gain_ffn, w_gate, w_up, w_down, gain_final, w_proj = params
    row_count, length = (rows_x.shape[0], rows_x.shape[1])
    flat_rows = rows_x.reshape(row_count * length, D)
    pos_bias = relative_bias(bias_table, length)
    normed = low(rms_norm(flat_rows, gain_attn)).reshape(row_count, length, D)
    attended = jax.vmap(attend_row, in_axes=(0, 0, None, None, None, None, None))(normed, allowed, pos_bias, w_query, w_key, w_value, w_out)
    middle = flat_rows + attended.reshape(row_count * length, D)
    normed = low(rms_norm(middle, gain_ffn))
    gate_pre = low_back(jnp.dot(normed, w_gate, precision=highest))
    upward = low_back(jnp.dot(normed, w_up, precision=highest))
    hidden = low(jax.nn.gelu(gate_pre, approximate=True) * upward)
    output = middle + low_back(jnp.dot(hidden, w_down, precision=highest))
    normed = low(rms_norm(output, gain_final))
    projected = low_back(jnp.dot(normed, w_proj, precision=highest))
    return low(projected * lax.rsqrt(lax.optimization_barrier(jnp.sum(projected * projected, axis=-1, keepdims=True)) + eps_norm))

def doc_encode(params, rows_x, lengths_rows):
    allowed, _ = document_mask(lengths_rows, DLEN)
    return encode(rows_x, allowed, params)

def query_encode(params, rows_x, query_lens):
    allowed, _ = query_mask(query_lens, QLEN)
    return encode(rows_x, allowed, params)

def block_maxima(query_block, docs, word_present_flag):
    pairwise_match_matrix = low_back(jnp.dot(query_block, docs.T, precision=highest)).reshape(query_block.shape[0], -1, BLK)
    exponentiated_logit = jnp.where(word_present_flag[None], pairwise_match_matrix / normalizer_sharpness, excluded_entry_default)
    return normalizer_sharpness * jax.nn.logsumexp(exponentiated_logit, axis=-1)

def reference(doc_tokens, doc_lengths, query_tokens, query_lengths, candidates, labels, gain_attn, w_query, w_key, w_value, w_out, bias_table, gain_ffn, w_gate, w_up, w_down, gain_final, w_proj):
    params = tuple((item.astype(jnp.float32) for item in (gain_attn, w_query, w_key, w_value, w_out, bias_table, gain_ffn, w_gate, w_up, w_down, gain_final, w_proj)))
    _, doc_valid = document_mask(doc_lengths, DLEN)
    doc_valid = doc_valid.reshape(N_DP, N_GRP, DOC_DEV * DLEN)
    _, token_ok = query_mask(query_lengths, QLEN)
    token_mask = token_ok.astype(jnp.float32).reshape(N_DP, N_GRP, QRY_DEV, QLEN)
    cand_grid = candidates.reshape(N_DP, N_GRP, QRY_DEV, C)
    label_grid = labels.reshape(N_DP, N_GRP, QRY_DEV)
    row_total = N_DP * QRY_DEV * QLEN
    block_rows = 512 if row_total % 512 == 0 else row_total
    doc_fn = jax.checkpoint(doc_encode)
    query_fn = jax.checkpoint(query_encode)
    score_fn = jax.checkpoint(block_maxima)

    def total_loss(params, doc_x, query_x):
        doc_emb = lax.map(lambda pair: doc_fn(params, pair[0], pair[1]), (doc_x.reshape(N_DP * N_GRP, DOC_DEV, DLEN, D), doc_lengths.reshape(N_DP * N_GRP, DOC_DEV, DOCS_ROW)))
        doc_emb = doc_emb.reshape(N_DP, N_GRP, DOC_DEV * DLEN, PROJ)
        query_emb = lax.map(lambda pair: query_fn(params, pair[0], pair[1]), (query_x.reshape(N_DP, N_GRP * QRY_DEV, QLEN, D), query_lengths.reshape(N_DP, N_GRP * QRY_DEV)))
        query_emb = query_emb.reshape(N_DP, N_GRP, QRY_DEV * QLEN, PROJ)
        total = jnp.zeros((), jnp.float32)
        for group in range(N_GRP):
            docs = doc_emb[:, group].reshape(N_DP * DOC_DEV * DLEN, PROJ)
            word_present_flag = doc_valid[:, group].reshape(NBLK, BLK)
            queries = query_emb[:, group].reshape(row_total // block_rows, block_rows, PROJ)
            maxima = lax.map(lambda block: score_fn(block, docs, word_present_flag), queries)
            maxima = maxima.reshape(N_DP * QRY_DEV, QLEN, NBLK)
            cand_group = cand_grid[:, group].reshape(N_DP * QRY_DEV, C)
            picked = jnp.take_along_axis(maxima, jnp.broadcast_to(cand_group[:, None, :], (N_DP * QRY_DEV, QLEN, C)), axis=2)
            mask_group = token_mask[:, group].reshape(N_DP * QRY_DEV, QLEN)
            logits = logit_scale * lax.optimization_barrier(jnp.sum(picked * mask_group[:, :, None], axis=1))
            label_group = label_grid[:, group].reshape(N_DP * QRY_DEV)
            target = jnp.take_along_axis(logits, label_group[:, None], axis=1)[:, 0]
            total = total + jnp.sum(jax.nn.logsumexp(logits, axis=1) - target)
        return total
    total, pullback = jax.vjp(total_loss, params, doc_tokens.astype(jnp.float32), query_tokens.astype(jnp.float32))
    param_grads, doc_grad, query_grad = pullback(jnp.ones_like(total))
    loss = total / (QRY_DEV * N_DP * N_GRP)
    return (loss, doc_grad, query_grad, param_grads[0], param_grads[1], param_grads[2], param_grads[3], param_grads[4], param_grads[5], param_grads[6], param_grads[7], param_grads[8], param_grads[9], param_grads[10], param_grads[11])
```

```python
import functools
import math

import jax
import jax.numpy as jnp
import numpy as np
from jax import lax
from jax.experimental import pallas as pl
from jax.experimental.pallas import tpu as pltpu
from jax.sharding import PartitionSpec as P

F32, BF16 = jnp.float32, jnp.bfloat16
BUCKETS = 32
DIST = 128
BLK = 128
EPS = 1e-6
SHARP = 0.25
SCALE = 16.0
NEG = -1e30
GELU_A = math.sqrt(2.0 / math.pi)
GELU_B = 0.044715
SPAN = 512
CH = 512
LANE = 128
PACK_INT = 48
highest = lax.Precision.HIGHEST


def nn(a, b):
    return jnp.dot(a, b, preferred_element_type=F32)


def nt(a, b):
    return lax.dot_general(a, b, (((1,), (1,)), ((), ())), preferred_element_type=F32)


def tn(a, b):
    return lax.dot_general(a, b, (((0,), (0,)), ((), ())), preferred_element_type=F32)


def bucket_of(offsets):
    half = BUCKETS // 2
    exact = half // 2
    dist = np.abs(offsets)
    scaled = np.log(np.maximum(dist, 1) / exact) / np.log(DIST / exact) * (half - exact)
    far = np.minimum(exact + np.maximum(scaled, 0).astype(np.int64), half - 1)
    return (offsets > 0) * half + np.where(dist < exact, dist, far)


def strip_onehot():
    j = np.arange(SPAN)
    offset = np.where(j < 384, 128 - j, 640 - j)
    index = np.stack([bucket_of(offset[(j - r) % SPAN]) for r in range(8)]).reshape(-1)
    return (index[None, :] == np.arange(BUCKETS)[:, None]).astype(np.float32)


VM = pl.BlockSpec(memory_space=pltpu.VMEM)
SM = pl.BlockSpec(memory_space=pltpu.SMEM)
HB = pl.BlockSpec(memory_space=pl.ANY)


def shape_of(shape, dtype):
    return jax.ShapeDtypeStruct(shape, dtype)


def call(kernel, name, outs, args, specs, scratch, mib, flops, moved=8 << 20):
    return pl.pallas_call(
        kernel,
        name=name,
        out_shape=outs,
        in_specs=specs,
        out_specs=[VM] * len(outs),
        scratch_shapes=scratch,
        compiler_params=pltpu.CompilerParams(vmem_limit_bytes=mib << 20),
        cost_estimate=pl.CostEstimate(flops=int(flops), bytes_accessed=int(moved), transcendentals=0),
    )(*args)


def fetch(pairs, sems):
    copies = []
    for i, (src, dst) in enumerate(pairs):
        copy = pltpu.make_async_copy(src, dst, sems.at[i])
        copy.start()
        copies.append(copy)
    return copies


def half_lanes(values, side):
    lane = lax.broadcasted_iota(jnp.int32, (1, LANE), 1)
    return jnp.where((lane // 64) == side, values.astype(F32), 0.0).astype(BF16)


def norm_back(values, gain, dn):
    s = lax.rsqrt(jnp.mean(values * values, axis=-1, keepdims=True) + EPS)
    unit = values * s
    t = dn * gain
    dv = s * (t - unit * jnp.mean(t * unit, axis=-1, keepdims=True))
    return dv, jnp.sum(dn * unit, axis=0, keepdims=True)


def forward_kernel(
    is_doc, x_ref, lens_ref, gains_ref, extra_ref, wq, wk, wv, wo, wg, wu, wd, wp,
    q_ref, k_ref, v_ref, e_ref, il_ref, mixt_ref, mid_ref, n1_ref, n2_ref, hid_ref, a_ref, b_ref,
    out_ref, n3_ref, proj_ref, emb_ref, *rest,
):
    if is_doc:
        base_ref, tail = extra_ref, rest
    else:
        tab_ref, hot_ref, ints_ref = extra_ref
        base_ref, tail = rest[0], rest[1:]
    wq_s, wk_s, wv_s, wo_s, wg_s, wu_s, wd_s, wp_s, mask_s, strip_s, s_s, vt_s, sems = tail
    tokens, width = x_ref.shape
    hidden = wg.shape[1]
    copies = fetch(
        ((wq, wq_s), (wk, wk_s), (wv, wv_s), (wo, wo_s), (wg, wg_s), (wu, wu_s), (wd, wd_s), (wp, wp_s)), sems
    )
    heads = e_ref.shape[0]
    if not is_doc:
        for r in range(8):
            rows = tn(tab_ref[...], hot_ref[:, r * SPAN:(r + 1) * SPAN])
            for h in range(heads):
                base_ref[h, r:r + 1, :] = rows[h:h + 1, :]
    x = x_ref[...].astype(F32)
    s1 = lax.rsqrt(jnp.mean(x * x, axis=-1, keepdims=True) + EPS)
    n1_ref[...] = (x * s1 * gains_ref[0:1, :]).astype(BF16)
    tile = min(tokens, 128)
    wide = min(tokens, 256)
    blocks = tokens // tile
    row_id = lax.broadcasted_iota(jnp.int32, (tokens, 1), 0)
    col_id = lax.broadcasted_iota(jnp.int32, (1, tokens), 1)
    if is_doc:
        seg_k = jnp.zeros((tokens, 1), jnp.int32)
        seg_q = jnp.zeros((1, tokens), jnp.int32)
        end = jnp.int32(0)
        for i in range(lens_ref.shape[1]):
            end = end + lens_ref[0, i]
            seg_k = seg_k + (row_id >= end).astype(jnp.int32)
            seg_q = seg_q + (col_id >= end).astype(jnp.int32)
    else:
        count = lens_ref.shape[0]
        length = tokens // count
        seg_q = col_id // length
        seg_k = jnp.full((tokens, 1), -1, jnp.int32)
        for i in range(count):
            inside = (row_id >= i * length) & (row_id < i * length + lens_ref[i])
            seg_k = jnp.where(inside, i, seg_k)
    mask_s[...] = jnp.where(seg_k == seg_q, 0.0, NEG)
    for i, (w, o) in enumerate(((wq_s, q_ref), (wk_s, k_ref), (wv_s, v_ref))):
        copies[i].wait()
        o[...] = nn(n1_ref[...], w[...]).astype(BF16)
    vt_s[...] = v_ref[...].T

    def pair_body(p, carry):
        col = pl.ds(pl.multiple_of(p * LANE, LANE), LANE)
        for s in range(2):
            h = 2 * p + s
            first = base_ref[h]
            for g in range(tile // 8):
                strip_s[8 * g:8 * g + 8, :] = pltpu.roll(first, 8 * g, 1) if g else first
            low_far, high_far = first[0:1, 256:256 + tile], first[0:1, 384:384 + tile]
            kp = half_lanes(k_ref[:, col], s)
            rows = pl.ds(pl.multiple_of(p * LANE + 64 * s, 64), 64)
            for qc in range(tokens // wide):
                cols = slice(qc * wide, (qc + 1) * wide)
                qp = q_ref[cols, col]
                top = None
                for kb in range(blocks):
                    ks = slice(kb * tile, (kb + 1) * tile)
                    scores = nt(kp[ks], qp)
                    tops = []
                    for qs in range(wide // tile):
                        qb = qc * (wide // tile) + qs
                        d = kb - qb
                        t = scores[:, qs * tile:(qs + 1) * tile]
                        if abs(d) <= 1:
                            lo = (1 - d) * 128
                            t = t + strip_s[:, lo:lo + tile]
                        else:
                            t = t + (high_far if d > 0 else low_far)
                        t = t + mask_s[ks, qb * tile:(qb + 1) * tile]
                        s_s[ks, qs * tile:(qs + 1) * tile] = t
                        tops.append(jnp.max(t, axis=0, keepdims=True))
                    mk = jnp.concatenate(tops, axis=1) if len(tops) > 1 else tops[0]
                    top = mk if top is None else jnp.maximum(top, mk)
                total = None
                for kb in range(blocks):
                    ks = slice(kb * tile, (kb + 1) * tile)
                    e = jnp.exp(s_s[ks, :] - top)
                    part = jnp.sum(e, axis=0, keepdims=True)
                    total = part if total is None else total + part
                    e_ref[h, ks, cols] = e.astype(BF16)
                inverse = 1.0 / total
                il_ref[h, :, cols] = inverse
                o = nn(vt_s[rows, :], e_ref[h, :, cols])
                mixt_ref[rows, cols] = (o * inverse).astype(BF16)
        return carry

    lax.fori_loop(0, width // LANE, pair_body, 0)
    copies[3].wait()
    mid_ref[...] = x_ref[...].astype(F32) + nn(mixt_ref[...].T, wo_s[...])
    mid = mid_ref[...]
    s2 = lax.rsqrt(jnp.mean(mid * mid, axis=-1, keepdims=True) + EPS)
    n2_ref[...] = (mid * s2 * gains_ref[1:2, :]).astype(BF16)
    copies[4].wait()
    copies[5].wait()

    def ff_body(j, carry):
        col = pl.ds(pl.multiple_of(j * CH, CH), CH)
        g = nn(n2_ref[...], wg_s[:, col])
        u = nn(n2_ref[...], wu_s[:, col])
        sq = g * g
        t = jnp.tanh(GELU_A * g * (1.0 + GELU_B * sq))
        half = 0.5 + 0.5 * t
        gel = g * half
        slope = half + (0.5 * GELU_A) * g * (1.0 - t * t) * (1.0 + 3.0 * GELU_B * sq)
        hid_ref[:, col] = (gel * u).astype(BF16)
        a_ref[:, col] = (u * slope).astype(BF16)
        b_ref[:, col] = gel.astype(BF16)
        return carry

    lax.fori_loop(0, hidden // CH, ff_body, 0)
    copies[6].wait()
    out_ref[...] = mid_ref[...] + nn(hid_ref[...], wd_s[...])
    o = out_ref[...]
    s3 = lax.rsqrt(jnp.mean(o * o, axis=-1, keepdims=True) + EPS)
    n3_ref[...] = (o * s3 * gains_ref[2:3, :]).astype(BF16)
    copies[7].wait()
    pr = nn(n3_ref[...], wp_s[...])
    proj_ref[...] = pr
    emb = (pr * lax.rsqrt(jnp.sum(pr * pr, axis=-1, keepdims=True) + EPS)).astype(BF16)
    if is_doc:
        emb_ref[...] = emb
    else:
        emb_ref[0:tokens, :] = emb
        emb_ref[tokens:, :] = ints_ref[...]


def forward(x, lens, gains, extra, weights, is_doc, heads):
    tokens, width = x.shape
    hidden = weights[4].shape[1]
    proj = weights[7].shape[1]
    outs = [shape_of((tokens, width), BF16)] * 3 + [
        shape_of((heads, tokens, tokens), BF16),
        shape_of((heads, 1, tokens), F32),
        shape_of((width, tokens), BF16),
        shape_of((tokens, width), F32),
        shape_of((tokens, width), BF16),
        shape_of((tokens, width), BF16),
        shape_of((tokens, hidden), BF16),
        shape_of((tokens, hidden), BF16),
        shape_of((tokens, hidden), BF16),
        shape_of((tokens, width), F32),
        shape_of((tokens, width), BF16),
        shape_of((tokens, proj), F32),
        shape_of((tokens + (0 if is_doc else PACK_INT), proj), BF16),
    ]
    tile = min(tokens, 128)
    scratch = [pltpu.VMEM(w.shape, BF16) for w in weights] + [
        pltpu.VMEM((tokens, tokens), F32),
        pltpu.VMEM((tile, SPAN), F32),
        pltpu.VMEM((tokens, min(tokens, 256)), F32),
        pltpu.VMEM((width, tokens), BF16),
        pltpu.SemaphoreType.DMA((8,)),
    ]
    if is_doc:
        kernel = functools.partial(forward_kernel, True)
        args, specs = [x, lens, gains, extra, *weights], [VM, SM, VM, VM] + [HB] * 8
    else:
        outs.append(shape_of((heads, 8, SPAN), F32))

        def kernel(x_ref, lens_ref, gains_ref, tab_ref, hot_ref, ints_ref, *rest):
            forward_kernel(False, x_ref, lens_ref, gains_ref, (tab_ref, hot_ref, ints_ref), *rest)

        args, specs = [x, lens, gains, *extra, *weights], [VM, SM, VM, VM, VM, VM] + [HB] * 8
    flops = 2 * tokens * (4 * width * width + 3 * width * hidden + width * proj) + 4 * tokens * tokens * width
    return call(
        kernel, "doc_forward" if is_doc else "query_forward", outs, args, specs, scratch, 58, flops, 30 << 20
    )


def unpack(got_ref, tokens):
    parts = got_ref.shape[0]
    own = 2
    lane = lax.broadcasted_iota(jnp.int32, (1, LANE), 1)
    ints = None
    for i in range(parts):
        block = got_ref[i, tokens:, :].astype(F32)
        if i:
            block = pltpu.roll(block, own * i, 1)
        block = jnp.where((lane // own) == i, block, 0.0)
        ints = block if ints is None else ints + block
    return ints[0:32, :], ints[32:33, :], ints[33:34, :]


def expand_onehot(queries, length):
    col = lax.broadcasted_iota(jnp.int32, (LANE, queries * length), 1)
    row = lax.broadcasted_iota(jnp.int32, (LANE, queries * length), 0)
    return ((col // length) == row).astype(F32)


def token_valid(lens, queries, length):
    hot = expand_onehot(queries, length)
    spread = jnp.dot(jnp.broadcast_to(lens, (8, LANE)), hot, precision=highest, preferred_element_type=F32)[0:1]
    place = lax.broadcasted_iota(jnp.int32, (1, queries * length), 1) % length
    return place.astype(F32) < spread, hot


def total_length(lens_ref):
    end = jnp.int32(0)
    for i in range(lens_ref.shape[1]):
        end = end + lens_ref[0, i]
    return end


def block_scores(emb_ref, q_s, b, end):
    t = nt(emb_ref[b * BLK:(b + 1) * BLK, :], q_s[...]) * (1.0 / SHARP)
    row = lax.broadcasted_iota(jnp.int32, (BLK, 1), 0) + b * BLK
    return jnp.where(row < end, t, NEG)


def score_kernel(length, got_ref, emb_ref, lens_ref, sums_ref, lse_ref, q_s):
    parts = got_ref.shape[0]
    tokens = q_s.shape[0] // parts
    queries = q_s.shape[0] // length
    for i in range(parts):
        q_s[i * tokens:(i + 1) * tokens, :] = got_ref[i, 0:tokens, :]
    _, _, lens = unpack(got_ref, tokens)
    valid, hot = token_valid(lens, queries, length)
    end = total_length(lens_ref)
    blocks = emb_ref.shape[0] // BLK
    rows = []
    for b in range(blocks):
        t = block_scores(emb_ref, q_s, b, end)
        top = jnp.max(t, axis=0, keepdims=True)
        lse = top + jnp.log(jnp.sum(jnp.exp(t - top), axis=0, keepdims=True))
        lse_ref[b:b + 1, :] = lse
        rows.append(jnp.where(valid, SHARP * lse, 0.0))
    rows.append(jnp.zeros((8 - blocks, rows[0].shape[1]), F32))
    sums = lax.dot_general(
        jnp.concatenate(rows, axis=0), hot, (((1,), (1,)), ((), ())), precision=highest, preferred_element_type=F32
    )
    for i in range(parts):
        sums_ref[i] = sums


def scores(got, emb, lens, length):
    parts = got.shape[0]
    tokens = got.shape[1] - PACK_INT
    total = parts * tokens
    return call(
        functools.partial(score_kernel, length),
        "block_sums",
        [shape_of((parts, 8, LANE), F32), shape_of((8, total), F32)],
        [got, emb, lens],
        [VM, VM, SM],
        [pltpu.VMEM((total, emb.shape[1]), BF16)],
        24,
        2 * emb.shape[0] * total * 128,
        1 << 20,
    )


def loss_kernel(length, got_ref, sums_ref, emb_ref, lse_ref, lens_ref, me_ref, doc_ref, qry_ref, loss_ref, q_s, d_s, s_s):
    parts = got_ref.shape[0]
    tokens = q_s.shape[0] // parts
    queries = q_s.shape[0] // length
    for i in range(parts):
        q_s[i * tokens:(i + 1) * tokens, :] = got_ref[i, 0:tokens, :]
    cand, label, lens = unpack(got_ref, tokens)
    valid, hot = token_valid(lens, queries, length)
    blocks = emb_ref.shape[0] // BLK
    logits = jnp.zeros(cand.shape, F32)
    for i in range(parts):
        for b in range(blocks):
            logits = logits + jnp.where(cand == float(i * blocks + b), sums_ref[i, b:b + 1, :], 0.0)
    logits = SCALE * logits
    top = jnp.max(logits, axis=0, keepdims=True)
    lse = top + jnp.log(jnp.sum(jnp.exp(logits - top), axis=0, keepdims=True))
    choice = lax.broadcasted_iota(jnp.int32, cand.shape, 0).astype(F32) == label
    lane = lax.broadcasted_iota(jnp.int32, (1, LANE), 1)
    picked = jnp.sum(jnp.where(choice, logits, 0.0), axis=0, keepdims=True)
    each = jnp.where(lane < queries, lse - picked, 0.0)
    loss_ref[...] = jnp.broadcast_to(jnp.sum(each, axis=1, keepdims=True), (1, LANE))
    dlogits = SCALE * (jnp.exp(logits - lse) - jnp.where(choice, 1.0, 0.0))
    rows = []
    for b in range(blocks):
        mine = (me_ref[0] * blocks + b).astype(F32)
        rows.append(jnp.sum(jnp.where(cand == mine, dlogits, 0.0), axis=0, keepdims=True))
    rows.append(jnp.zeros((8 - blocks, LANE), F32))
    spread = jnp.dot(jnp.concatenate(rows, axis=0), hot, precision=highest, preferred_element_type=F32)
    end = total_length(lens_ref)
    for b in range(blocks):
        t = block_scores(emb_ref, q_s, b, end)
        weight = jnp.where(valid, spread[b:b + 1, :], 0.0)
        d_s[b * BLK:(b + 1) * BLK, :] = (weight * jnp.exp(t - lse_ref[b:b + 1, :])).astype(BF16)
    doc_ref[...] = nn(d_s[...], q_s[...])
    s_s[...] = d_s[...].T
    qry_ref[...] = nn(s_s[...], emb_ref[...]).reshape(qry_ref.shape)


def retrieval_back(got, sums, emb, lse, lens, me, length):
    parts = got.shape[0]
    tokens = got.shape[1] - PACK_INT
    total = parts * tokens
    docs, proj = emb.shape
    return call(
        functools.partial(loss_kernel, length),
        "retrieval_back",
        [shape_of((docs, proj), F32), shape_of((parts, tokens, proj), F32), shape_of((1, LANE), F32)],
        [got, sums, emb, lse, lens, me],
        [VM, VM, VM, VM, SM, SM],
        [pltpu.VMEM((total, proj), BF16), pltpu.VMEM((docs, total), BF16), pltpu.VMEM((total, docs), BF16)],
        32,
        6 * docs * total * proj,
        2 << 20,
    )


def chain_kernel(
    demb_ref, proj_ref, out_ref, mid_ref, a_ref, b_ref, gains_ref, wp, wd, wg, wu, wo,
    dpj_ref, dbr_ref, dg_ref, du_ref, datt_ref, dmid_ref, dmix_ref, dmixt_ref, dgain_ref,
    wp_s, wd_s, wg_s, wu_s, wo_s, acc_s, sems,
):
    copies = fetch(((wp, wp_s), (wd, wd_s), (wg, wg_s), (wu, wu_s), (wo, wo_s)), sems)
    hidden = a_ref.shape[1]
    if len(demb_ref.shape) == 3:
        dy = demb_ref[0]
        for i in range(1, demb_ref.shape[0]):
            dy = dy + demb_ref[i]
    else:
        dy = demb_ref[...]
    pr = proj_ref[...]
    r = lax.rsqrt(jnp.sum(pr * pr, axis=-1, keepdims=True) + EPS)
    unit = pr * r
    dpj_ref[...] = (r * (dy - unit * jnp.sum(dy * unit, axis=-1, keepdims=True))).astype(BF16)
    copies[0].wait()
    dn3 = nt(dpj_ref[...], wp_s[...])
    dout, dgain3 = norm_back(out_ref[...], gains_ref[2:3, :], dn3)
    dgain_ref[1:2, :] = dgain3
    dmid_ref[...] = dout
    dbr_ref[...] = dout.astype(BF16)
    acc_s[...] = jnp.zeros_like(acc_s)
    for i in range(1, 4):
        copies[i].wait()

    def body(j, carry):
        col = pl.ds(pl.multiple_of(j * CH, CH), CH)
        dh = nt(dbr_ref[...], wd_s[col, :])
        dg = (dh * a_ref[:, col].astype(F32)).astype(BF16)
        du = (dh * b_ref[:, col].astype(F32)).astype(BF16)
        dg_ref[:, col] = dg
        du_ref[:, col] = du
        acc_s[...] += nt(dg, wg_s[:, col]) + nt(du, wu_s[:, col])
        return carry

    lax.fori_loop(0, hidden // CH, body, 0)
    dpart, dgain2 = norm_back(mid_ref[...], gains_ref[1:2, :], acc_s[...])
    dgain_ref[0:1, :] = dgain2
    dmid = dmid_ref[...] + dpart
    dmid_ref[...] = dmid
    datt_ref[...] = dmid.astype(BF16)
    copies[4].wait()
    dmix = nt(datt_ref[...], wo_s[...]).astype(BF16)
    dmix_ref[...] = dmix
    dmixt_ref[...] = dmix.T


def chain(demb, proj, out, mid, a, b, gains, wp, wd, wg, wu, wo, name):
    tokens, width = out.shape
    hidden = a.shape[1]
    weights = (wp, wd, wg, wu, wo)
    return call(
        chain_kernel,
        name,
        [
            shape_of(proj.shape, BF16),
            shape_of((tokens, width), BF16),
            shape_of((tokens, hidden), BF16),
            shape_of((tokens, hidden), BF16),
            shape_of((tokens, width), BF16),
            shape_of((tokens, width), F32),
            shape_of((tokens, width), BF16),
            shape_of((width, tokens), BF16),
            shape_of((2, width), F32),
        ],
        [demb, proj, out, mid, a, b, gains, *weights],
        [VM] * 7 + [HB] * 5,
        [pltpu.VMEM(w.shape, BF16) for w in weights]
        + [pltpu.VMEM((tokens, width), F32), pltpu.SemaphoreType.DMA((5,))],
        56,
        2 * tokens * (width * width + 3 * width * hidden + width * 128),
        30 << 20,
    )


def attention_back_kernel(
    q_ref, k_ref, v_ref, e_ref, il_ref, mixt_ref, dmix_ref, dmixt_ref, dqkv_ref, diag_ref, far_ref,
    kt_s, dqt_s, p_s, ds_s, strip_s, dk_s, dv_s,
):
    tokens, width = q_ref.shape
    tile = min(tokens, 128)
    wide = min(tokens, 256)
    blocks = tokens // tile
    kt_s[...] = k_ref[...].T

    def pair_body(p, carry):
        col = pl.ds(pl.multiple_of(p * LANE, LANE), LANE)
        for s in range(2):
            h = 2 * p + s
            vp = half_lanes(v_ref[:, col], s)
            dm = half_lanes(dmix_ref[:, col], s)
            qm = half_lanes(q_ref[:, col], s)
            rows = pl.ds(pl.multiple_of(p * LANE + 64 * s, 64), 64)
            strip_s[...] = jnp.zeros_like(strip_s)
            far_low = jnp.zeros((8, LANE), F32)
            far_high = jnp.zeros((8, LANE), F32)
            for qc in range(tokens // wide):
                cols = slice(qc * wide, (qc + 1) * wide)
                dt = dmixt_ref[col, cols]
                delta = jnp.sum(
                    dmixt_ref[rows, cols].astype(F32) * mixt_ref[rows, cols].astype(F32), axis=0, keepdims=True
                )
                inverse = il_ref[h, :, cols]
                for kb in range(blocks):
                    ks = slice(kb * tile, (kb + 1) * tile)
                    dp = nn(vp[ks], dt)
                    prob = e_ref[h, ks, cols].astype(F32) * inverse
                    p_s[ks, :] = prob.astype(BF16)
                    ds = (prob * (dp - delta)).astype(BF16)
                    ds_s[ks, :] = ds
                    kept = ds.astype(F32)
                    for qs in range(wide // tile):
                        d = kb - (qc * (wide // tile) + qs)
                        t = kept[:, qs * tile:(qs + 1) * tile]
                        if abs(d) <= 1:
                            lo = (1 - d) * 128
                            strip_s[0:tile, lo:lo + tile] += t
                        else:
                            part = t[0:8]
                            for g in range(1, tile // 8):
                                part = part + t[8 * g:8 * g + 8]
                            if d > 0:
                                far_high = far_high + part
                            else:
                                far_low = far_low + part
                dv = nn(p_s[...], dm[cols])
                dk = nn(ds_s[...], qm[cols])
                if s == 0 and qc == 0:
                    dv_s[...] = dv
                    dk_s[...] = dk
                else:
                    dv_s[...] += dv
                    dk_s[...] += dk
                dqt_s[rows, cols] = nn(kt_s[rows, :], ds_s[...]).astype(BF16)
            fold = strip_s[...]
            size = strip_s.shape[0]
            while size > 8:
                size //= 2
                fold = fold[:size] + pltpu.roll(fold[size:], SPAN - size, 1)
            diag_ref[h] = fold
            far_ref[h, 0:8, :] = far_low
            far_ref[h, 8:16, :] = far_high
        kcol = pl.ds(pl.multiple_of(width + p * LANE, LANE), LANE)
        vcol = pl.ds(pl.multiple_of(2 * width + p * LANE, LANE), LANE)
        dqkv_ref[:, kcol] = dk_s[...].astype(BF16)
        dqkv_ref[:, vcol] = dv_s[...].astype(BF16)
        return carry

    lax.fori_loop(0, width // LANE, pair_body, 0)
    dqkv_ref[:, 0:width] = dqt_s[...].T


def attention_back(q, k, v, e, il, mixt, dmix, dmixt, name):
    tokens, width = q.shape
    heads = e.shape[0]
    tile, wide = min(tokens, 128), min(tokens, 256)
    return call(
        attention_back_kernel,
        name,
        [
            shape_of((tokens, 3 * width), BF16),
            shape_of((heads, 8, SPAN), F32),
            shape_of((heads, 16, LANE), F32),
        ],
        [q, k, v, e, il, mixt, dmix, dmixt],
        [VM] * 8,
        [
            pltpu.VMEM((width, tokens), BF16),
            pltpu.VMEM((width, tokens), BF16),
            pltpu.VMEM((tokens, wide), BF16),
            pltpu.VMEM((tokens, wide), BF16),
            pltpu.VMEM((tile, SPAN), F32),
            pltpu.VMEM((tokens, LANE), F32),
            pltpu.VMEM((tokens, LANE), F32),
        ],
        40,
        10 * tokens * tokens * width,
        16 << 20,
    )


def input_kernel(dqkv_ref, dmid_ref, x_ref, gains_ref, wq, wk, wv, dx_ref, dgain_ref, wq_s, wk_s, wv_s, sems):
    copies = fetch(((wq, wq_s), (wk, wk_s), (wv, wv_s)), sems)
    width = x_ref.shape[1]
    total = None
    for i, w in enumerate((wq_s, wk_s, wv_s)):
        copies[i].wait()
        part = nt(dqkv_ref[:, i * width:(i + 1) * width], w[...])
        total = part if total is None else total + part
    dv, dgain = norm_back(x_ref[...].astype(F32), gains_ref[0:1, :], total)
    dx_ref[...] = dmid_ref[...] + dv
    dgain_ref[...] = dgain


def input_back(dqkv, dmid, x, gains, wq, wk, wv, name):
    tokens, width = x.shape
    return call(
        input_kernel,
        name,
        [shape_of((tokens, width), F32), shape_of((1, width), F32)],
        [dqkv, dmid, x, gains, wq, wk, wv],
        [VM] * 4 + [HB] * 3,
        [pltpu.VMEM(wq.shape, BF16)] * 3 + [pltpu.SemaphoreType.DMA((3,))],
        32,
        6 * tokens * width * width,
        8 << 20,
    )


def put_rows(own_ref, send_ref, core, acc_s, per, offset, lanes, pad=0, extra=None):
    count = own_ref.shape[0]
    for j in range(count):
        for ref, side in ((own_ref, core), (send_ref, 1 - core)):
            rows = pl.ds(pl.multiple_of(2 * per * j + per * side, 8), per)
            pieces = [acc_s[rows, lo:lo + 256] for lo in lanes]
            if extra is not None:
                pieces.append(extra(rows))
            if pad:
                pieces.append(jnp.zeros((pad, 256), F32))
            block = jnp.concatenate(pieces, axis=0) if len(pieces) > 1 else pieces[0]
            ref[j, pl.ds(offset, block.shape[0]), :] = block.astype(BF16)


def ff_grad_kernel(
    core_ref, n2_ref, n2q_ref, hid_ref, hidq_ref, n3_ref, n3q_ref, mixt_ref, mixtq_ref,
    dg_ref, dgq_ref, du_ref, duq_ref, dbr_ref, dbrq_ref, dpj_ref, dpjq_ref, datt_ref, dattq_ref,
    own_ref, send_ref, n2t_s, n2tq_s, hidt_s, hidtq_s, acc_s, accd_s, accp_s,
):
    core = core_ref[0]
    width = n2_ref.shape[1]
    hidden = hid_ref.shape[1]
    count = own_ref.shape[0]
    per, per_down = width // (2 * count), hidden // (2 * count)
    hidt_s[...] = hid_ref[...].T
    hidtq_s[...] = hidq_ref[...].T

    def down(i, carry):
        col = pl.ds(pl.multiple_of(i * 256, 256), 256)
        accd_s[...] = nn(hidt_s[...], dbr_ref[:, col]) + nn(hidtq_s[...], dbrq_ref[:, col])
        put_rows(own_ref, send_ref, core, accd_s, per_down, pl.multiple_of(i * per_down, 16), (0,))
        return carry

    lax.fori_loop(0, width // 256, down, 0)
    base = (width // 256) * per_down
    n2t_s[...] = n2_ref[...].T
    n2tq_s[...] = n2q_ref[...].T
    steps = hidden // 512
    for which, (d, dq) in enumerate(((dg_ref, dgq_ref), (du_ref, duq_ref))):

        def gate(i, carry, d=d, dq=dq, start=base + which * steps * 2 * per):
            col = pl.ds(pl.multiple_of(i * 512, 512), 512)
            acc_s[...] = nn(n2t_s[...], d[:, col]) + nn(n2tq_s[...], dq[:, col])
            put_rows(own_ref, send_ref, core, acc_s, per, pl.multiple_of(start + i * 2 * per, 16), (0, 256))
            return carry

        lax.fori_loop(0, steps, gate, 0)
    base = base + 2 * steps * 2 * per
    acc_s[...] = nn(mixt_ref[...], datt_ref[:, 0:512]) + nn(mixtq_ref[...], dattq_ref[:, 0:512])
    put_rows(own_ref, send_ref, core, acc_s, per, base, (0, 256))
    base = base + 2 * per
    acc_s[:, 0:256] = nn(mixt_ref[...], datt_ref[:, 512:768]) + nn(mixtq_ref[...], dattq_ref[:, 512:768])
    accp_s[...] = nn(n3_ref[...].T, dpj_ref[...]) + nn(n3q_ref[...].T, dpjq_ref[...])

    def proj_rows(rows):
        return jnp.concatenate([accp_s[rows, :], jnp.zeros((per, LANE), F32)], axis=1)

    put_rows(own_ref, send_ref, core, acc_s, per, base, (0,), extra=proj_rows)


def ff_grads(core, pairs, count):
    flat = [a for pair in pairs for a in pair]
    tokens, width = pairs[0][0].shape
    qtokens = pairs[0][1].shape[0]
    hidden = pairs[1][0].shape[1]
    per, per_down = width // (2 * count), hidden // (2 * count)
    rows = (width // 256) * per_down + (2 * (hidden // 256) + 4) * per
    out = shape_of((count, rows, 256), BF16)
    return call(
        ff_grad_kernel,
        "ff_weight_grads",
        [out, out],
        [core, *flat],
        [SM] + [VM] * len(flat),
        [
            pltpu.VMEM((width, tokens), BF16),
            pltpu.VMEM((width, qtokens), BF16),
            pltpu.VMEM((hidden, tokens), BF16),
            pltpu.VMEM((hidden, qtokens), BF16),
            pltpu.VMEM((width, 512), F32),
            pltpu.VMEM((hidden, 256), F32),
            pltpu.VMEM((width, LANE), F32),
        ],
        48,
        2 * (tokens + 256) * (width * width + 3 * width * hidden),
        24 << 20,
    )


def qkv_grad_kernel(core_ref, n1_ref, n1q_ref, d_ref, dq_ref, own_ref, send_ref, n1t_s, n1tq_s, acc_s):
    core = core_ref[0]
    width = n1_ref.shape[1]
    count = own_ref.shape[0]
    per = width // (2 * count)
    n1t_s[...] = n1_ref[...].T
    n1tq_s[...] = n1q_ref[...].T
    steps = (3 * width) // 512

    def body(i, carry):
        col = pl.ds(pl.multiple_of(i * 512, 512), 512)
        acc_s[...] = nn(n1t_s[...], d_ref[:, col]) + nn(n1tq_s[...], dq_ref[:, col])
        put_rows(own_ref, send_ref, core, acc_s, per, pl.multiple_of(i * 2 * per, 16), (0, 256))
        return carry

    lax.fori_loop(0, steps, body, 0)
    lo = steps * 512
    acc_s[:, 0:256] = nn(n1t_s[...], d_ref[:, lo:lo + 256]) + nn(n1tq_s[...], dq_ref[:, lo:lo + 256])
    put_rows(own_ref, send_ref, core, acc_s, per, steps * 2 * per, (0,), pad=8)


def qkv_grads(core, n1, n1q, d, dq, count):
    tokens, width = n1.shape
    per = width // (2 * count)
    rows = 9 * per + 8
    out = shape_of((count, rows, 256), BF16)
    return call(
        qkv_grad_kernel,
        "qkv_weight_grads",
        [out, out],
        [core, n1, n1q, d, dq],
        [SM] + [VM] * 4,
        [
            pltpu.VMEM((width, tokens), BF16),
            pltpu.VMEM((width, n1q.shape[0]), BF16),
            pltpu.VMEM((width, 512), F32),
        ],
        32,
        2 * (tokens + 256) * 3 * width * width,
        10 << 20,
    )


def shard_sum(own, send, n_dp, n_grp):
    dp, grp = lax.axis_index("dp"), lax.axis_index("grp")
    nz = n_dp // 2
    z, x, y = dp // 2, dp % 2, grp // 2
    rows, cols = own.shape[1:]
    got = lax.ppermute(send, "grp", [(i, i ^ 1) for i in range(n_grp)])
    own5, got5 = own.reshape(nz, 2, 2, rows, cols), got.reshape(nz, 2, 2, rows, cols)

    def piece(xx, yy):
        take = lambda a: lax.dynamic_slice(a, (0, xx, yy, 0, 0), (nz, 1, 1, rows, cols)).reshape(nz, rows, cols)
        return take(own5).astype(F32) + take(got5).astype(F32)

    across = [(d * n_grp + g, (d ^ 1) * n_grp + (g ^ 2)) for d in range(n_dp) for g in range(n_grp)]
    from_xy = lax.ppermute(piece(1 - x, 1 - y).astype(BF16), ("dp", "grp"), across)
    from_x = lax.ppermute(piece(1 - x, y).astype(BF16), "dp", [(d, d ^ 1) for d in range(n_dp)])
    from_y = lax.ppermute(piece(x, 1 - y).astype(BF16), "grp", [(g, g ^ 2) for g in range(n_grp)])
    line = piece(x, y) + from_x.astype(F32) + from_y.astype(F32) + from_xy.astype(F32)
    total = lax.dynamic_slice(line, (z, 0, 0), (1, rows, cols))[0]
    for k in range(1, nz):
        part = lax.dynamic_slice(line, ((z + k) % nz, 0, 0), (1, rows, cols))[0].astype(BF16)
        total = total + lax.ppermute(part, "dp", [(d, (d + 2 * k) % n_dp) for d in range(n_dp)]).astype(F32)
    return total


def unfold(rows, per, width):
    parts = width // 256
    return jnp.transpose(rows.reshape(parts, per, 256), (1, 0, 2)).reshape(per, width)


def on_device(
    n_dp, n_grp, doc_tokens, doc_lengths, query_tokens, query_lengths, candidates, labels, gain_attn, w_query, w_key,
    w_value, w_out, bias_table, gain_ffn, w_gate, w_up, w_down, gain_final, w_proj,
):
    doc_rows, doc_len, width = doc_tokens.shape
    query_rows, query_len = query_tokens.shape[:2]
    hidden = w_gate.shape[1]
    bucket_total, heads = bias_table.shape
    devices = n_dp * n_grp
    axes = ("dp", "grp")
    dp, grp = lax.axis_index("dp"), lax.axis_index("grp")
    x_doc = doc_tokens.reshape(doc_len, width)
    x_qry = query_tokens.reshape(query_rows * query_len, width)
    gains = jnp.stack([gain_attn, gain_ffn, gain_final]).astype(F32)
    weights = (w_query, w_key, w_value, w_out, w_gate, w_up, w_down, w_proj)
    hot = jnp.asarray(strip_onehot(), BF16)
    ints = jnp.concatenate([candidates.T, labels[None, :], query_lengths[None, :]]).astype(BF16)
    ints = jnp.pad(ints, ((0, PACK_INT - ints.shape[0]), (0, LANE - query_rows)))

    (q_q, q_k, q_v, q_e, q_il, q_mixt, q_mid, q_n1, q_n2, q_hid, q_a, q_b, q_out, q_n3, q_proj, packed, base) = forward(
        x_qry, query_lengths, gains, (bias_table, hot, ints), weights, False, heads
    )
    got = lax.all_to_all(jnp.broadcast_to(packed[None], (n_dp, *packed.shape)), "dp", 0, 0, tiled=True)
    (d_q, d_k, d_v, d_e, d_il, d_mixt, d_mid, d_n1, d_n2, d_hid, d_a, d_b, d_out, d_n3, d_proj, emb) = forward(
        x_doc, doc_lengths, gains, base, weights, True, heads
    )
    sums, lse = scores(got, emb, doc_lengths, query_len)
    sums = lax.all_to_all(sums, "dp", 0, 0, tiled=True)
    demb_doc, demb_part, loss_group = retrieval_back(
        got, sums, emb, lse, doc_lengths, dp.astype(jnp.int32).reshape(1), query_len
    )
    demb_qry = lax.all_to_all(demb_part, "dp", 0, 0, tiled=True)
    back = (w_proj, w_down, w_gate, w_up, w_out)
    d_dpj, d_dbr, d_dg, d_du, d_datt, d_dmid, d_dmix, d_dmixt, d_dgain = chain(
        demb_doc, d_proj, d_out, d_mid, d_a, d_b, gains, *back, "doc_ff_back"
    )
    q_dpj, q_dbr, q_dg, q_du, q_datt, q_dmid, q_dmix, q_dmixt, q_dgain = chain(
        demb_qry, q_proj, q_out, q_mid, q_a, q_b, gains, *back, "query_ff_back"
    )
    fast = (n_dp, n_grp) == (8, 4)
    core = (grp % 2).astype(jnp.int32).reshape(1)
    if fast:
        ff_own, ff_send = ff_grads(
            core,
            (
                (d_n2, q_n2), (d_hid, q_hid), (d_n3, q_n3), (d_mixt, q_mixt), (d_dg, q_dg), (d_du, q_du),
                (d_dbr, q_dbr), (d_dpj, q_dpj), (d_datt, q_datt),
            ),
            devices // 2,
        )
        ff = shard_sum(ff_own, ff_send, n_dp, n_grp)
    d_dqkv, d_diag, d_far = attention_back(d_q, d_k, d_v, d_e, d_il, d_mixt, d_dmix, d_dmixt, "doc_attention_back")
    q_dqkv, q_diag, q_far = attention_back(q_q, q_k, q_v, q_e, q_il, q_mixt, q_dmix, q_dmixt, "query_attention_back")
    if fast:
        qkv_own, qkv_send = qkv_grads(core, d_n1, q_n1, d_dqkv, q_dqkv, devices // 2)
        qkv = shard_sum(qkv_own, qkv_send, n_dp, n_grp)
    doc_grad, d_dgain1 = input_back(d_dqkv, d_dmid, x_doc, gains, w_query, w_key, w_value, "doc_input_back")
    query_grad, q_dgain1 = input_back(q_dqkv, q_dmid, x_qry, gains, w_query, w_key, w_value, "query_input_back")

    far = jnp.sum((d_far + q_far).reshape(heads, 2, -1), axis=-1)
    dtable = lax.dot_general(
        hot.astype(F32),
        (d_diag + q_diag).reshape(heads, -1),
        (((1,), (1,)), ((), ())),
        precision=highest,
        preferred_element_type=F32,
    )
    half = bucket_total // 2
    dtable = dtable.at[half - 1].add(far[:, 0]).at[bucket_total - 1].add(far[:, 1])
    dgains = jnp.concatenate([d_dgain1 + q_dgain1, d_dgain + q_dgain])
    part_loss = loss_group[0, 0] / n_dp
    query_total = query_rows * devices
    per = width // devices

    small = jnp.transpose(dgains.reshape(3, devices, per), (1, 0, 2)).reshape(devices, 3 * per)
    same = jnp.concatenate([dtable.reshape(-1), part_loss.reshape(1)])
    small = jnp.concatenate([small, jnp.broadcast_to(same[None], (devices, same.shape[0]))], axis=1)
    cut = -(-small.shape[1] // LANE) * LANE
    small = jnp.pad(small, ((0, 0), (0, cut - small.shape[1])))
    small = jnp.sum(lax.all_to_all(small, axes, 0, 0, tiled=True), axis=0)
    shard_gains = small[: 3 * per].reshape(3, per)
    table_grad = small[3 * per:3 * per + bucket_total * heads].reshape(bucket_total, heads)
    loss = small[3 * per + bucket_total * heads] / query_total

    if fast:
        per_down = hidden // devices
        at = (width // 256) * per_down
        shard_down = unfold(ff[:at], per_down, width)
        shard_gate = unfold(ff[at:at + (hidden // 256) * per], per, hidden)
        at = at + (hidden // 256) * per
        shard_up = unfold(ff[at:at + (hidden // 256) * per], per, hidden)
        at = at + (hidden // 256) * per
        shard_out = unfold(ff[at:at + 3 * per], per, width)
        shard_proj = ff[at + 3 * per:at + 4 * per, : w_proj.shape[1]]
        shard_query, shard_key, shard_value = (unfold(qkv[i * 3 * per:(i + 1) * 3 * per], per, width) for i in range(3))
    else:

        def grad(left, right):
            product = tn(jnp.concatenate(left), jnp.concatenate(right))
            return lax.psum_scatter(product, axes, scatter_dimension=0, tiled=True)

        n1s = (d_n1, q_n1)
        shard_query, shard_key, shard_value = (
            grad(n1s, (d_dqkv[:, i * width:(i + 1) * width], q_dqkv[:, i * width:(i + 1) * width])) for i in range(3)
        )
        shard_out = grad((d_mixt.T, q_mixt.T), (d_datt, q_datt))
        shard_gate = grad((d_n2, q_n2), (d_dg, q_dg))
        shard_up = grad((d_n2, q_n2), (d_du, q_du))
        shard_down = grad((d_hid, q_hid), (d_dbr, q_dbr))
        shard_proj = grad((d_n3, q_n3), (d_dpj, q_dpj))
    return (
        loss,
        doc_grad.reshape(doc_rows, doc_len, width),
        query_grad.reshape(query_rows, query_len, width),
        shard_gains[0],
        shard_query,
        shard_key,
        shard_value,
        shard_out,
        table_grad,
        shard_gains[1],
        shard_gate,
        shard_up,
        shard_down,
        shard_gains[2],
        shard_proj,
    )


def solution(mesh):
    both = ("dp", "grp")
    rows3, rows2, rows1 = P(both, None, None), P(both, None), P(both)
    in_specs = (rows3, rows2, rows3, rows1, rows2, rows1) + (P(),) * 12
    out_specs = (
        P(), rows3, rows3, rows1, rows2, rows2, rows2, rows2, P(), rows1, rows2, rows2, rows2, rows1, rows2,
    )
    body = functools.partial(on_device, mesh.shape["dp"], mesh.shape["grp"])
    return jax.shard_map(body, mesh=mesh, in_specs=in_specs, out_specs=out_specs, check_vma=False)
```

```python
import functools
import itertools
import math

import jax
import jax.numpy as jnp
import numpy as np
from jax import lax
from jax.experimental import pallas as pl
from jax.experimental.pallas import tpu as pltpu
from jax.sharding import PartitionSpec as P

F32, BF16 = jnp.float32, jnp.bfloat16
BUCKETS = 32
DIST = 128
BLK = 128
EPS = 1e-6
SHARP = 0.25
SCALE = 16.0
NEG = -1e30
GELU_A = math.sqrt(2.0 / math.pi)
GELU_B = 0.044715
SPAN = 512
CH = 512
LANE = 128
COST = 20
AHEAD = 1 << 30
PACK_INT = 48
highest = lax.Precision.HIGHEST


def nn(a, b):
    return jnp.dot(a, b, preferred_element_type=F32)


def nt(a, b):
    return lax.dot_general(a, b, (((1,), (1,)), ((), ())), preferred_element_type=F32)


def tn(a, b):
    return lax.dot_general(a, b, (((0,), (0,)), ((), ())), preferred_element_type=F32)


def bucket_of(offsets):
    half = BUCKETS // 2
    exact = half // 2
    dist = np.abs(offsets)
    scaled = np.log(np.maximum(dist, 1) / exact) / np.log(DIST / exact) * (half - exact)
    far = np.minimum(exact + np.maximum(scaled, 0).astype(np.int64), half - 1)
    return (offsets > 0) * half + np.where(dist < exact, dist, far)


def strip_onehot():
    j = np.arange(SPAN)
    offset = np.where(j < 384, 128 - j, 640 - j)
    index = np.stack([bucket_of(offset[(j - r) % SPAN]) for r in range(8)]).reshape(-1)
    return (index[None, :] == np.arange(BUCKETS)[:, None]).astype(np.float32)


VM = pl.BlockSpec(memory_space=pltpu.VMEM)
HB = pl.BlockSpec(memory_space=pl.ANY)


def by_part(run):
    return run if run[0][3] == 1 else sorted(run, key=lambda entry: entry[1])


class Io:
    def __init__(self, ins, outs, sems):
        self.ins, self.outs, self.sems, self.used = {}, {}, sems, 0
        self.going, self.queue, self.flying = [], [], 0
        for src, buf, parts in ins:
            self.ins[id(buf)] = (src, buf, parts, self.used)
            size = math.prod(buf.shape) * buf.dtype.itemsize // abs(parts)
            self.queue += [(id(buf), p, size, abs(parts)) for p in range(abs(parts))]
            self.used += abs(parts)
        for buf, dst in outs:
            self.outs[id(buf)] = (buf, dst)
        self.queue = [entry for _, run in itertools.groupby(self.queue, lambda e: e[3]) for entry in by_part(list(run))]
        self.feed()

    def feed(self, upto=()):
        upto = {id(buf) for buf in upto}
        while self.queue and (self.flying < AHEAD or any(entry[0] in upto for entry in self.queue)):
            key, p, size, _ = self.queue.pop(0)
            self.chunk(*self.ins[key], p).start()
            self.flying += size

    def landed(self, buf):
        self.flying -= math.prod(buf.shape) * buf.dtype.itemsize
        self.feed()

    def chunk(self, src, buf, parts, first, p):
        if parts == 1:
            return pltpu.make_async_copy(src, buf, self.sems.at[first])
        if parts > 0:
            size = buf.shape[0] // parts
            cut = (pl.ds(p * size if isinstance(p, int) else pl.multiple_of(p * size, 2), size),)
        else:
            size = buf.shape[1] // -parts
            cut = (slice(None), pl.ds(p * size if isinstance(p, int) else pl.multiple_of(p * size, LANE), size))
        return pltpu.make_async_copy(src.at[cut], buf.at[cut], self.sems.at[first + p])

    def need(self, *bufs):
        for buf in bufs:
            entry = self.ins.get(id(buf))
            if entry is not None:
                self.feed((buf,))
                for p in range(abs(entry[2])):
                    self.chunk(*entry, p).wait()
                del self.ins[id(buf)]
                self.landed(buf)

    def need_part(self, p, *bufs):
        for buf in bufs:
            self.chunk(*self.ins[id(buf)], p).wait()

    def had(self, *bufs):
        for buf in bufs:
            self.ins.pop(id(buf))
            self.landed(buf)

    def done(self, *bufs):
        for buf in bufs:
            if id(buf) in self.outs:
                src, dst = self.outs.pop(id(buf))
                self.push(src, dst)

    def done_rows(self, buf, start, size):
        src, dst = self.outs[id(buf)]
        rows = (slice(None), pl.ds(start, size))
        self.push(src.at[rows], dst.at[rows])

    def gone(self, buf):
        self.outs.pop(id(buf))

    def push(self, src, dst):
        copy = pltpu.make_async_copy(src, dst, self.sems.at[self.used])
        self.used += 1
        copy.start()
        self.going.append(copy)

    def close(self):
        self.need(*[entry[1] for entry in list(self.ins.values())])
        self.done(*[entry[0] for entry in list(self.outs.values())])
        for copy in self.going:
            copy.wait()


def call(kernel, name, ins, outs, scratch, mib, flops, moved=8 << 20):
    args, in_specs, out_specs, out_shape, buffers, sems = [], [], [], [], [], 0
    for array, kind in ins:
        if kind == "r":
            args.append(array)
            in_specs.append(HB)
        elif kind[0] == "h":
            args.append(pltpu.with_memory_space_constraint(array, pltpu.HBM))
            in_specs.append(HB)
            buffers.append(pltpu.VMEM(array.shape, array.dtype))
            sems += abs(int(kind[1:] or 1))
        else:
            args.append(array)
            in_specs.append(VM)
    for shape, dtype, kind in outs:
        if kind == "h":
            out_shape.append(pltpu.HBM(shape, dtype))
            out_specs.append(HB)
            buffers.append(pltpu.VMEM(shape, dtype))
            sems += 4
        else:
            out_shape.append(jax.ShapeDtypeStruct(shape, dtype))
            out_specs.append(VM)

    def body(*refs):
        n_in, n_out, n_buf = len(ins), len(outs), len(buffers)
        given, made = list(refs[:n_in]), list(refs[n_in:n_in + n_out])
        bufs = iter(refs[n_in + n_out:n_in + n_out + n_buf])
        rest = refs[n_in + n_out + n_buf:]
        reads, writes = [], []
        for i, (_, kind) in enumerate(ins):
            if kind[0] == "h":
                buf = next(bufs)
                reads.append((given[i], buf, int(kind[1:] or 1)))
                given[i] = buf
        for i, (_, _, kind) in enumerate(outs):
            if kind == "h":
                buf = next(bufs)
                writes.append((buf, made[i]))
                made[i] = buf
        io = Io(reads, writes, rest[-1])
        kernel(io, *given, *made, *rest[:-1])
        io.close()

    return pl.pallas_call(
        body,
        name=name,
        out_shape=out_shape,
        in_specs=in_specs,
        out_specs=out_specs,
        scratch_shapes=buffers + scratch + [pltpu.SemaphoreType.DMA((max(sems, 1),))],
        compiler_params=pltpu.CompilerParams(vmem_limit_bytes=mib << 20),
        cost_estimate=pl.CostEstimate(flops=int(flops) * COST, bytes_accessed=int(moved) * COST, transcendentals=0),
    )(*args)


def half_lanes(values, side):
    lane = lax.broadcasted_iota(jnp.int32, (1, LANE), 1)
    return jnp.where((lane // 64) == side, values.astype(F32), 0.0).astype(BF16)


def norm_back(values, gain, dn):
    s = lax.rsqrt(jnp.mean(values * values, axis=-1, keepdims=True) + EPS)
    unit = values * s
    t = dn * gain
    return s * (t - unit * jnp.mean(t * unit, axis=-1, keepdims=True))


def forward_kernel(
    is_doc, io, x_ref, lens_ref, gains_ref, extra_ref, wq_s, wk_s, wv_s, wo_s, wg_s, wu_s, wd_s, wp_s,
    q_ref, k_ref, v_ref, e_ref, il_ref, mixt_ref, mid_ref, n1_ref, n2_ref, hid_ref, a_ref, b_ref,
    out_ref, n3_ref, proj_ref, emb_ref, *rest,
):
    if is_doc:
        base_ref, tail = extra_ref, rest
    else:
        tab_ref, hot_ref, cand_ref, label_ref = extra_ref
        base_ref, tail = rest[0], rest[1:]
    mask_s, strip_s, s_s, vt_s = tail
    tokens, width = x_ref.shape
    hidden = wg_s.shape[1]
    heads = e_ref.shape[0]
    io.need(lens_ref)
    if not is_doc:
        io.need(tab_ref, hot_ref)
        for r in range(8):
            rows = tn(tab_ref[...], hot_ref[:, r * SPAN:(r + 1) * SPAN])
            for h in range(heads):
                base_ref[h, r:r + 1, :] = rows[h:h + 1, :]
    io.need(x_ref)
    x = x_ref[...].astype(F32)
    s1 = lax.rsqrt(jnp.mean(x * x, axis=-1, keepdims=True) + EPS)
    n1_ref[...] = (x * s1 * gains_ref[0:1, :]).astype(BF16)
    io.done(n1_ref)
    tile = min(tokens, 128)
    wide = min(tokens, 256)
    blocks = tokens // tile
    row_id = lax.broadcasted_iota(jnp.int32, (tokens, 1), 0)
    col_id = lax.broadcasted_iota(jnp.int32, (1, tokens), 1)
    if is_doc:
        seg_k = jnp.zeros((tokens, 1), jnp.int32)
        seg_q = jnp.zeros((1, tokens), jnp.int32)
        end = jnp.zeros((1, 1), jnp.int32)
        for i in range(lens_ref.shape[1]):
            end = end + lens_ref[0:1, i:i + 1]
            seg_k = seg_k + (row_id >= end).astype(jnp.int32)
            seg_q = seg_q + (col_id >= end).astype(jnp.int32)
    else:
        count = lens_ref.shape[1]
        length = tokens // count
        seg_q = col_id // length
        seg_k = jnp.full((tokens, 1), -1, jnp.int32)
        for i in range(count):
            inside = (row_id >= i * length) & (row_id < i * length + lens_ref[0:1, i:i + 1])
            seg_k = jnp.where(inside, i, seg_k)
    mask_s[...] = jnp.where(seg_k == seg_q, 0.0, NEG)
    for i, (w, o) in enumerate(((wq_s, q_ref), (wk_s, k_ref), (wv_s, v_ref))):
        io.need(w)
        o[...] = nn(n1_ref[...], w[...]).astype(BF16)
        io.done(o)
    vt_s[...] = v_ref[...].T
    if is_doc:
        io.need(base_ref)
    else:
        io.done(base_ref)

    def pair_body(p, carry):
        col = pl.ds(pl.multiple_of(p * LANE, LANE), LANE)
        for s in range(2):
            h = 2 * p + s
            first = base_ref[h]
            for g in range(tile // 8):
                strip_s[8 * g:8 * g + 8, :] = pltpu.roll(first, 8 * g, 1) if g else first
            low_far, high_far = first[0:1, 256:256 + tile], first[0:1, 384:384 + tile]
            kp = half_lanes(k_ref[:, col], s)
            rows = pl.ds(pl.multiple_of(p * LANE + 64 * s, 64), 64)
            for qc in range(tokens // wide):
                cols = slice(qc * wide, (qc + 1) * wide)
                qp = q_ref[cols, col]
                top = None
                for kb in range(blocks):
                    ks = slice(kb * tile, (kb + 1) * tile)
                    scores = nt(kp[ks], qp)
                    tops = []
                    for qs in range(wide // tile):
                        qb = qc * (wide // tile) + qs
                        d = kb - qb
                        t = scores[:, qs * tile:(qs + 1) * tile]
                        if abs(d) <= 1:
                            lo = (1 - d) * 128
                            t = t + strip_s[:, lo:lo + tile]
                        else:
                            t = t + (high_far if d > 0 else low_far)
                        t = t + mask_s[ks, qb * tile:(qb + 1) * tile]
                        s_s[ks, qs * tile:(qs + 1) * tile] = t
                        tops.append(jnp.max(t, axis=0, keepdims=True))
                    mk = jnp.concatenate(tops, axis=1) if len(tops) > 1 else tops[0]
                    top = mk if top is None else jnp.maximum(top, mk)
                total = None
                for kb in range(blocks):
                    ks = slice(kb * tile, (kb + 1) * tile)
                    e = jnp.exp(s_s[ks, :] - top)
                    part = jnp.sum(e, axis=0, keepdims=True)
                    total = part if total is None else total + part
                    e_ref[h, ks, cols] = e.astype(BF16)
                inverse = 1.0 / total
                il_ref[h, :, cols] = inverse
                o = nn(vt_s[rows, :], e_ref[h, :, cols])
                mixt_ref[rows, cols] = (o * inverse).astype(BF16)
        return carry

    lax.fori_loop(0, width // LANE, pair_body, 0)
    io.done(e_ref, mixt_ref)
    io.need(wo_s)
    mid_ref[...] = x_ref[...].astype(F32) + nn(mixt_ref[...].T, wo_s[...])
    mid = mid_ref[...]
    s2 = lax.rsqrt(jnp.mean(mid * mid, axis=-1, keepdims=True) + EPS)
    n2_ref[...] = (mid * s2 * gains_ref[1:2, :]).astype(BF16)
    io.done(mid_ref, n2_ref)

    io.feed((wg_s, wu_s))

    def ff_body(j, carry):
        io.need_part(j, wg_s, wu_s)
        col = pl.ds(pl.multiple_of(j * CH, CH), CH)
        g = nn(n2_ref[...], wg_s[:, col])
        u = nn(n2_ref[...], wu_s[:, col])
        sq = g * g
        t = jnp.tanh(GELU_A * g * (1.0 + GELU_B * sq))
        half = 0.5 + 0.5 * t
        gel = g * half
        slope = half + (0.5 * GELU_A) * g * (1.0 - t * t) * (1.0 + 3.0 * GELU_B * sq)
        hid_ref[:, col] = (gel * u).astype(BF16)
        a_ref[:, col] = (u * slope).astype(BF16)
        b_ref[:, col] = gel.astype(BF16)
        return carry

    lax.fori_loop(0, hidden // CH, ff_body, 0)
    io.had(wg_s, wu_s)
    io.done(hid_ref, a_ref, b_ref)
    io.need(wd_s)
    out_ref[...] = mid_ref[...] + nn(hid_ref[...], wd_s[...])
    o = out_ref[...]
    s3 = lax.rsqrt(jnp.mean(o * o, axis=-1, keepdims=True) + EPS)
    n3_ref[...] = (o * s3 * gains_ref[2:3, :]).astype(BF16)
    io.done(out_ref, n3_ref)
    io.need(wp_s)
    pr = nn(n3_ref[...], wp_s[...])
    proj_ref[...] = pr
    emb = (pr * lax.rsqrt(jnp.sum(pr * pr, axis=-1, keepdims=True) + EPS)).astype(BF16)
    if is_doc:
        emb_ref[...] = emb
    else:
        emb_ref[0:tokens, :] = emb
        io.need(cand_ref, label_ref)
        emb_ref[tokens:, :] = pack_ints(cand_ref, label_ref, lens_ref)


def pack_ints(cand_ref, label_ref, lens_ref):
    count = cand_ref.shape[1]
    eye = lax.broadcasted_iota(jnp.int32, (count, count), 0) == lax.broadcasted_iota(jnp.int32, (count, count), 1)
    lane = lax.broadcasted_iota(jnp.int32, (1, LANE), 1)
    row = lax.broadcasted_iota(jnp.int32, (PACK_INT, 1), 0)
    packed = jnp.zeros((PACK_INT, LANE), F32)
    for a in range(cand_ref.shape[0]):
        values = jnp.where(eye, cand_ref[a:a + 1, :].astype(F32), 0.0)
        column = jnp.sum(values, axis=1, keepdims=True)
        column = jnp.concatenate([column, jnp.zeros((PACK_INT - count, 1), F32)], axis=0)
        column = jnp.where(row == count, label_ref[0:1, a:a + 1].astype(F32), column)
        column = jnp.where(row == count + 1, lens_ref[0:1, a:a + 1].astype(F32), column)
        packed = jnp.where(lane == a, column, packed)
    return packed.astype(BF16)


def forward(x, lens, gains, extra, weights, is_doc, heads):
    tokens, width = x.shape
    hidden = weights[4].shape[1]
    proj = weights[7].shape[1]
    outs = [((tokens, width), BF16, "h")] * 3 + [
        ((heads, tokens, tokens), BF16, "h"),
        ((heads, 1, tokens), F32, "v"),
        ((width, tokens), BF16, "h"),
        ((tokens, width), F32, "h"),
        ((tokens, width), BF16, "h"),
        ((tokens, width), BF16, "h"),
        ((tokens, hidden), BF16, "h"),
        ((tokens, hidden), BF16, "h"),
        ((tokens, hidden), BF16, "h"),
        ((tokens, width), F32, "h"),
        ((tokens, width), BF16, "h"),
        ((tokens, proj), F32, "h"),
        ((tokens + (0 if is_doc else PACK_INT), proj), BF16, "v"),
    ]
    tile = min(tokens, 128)
    scratch = [
        pltpu.VMEM((tokens, tokens), F32),
        pltpu.VMEM((tile, SPAN), F32),
        pltpu.VMEM((tokens, min(tokens, 256)), F32),
        pltpu.VMEM((width, tokens), BF16),
    ]
    steps = weights[4].shape[1] // CH
    streams = [(w, f"h-{steps}" if w.shape == weights[4].shape else "h") for w in weights]
    ins = [(x, "h"), (lens, "h"), (gains, "v")]
    if is_doc:
        kernel = functools.partial(forward_kernel, True)
        ins = ins + [(extra, "h")] + streams
    else:
        outs.append(((heads, 8, SPAN), F32, "h"))

        def kernel(io, x_ref, lens_ref, gains_ref, tab_ref, hot_ref, cand_ref, label_ref, *rest):
            forward_kernel(False, io, x_ref, lens_ref, gains_ref, (tab_ref, hot_ref, cand_ref, label_ref), *rest)

        ins = ins + [(item, "h") for item in extra] + streams
    flops = 2 * tokens * (4 * width * width + 3 * width * hidden + width * proj) + 4 * tokens * tokens * width
    return call(kernel, "doc_forward" if is_doc else "query_forward", ins, outs, scratch, 50, flops, 30 << 20)


def unpack(got_ref, tokens):
    parts = got_ref.shape[0]
    own = 2
    lane = lax.broadcasted_iota(jnp.int32, (1, LANE), 1)
    ints = None
    for i in range(parts):
        block = got_ref[i, tokens:, :].astype(F32)
        if i:
            block = pltpu.roll(block, own * i, 1)
        block = jnp.where((lane // own) == i, block, 0.0)
        ints = block if ints is None else ints + block
    return ints[0:32, :], ints[32:33, :], ints[33:34, :]


def expand_onehot(queries, length):
    col = lax.broadcasted_iota(jnp.int32, (LANE, queries * length), 1)
    row = lax.broadcasted_iota(jnp.int32, (LANE, queries * length), 0)
    return ((col // length) == row).astype(F32)


def token_valid(lens, queries, length):
    hot = expand_onehot(queries, length)
    spread = jnp.dot(jnp.broadcast_to(lens, (8, LANE)), hot, precision=highest, preferred_element_type=F32)[0:1]
    place = lax.broadcasted_iota(jnp.int32, (1, queries * length), 1) % length
    return place.astype(F32) < spread, hot


def total_length(lens_ref):
    end = jnp.zeros((1, 1), jnp.int32)
    for i in range(lens_ref.shape[1]):
        end = end + lens_ref[0:1, i:i + 1]
    return end


def block_scores(emb_ref, q_s, b, end):
    t = nt(emb_ref[b * BLK:(b + 1) * BLK, :], q_s[...]) * (1.0 / SHARP)
    row = lax.broadcasted_iota(jnp.int32, (BLK, 1), 0) + b * BLK
    return jnp.where(row < end, t, NEG)


def score_kernel(length, io, got_ref, emb_ref, lens_ref, sums_ref, lse_ref, q_s):
    parts = got_ref.shape[0]
    tokens = q_s.shape[0] // parts
    queries = q_s.shape[0] // length
    for i in range(parts):
        q_s[i * tokens:(i + 1) * tokens, :] = got_ref[i, 0:tokens, :]
    _, _, lens = unpack(got_ref, tokens)
    valid, hot = token_valid(lens, queries, length)
    io.need(lens_ref)
    end = total_length(lens_ref)
    blocks = emb_ref.shape[0] // BLK
    rows = []
    for b in range(blocks):
        t = block_scores(emb_ref, q_s, b, end)
        top = jnp.max(t, axis=0, keepdims=True)
        lse = top + jnp.log(jnp.sum(jnp.exp(t - top), axis=0, keepdims=True))
        lse_ref[b:b + 1, :] = lse
        rows.append(jnp.where(valid, SHARP * lse, 0.0))
    rows.append(jnp.zeros((8 - blocks, rows[0].shape[1]), F32))
    sums = lax.dot_general(
        jnp.concatenate(rows, axis=0), hot, (((1,), (1,)), ((), ())), precision=highest, preferred_element_type=F32
    )
    for i in range(parts):
        sums_ref[i] = sums


def scores(got, emb, lens, length):
    parts = got.shape[0]
    tokens = got.shape[1] - PACK_INT
    total = parts * tokens
    return call(
        functools.partial(score_kernel, length),
        "block_sums",
        [(got, "v"), (emb, "v"), (lens, "h")],
        [((parts, 8, LANE), F32, "v"), ((8, total), F32, "v")],
        [pltpu.VMEM((total, emb.shape[1]), BF16)],
        24,
        2 * emb.shape[0] * total * 128,
        1 << 20,
    )


def loss_kernel(length, io, got_ref, sums_ref, emb_ref, lse_ref, lens_ref, doc_ref, qry_ref, loss_ref, q_s, d_s, s_s):
    parts = got_ref.shape[0]
    tokens = q_s.shape[0] // parts
    queries = q_s.shape[0] // length
    for i in range(parts):
        q_s[i * tokens:(i + 1) * tokens, :] = got_ref[i, 0:tokens, :]
    cand, label, lens = unpack(got_ref, tokens)
    valid, hot = token_valid(lens, queries, length)
    blocks = emb_ref.shape[0] // BLK
    logits = jnp.zeros(cand.shape, F32)
    for i in range(parts):
        for b in range(blocks):
            logits = logits + jnp.where(cand == float(i * blocks + b), sums_ref[i, b:b + 1, :], 0.0)
    logits = SCALE * logits
    top = jnp.max(logits, axis=0, keepdims=True)
    lse = top + jnp.log(jnp.sum(jnp.exp(logits - top), axis=0, keepdims=True))
    choice = lax.broadcasted_iota(jnp.int32, cand.shape, 0).astype(F32) == label
    lane = lax.broadcasted_iota(jnp.int32, (1, LANE), 1)
    picked = jnp.sum(jnp.where(choice, logits, 0.0), axis=0, keepdims=True)
    each = jnp.where(lane < queries, lse - picked, 0.0)
    loss_ref[...] = jnp.broadcast_to(jnp.sum(each, axis=1, keepdims=True), (1, LANE))
    dlogits = SCALE * (jnp.exp(logits - lse) - jnp.where(choice, 1.0, 0.0))
    me = lax.axis_index("dp").astype(jnp.int32)
    rows = []
    for b in range(blocks):
        mine = (me * blocks + b).astype(F32)
        rows.append(jnp.sum(jnp.where(cand == mine, dlogits, 0.0), axis=0, keepdims=True))
    rows.append(jnp.zeros((8 - blocks, LANE), F32))
    spread = jnp.dot(jnp.concatenate(rows, axis=0), hot, precision=highest, preferred_element_type=F32)
    io.need(lens_ref)
    end = total_length(lens_ref)
    for b in range(blocks):
        t = block_scores(emb_ref, q_s, b, end)
        weight = jnp.where(valid, spread[b:b + 1, :], 0.0)
        d_s[b * BLK:(b + 1) * BLK, :] = (weight * jnp.exp(t - lse_ref[b:b + 1, :])).astype(BF16)
    doc_ref[...] = nn(d_s[...], q_s[...])
    s_s[...] = d_s[...].T
    qry_ref[...] = nn(s_s[...], emb_ref[...]).reshape(qry_ref.shape)


def retrieval_back(got, sums, emb, lse, lens, length):
    parts = got.shape[0]
    tokens = got.shape[1] - PACK_INT
    total = parts * tokens
    docs, proj = emb.shape
    return call(
        functools.partial(loss_kernel, length),
        "retrieval_back",
        [(got, "v"), (sums, "v"), (emb, "v"), (lse, "v"), (lens, "h")],
        [((docs, proj), F32, "v"), ((parts, tokens, proj), F32, "v"), ((1, LANE), F32, "v")],
        [pltpu.VMEM((total, proj), BF16), pltpu.VMEM((docs, total), BF16), pltpu.VMEM((total, docs), BF16)],
        32,
        6 * docs * total * proj,
        2 << 20,
    )


def chain_kernel(
    io, demb_ref, gains_ref, proj_ref, wp_s, out_ref, wd_s, a_ref, b_ref, wg_s, wu_s, mid_ref, wo_s,
    dpj_ref, dbr_ref, dg_ref, du_ref, datt_ref, dmid_ref, dmix_ref, dmixt_ref, acc_s,
):
    hidden = a_ref.shape[1]
    if len(demb_ref.shape) == 3:
        dy = demb_ref[0]
        for i in range(1, demb_ref.shape[0]):
            dy = dy + demb_ref[i]
    else:
        dy = demb_ref[...]
    io.need(proj_ref)
    pr = proj_ref[...]
    r = lax.rsqrt(jnp.sum(pr * pr, axis=-1, keepdims=True) + EPS)
    unit = pr * r
    dpj_ref[...] = (r * (dy - unit * jnp.sum(dy * unit, axis=-1, keepdims=True))).astype(BF16)
    io.done(dpj_ref)
    io.need(wp_s, out_ref)
    dn3 = nt(dpj_ref[...], wp_s[...])
    dout = norm_back(out_ref[...], gains_ref[2:3, :], dn3)
    dmid_ref[...] = dout
    dbr_ref[...] = dout.astype(BF16)
    io.done(dbr_ref)
    acc_s[...] = jnp.zeros_like(acc_s)

    io.feed((wd_s, a_ref, b_ref, wg_s, wu_s))

    def body(j, carry):
        io.need_part(j, wd_s, a_ref, b_ref, wg_s, wu_s)
        col = pl.ds(pl.multiple_of(j * CH, CH), CH)
        dh = nt(dbr_ref[...], wd_s[col, :])
        dg = (dh * a_ref[:, col].astype(F32)).astype(BF16)
        du = (dh * b_ref[:, col].astype(F32)).astype(BF16)
        dg_ref[:, col] = dg
        du_ref[:, col] = du
        acc_s[...] += nt(dg, wg_s[:, col]) + nt(du, wu_s[:, col])
        return carry

    lax.fori_loop(0, hidden // CH, body, 0)
    io.had(wd_s, a_ref, b_ref, wg_s, wu_s)
    io.done(dg_ref, du_ref)
    io.need(mid_ref)
    dmid = dmid_ref[...] + norm_back(mid_ref[...], gains_ref[1:2, :], acc_s[...])
    dmid_ref[...] = dmid
    datt_ref[...] = dmid.astype(BF16)
    io.done(dmid_ref, datt_ref)
    io.need(wo_s)
    dmix = nt(datt_ref[...], wo_s[...]).astype(BF16)
    dmix_ref[...] = dmix
    dmixt_ref[...] = dmix.T


def chain_ins(demb, gains, proj, wp, out, wd, a, b, wg, wu, mid, wo):
    steps = a.shape[1] // CH
    plain = lambda *items: [(item, "h") for item in items]
    parts = [(wd, f"h{steps}")] + [(item, f"h-{steps}") for item in (a, b, wg, wu)]
    return [(demb, "v"), (gains, "v")] + plain(proj, wp, out) + parts + plain(mid, wo)


def chain(demb, proj, out, mid, a, b, gains, wp, wd, wg, wu, wo, name):
    tokens, width = out.shape
    hidden = a.shape[1]
    return call(
        chain_kernel,
        name,
        chain_ins(demb, gains, proj, wp, out, wd, a, b, wg, wu, mid, wo),
        [
            (proj.shape, BF16, "h"),
            ((tokens, width), BF16, "h"),
            ((tokens, hidden), BF16, "h"),
            ((tokens, hidden), BF16, "h"),
            ((tokens, width), BF16, "h"),
            ((tokens, width), F32, "h"),
            ((tokens, width), BF16, "h"),
            ((width, tokens), BF16, "h"),
        ],
        [pltpu.VMEM((tokens, width), F32)],
        44,
        2 * tokens * (width * width + 3 * width * hidden + width * 128),
        30 << 20,
    )


def attention_back_kernel(
    io, k_ref, v_ref, q_ref, dmix_ref, dmixt_ref, mixt_ref, il_ref, e_ref, dqkv_ref, diag_ref, far_ref,
    dqt_s, p_s, ds_s, strip_s, dk_s, dv_s,
):
    tokens, width = q_ref.shape
    tile = min(tokens, 128)
    wide = min(tokens, 256)
    blocks = tokens // tile
    io.feed((k_ref, v_ref, q_ref, dmix_ref, dmixt_ref, mixt_ref, e_ref))

    def pair_body(p, carry):
        io.need_part(p, k_ref, v_ref, q_ref, dmix_ref, dmixt_ref, mixt_ref, e_ref)
        col = pl.ds(pl.multiple_of(p * LANE, LANE), LANE)
        kt = k_ref[:, col].T
        for s in range(2):
            h = 2 * p + s
            vp = half_lanes(v_ref[:, col], s)
            dm = half_lanes(dmix_ref[:, col], s)
            qm = half_lanes(q_ref[:, col], s)
            rows = pl.ds(pl.multiple_of(p * LANE + 64 * s, 64), 64)
            strip_s[...] = jnp.zeros_like(strip_s)
            far_low = jnp.zeros((8, LANE), F32)
            far_high = jnp.zeros((8, LANE), F32)
            for qc in range(tokens // wide):
                cols = slice(qc * wide, (qc + 1) * wide)
                dt = dmixt_ref[col, cols]
                delta = jnp.sum(
                    dmixt_ref[rows, cols].astype(F32) * mixt_ref[rows, cols].astype(F32), axis=0, keepdims=True
                )
                inverse = il_ref[h, :, cols]
                for kb in range(blocks):
                    ks = slice(kb * tile, (kb + 1) * tile)
                    dp = nn(vp[ks], dt)
                    prob = e_ref[h, ks, cols].astype(F32) * inverse
                    p_s[ks, :] = prob.astype(BF16)
                    ds = (prob * (dp - delta)).astype(BF16)
                    ds_s[ks, :] = ds
                    kept = ds.astype(F32)
                    for qs in range(wide // tile):
                        d = kb - (qc * (wide // tile) + qs)
                        t = kept[:, qs * tile:(qs + 1) * tile]
                        if abs(d) <= 1:
                            lo = (1 - d) * 128
                            strip_s[0:tile, lo:lo + tile] += t
                        else:
                            part = t[0:8]
                            for g in range(1, tile // 8):
                                part = part + t[8 * g:8 * g + 8]
                            if d > 0:
                                far_high = far_high + part
                            else:
                                far_low = far_low + part
                dv = nn(p_s[...], dm[cols])
                dk = nn(ds_s[...], qm[cols])
                if s == 0 and qc == 0:
                    dv_s[...] = dv
                    dk_s[...] = dk
                else:
                    dv_s[...] += dv
                    dk_s[...] += dk
                dqt_s[rows, cols] = nn(kt[64 * s:64 * s + 64], ds_s[...]).astype(BF16)
            fold = strip_s[...]
            size = strip_s.shape[0]
            while size > 8:
                size //= 2
                fold = fold[:size] + pltpu.roll(fold[size:], SPAN - size, 1)
            diag_ref[h] = fold
            far_ref[h, 0:8, :] = far_low
            far_ref[h, 8:16, :] = far_high
        kcol = pl.ds(pl.multiple_of(width + p * LANE, LANE), LANE)
        vcol = pl.ds(pl.multiple_of(2 * width + p * LANE, LANE), LANE)
        dqkv_ref[:, kcol] = dk_s[...].astype(BF16)
        dqkv_ref[:, vcol] = dv_s[...].astype(BF16)
        return carry

    lax.fori_loop(0, width // LANE, pair_body, 0)
    io.had(k_ref, v_ref, q_ref, dmix_ref, dmixt_ref, mixt_ref, e_ref)
    dqkv_ref[:, 0:width] = dqt_s[...].T


def attention_ins(q, k, v, e, il, mixt, dmix, dmixt):
    pairs = q.shape[1] // LANE
    wide = [(item, f"h-{pairs}") for item in (k, v, q, dmix)]
    return wide + [(item, f"h{pairs}") for item in (dmixt, mixt)] + [(il, "v"), (e, f"h{pairs}")]


def attention_outs(q, heads):
    tokens, width = q.shape
    return [((tokens, 3 * width), BF16, "h"), ((heads, 8, SPAN), F32, "v"), ((heads, 16, LANE), F32, "v")]


def attention_scratch(q):
    tokens, width = q.shape
    tile, wide = min(tokens, 128), min(tokens, 256)
    return [
        pltpu.VMEM((width, tokens), BF16),
        pltpu.VMEM((tokens, wide), BF16),
        pltpu.VMEM((tokens, wide), BF16),
        pltpu.VMEM((tile, SPAN), F32),
        pltpu.VMEM((tokens, LANE), F32),
        pltpu.VMEM((tokens, LANE), F32),
    ]


def attention_back(q, k, v, e, il, mixt, dmix, dmixt, name):
    tokens, width = q.shape
    return call(
        attention_back_kernel,
        name,
        attention_ins(q, k, v, e, il, mixt, dmix, dmixt),
        attention_outs(q, e.shape[0]),
        attention_scratch(q),
        32,
        10 * tokens * tokens * width,
        16 << 20,
    )


def input_kernel(io, gains_ref, *refs):
    kinds = (len(refs) - 3) // 4
    reads, weights, writes = refs[:3 * kinds], refs[3 * kinds:3 * kinds + 3], refs[3 * kinds + 3:]
    for kind in range(kinds):
        dqkv_ref, x_ref, dmid_ref = reads[3 * kind:3 * kind + 3]
        width = x_ref.shape[1]
        io.need(dqkv_ref)
        total = None
        for i, w in enumerate(weights):
            io.need(w)
            part = nt(dqkv_ref[:, i * width:(i + 1) * width], w[...])
            total = part if total is None else total + part
        io.need(x_ref, dmid_ref)
        writes[kind][...] = dmid_ref[...] + norm_back(x_ref[...].astype(F32), gains_ref[0:1, :], total)
        io.done(writes[kind])


def input_back(gains, kinds, weights, name):
    width = weights[0].shape[0]
    tokens = sum(x.shape[0] for _, x, _ in kinds)
    return call(
        input_kernel,
        name,
        [(gains, "v")] + [(item, "h") for kind in kinds for item in kind] + [(w, "h") for w in weights],
        [(x.shape, F32, "h") for _, x, _ in kinds],
        [],
        32,
        6 * tokens * width * width,
        8 << 20,
    )


def put_rows(own_ref, send_ref, core, acc_s, per, offset, lanes, pad=0, extra=None):
    count = own_ref.shape[0]
    for j in range(count):
        for ref, side in ((own_ref, core), (send_ref, 1 - core)):
            rows = pl.ds(pl.multiple_of(2 * per * j + per * side, 8), per)
            pieces = [acc_s[rows, lo:lo + 256] for lo in lanes]
            if extra is not None:
                pieces.append(extra(rows))
            if pad:
                pieces.append(jnp.zeros((pad, 256), F32))
            block = jnp.concatenate(pieces, axis=0) if len(pieces) > 1 else pieces[0]
            ref[j, pl.ds(offset, block.shape[0]), :] = block.astype(BF16)


def core_index():
    return (lax.axis_index("grp") % 2).astype(jnp.int32)


def halves(count, rows):
    return [((count, rows, 256), BF16, "h")] * 2


def down_grad_kernel(
    io, demb_ref, gains_ref, proj_ref, wp_s, out_ref, wd_s, a_ref, b_ref, wg_s, wu_s, mid_ref, wo_s,
    hid_ref, hidq_ref, dbr_ref, mixt_ref, mixtq_ref, datt_ref, n3_ref, n3q_ref, dpj_ref,
    dg_ref, du_ref, dmid_ref, dmix_ref, dmixt_ref, own_ref, send_ref,
    acc1_s, dpjq_s, dbrq_s, dattq_s, hidt_s, hidtq_s, acc_s, accd_s, accp_s,
):
    chain_kernel(
        io, demb_ref, gains_ref, proj_ref, wp_s, out_ref, wd_s, a_ref, b_ref, wg_s, wu_s, mid_ref, wo_s,
        dpjq_s, dbrq_s, dg_ref, du_ref, dattq_s, dmid_ref, dmix_ref, dmixt_ref, acc1_s,
    )
    io.done(dmix_ref, dmixt_ref)
    core = core_index()
    hidden, width = hid_ref.shape[1], dbr_ref.shape[1]
    count = own_ref.shape[0]
    per, per_down = width // (2 * count), hidden // (2 * count)
    io.need(hid_ref, hidq_ref)
    hidt_s[...] = hid_ref[...].T
    hidtq_s[...] = hidq_ref[...].T
    io.need(dbr_ref)

    def down(i, carry):
        col = pl.ds(pl.multiple_of(i * 256, 256), 256)
        accd_s[...] = nn(hidt_s[...], dbr_ref[:, col]) + nn(hidtq_s[...], dbrq_s[:, col])
        put_rows(own_ref, send_ref, core, accd_s, per_down, pl.multiple_of(i * per_down, 16), (0,))
        return carry

    lax.fori_loop(0, width // 256, down, 0)
    base = (width // 256) * per_down
    for ref in (send_ref, own_ref):
        io.done_rows(ref, 0, base)
    io.need(mixt_ref, mixtq_ref, datt_ref, n3_ref, n3q_ref, dpj_ref)
    acc_s[...] = nn(mixt_ref[...], datt_ref[:, 0:512]) + nn(mixtq_ref[...], dattq_s[:, 0:512])
    put_rows(own_ref, send_ref, core, acc_s, per, base, (0, 256))
    base = base + 2 * per
    acc_s[:, 0:256] = nn(mixt_ref[...], datt_ref[:, 512:768]) + nn(mixtq_ref[...], dattq_s[:, 512:768])
    accp_s[...] = nn(n3_ref[...].T, dpj_ref[...]) + nn(n3q_ref[...].T, dpjq_s[...])

    def proj_rows(rows):
        return jnp.concatenate([accp_s[rows, :], jnp.zeros((per, LANE), F32)], axis=1)

    put_rows(own_ref, send_ref, core, acc_s, per, base, (0,), extra=proj_rows)
    for ref in (send_ref, own_ref):
        io.done_rows(ref, base - 2 * per, 4 * per)
        io.gone(ref)


def down_grads(query, doc, count):
    (demb, proj, out, mid, a, b, gains, wp, wd, wg, wu, wo), (hidq, mixtq, n3q) = query
    hid, dbr, mixt, datt, n3, dpj = doc
    tokens, hidden = hid.shape
    qtokens, width = out.shape
    per, per_down = width // (2 * count), hidden // (2 * count)
    plain = [(item, "h") for item in (hid, hidq, dbr, mixt, mixtq, datt, n3, n3q, dpj)]
    return call(
        down_grad_kernel,
        "query_ff_back_down_grads",
        chain_ins(demb, gains, proj, wp, out, wd, a, b, wg, wu, mid, wo) + plain,
        [
            ((qtokens, hidden), BF16, "h"),
            ((qtokens, hidden), BF16, "h"),
            ((qtokens, width), F32, "h"),
            ((qtokens, width), BF16, "h"),
            ((width, qtokens), BF16, "h"),
        ]
        + halves(count, (width // 256) * per_down + 4 * per),
        [
            pltpu.VMEM((qtokens, width), F32),
            pltpu.VMEM(proj.shape, BF16),
            pltpu.VMEM((qtokens, width), BF16),
            pltpu.VMEM((qtokens, width), BF16),
            pltpu.VMEM((hidden, tokens), BF16),
            pltpu.VMEM((hidden, qtokens), BF16),
            pltpu.VMEM((width, 512), F32),
            pltpu.VMEM((hidden, 256), F32),
            pltpu.VMEM((width, LANE), F32),
        ],
        50,
        2 * (tokens + 256) * (width * width + width * hidden),
        24 << 20,
    )


def gate_grad_kernel(io, n2_ref, n2q_ref, dg_ref, dgq_ref, du_ref, duq_ref, own_ref, send_ref, n2t_s, n2tq_s, acc_s):
    core = core_index()
    width, hidden = n2_ref.shape[1], dg_ref.shape[1]
    count = own_ref.shape[0]
    per = width // (2 * count)
    io.need(n2_ref, n2q_ref)
    n2t_s[...] = n2_ref[...].T
    n2tq_s[...] = n2q_ref[...].T
    steps = hidden // 512
    for which, (d, dq) in enumerate(((dg_ref, dgq_ref), (du_ref, duq_ref))):
        io.need(d, dq)

        def gate(i, carry, d=d, dq=dq, start=which * steps * 2 * per):
            col = pl.ds(pl.multiple_of(i * 512, 512), 512)
            acc_s[...] = nn(n2t_s[...], d[:, col]) + nn(n2tq_s[...], dq[:, col])
            put_rows(own_ref, send_ref, core, acc_s, per, pl.multiple_of(start + i * 2 * per, 16), (0, 256))
            return carry

        lax.fori_loop(0, steps, gate, 0)
        for ref in (send_ref, own_ref):
            io.done_rows(ref, which * steps * 2 * per, steps * 2 * per)
    io.gone(own_ref)
    io.gone(send_ref)


def gate_grads(n2, n2q, dg, dgq, du, duq, count):
    tokens, width = n2.shape
    qtokens, hidden = dgq.shape
    per = width // (2 * count)
    return call(
        gate_grad_kernel,
        "gate_up_grads",
        [(item, "h") for item in (n2, n2q, dg, dgq, du, duq)],
        halves(count, 2 * (hidden // 256) * per),
        [pltpu.VMEM((width, tokens), BF16), pltpu.VMEM((width, qtokens), BF16), pltpu.VMEM((width, 512), F32)],
        32,
        4 * (tokens + 256) * width * hidden,
        16 << 20,
    )


def qkv_grad_kernel(
    io, k_ref, v_ref, q_ref, dmix_ref, dmixt_ref, mixt_ref, il_ref, e_ref, n1_ref, n1q_ref, d_ref,
    diagd_ref, fard_ref, hot_ref, loss_ref, dq_ref, diag_ref, far_ref, own_ref, send_ref, *rest,
):
    own_parts = lax.axis_size("dp")
    n1t_s, n1tq_s, acc_s = rest[-3:]
    attention_back_kernel(
        io, k_ref, v_ref, q_ref, dmix_ref, dmixt_ref, mixt_ref, il_ref, e_ref, dq_ref, diag_ref, far_ref, *rest[:-3]
    )
    io.done(dq_ref)
    core = core_index()
    width = n1_ref.shape[1]
    count = own_ref.shape[0]
    per = width // (2 * count)
    io.need(n1_ref, n1q_ref)
    n1t_s[...] = n1_ref[...].T
    n1tq_s[...] = n1q_ref[...].T
    io.need(d_ref)
    steps = (3 * width) // 512

    def body(i, carry):
        col = pl.ds(pl.multiple_of(i * 512, 512), 512)
        acc_s[...] = nn(n1t_s[...], d_ref[:, col]) + nn(n1tq_s[...], dq_ref[:, col])
        put_rows(own_ref, send_ref, core, acc_s, per, pl.multiple_of(i * 2 * per, 16), (0, 256))
        return carry

    lax.fori_loop(0, steps, body, 0)
    lo = steps * 512
    for ref in (send_ref, own_ref):
        io.done_rows(ref, 0, steps * 2 * per)
    acc_s[:, 0:256] = nn(n1t_s[...], d_ref[:, lo:lo + 256]) + nn(n1tq_s[...], dq_ref[:, lo:lo + 256])
    io.need(hot_ref)
    heads = diag_ref.shape[0]
    buckets = hot_ref.shape[0]
    table = jnp.zeros((heads, buckets), F32)
    for r in range(8):
        both = diagd_ref[:, r, :] + diag_ref[:, r, :]
        table = table + lax.dot_general(
            both, hot_ref[:, r * SPAN:(r + 1) * SPAN].astype(F32), (((1,), (1,)), ((), ())),
            precision=highest, preferred_element_type=F32,
        )
    far = fard_ref[...] + far_ref[...]
    low = jnp.sum(jnp.sum(far[:, 0:8, :], axis=1), axis=-1, keepdims=True)
    high = jnp.sum(jnp.sum(far[:, 8:16, :], axis=1), axis=-1, keepdims=True)
    column = lax.broadcasted_iota(jnp.int32, (1, buckets), 1)
    table = table + jnp.where(column == buckets // 2 - 1, low, 0.0) + jnp.where(column == buckets - 1, high, 0.0)
    table = jnp.concatenate([table, jnp.zeros((16 - heads, buckets), F32)], axis=0)
    loss = jnp.broadcast_to(loss_ref[...] * (1.0 / own_parts), (8, LANE))
    spare = jnp.concatenate([table[0:8], table[8:16], jnp.zeros((8, LANE - 2 * buckets), F32), loss], axis=1)
    put_rows(own_ref, send_ref, core, acc_s, per, steps * 2 * per, (0,), extra=lambda rows: spare)
    for ref in (send_ref, own_ref):
        io.done_rows(ref, steps * 2 * per, per + 8)
        io.gone(ref)


def qkv_grads(query, n1, n1q, d, diag, far, hot, loss, count):
    tokens, width = n1.shape
    per = width // (2 * count)
    return call(
        qkv_grad_kernel,
        "query_attention_back_qkv_grads",
        attention_ins(*query)
        + [(item, "h") for item in (n1, n1q, d)]
        + [(diag, "v"), (far, "v"), (hot, "h"), (loss, "v")],
        attention_outs(query[0], query[3].shape[0]) + halves(count, 9 * per + 8),
        attention_scratch(query[0])
        + [
            pltpu.VMEM((width, tokens), BF16),
            pltpu.VMEM((width, n1q.shape[0]), BF16),
            pltpu.VMEM((width, 512), F32),
        ],
        32,
        2 * (tokens + 256) * 3 * width * width,
        10 << 20,
    )


def after(values, *deps):
    return lax.optimization_barrier((values, deps))[0]


def position(n_dp):
    dp, grp = lax.axis_index("dp").astype(jnp.int32), lax.axis_index("grp").astype(jnp.int32)
    return dp // 2, dp % 2, grp // 2


def slices(io_sems, moves):
    copies = [pltpu.make_async_copy(src, dst, io_sems.at[i]) for i, (src, dst) in enumerate(moves)]
    for copy in copies:
        copy.start()
    return copies


class Halves:
    def __init__(self, rows):
        self.rows, self.cut = rows, (rows // 32) * 16

    def sizes(self):
        return self.cut, self.rows - self.cut

    def spans(self):
        return pl.ds(0, self.cut), pl.ds(self.cut, self.rows - self.cut)


def first_kernel(n_dp, halves, io, own_ref, got_ref, x_ref, y_ref, ox_s, gx_s, oy_s, gy_s, sems):
    _, x, y = position(n_dp)
    top, low = halves.spans()
    moves = []
    for ref, a, b in ((own_ref, ox_s, oy_s), (got_ref, gx_s, gy_s)):
        moves += [(ref.at[:, 1 - x, :, top], a), (ref.at[:, :, 1 - y, low], b)]
    copies = slices(sems, moves)
    for i, (a, b, out) in enumerate(((ox_s, gx_s, x_ref), (oy_s, gy_s, y_ref))):
        copies[i].wait()
        copies[i + 2].wait()
        out[...] = (a[...].astype(F32) + b[...].astype(F32)).astype(BF16)
        io.done(out)


def pair_rows(n_dp, halves, flip, own_ref, got_ref, gx_ref, gy_ref, bufs, sems):
    _, x, y = position(n_dp)
    top, low = halves.spans()
    yt, xl = (1 - y, 1 - x) if flip else (y, x)
    ot_s, gt_s, rt_s, ol_s, gl_s, rl_s = bufs
    copies = slices(sems, [
        (own_ref.at[:, x, yt, top], ot_s), (got_ref.at[:, x, yt, top], gt_s), (gx_ref.at[:, yt], rt_s),
        (own_ref.at[:, xl, y, low], ol_s), (got_ref.at[:, xl, y, low], gl_s), (gy_ref.at[:, xl], rl_s),
    ])
    out = []
    for i in (0, 3):
        for copy in copies[i:i + 3]:
            copy.wait()
        a, b, c = bufs[i:i + 3]
        out.append(a[...].astype(F32) + b[...].astype(F32) + c[...].astype(F32))
    return out


def second_kernel(n_dp, halves, io, own_ref, got_ref, gx_ref, gy_ref, y_ref, x_ref, *refs):
    for out, value in zip((y_ref, x_ref), pair_rows(n_dp, halves, True, own_ref, got_ref, gx_ref, gy_ref, refs[:-1], refs[-1])):
        out[...] = value.astype(BF16)
        io.done(out)


def cross_kernel(n_dp, halves, io, own_ref, got_ref, xy_ref, x_ref, y_ref, own_s, got_s, sems):
    _, x, y = position(n_dp)
    moves = []
    for i, (xx, yy) in enumerate(((1 - x, 1 - y), (1 - x, y), (x, 1 - y))):
        moves += [(own_ref.at[:, xx, yy], own_s.at[i]), (got_ref.at[:, xx, yy], got_s.at[i])]
    copies = slices(sems, moves)
    for i, out in enumerate((xy_ref, x_ref, y_ref)):
        copies[2 * i].wait()
        copies[2 * i + 1].wait()
        out[...] = (own_s[i].astype(F32) + got_s[i].astype(F32)).astype(BF16)
        io.done(out)


def leave(z, line_s, outs, total_ref, io):
    nz = line_s.shape[0]
    for k, out in enumerate(outs, 1):
        out[...] = line_s[(z + k) % nz].astype(BF16)
        io.done(out)
    total_ref[...] = line_s[z]


def cross_line_kernel(n_dp, halves, io, own_ref, got_ref, xy_ref, x_ref, y_ref, *refs):
    outs, total_ref, (line_s, own_s, got_s, sems) = refs[:-5], refs[-5], refs[-4:]
    z, x, y = position(n_dp)
    copies = slices(sems, [(own_ref.at[:, x, y], own_s), (got_ref.at[:, x, y], got_s)])
    for copy in copies:
        copy.wait()
    io.need(xy_ref, x_ref, y_ref)
    line_s[...] = own_s[...].astype(F32) + got_s[...].astype(F32) + xy_ref[...].astype(F32)
    line_s[...] += x_ref[...].astype(F32) + y_ref[...].astype(F32)
    leave(z, line_s, outs, total_ref, io)


def line_kernel(n_dp, halves, io, own_ref, got_ref, gx_ref, gy_ref, y_ref, x_ref, *refs):
    outs, total_ref, line_s, bufs, sems = refs[:-9], refs[-9], refs[-8], refs[-7:-1], refs[-1]
    z, _, _ = position(n_dp)
    top, low = pair_rows(n_dp, halves, False, own_ref, got_ref, gx_ref, gy_ref, bufs, sems)
    io.need(x_ref, y_ref)
    line_s[:, 0:halves.cut] = top + y_ref[...].astype(F32)
    line_s[:, halves.cut:] = low + x_ref[...].astype(F32)
    leave(z, line_s, outs, total_ref, io)


class Batch:
    def __init__(self, own, send, n_dp, n_grp, name):
        self.n_dp, self.n_grp, self.nz, self.name = n_dp, n_grp, n_dp // 2, name
        self.rows, self.cols = own.shape[1:]
        self.halves = Halves(self.rows)
        self.own = own
        self.got = lax.ppermute(send, "grp", [(i, i ^ 1) for i in range(n_grp)])

    def both(self):
        grid = lambda a: (a.reshape(self.nz, 2, 2, self.rows, self.cols), "r")
        return [grid(self.own), grid(self.got)]

    def along_x(self, array):
        return lax.ppermute(array, "dp", [(d, d ^ 1) for d in range(self.n_dp)])

    def along_y(self, array):
        return lax.ppermute(array, "grp", [(g, g ^ 2) for g in range(self.n_grp)])

    def run(self, kernel, step, ins, outs, scratch):
        body = functools.partial(kernel, self.n_dp, self.halves)
        return call(body, self.name + step, ins, outs, scratch, 24, 0, 0)

    def first(self):
        sizes = [(self.nz, 2, n, self.cols) for n in self.halves.sizes()]
        bufs = [pltpu.VMEM(size, BF16) for size in sizes for _ in range(2)]
        outs = [(size, BF16, "h") for size in sizes]
        sent = self.run(first_kernel, "_first", self.both(), outs, bufs + [pltpu.SemaphoreType.DMA((4,))])
        self.back1 = self.along_x(sent[0]), self.along_y(sent[1])
        return tuple(sent)

    def second_bufs(self):
        return [pltpu.VMEM((self.nz, n, self.cols), BF16) for n in self.halves.sizes() for _ in range(3)] + [
            pltpu.SemaphoreType.DMA((6,))
        ]

    def second(self):
        outs = [((self.nz, n, self.cols), BF16, "h") for n in self.halves.sizes()]
        ins = self.both() + [(a, "r") for a in self.back1]
        sent = self.run(second_kernel, "_second", ins, outs, self.second_bufs())
        self.back2 = self.along_y(sent[0]), self.along_x(sent[1])
        return tuple(sent)

    def cross(self):
        n_dp, n_grp = self.n_dp, self.n_grp
        piece = (self.nz, self.rows, self.cols)
        bufs = [pltpu.VMEM((3, *piece), BF16)] * 2 + [pltpu.SemaphoreType.DMA((6,))]
        sent = self.run(cross_kernel, "_cross", self.both(), [(piece, BF16, "h")] * 3, bufs)
        across = [(d * n_grp + g, (d ^ 1) * n_grp + (g ^ 2)) for d in range(n_dp) for g in range(n_grp)]
        self.back1 = ()
        self.back2 = lax.ppermute(sent[0], ("dp", "grp"), across), self.along_x(sent[1]), self.along_y(sent[2])
        return tuple(sent)

    def line(self):
        n_dp, nz = self.n_dp, self.nz
        piece, part = (nz, self.rows, self.cols), (self.rows, self.cols)
        outs = [(part, BF16, "h")] * (nz - 1) + [(part, F32, "v")]
        ins = self.both() + [(a, "r") for a in self.back1] + [(a, "h") for a in self.back2]
        if self.back1:
            kernel, bufs = line_kernel, self.second_bufs()
        else:
            kernel, bufs = cross_line_kernel, [pltpu.VMEM(piece, BF16)] * 2 + [pltpu.SemaphoreType.DMA((2,))]
        *sent, total = self.run(kernel, "_line", ins, outs, [pltpu.VMEM(piece, F32)] + bufs)
        self.parts = [total] + [
            lax.ppermute(one, "dp", [(d, (d + 2 * k) % n_dp) for d in range(n_dp)]) for k, one in enumerate(sent, 1)
        ]
        return tuple(sent)


def weight_rows(weights, start):
    aligned = (start // 16) * 16
    return start - aligned, [w.at[pl.ds(pl.multiple_of(aligned, 16), 32)] for w in weights]


def finish_kernel(n_parts, places, gain_row, with_table, io, *refs):
    total, gains_ref, rest = refs[:n_parts], refs[n_parts], refs[n_parts + 1:]
    n_out, n_weights = len(places), len(gain_row[1])
    weights, rest = rest[:n_weights], rest[n_weights:]
    outs, rest = rest[:n_out], rest[n_out:]
    gain_ref, rest = rest[0], rest[1:]
    extra, rest = (rest[:2], rest[2:]) if with_table else ((), rest)
    sum_s, wide_s, bufs, sems = rest[0], rest[1], rest[2:-1], rest[-1]
    device = lax.axis_index("dp") * lax.axis_size("grp") + lax.axis_index("grp")
    per = outs[gain_row[1][0]].shape[0]
    start = device.astype(jnp.int32) * per
    shift, sources = weight_rows(weights, start)
    copies = slices(sems, list(zip(sources, bufs)))
    io.need(*total)
    value = total[0][...].astype(F32)
    for one in total[1:]:
        value = value + one[...].astype(F32)
    sum_s[...] = value
    for out, at in zip(outs, places):
        rows, width = out.shape
        for i in range(-(-width // 256)):
            cols = min(256, width - i * 256)
            out[:, i * 256:i * 256 + cols] = sum_s[at + i * rows:at + (i + 1) * rows, 0:cols]
    inner = jnp.zeros((per, 1), F32)
    for which, copy, buf in zip(gain_row[1], copies, bufs):
        copy.wait()
        width = buf.shape[1]
        wide_s[:, 0:width] = buf[...].astype(F32)
        mine = wide_s[pl.ds(pl.multiple_of(shift, 8), per), 0:width]
        inner = inner + jnp.sum(mine * outs[which][...], axis=-1, keepdims=True)
    lane = lax.broadcasted_iota(jnp.int32, (per, gains_ref.shape[1]), 1)
    row = lax.broadcasted_iota(jnp.int32, (per, gains_ref.shape[1]), 0)
    gain = jnp.sum(jnp.where(lane == row + start, gains_ref[gain_row[0]:gain_row[0] + 1, :], 0.0), axis=-1, keepdims=True)
    lane, row = lane[:, 0:LANE], row[:, 0:LANE]
    gain_ref[...] = jnp.sum(jnp.where(lane == row, inner / gain, 0.0), axis=0, keepdims=True)
    if with_table:
        table_ref, loss_ref = extra
        buckets, heads = table_ref.shape
        spare = sum_s[sum_s.shape[0] - 8:, :]
        table = jnp.concatenate([spare[:, 0:buckets], spare[:, buckets:2 * buckets]], axis=0)
        table = jnp.concatenate([table, jnp.zeros((16, LANE - buckets), F32)], axis=1)
        table = jnp.concatenate([table, jnp.zeros((LANE - 16, LANE), F32)], axis=0).T
        table_ref[...] = table[0:buckets, 0:heads]
        loss_ref[...] = spare[0:1, LANE:2 * LANE]


def finish(batch, places, shapes, gain_row, gains, weights, table=None):
    outs = [(shape, F32, "v") for shape in shapes] + [((1, LANE), F32, "v")]
    if table is not None:
        outs += [(table, F32, "v"), ((1, LANE), F32, "v")]
    width = max(w.shape[1] for w in weights)
    return call(
        functools.partial(finish_kernel, len(batch.parts), places, gain_row, table is not None),
        batch.name + "_finish",
        [(one, "v" if one.dtype == F32 else "h") for one in batch.parts] + [(gains, "v")] + [(w, "r") for w in weights],
        outs,
        [pltpu.VMEM((batch.rows, batch.cols), F32), pltpu.VMEM((32, width), F32)]
        + [pltpu.VMEM((32, w.shape[1]), BF16) for w in weights]
        + [pltpu.SemaphoreType.DMA((len(weights),))],
        16,
        0,
        0,
    )


def on_device(
    n_dp, n_grp, doc_tokens, doc_lengths, query_tokens, query_lengths, candidates, labels, gain_attn, w_query, w_key,
    w_value, w_out, bias_table, gain_ffn, w_gate, w_up, w_down, gain_final, w_proj,
):
    doc_rows, doc_len, width = doc_tokens.shape
    query_rows, query_len = query_tokens.shape[:2]
    hidden = w_gate.shape[1]
    bucket_total, heads = bias_table.shape
    devices = n_dp * n_grp
    axes = ("dp", "grp")
    x_doc = doc_tokens.reshape(doc_len, width)
    x_qry = query_tokens.reshape(query_rows * query_len, width)
    which = lax.broadcasted_iota(jnp.int32, (8, width), 0)
    gains = jnp.where(which == 0, gain_attn[None], jnp.where(which == 1, gain_ffn[None], gain_final[None])).astype(F32)
    weights = (w_query, w_key, w_value, w_out, w_gate, w_up, w_down, w_proj)
    hot = jnp.asarray(strip_onehot(), BF16)
    (q_q, q_k, q_v, q_e, q_il, q_mixt, q_mid, q_n1, q_n2, q_hid, q_a, q_b, q_out, q_n3, q_proj, packed, base) = forward(
        x_qry, query_lengths[None], gains, (bias_table, hot, candidates, labels[None]), weights, False, heads
    )
    got = lax.all_to_all(jnp.broadcast_to(packed[None], (n_dp, *packed.shape)), "dp", 0, 0, tiled=True)
    (d_q, d_k, d_v, d_e, d_il, d_mixt, d_mid, d_n1, d_n2, d_hid, d_a, d_b, d_out, d_n3, d_proj, emb) = forward(
        x_doc, doc_lengths, gains, base, weights, True, heads
    )
    sums, lse = scores(got, emb, doc_lengths, query_len)
    sums = lax.all_to_all(sums, "dp", 0, 0, tiled=True)
    demb_doc, demb_part, loss_group = retrieval_back(
        got, sums, emb, lse, doc_lengths, query_len
    )
    demb_qry = lax.all_to_all(demb_part, "dp", 0, 0, tiled=True)
    back = (w_proj, w_down, w_gate, w_up, w_out)
    d_dpj, d_dbr, d_dg, d_du, d_datt, d_dmid, d_dmix, d_dmixt = chain(
        demb_doc, d_proj, d_out, d_mid, d_a, d_b, gains, *back, "doc_ff_back"
    )
    q_chain = (demb_qry, q_proj, q_out, q_mid, q_a, q_b, gains, *back)
    d_attention = lambda il: (d_q, d_k, d_v, d_e, il, d_mixt, d_dmix, d_dmixt)
    q_attention = lambda il, dmix, dmixt: (q_q, q_k, q_v, q_e, il, q_mixt, dmix, dmixt)
    qkv_weights = (w_query, w_key, w_value)
    fast = (n_dp, n_grp) == (8, 4)
    if fast:
        pairs = devices // 2
        q_dg, q_du, q_dmid, q_dmix, q_dmixt, own, send = down_grads(
            (q_chain, (q_hid, q_mixt, q_n3)), (d_hid, d_dbr, d_mixt, d_datt, d_n3, d_dpj), pairs
        )
        down = Batch(own, send, n_dp, n_grp, "down")
        own, send = gate_grads(d_n2, q_n2, d_dg, q_dg, d_du, q_du, pairs)
        gate = Batch(own, send, n_dp, n_grp, "gate")
        down.got = after(down.got, send)
        d_il = after(d_il, down.cross(), send)
        d_dqkv, d_diag, d_far = attention_back(*d_attention(d_il), "doc_attention_back")
        gate.got = after(gate.got, d_diag)
        q_il = after(q_il, gate.cross())
        q_dqkv, q_diag, q_far, own, send = qkv_grads(
            q_attention(q_il, q_dmix, q_dmixt), d_n1, q_n1, d_dqkv, d_diag, d_far, hot, loss_group, pairs
        )
        qkv = Batch(own, send, n_dp, n_grp, "qkv")
        (doc_grad,) = input_back(after(gains, send), ((d_dqkv, x_doc, d_dmid),), qkv_weights, "doc_input_back")
        down.back2 = after(down.back2, doc_grad)
        qkv.got = after(qkv.got, down.line())
        last_gains = after(gains, qkv.cross())
    else:
        q_dpj, q_dbr, q_dg, q_du, q_datt, q_dmid, q_dmix, q_dmixt = chain(*q_chain, "query_ff_back")
        d_dqkv, d_diag, d_far = attention_back(*d_attention(d_il), "doc_attention_back")
        q_dqkv, q_diag, q_far = attention_back(*q_attention(q_il, q_dmix, q_dmixt), "query_attention_back")
        last_gains = gains
        (doc_grad,) = input_back(gains, ((d_dqkv, x_doc, d_dmid),), qkv_weights, "doc_input_back")
    (query_grad,) = input_back(last_gains, ((q_dqkv, x_qry, q_dmid),), qkv_weights, "query_input_back")

    query_total = query_rows * devices
    per, per_down = width // devices, hidden // devices
    if fast:
        gate.back2 = after(gate.back2, query_grad)
        qkv.back2 = after(qkv.back2, gate.line())
        qkv.line()
        at = (width // 256) * per_down
        shard_down, shard_out, shard_proj, gain3 = finish(
            down, (0, at, at + 3 * per), ((per_down, width), (per, width), (per, w_proj.shape[1])), (2, (2,)), gains, [w_proj]
        )
        shard_gate, shard_up, gain2 = finish(
            gate, (0, (hidden // 256) * per), ((per, hidden),) * 2, (1, (0, 1)), gains, [w_gate, w_up]
        )
        shard_query, shard_key, shard_value, gain1, table_grad, loss = finish(
            qkv, (0, 3 * per, 6 * per), ((per, width),) * 3, (0, (0, 1, 2)), gains, qkv_weights, (bucket_total, heads)
        )
        shard_gains = [g[0, :per] for g in (gain1, gain2, gain3)]
        loss = loss[0, 0] / query_total
    else:

        def grad(left, right):
            product = tn(jnp.concatenate(left), jnp.concatenate(right))
            return lax.psum_scatter(product, axes, scatter_dimension=0, tiled=True)

        n1s = (d_n1, q_n1)
        shard_query, shard_key, shard_value = (
            grad(n1s, (d_dqkv[:, i * width:(i + 1) * width], q_dqkv[:, i * width:(i + 1) * width])) for i in range(3)
        )
        shard_out = grad((d_mixt.T, q_mixt.T), (d_datt, q_datt))
        shard_gate = grad((d_n2, q_n2), (d_dg, q_dg))
        shard_up = grad((d_n2, q_n2), (d_du, q_du))
        shard_down = grad((d_hid, q_hid), (d_dbr, q_dbr))
        shard_proj = grad((d_n3, q_n3), (d_dpj, q_dpj))
        start = (lax.axis_index("dp") * n_grp + lax.axis_index("grp")) * per
        mine = lambda a: lax.dynamic_slice_in_dim(a.astype(F32), start, per, 0)
        shard_gains = [
            sum(jnp.sum(mine(w) * g, axis=1) for w, g in pairs) / mine(gain)
            for gain, pairs in (
                (gain_attn, ((w_query, shard_query), (w_key, shard_key), (w_value, shard_value))),
                (gain_ffn, ((w_gate, shard_gate), (w_up, shard_up))),
                (gain_final, ((w_proj, shard_proj),)),
            )
        ]
        far = jnp.sum((d_far + q_far).reshape(heads, 2, -1), axis=-1)
        table = lax.dot_general(
            hot.astype(F32), (d_diag + q_diag).reshape(heads, -1), (((1,), (1,)), ((), ())),
            precision=highest, preferred_element_type=F32,
        )
        table = table.at[bucket_total // 2 - 1].add(far[:, 0]).at[bucket_total - 1].add(far[:, 1])
        table_grad, loss = lax.psum((table, loss_group[0, 0] / n_dp), axes)
        loss = loss / query_total
    return (
        loss,
        doc_grad.reshape(doc_rows, doc_len, width),
        query_grad.reshape(query_rows, query_len, width),
        shard_gains[0],
        shard_query,
        shard_key,
        shard_value,
        shard_out,
        table_grad,
        shard_gains[1],
        shard_gate,
        shard_up,
        shard_down,
        shard_gains[2],
        shard_proj,
    )


def solution(mesh):
    both = ("dp", "grp")
    rows3, rows2, rows1 = P(both, None, None), P(both, None), P(both)
    in_specs = (rows3, rows2, rows3, rows1, rows2, rows1) + (P(),) * 12
    out_specs = (
        P(), rows3, rows3, rows1, rows2, rows2, rows2, rows2, P(), rows1, rows2, rows2, rows2, rows1, rows2,
    )
    body = functools.partial(on_device, mesh.shape["dp"], mesh.shape["grp"])
    return jax.shard_map(body, mesh=mesh, in_specs=in_specs, out_specs=out_specs, check_vma=False)
```

```python
import functools
import itertools
import math

import jax
import jax.numpy as jnp
import numpy as np
from jax import lax
from jax.experimental import pallas as pl
from jax.experimental.pallas import tpu as pltpu
from jax.sharding import PartitionSpec as P

F32, BF16 = jnp.float32, jnp.bfloat16
BUCKETS = 32
DIST = 128
BLK = 128
ROW_FILL = 480
EPS = 1e-6
SHARP = 0.25
SCALE = 16.0
NEG = -1e30
GELU_A = math.sqrt(2.0 / math.pi)
GELU_B = 0.044715
SPAN = 512
CH = 512
LANE = 128
COST = 20
AHEAD = 1 << 30
PACK_INT = 48
highest = lax.Precision.HIGHEST


def nn(a, b):
    return jnp.dot(a, b, preferred_element_type=F32)


def nt(a, b):
    return lax.dot_general(a, b, (((1,), (1,)), ((), ())), preferred_element_type=F32)


def tn(a, b):
    return lax.dot_general(a, b, (((0,), (0,)), ((), ())), preferred_element_type=F32)


def bucket_of(offsets):
    half = BUCKETS // 2
    exact = half // 2
    dist = np.abs(offsets)
    scaled = np.log(np.maximum(dist, 1) / exact) / np.log(DIST / exact) * (half - exact)
    far = np.minimum(exact + np.maximum(scaled, 0).astype(np.int64), half - 1)
    return (offsets > 0) * half + np.where(dist < exact, dist, far)


def strip_onehot():
    j = np.arange(SPAN)
    offset = np.where(j < 384, 128 - j, 640 - j)
    index = np.stack([bucket_of(offset[(j - r) % SPAN]) for r in range(8)]).reshape(-1)
    return (index[None, :] == np.arange(BUCKETS)[:, None]).astype(np.float32)


VM = pl.BlockSpec(memory_space=pltpu.VMEM)
HB = pl.BlockSpec(memory_space=pl.ANY)


def by_part(run):
    return run if run[0][3] == 1 else sorted(run, key=lambda entry: entry[1])


class Io:
    def __init__(self, ins, outs, sems):
        self.ins, self.outs, self.sems, self.used = {}, {}, sems, 0
        self.going, self.queue, self.flying = [], [], 0
        for src, buf, parts in ins:
            self.ins[id(buf)] = (src, buf, parts, self.used)
            size = math.prod(buf.shape) * buf.dtype.itemsize // abs(parts)
            self.queue += [(id(buf), p, size, abs(parts)) for p in range(abs(parts))]
            self.used += abs(parts)
        for buf, dst in outs:
            self.outs[id(buf)] = (buf, dst)
        self.queue = [entry for _, run in itertools.groupby(self.queue, lambda e: e[3]) for entry in by_part(list(run))]
        self.feed()

    def feed(self, upto=()):
        upto = {id(buf) for buf in upto}
        while self.queue and (self.flying < AHEAD or any(entry[0] in upto for entry in self.queue)):
            key, p, size, _ = self.queue.pop(0)
            self.chunk(*self.ins[key], p).start()
            self.flying += size

    def landed(self, buf):
        self.flying -= math.prod(buf.shape) * buf.dtype.itemsize
        self.feed()

    def chunk(self, src, buf, parts, first, p):
        if parts == 1:
            return pltpu.make_async_copy(src, buf, self.sems.at[first])
        if parts > 0:
            size = buf.shape[0] // parts
            cut = (pl.ds(p * size if isinstance(p, int) else pl.multiple_of(p * size, 2), size),)
        else:
            size = buf.shape[1] // -parts
            cut = (slice(None), pl.ds(p * size if isinstance(p, int) else pl.multiple_of(p * size, LANE), size))
        return pltpu.make_async_copy(src.at[cut], buf.at[cut], self.sems.at[first + p])

    def need(self, *bufs):
        for buf in bufs:
            entry = self.ins.get(id(buf))
            if entry is not None:
                self.feed((buf,))
                for p in range(abs(entry[2])):
                    self.chunk(*entry, p).wait()
                del self.ins[id(buf)]
                self.landed(buf)

    def need_part(self, p, *bufs):
        for buf in bufs:
            if id(buf) in self.ins:
                self.chunk(*self.ins[id(buf)], p).wait()

    def had(self, *bufs):
        for buf in bufs:
            if self.ins.pop(id(buf), None) is not None:
                self.landed(buf)

    def done(self, *bufs):
        for buf in bufs:
            if id(buf) in self.outs:
                src, dst = self.outs.pop(id(buf))
                self.push(src, dst)

    def done_rows(self, buf, start, size):
        src, dst = self.outs[id(buf)]
        rows = (slice(None), pl.ds(start, size))
        self.push(src.at[rows], dst.at[rows])

    def gone(self, buf):
        self.outs.pop(id(buf))

    def push(self, src, dst):
        copy = pltpu.make_async_copy(src, dst, self.sems.at[self.used])
        self.used += 1
        copy.start()
        self.going.append(copy)

    def close(self):
        self.need(*[entry[1] for entry in list(self.ins.values())])
        self.done(*[entry[0] for entry in list(self.outs.values())])
        for copy in self.going:
            copy.wait()


def call(kernel, name, ins, outs, scratch, mib, flops, moved=8 << 20):
    args, in_specs, out_specs, out_shape, buffers, sems = [], [], [], [], [], 0
    for array, kind in ins:
        if kind == "r":
            args.append(array)
            in_specs.append(HB)
        elif kind[0] == "h":
            args.append(pltpu.with_memory_space_constraint(array, pltpu.HBM))
            in_specs.append(HB)
            buffers.append(pltpu.VMEM(array.shape, array.dtype))
            sems += abs(int(kind[1:] or 1))
        else:
            args.append(array)
            in_specs.append(VM)
    for shape, dtype, kind in outs:
        if kind == "a":
            out_shape.append(pltpu.HBM(shape, dtype))
            out_specs.append(HB)
            sems += 8
        elif kind == "h":
            out_shape.append(pltpu.HBM(shape, dtype))
            out_specs.append(HB)
            buffers.append(pltpu.VMEM(shape, dtype))
            sems += 4
        else:
            out_shape.append(jax.ShapeDtypeStruct(shape, dtype))
            out_specs.append(VM)

    def body(*refs):
        n_in, n_out, n_buf = len(ins), len(outs), len(buffers)
        given, made = list(refs[:n_in]), list(refs[n_in:n_in + n_out])
        bufs = iter(refs[n_in + n_out:n_in + n_out + n_buf])
        rest = refs[n_in + n_out + n_buf:]
        reads, writes = [], []
        for i, (_, kind) in enumerate(ins):
            if kind[0] == "h":
                buf = next(bufs)
                reads.append((given[i], buf, int(kind[1:] or 1)))
                given[i] = buf
        for i, (_, _, kind) in enumerate(outs):
            if kind == "h":
                buf = next(bufs)
                writes.append((buf, made[i]))
                made[i] = buf
        io = Io(reads, writes, rest[-1])
        kernel(io, *given, *made, *rest[:-1])
        io.close()

    return pl.pallas_call(
        body,
        name=name,
        out_shape=out_shape,
        in_specs=in_specs,
        out_specs=out_specs,
        scratch_shapes=buffers + scratch + [pltpu.SemaphoreType.DMA((max(sems, 1),))],
        compiler_params=pltpu.CompilerParams(vmem_limit_bytes=mib << 20),
        cost_estimate=pl.CostEstimate(flops=int(flops) * COST, bytes_accessed=int(moved) * COST, transcendentals=0),
    )(*args)


def half_lanes(values, side):
    lane = lax.broadcasted_iota(jnp.int32, (1, LANE), 1)
    return jnp.where((lane // 64) == side, values.astype(F32), 0.0).astype(BF16)


def norm_back(values, gain, dn):
    s = lax.rsqrt(jnp.mean(values * values, axis=-1, keepdims=True) + EPS)
    unit = values * s
    t = dn * gain
    return s * (t - unit * jnp.mean(t * unit, axis=-1, keepdims=True))


def forward_kernel(
    is_doc, io, x_ref, lens_ref, gains_ref, extra_ref, wq_s, wk_s, wv_s, wo_s, wg_s, wu_s, wd_s, wp_s,
    q_ref, k_ref, v_ref, e_ref, il_ref, mixt_ref, mid_ref, n1_ref, n2_ref, hid_ref, a_ref, b_ref,
    out_ref, n3_ref, proj_ref, emb_ref, *rest,
):
    if is_doc:
        base_ref, tail = extra_ref, rest
    else:
        hot_ref, cand_ref, label_ref = extra_ref
        base_ref, tail = rest[0], rest[1:]
    mask_s, strip_s, s_s, e_s, vt_s = tail
    tokens, width = x_ref.shape
    hidden = wg_s.shape[1]
    heads = e_ref.shape[0]
    io.need(lens_ref)
    if not is_doc:
        io.need(hot_ref)
        tab = gains_ref[8:, 0:LANE].astype(BF16)
        for r in range(8):
            rows = tn(tab, hot_ref[:, r * SPAN:(r + 1) * SPAN])
            for h in range(heads):
                base_ref[h, r:r + 1, :] = rows[h:h + 1, :]
    io.need(x_ref)
    x = x_ref[...].astype(F32)
    s1 = lax.rsqrt(jnp.mean(x * x, axis=-1, keepdims=True) + EPS)
    n1_ref[...] = (x * s1 * gains_ref[0:1, :]).astype(BF16)
    io.done(n1_ref)
    tile = min(tokens, 128)
    blocks = tokens // tile
    row_id = lax.broadcasted_iota(jnp.int32, (tokens, 1), 0)
    col_id = lax.broadcasted_iota(jnp.int32, (1, tokens), 1)
    if is_doc:
        seg_k = jnp.zeros((tokens, 1), jnp.int32)
        seg_q = jnp.zeros((1, tokens), jnp.int32)
        end = jnp.zeros((1, 1), jnp.int32)
        for i in range(lens_ref.shape[1]):
            end = end + lens_ref[0:1, i:i + 1]
            seg_k = seg_k + (row_id >= end).astype(jnp.int32)
            seg_q = seg_q + (col_id >= end).astype(jnp.int32)
    else:
        count = lens_ref.shape[1]
        length = tokens // count
        seg_q = col_id // length
        seg_k = jnp.full((tokens, 1), -1, jnp.int32)
        for i in range(count):
            inside = (row_id >= i * length) & (row_id < i * length + lens_ref[0:1, i:i + 1])
            seg_k = jnp.where(inside, i, seg_k)
    mask_s[...] = jnp.where(seg_k == seg_q, 0.0, NEG)
    for i, (w, o) in enumerate(((wq_s, q_ref), (wk_s, k_ref), (wv_s, v_ref))):
        io.need(w)
        o[...] = nn(n1_ref[...], w[...]).astype(BF16)
        io.done(o)
    vt_s[...] = v_ref[...].T
    if is_doc:
        io.need(base_ref)
    else:
        io.done(base_ref)

    def softmax_pair(p, slot):
        col = pl.ds(pl.multiple_of(p * LANE, LANE), LANE)
        for s in range(2):
            h = 2 * p + s
            first = base_ref[h]
            for g in range(tile // 8):
                strip_s[s, 8 * g:8 * g + 8, :] = pltpu.roll(first, 8 * g, 1) if g else first
            low_far, high_far = first[0:1, 256:256 + tile], first[0:1, 384:384 + tile]
            scores = nt(half_lanes(k_ref[:, col], s), q_ref[:, col])
            for qb in range(blocks):
                cols = slice(qb * tile, (qb + 1) * tile)
                tops = []
                for kb in range(blocks):
                    ks = slice(kb * tile, (kb + 1) * tile)
                    d = kb - qb
                    t = scores[ks, cols]
                    if abs(d) <= 1:
                        lo = (1 - d) * 128
                        t = t + strip_s[s, :, lo:lo + tile]
                    else:
                        t = t + (high_far if d > 0 else low_far)
                    t = t + mask_s[ks, cols]
                    s_s[s, ks, cols] = t
                    tops.append(jnp.max(t, axis=0, keepdims=True))
                top = functools.reduce(jnp.maximum, tops)
                total = None
                for kb in range(blocks):
                    ks = slice(kb * tile, (kb + 1) * tile)
                    e = jnp.exp(s_s[s, ks, cols] - top)
                    part = jnp.sum(e, axis=0, keepdims=True)
                    total = part if total is None else total + part
                    kept = e.astype(BF16)
                    e_ref[h, ks, cols] = kept
                    e_s[slot, s, ks, cols] = kept
                il_ref[h, :, cols] = 1.0 / total

    def mix_pair(p, slot):
        for s in range(2):
            rows = pl.ds(pl.multiple_of(p * LANE + 64 * s, 64), 64)
            mixt_ref[rows, :] = (nn(vt_s[rows, :], e_s[slot, s]) * il_ref[2 * p + s]).astype(BF16)

    def pair_step(i, carry):
        mix_pair(2 * i, 0)
        softmax_pair(2 * i + 1, 1)
        mix_pair(2 * i + 1, 1)
        softmax_pair(2 * i + 2, 0)
        return carry

    pairs = width // LANE
    softmax_pair(0, 0)
    lax.fori_loop(0, pairs // 2 - 1, pair_step, 0)
    mix_pair(pairs - 2, 0)
    softmax_pair(pairs - 1, 1)
    mix_pair(pairs - 1, 1)
    io.done(e_ref, mixt_ref)
    io.need(wo_s)
    mid_ref[...] = x_ref[...].astype(F32) + nn(mixt_ref[...].T, wo_s[...])
    mid = mid_ref[...]
    s2 = lax.rsqrt(jnp.mean(mid * mid, axis=-1, keepdims=True) + EPS)
    n2_ref[...] = (mid * s2 * gains_ref[1:2, :]).astype(BF16)
    io.done(mid_ref, n2_ref)

    io.feed((wg_s, wu_s))

    def ff_body(j, carry):
        io.need_part(j, wg_s, wu_s)
        col = pl.ds(pl.multiple_of(j * CH, CH), CH)
        g = nn(n2_ref[...], wg_s[:, col])
        u = nn(n2_ref[...], wu_s[:, col])
        sq = g * g
        t = jnp.tanh(GELU_A * g * (1.0 + GELU_B * sq))
        half = 0.5 + 0.5 * t
        gel = g * half
        slope = half + (0.5 * GELU_A) * g * (1.0 - t * t) * (1.0 + 3.0 * GELU_B * sq)
        hid_ref[:, col] = (gel * u).astype(BF16)
        a_ref[:, col] = (u * slope).astype(BF16)
        b_ref[:, col] = gel.astype(BF16)
        return carry

    lax.fori_loop(0, hidden // CH, ff_body, 0)
    io.had(wg_s, wu_s)
    io.done(hid_ref, a_ref, b_ref)
    io.need(wd_s)
    out_ref[...] = mid_ref[...] + nn(hid_ref[...], wd_s[...])
    o = out_ref[...]
    s3 = lax.rsqrt(jnp.mean(o * o, axis=-1, keepdims=True) + EPS)
    n3_ref[...] = (o * s3 * gains_ref[2:3, :]).astype(BF16)
    io.done(out_ref, n3_ref)
    io.need(wp_s)
    pr = nn(n3_ref[...], wp_s[...])
    proj_ref[...] = pr
    emb = (pr * lax.rsqrt(jnp.sum(pr * pr, axis=-1, keepdims=True) + EPS)).astype(BF16)
    if is_doc:
        emb_ref[...] = emb
    else:
        emb_ref[0:tokens, :] = emb
        io.need(cand_ref, label_ref)
        emb_ref[tokens:, :] = pack_ints(cand_ref, label_ref, lens_ref)


def pack_ints(cand_ref, label_ref, lens_ref):
    count = cand_ref.shape[1]
    eye = lax.broadcasted_iota(jnp.int32, (count, count), 0) == lax.broadcasted_iota(jnp.int32, (count, count), 1)
    lane = lax.broadcasted_iota(jnp.int32, (1, LANE), 1)
    row = lax.broadcasted_iota(jnp.int32, (PACK_INT, 1), 0)
    packed = jnp.zeros((PACK_INT, LANE), F32)
    for a in range(cand_ref.shape[0]):
        values = jnp.where(eye, cand_ref[a:a + 1, :].astype(F32), 0.0)
        column = jnp.sum(values, axis=1, keepdims=True)
        column = jnp.concatenate([column, jnp.zeros((PACK_INT - count, 1), F32)], axis=0)
        column = jnp.where(row == count, label_ref[0:1, a:a + 1].astype(F32), column)
        column = jnp.where(row == count + 1, lens_ref[0:1, a:a + 1].astype(F32), column)
        packed = jnp.where(lane == a, column, packed)
    return packed.astype(BF16)


def forward(x, lens, gains, extra, weights, is_doc, heads):
    tokens, width = x.shape
    hidden = weights[4].shape[1]
    proj = weights[7].shape[1]
    outs = [((tokens, width), BF16, "h")] * 3 + [
        ((heads, tokens, tokens), BF16, "h"),
        ((heads, 1, tokens), F32, "v"),
        ((width, tokens), BF16, "h"),
        ((tokens, width), F32, "h"),
        ((tokens, width), BF16, "h"),
        ((tokens, width), BF16, "h"),
        ((tokens, hidden), BF16, "h"),
        ((tokens, hidden), BF16, "h"),
        ((tokens, hidden), BF16, "h"),
        ((tokens, width), F32, "h"),
        ((tokens, width), BF16, "h"),
        ((tokens, proj), F32, "h"),
        ((tokens + (0 if is_doc else PACK_INT), proj), BF16, "v"),
    ]
    tile = min(tokens, 128)
    scratch = [
        pltpu.VMEM((tokens, tokens), F32),
        pltpu.VMEM((2, tile, SPAN), F32),
        pltpu.VMEM((2, tokens, tokens), F32),
        pltpu.VMEM((2, 2, tokens, tokens), BF16),
        pltpu.VMEM((width, tokens), BF16),
    ]
    steps = weights[4].shape[1] // CH
    streams = [(w, f"h-{steps}" if w.shape == weights[4].shape else "h") for w in weights]
    ins = [(x, "h"), (lens, "h"), (gains, "v")]
    if is_doc:
        kernel = functools.partial(forward_kernel, True)
        ins = ins + [(extra, "h")] + streams
    else:
        outs.append(((heads, 8, SPAN), F32, "h"))

        def kernel(io, x_ref, lens_ref, gains_ref, hot_ref, cand_ref, label_ref, *rest):
            forward_kernel(False, io, x_ref, lens_ref, gains_ref, (hot_ref, cand_ref, label_ref), *rest)

        ins = ins + [(item, "h") for item in extra] + streams
    flops = 2 * tokens * (4 * width * width + 3 * width * hidden + width * proj) + 4 * tokens * tokens * width
    return call(kernel, "doc_forward" if is_doc else "query_forward", ins, outs, scratch, 50, flops, 30 << 20)


def unpack(got_ref, tokens):
    parts = got_ref.shape[0]
    own = 2
    lane = lax.broadcasted_iota(jnp.int32, (1, LANE), 1)
    ints = None
    for i in range(parts):
        block = got_ref[i, tokens:, :].astype(F32)
        if i:
            block = pltpu.roll(block, own * i, 1)
        block = jnp.where((lane // own) == i, block, 0.0)
        ints = block if ints is None else ints + block
    return ints[0:32, :], ints[32:33, :], ints[33:34, :]


def expand_onehot(queries, length):
    col = lax.broadcasted_iota(jnp.int32, (LANE, queries * length), 1)
    row = lax.broadcasted_iota(jnp.int32, (LANE, queries * length), 0)
    return ((col // length) == row).astype(F32)


def token_valid(lens, queries, length):
    hot = expand_onehot(queries, length)
    spread = jnp.dot(jnp.broadcast_to(lens, (8, LANE)), hot, precision=highest, preferred_element_type=F32)[0:1]
    place = lax.broadcasted_iota(jnp.int32, (1, queries * length), 1) % length
    return place.astype(F32) < spread, hot


def block_scores(emb_ref, q_s, b):
    t = nt(emb_ref[b * BLK:(b + 1) * BLK, :], q_s[...]) * (1.0 / SHARP)
    row = lax.broadcasted_iota(jnp.int32, (BLK, 1), 0) + b * BLK
    return jnp.where(row < ROW_FILL, t, NEG) if (b + 1) * BLK > ROW_FILL else t


def score_kernel(length, io, got_ref, emb_ref, sums_ref, lse_ref, q_s):
    parts = got_ref.shape[0]
    tokens = q_s.shape[0] // parts
    queries = q_s.shape[0] // length
    for i in range(parts):
        q_s[i * tokens:(i + 1) * tokens, :] = got_ref[i, 0:tokens, :]
    _, _, lens = unpack(got_ref, tokens)
    valid, hot = token_valid(lens, queries, length)
    blocks = emb_ref.shape[0] // BLK
    rows = []
    for b in range(blocks):
        t = block_scores(emb_ref, q_s, b)
        top = jnp.max(t, axis=0, keepdims=True)
        lse = top + jnp.log(jnp.sum(jnp.exp(t - top), axis=0, keepdims=True))
        lse_ref[b:b + 1, :] = lse
        rows.append(jnp.where(valid, SHARP * lse, 0.0))
    rows.append(jnp.zeros((8 - blocks, rows[0].shape[1]), F32))
    sums = lax.dot_general(
        jnp.concatenate(rows, axis=0), hot, (((1,), (1,)), ((), ())), precision=highest, preferred_element_type=F32
    )
    for i in range(parts):
        sums_ref[i] = sums


def scores(got, emb, length):
    parts = got.shape[0]
    tokens = got.shape[1] - PACK_INT
    total = parts * tokens
    return call(
        functools.partial(score_kernel, length),
        "block_sums",
        [(got, "v"), (emb, "v")],
        [((parts, 8, LANE), F32, "v"), ((8, total), F32, "v")],
        [pltpu.VMEM((total, emb.shape[1]), BF16)],
        24,
        2 * emb.shape[0] * total * 128,
        1 << 20,
    )


def loss_kernel(length, io, got_ref, sums_ref, emb_ref, lse_ref, doc_ref, qry_ref, loss_ref, q_s, d_s, s_s):
    parts = got_ref.shape[0]
    tokens = q_s.shape[0] // parts
    queries = q_s.shape[0] // length
    for i in range(parts):
        q_s[i * tokens:(i + 1) * tokens, :] = got_ref[i, 0:tokens, :]
    cand, label, lens = unpack(got_ref, tokens)
    valid, hot = token_valid(lens, queries, length)
    blocks = emb_ref.shape[0] // BLK
    logits = jnp.zeros(cand.shape, F32)
    for i in range(parts):
        for b in range(blocks):
            logits = logits + jnp.where(cand == float(i * blocks + b), sums_ref[i, b:b + 1, :], 0.0)
    logits = SCALE * logits
    top = jnp.max(logits, axis=0, keepdims=True)
    lse = top + jnp.log(jnp.sum(jnp.exp(logits - top), axis=0, keepdims=True))
    choice = lax.broadcasted_iota(jnp.int32, cand.shape, 0).astype(F32) == label
    lane = lax.broadcasted_iota(jnp.int32, (1, LANE), 1)
    picked = jnp.sum(jnp.where(choice, logits, 0.0), axis=0, keepdims=True)
    each = jnp.where(lane < queries, lse - picked, 0.0)
    loss_ref[...] = jnp.broadcast_to(jnp.sum(each, axis=1, keepdims=True), (1, LANE))
    dlogits = SCALE * (jnp.exp(logits - lse) - jnp.where(choice, 1.0, 0.0))
    me = lax.axis_index("dp").astype(jnp.int32)
    rows = []
    for b in range(blocks):
        mine = (me * blocks + b).astype(F32)
        rows.append(jnp.sum(jnp.where(cand == mine, dlogits, 0.0), axis=0, keepdims=True))
    rows.append(jnp.zeros((8 - blocks, LANE), F32))
    spread = jnp.dot(jnp.concatenate(rows, axis=0), hot, precision=highest, preferred_element_type=F32)
    for b in range(blocks):
        t = block_scores(emb_ref, q_s, b)
        weight = jnp.where(valid, spread[b:b + 1, :], 0.0)
        d_s[b * BLK:(b + 1) * BLK, :] = (weight * jnp.exp(t - lse_ref[b:b + 1, :])).astype(BF16)
    doc_ref[...] = nn(d_s[...], q_s[...])
    s_s[...] = d_s[...].T
    qry_ref[...] = nn(s_s[...], emb_ref[...]).reshape(qry_ref.shape)


def retrieval_back(got, sums, emb, lse, length):
    parts = got.shape[0]
    tokens = got.shape[1] - PACK_INT
    total = parts * tokens
    docs, proj = emb.shape
    return call(
        functools.partial(loss_kernel, length),
        "retrieval_back",
        [(got, "v"), (sums, "v"), (emb, "v"), (lse, "v")],
        [((docs, proj), F32, "v"), ((parts, tokens, proj), F32, "v"), ((1, LANE), F32, "v")],
        [pltpu.VMEM((total, proj), BF16), pltpu.VMEM((docs, total), BF16), pltpu.VMEM((total, docs), BF16)],
        32,
        6 * docs * total * proj,
        2 << 20,
    )


def chain_kernel(
    io, demb_ref, gains_ref, proj_ref, wp_s, out_ref, wd_s, a_ref, b_ref, wg_s, wu_s, mid_ref, wo_s,
    dpj_ref, dbr_ref, dg_ref, du_ref, datt_ref, dmid_ref, dmix_ref, dmixt_ref, acc_s,
):
    hidden = a_ref.shape[1]
    if len(demb_ref.shape) == 3:
        dy = demb_ref[0]
        for i in range(1, demb_ref.shape[0]):
            dy = dy + demb_ref[i]
    else:
        dy = demb_ref[...]
    io.need(proj_ref)
    pr = proj_ref[...]
    r = lax.rsqrt(jnp.sum(pr * pr, axis=-1, keepdims=True) + EPS)
    unit = pr * r
    dpj_ref[...] = (r * (dy - unit * jnp.sum(dy * unit, axis=-1, keepdims=True))).astype(BF16)
    io.done(dpj_ref)
    io.need(wp_s, out_ref)
    dn3 = nt(dpj_ref[...], wp_s[...])
    dout = norm_back(out_ref[...], gains_ref[2:3, :], dn3)
    dmid_ref[...] = dout
    dbr_ref[...] = dout.astype(BF16)
    io.done(dbr_ref)

    io.feed((wd_s, a_ref, b_ref, wg_s, wu_s))

    def body(j, carry):
        io.need_part(j, wd_s, a_ref, b_ref)
        col = pl.ds(pl.multiple_of(j * CH, CH), CH)
        dh = nt(dbr_ref[...], wd_s[col, :])
        dg_ref[:, col] = (dh * a_ref[:, col].astype(F32)).astype(BF16)
        du_ref[:, col] = (dh * b_ref[:, col].astype(F32)).astype(BF16)
        return carry

    lax.fori_loop(0, hidden // CH, body, 0)
    io.had(wd_s, a_ref, b_ref)
    io.done(dg_ref, du_ref)
    io.need(wg_s, wu_s)
    acc_s[...] = nt(dg_ref[...], wg_s[...]) + nt(du_ref[...], wu_s[...])
    io.need(mid_ref)
    dmid = dmid_ref[...] + norm_back(mid_ref[...], gains_ref[1:2, :], acc_s[...])
    dmid_ref[...] = dmid
    datt_ref[...] = dmid.astype(BF16)
    io.done(dmid_ref, datt_ref)
    io.need(wo_s)
    dmix = nt(datt_ref[...], wo_s[...]).astype(BF16)
    dmix_ref[...] = dmix
    dmixt_ref[...] = dmix.T


def chain_ins(demb, gains, proj, wp, out, wd, a, b, wg, wu, mid, wo):
    steps = a.shape[1] // CH
    plain = lambda *items: [(item, "h") for item in items]
    parts = [(wd, f"h{steps}")] + [(item, f"h-{steps}") for item in (a, b)]
    return [(demb, "v"), (gains, "v")] + plain(proj, wp, out) + parts + plain(wg, wu, mid, wo)


def chain(demb, proj, out, mid, a, b, gains, wp, wd, wg, wu, wo, name):
    tokens, width = out.shape
    hidden = a.shape[1]
    return call(
        chain_kernel,
        name,
        chain_ins(demb, gains, proj, wp, out, wd, a, b, wg, wu, mid, wo),
        [
            (proj.shape, BF16, "h"),
            ((tokens, width), BF16, "h"),
            ((tokens, hidden), BF16, "h"),
            ((tokens, hidden), BF16, "h"),
            ((tokens, width), BF16, "h"),
            ((tokens, width), F32, "h"),
            ((tokens, width), BF16, "h"),
            ((width, tokens), BF16, "h"),
        ],
        [pltpu.VMEM((tokens, width), F32)],
        44,
        2 * tokens * (width * width + 3 * width * hidden + width * 128),
        30 << 20,
    )


def attention_back_kernel(
    io, k_ref, v_ref, q_ref, dmix_ref, dmixt_ref, mixt_ref, il_ref, e_ref, dqkv_ref, diag_ref, far_ref,
    dqt_s, p_s, ds_s, strip_s, dk_s, dv_s,
):
    tokens, width = q_ref.shape
    tile = min(tokens, 128)
    wide = min(tokens, 256)
    blocks = tokens // tile
    io.feed((k_ref, v_ref, q_ref, dmix_ref, dmixt_ref, mixt_ref, e_ref))

    def pair_body(p, carry):
        io.need_part(p, k_ref, v_ref, q_ref, dmix_ref, dmixt_ref, mixt_ref, e_ref)
        col = pl.ds(pl.multiple_of(p * LANE, LANE), LANE)
        kt = k_ref[:, col].T
        for s in range(2):
            h = 2 * p + s
            vp = half_lanes(v_ref[:, col], s)
            dm = half_lanes(dmix_ref[:, col], s)
            qm = half_lanes(q_ref[:, col], s)
            rows = pl.ds(pl.multiple_of(p * LANE + 64 * s, 64), 64)
            strip_s[...] = jnp.zeros_like(strip_s)
            far_low = jnp.zeros((8, LANE), F32)
            far_high = jnp.zeros((8, LANE), F32)
            for qc in range(tokens // wide):
                cols = slice(qc * wide, (qc + 1) * wide)
                dt = dmixt_ref[col, cols]
                delta = jnp.sum(
                    dmixt_ref[rows, cols].astype(F32) * mixt_ref[rows, cols].astype(F32), axis=0, keepdims=True
                )
                inverse = il_ref[h, :, cols]
                for kb in range(blocks):
                    ks = slice(kb * tile, (kb + 1) * tile)
                    dp = nn(vp[ks], dt)
                    prob = e_ref[h, ks, cols].astype(F32) * inverse
                    p_s[ks, :] = prob.astype(BF16)
                    ds = (prob * (dp - delta)).astype(BF16)
                    ds_s[ks, :] = ds
                    kept = ds.astype(F32)
                    for qs in range(wide // tile):
                        d = kb - (qc * (wide // tile) + qs)
                        t = kept[:, qs * tile:(qs + 1) * tile]
                        if abs(d) <= 1:
                            lo = (1 - d) * 128
                            strip_s[0:tile, lo:lo + tile] += t
                        else:
                            part = t[0:8]
                            for g in range(1, tile // 8):
                                part = part + t[8 * g:8 * g + 8]
                            if d > 0:
                                far_high = far_high + part
                            else:
                                far_low = far_low + part
                dv = nn(p_s[...], dm[cols])
                dk = nn(ds_s[...], qm[cols])
                if s == 0 and qc == 0:
                    dv_s[...] = dv
                    dk_s[...] = dk
                else:
                    dv_s[...] += dv
                    dk_s[...] += dk
                dqt_s[rows, cols] = nn(kt[64 * s:64 * s + 64], ds_s[...]).astype(BF16)
            fold = strip_s[...]
            size = strip_s.shape[0]
            while size > 8:
                size //= 2
                fold = fold[:size] + pltpu.roll(fold[size:], SPAN - size, 1)
            diag_ref[h] = fold
            far_ref[h, 0:8, :] = far_low
            far_ref[h, 8:16, :] = far_high
        kcol = pl.ds(pl.multiple_of(width + p * LANE, LANE), LANE)
        vcol = pl.ds(pl.multiple_of(2 * width + p * LANE, LANE), LANE)
        dqkv_ref[:, kcol] = dk_s[...].astype(BF16)
        dqkv_ref[:, vcol] = dv_s[...].astype(BF16)
        return carry

    lax.fori_loop(0, width // LANE, pair_body, 0)
    io.had(k_ref, v_ref, q_ref, dmix_ref, dmixt_ref, mixt_ref, e_ref)
    dqkv_ref[:, 0:width] = dqt_s[...].T


def attention_ins(q, k, v, e, il, mixt, dmix, dmixt):
    pairs = q.shape[1] // LANE
    return [(item, "v") for item in (k, v, q, dmix, dmixt, mixt, il, e)]


def attention_outs(q, heads):
    tokens, width = q.shape
    return [((tokens, 3 * width), BF16, "v"), ((heads, 8, SPAN), F32, "v"), ((heads, 16, LANE), F32, "v")]


def attention_scratch(q):
    tokens, width = q.shape
    tile, wide = min(tokens, 128), min(tokens, 256)
    return [
        pltpu.VMEM((width, tokens), BF16),
        pltpu.VMEM((tokens, wide), BF16),
        pltpu.VMEM((tokens, wide), BF16),
        pltpu.VMEM((tile, SPAN), F32),
        pltpu.VMEM((tokens, LANE), F32),
        pltpu.VMEM((tokens, LANE), F32),
    ]


def attention_back(q, k, v, e, il, mixt, dmix, dmixt, name):
    tokens, width = q.shape
    return call(
        attention_back_kernel,
        name,
        attention_ins(q, k, v, e, il, mixt, dmix, dmixt),
        attention_outs(q, e.shape[0]),
        attention_scratch(q),
        9,
        10 * tokens * tokens * width,
        16 << 20,
    )


def input_kernel(io, gains_ref, *refs):
    kinds = (len(refs) - 3) // 4
    reads, weights, writes = refs[:3 * kinds], refs[3 * kinds:3 * kinds + 3], refs[3 * kinds + 3:]
    for kind in range(kinds):
        dqkv_ref, x_ref, dmid_ref = reads[3 * kind:3 * kind + 3]
        width = x_ref.shape[1]
        io.need(dqkv_ref)
        total = None
        for i, w in enumerate(weights):
            io.need(w)
            part = nt(dqkv_ref[:, i * width:(i + 1) * width], w[...])
            total = part if total is None else total + part
        io.need(x_ref, dmid_ref)
        writes[kind][...] = dmid_ref[...] + norm_back(x_ref[...].astype(F32), gains_ref[0:1, :], total)
        io.done(writes[kind])


def input_back(gains, kinds, weights, name):
    width = weights[0].shape[0]
    tokens = sum(x.shape[0] for _, x, _ in kinds)
    return call(
        input_kernel,
        name,
        [(gains, "v")] + [(item, "h") for kind in kinds for item in kind] + [(w, "h") for w in weights],
        [(x.shape, F32, "h") for _, x, _ in kinds],
        [],
        32,
        6 * tokens * width * width,
        8 << 20,
    )


def put_rows(buf, value, per, offset, lanes, extra=None):
    for j in range(buf.shape[1]):
        for core in range(2):
            rows = slice((2 * j + core) * per, (2 * j + core + 1) * per)
            pieces = [value[rows, lo:lo + 256] for lo in lanes]
            if extra is not None:
                pieces.append(extra(rows))
            block = jnp.concatenate(pieces, axis=0) if len(pieces) > 1 else pieces[0]
            buf[core, j, pl.ds(offset, block.shape[0]), :] = block.astype(BF16)


def push_rows(io, buf, own_ref, send_ref, start, size):
    core = core_index()
    rows = pl.ds(start, size)
    for ref, side in ((send_ref, 1 - core), (own_ref, core)):
        io.push(buf.at[side, :, rows], ref.at[:, rows])


def halves_buffer(count, rows):
    return pltpu.VMEM((2, count, rows, 256), BF16)


def core_index():
    return (lax.axis_index("grp") % 2).astype(jnp.int32)


def halves(count, rows):
    return [((count, rows, 256), BF16, "a")] * 2


def down_grad_kernel(
    io, demb_ref, gains_ref, proj_ref, wp_s, out_ref, wd_s, a_ref, b_ref, wg_s, wu_s, mid_ref, wo_s,
    hid_ref, hidq_ref, dbr_ref, mixt_ref, mixtq_ref, datt_ref, n3_ref, n3q_ref, dpj_ref,
    dg_ref, du_ref, dmid_ref, dmix_ref, dmixt_ref, own_ref, send_ref,
    acc1_s, dpjq_s, dbrq_s, dattq_s, hidt_s, hidtq_s, buf_s,
):
    chain_kernel(
        io, demb_ref, gains_ref, proj_ref, wp_s, out_ref, wd_s, a_ref, b_ref, wg_s, wu_s, mid_ref, wo_s,
        dpjq_s, dbrq_s, dg_ref, du_ref, dattq_s, dmid_ref, dmix_ref, dmixt_ref, acc1_s,
    )
    io.done(dmix_ref, dmixt_ref)
    hidden, width = hid_ref.shape[1], dbr_ref.shape[1]
    count = own_ref.shape[0]
    per, per_down = width // (2 * count), hidden // (2 * count)
    io.need(hid_ref, hidq_ref)
    hidt_s[...] = hid_ref[...].T
    hidtq_s[...] = hidq_ref[...].T
    io.need(dbr_ref)
    for i in range(width // 256):
        col = slice(i * 256, (i + 1) * 256)
        value = nn(hidt_s[...], dbr_ref[:, col]) + nn(hidtq_s[...], dbrq_s[:, col])
        put_rows(buf_s, value, per_down, i * per_down, (0,))
        push_rows(io, buf_s, own_ref, send_ref, i * per_down, per_down)
    base = (width // 256) * per_down
    io.need(mixt_ref, mixtq_ref, datt_ref, n3_ref, n3q_ref, dpj_ref)
    value = nn(mixt_ref[...], datt_ref[:, 0:512]) + nn(mixtq_ref[...], dattq_s[:, 0:512])
    put_rows(buf_s, value, per, base, (0, 256))
    push_rows(io, buf_s, own_ref, send_ref, base, 2 * per)
    base = base + 2 * per
    value = nn(mixt_ref[...], datt_ref[:, 512:768]) + nn(mixtq_ref[...], dattq_s[:, 512:768])
    proj = nn(n3_ref[...].T, dpj_ref[...]) + nn(n3q_ref[...].T, dpjq_s[...])

    def proj_rows(rows):
        return jnp.concatenate([proj[rows], jnp.zeros((per, LANE), F32)], axis=1)

    put_rows(buf_s, value, per, base, (0,), extra=proj_rows)
    push_rows(io, buf_s, own_ref, send_ref, base, 2 * per)


def down_grads(query, doc, count):
    (demb, proj, out, mid, a, b, gains, wp, wd, wg, wu, wo), (hidq, mixtq, n3q) = query
    hid, dbr, mixt, datt, n3, dpj = doc
    tokens, hidden = hid.shape
    qtokens, width = out.shape
    per, per_down = width // (2 * count), hidden // (2 * count)
    plain = [(item, "h") for item in (hid, hidq, dbr, mixt, mixtq, datt, n3, n3q, dpj)]
    return call(
        down_grad_kernel,
        "query_ff_back_down_grads",
        chain_ins(demb, gains, proj, wp, out, wd, a, b, wg, wu, mid, wo) + plain,
        [
            ((qtokens, hidden), BF16, "h"),
            ((qtokens, hidden), BF16, "h"),
            ((qtokens, width), F32, "h"),
            ((qtokens, width), BF16, "h"),
            ((width, qtokens), BF16, "h"),
        ]
        + halves(count, (width // 256) * per_down + 4 * per),
        [
            pltpu.VMEM((qtokens, width), F32),
            pltpu.VMEM(proj.shape, BF16),
            pltpu.VMEM((qtokens, width), BF16),
            pltpu.VMEM((qtokens, width), BF16),
            pltpu.VMEM((hidden, tokens), BF16),
            pltpu.VMEM((hidden, qtokens), BF16),
            halves_buffer(count, (width // 256) * per_down + 4 * per),
        ],
        40,
        2 * (tokens + 256) * (width * width + width * hidden),
        24 << 20,
    )


def gate_grad_kernel(io, n2_ref, n2q_ref, dg_ref, dgq_ref, du_ref, duq_ref, own_ref, send_ref, n2t_s, n2tq_s, buf_s):
    width, hidden = n2_ref.shape[1], dg_ref.shape[1]
    count = own_ref.shape[0]
    per = width // (2 * count)
    io.need(n2_ref, n2q_ref)
    n2t_s[...] = n2_ref[...].T
    n2tq_s[...] = n2q_ref[...].T
    steps = hidden // 512
    for which, (d, dq) in enumerate(((dg_ref, dgq_ref), (du_ref, duq_ref))):
        io.need(dq)
        io.feed((d,))
        for i in range(steps):
            io.need_part(i, d)
            col = slice(i * 512, (i + 1) * 512)
            value = nn(n2t_s[...], d[:, col]) + nn(n2tq_s[...], dq[:, col])
            start = (which * steps + i) * 2 * per
            put_rows(buf_s, value, per, start, (0, 256))
            push_rows(io, buf_s, own_ref, send_ref, start, 2 * per)
        io.had(d)


def gate_grads(n2, n2q, dg, dgq, du, duq, count):
    tokens, width = n2.shape
    qtokens, hidden = dgq.shape
    per = width // (2 * count)
    return call(
        gate_grad_kernel,
        "gate_up_grads",
        [(n2, "h"), (n2q, "h"), (dg, f"h-{hidden // 512}"), (dgq, "h"), (du, f"h-{hidden // 512}"), (duq, "h")],
        halves(count, 2 * (hidden // 256) * per),
        [
            pltpu.VMEM((width, tokens), BF16),
            pltpu.VMEM((width, qtokens), BF16),
            halves_buffer(count, 2 * (hidden // 256) * per),
        ],
        22,
        4 * (tokens + 256) * width * hidden,
        16 << 20,
    )


def qkv_grad_kernel(
    io, k_ref, v_ref, q_ref, dmix_ref, dmixt_ref, mixt_ref, il_ref, e_ref, n1_ref, n1q_ref, d_ref,
    diagd_ref, fard_ref, hot_ref, loss_ref, dq_ref, diag_ref, far_ref, own_ref, send_ref, *rest,
):
    own_parts = lax.axis_size("dp")
    n1t_s, n1tq_s, buf_s = rest[-3:]
    attention_back_kernel(
        io, k_ref, v_ref, q_ref, dmix_ref, dmixt_ref, mixt_ref, il_ref, e_ref, dq_ref, diag_ref, far_ref, *rest[:-3]
    )
    io.done(dq_ref)
    width = n1_ref.shape[1]
    count = own_ref.shape[0]
    per = width // (2 * count)
    io.need(n1_ref, n1q_ref)
    n1t_s[...] = n1_ref[...].T
    n1tq_s[...] = n1q_ref[...].T
    io.need(d_ref)
    steps = (3 * width) // 512
    for i in range(steps):
        col = slice(i * 512, (i + 1) * 512)
        value = nn(n1t_s[...], d_ref[:, col]) + nn(n1tq_s[...], dq_ref[:, col])
        put_rows(buf_s, value, per, i * 2 * per, (0, 256))
        push_rows(io, buf_s, own_ref, send_ref, i * 2 * per, 2 * per)
    lo = steps * 512
    value = nn(n1t_s[...], d_ref[:, lo:lo + 256]) + nn(n1tq_s[...], dq_ref[:, lo:lo + 256])
    io.need(hot_ref)
    heads = diag_ref.shape[0]
    buckets = hot_ref.shape[0]
    table = jnp.zeros((heads, buckets), F32)
    for r in range(8):
        both = diagd_ref[:, r, :] + diag_ref[:, r, :]
        table = table + lax.dot_general(
            both, hot_ref[:, r * SPAN:(r + 1) * SPAN].astype(F32), (((1,), (1,)), ((), ())),
            precision=highest, preferred_element_type=F32,
        )
    far = fard_ref[...] + far_ref[...]
    low = jnp.sum(jnp.sum(far[:, 0:8, :], axis=1), axis=-1, keepdims=True)
    high = jnp.sum(jnp.sum(far[:, 8:16, :], axis=1), axis=-1, keepdims=True)
    column = lax.broadcasted_iota(jnp.int32, (1, buckets), 1)
    table = table + jnp.where(column == buckets // 2 - 1, low, 0.0) + jnp.where(column == buckets - 1, high, 0.0)
    table = jnp.concatenate([table, jnp.zeros((16 - heads, buckets), F32)], axis=0)
    loss = jnp.broadcast_to(loss_ref[...] * (1.0 / own_parts), (8, LANE))
    spare = jnp.concatenate([table[0:8], table[8:16], jnp.zeros((8, LANE - 2 * buckets), F32), loss], axis=1)
    put_rows(buf_s, value, per, steps * 2 * per, (0,), extra=lambda rows: spare)
    push_rows(io, buf_s, own_ref, send_ref, steps * 2 * per, per + 8)


def qkv_grads(query, n1, n1q, d, diag, far, hot, loss, count):
    tokens, width = n1.shape
    per = width // (2 * count)
    return call(
        qkv_grad_kernel,
        "query_attention_back_qkv_grads",
        attention_ins(*query)
        + [(item, "h") for item in (n1, n1q, d)]
        + [(diag, "v"), (far, "v"), (hot, "h"), (loss, "v")],
        attention_outs(query[0], query[3].shape[0]) + halves(count, 9 * per + 8),
        attention_scratch(query[0])
        + [
            pltpu.VMEM((width, tokens), BF16),
            pltpu.VMEM((width, n1q.shape[0]), BF16),
            halves_buffer(count, 9 * per + 8),
        ],
        24,
        2 * (tokens + 256) * 3 * width * width,
        10 << 20,
    )


def after(values, *deps):
    return lax.optimization_barrier((values, deps))[0]


def position(n_dp):
    dp, grp = lax.axis_index("dp").astype(jnp.int32), lax.axis_index("grp").astype(jnp.int32)
    return dp // 2, dp % 2, grp // 2


def slices(io_sems, moves):
    copies = [pltpu.make_async_copy(src, dst, io_sems.at[i]) for i, (src, dst) in enumerate(moves)]
    for copy in copies:
        copy.start()
    return copies


class Halves:
    def __init__(self, rows):
        self.rows, self.cut = rows, (rows // 32) * 16

    def sizes(self):
        return self.cut, self.rows - self.cut

    def spans(self):
        return pl.ds(0, self.cut), pl.ds(self.cut, self.rows - self.cut)


def first_kernel(n_dp, halves, io, own_ref, got_ref, x_ref, y_ref, ox_s, gx_s, oy_s, gy_s, sems):
    _, x, y = position(n_dp)
    top, low = halves.spans()
    moves = []
    for ref, a, b in ((own_ref, ox_s, oy_s), (got_ref, gx_s, gy_s)):
        moves += [(ref.at[:, 1 - x, :, top], a), (ref.at[:, :, 1 - y, low], b)]
    copies = slices(sems, moves)
    for i, (a, b, out) in enumerate(((ox_s, gx_s, x_ref), (oy_s, gy_s, y_ref))):
        copies[i].wait()
        copies[i + 2].wait()
        out[...] = (a[...].astype(F32) + b[...].astype(F32)).astype(BF16)
        io.done(out)


def pair_rows(n_dp, halves, flip, own_ref, got_ref, gx_ref, gy_ref, bufs, sems):
    _, x, y = position(n_dp)
    top, low = halves.spans()
    yt, xl = (1 - y, 1 - x) if flip else (y, x)
    ot_s, gt_s, rt_s, ol_s, gl_s, rl_s = bufs
    copies = slices(sems, [
        (own_ref.at[:, x, yt, top], ot_s), (got_ref.at[:, x, yt, top], gt_s), (gx_ref.at[:, yt], rt_s),
        (own_ref.at[:, xl, y, low], ol_s), (got_ref.at[:, xl, y, low], gl_s), (gy_ref.at[:, xl], rl_s),
    ])
    out = []
    for i in (0, 3):
        for copy in copies[i:i + 3]:
            copy.wait()
        a, b, c = bufs[i:i + 3]
        out.append(a[...].astype(F32) + b[...].astype(F32) + c[...].astype(F32))
    return out


def second_kernel(n_dp, halves, io, own_ref, got_ref, gx_ref, gy_ref, y_ref, x_ref, *refs):
    for out, value in zip((y_ref, x_ref), pair_rows(n_dp, halves, True, own_ref, got_ref, gx_ref, gy_ref, refs[:-1], refs[-1])):
        out[...] = value.astype(BF16)
        io.done(out)


def cross_kernel(n_dp, halves, io, own_ref, got_ref, xy_ref, x_ref, y_ref, own_s, got_s, sems):
    _, x, y = position(n_dp)
    moves = []
    for i, (xx, yy) in enumerate(((1 - x, 1 - y), (1 - x, y), (x, 1 - y))):
        moves += [(own_ref.at[:, xx, yy], own_s.at[i]), (got_ref.at[:, xx, yy], got_s.at[i])]
    copies = slices(sems, moves)
    for i, out in enumerate((xy_ref, x_ref, y_ref)):
        copies[2 * i].wait()
        copies[2 * i + 1].wait()
        out[...] = (own_s[i].astype(F32) + got_s[i].astype(F32)).astype(BF16)
        io.done(out)


def leave(z, line_s, outs, total_ref, io):
    nz = line_s.shape[0]
    if not outs:
        total_ref[...] = line_s[...].astype(BF16)
        return
    for k, out in enumerate(outs, 1):
        out[...] = line_s[(z + k) % nz].astype(BF16)
        io.done(out)
    total_ref[...] = line_s[z]


def cross_line_kernel(n_dp, halves, io, own_ref, got_ref, xy_ref, x_ref, y_ref, *refs):
    outs, total_ref, (line_s, own_s, got_s, sems) = refs[:-5], refs[-5], refs[-4:]
    z, x, y = position(n_dp)
    copies = slices(sems, [(own_ref.at[:, x, y], own_s), (got_ref.at[:, x, y], got_s)])
    for copy in copies:
        copy.wait()
    io.need(xy_ref, x_ref, y_ref)
    line_s[...] = own_s[...].astype(F32) + got_s[...].astype(F32) + xy_ref[...].astype(F32)
    line_s[...] += x_ref[...].astype(F32) + y_ref[...].astype(F32)
    leave(z, line_s, outs, total_ref, io)


def line_kernel(n_dp, halves, io, own_ref, got_ref, gx_ref, gy_ref, y_ref, x_ref, *refs):
    outs, total_ref, line_s, bufs, sems = refs[:-9], refs[-9], refs[-8], refs[-7:-1], refs[-1]
    z, _, _ = position(n_dp)
    top, low = pair_rows(n_dp, halves, False, own_ref, got_ref, gx_ref, gy_ref, bufs, sems)
    io.need(x_ref, y_ref)
    line_s[:, 0:halves.cut] = top + y_ref[...].astype(F32)
    line_s[:, halves.cut:] = low + x_ref[...].astype(F32)
    leave(z, line_s, outs, total_ref, io)


class Batch:
    def __init__(self, own, send, n_dp, n_grp, name):
        self.n_dp, self.n_grp, self.nz, self.name = n_dp, n_grp, n_dp // 2, name
        self.rows, self.cols = own.shape[1:]
        self.halves = Halves(self.rows)
        self.own = own
        self.got = lax.ppermute(send, "grp", [(i, i ^ 1) for i in range(n_grp)])

    def both(self):
        grid = lambda a: (a.reshape(self.nz, 2, 2, self.rows, self.cols), "r")
        return [grid(self.own), grid(self.got)]

    def along_x(self, array):
        return lax.ppermute(array, "dp", [(d, d ^ 1) for d in range(self.n_dp)])

    def along_y(self, array):
        return lax.ppermute(array, "grp", [(g, g ^ 2) for g in range(self.n_grp)])

    def run(self, kernel, step, ins, outs, scratch):
        body = functools.partial(kernel, self.n_dp, self.halves)
        return call(body, self.name + step, ins, outs, scratch, 24, 0, 0)

    def first(self):
        sizes = [(self.nz, 2, n, self.cols) for n in self.halves.sizes()]
        bufs = [pltpu.VMEM(size, BF16) for size in sizes for _ in range(2)]
        outs = [(size, BF16, "h") for size in sizes]
        sent = self.run(first_kernel, "_first", self.both(), outs, bufs + [pltpu.SemaphoreType.DMA((4,))])
        self.back1 = self.along_x(sent[0]), self.along_y(sent[1])
        return tuple(sent)

    def second_bufs(self):
        return [pltpu.VMEM((self.nz, n, self.cols), BF16) for n in self.halves.sizes() for _ in range(3)] + [
            pltpu.SemaphoreType.DMA((6,))
        ]

    def second(self):
        outs = [((self.nz, n, self.cols), BF16, "h") for n in self.halves.sizes()]
        ins = self.both() + [(a, "r") for a in self.back1]
        sent = self.run(second_kernel, "_second", ins, outs, self.second_bufs())
        self.back2 = self.along_y(sent[0]), self.along_x(sent[1])
        return tuple(sent)

    def cross(self):
        n_dp, n_grp = self.n_dp, self.n_grp
        piece = (self.nz, self.rows, self.cols)
        bufs = [pltpu.VMEM((3, *piece), BF16)] * 2 + [pltpu.SemaphoreType.DMA((6,))]
        sent = self.run(cross_kernel, "_cross", self.both(), [(piece, BF16, "h")] * 3, bufs)
        across = [(d * n_grp + g, (d ^ 1) * n_grp + (g ^ 2)) for d in range(n_dp) for g in range(n_grp)]
        self.back1 = ()
        self.back2 = lax.ppermute(sent[0], ("dp", "grp"), across), self.along_x(sent[1]), self.along_y(sent[2])
        return tuple(sent)

    def line(self, together=False):
        n_dp, nz = self.n_dp, self.nz
        piece, part = (nz, self.rows, self.cols), (self.rows, self.cols)
        outs = [(piece, BF16, "h")] if together else [(part, BF16, "h")] * (nz - 1) + [(part, F32, "v")]
        ins = self.both() + [(a, "r") for a in self.back1] + [(a, "h") for a in self.back2]
        if self.back1:
            kernel, bufs = line_kernel, self.second_bufs()
        else:
            kernel, bufs = cross_line_kernel, [pltpu.VMEM(piece, BF16)] * 2 + [pltpu.SemaphoreType.DMA((2,))]
        *sent, total = self.run(kernel, "_line", ins, outs, [pltpu.VMEM(piece, F32)] + bufs)
        if together:
            groups = [[2 * z + x for z in range(nz)] for x in range(2)]
            self.parts = [lax.all_to_all(total, "dp", 0, 0, tiled=True, axis_index_groups=groups)]
            return (total,)
        self.parts = [total] + [
            lax.ppermute(one, "dp", [(d, (d + 2 * k) % n_dp) for d in range(n_dp)]) for k, one in enumerate(sent, 1)
        ]
        return tuple(sent)


def weight_rows(weights, start):
    aligned = (start // 16) * 16
    return start - aligned, [w.at[pl.ds(pl.multiple_of(aligned, 16), 32)] for w in weights]


def finish_kernel(n_parts, places, gain_row, with_table, io, *refs):
    total, gains_ref, rest = refs[:n_parts], refs[n_parts], refs[n_parts + 1:]
    n_out, n_weights = len(places), len(gain_row[1])
    weights, rest = rest[:n_weights], rest[n_weights:]
    outs, rest = rest[:n_out], rest[n_out:]
    gain_ref, rest = rest[0], rest[1:]
    extra, rest = (rest[:2], rest[2:]) if with_table else ((), rest)
    sum_s, wide_s, bufs, sems = rest[0], rest[1], rest[2:-1], rest[-1]
    device = lax.axis_index("dp") * lax.axis_size("grp") + lax.axis_index("grp")
    per = outs[gain_row[1][0]].shape[0]
    start = device.astype(jnp.int32) * per
    shift, sources = weight_rows(weights, start)
    copies = slices(sems, list(zip(sources, bufs)))
    io.need(*total)
    if len(total) == 1:
        value = total[0][0].astype(F32)
        for i in range(1, total[0].shape[0]):
            value = value + total[0][i].astype(F32)
    else:
        value = total[0][...].astype(F32)
        for one in total[1:]:
            value = value + one[...].astype(F32)
    sum_s[...] = value
    for out, at in zip(outs, places):
        rows, width = out.shape
        for i in range(-(-width // 256)):
            cols = min(256, width - i * 256)
            out[:, i * 256:i * 256 + cols] = sum_s[at + i * rows:at + (i + 1) * rows, 0:cols]
    inner = jnp.zeros((per, 1), F32)
    for which, copy, buf in zip(gain_row[1], copies, bufs):
        copy.wait()
        width = buf.shape[1]
        wide_s[:, 0:width] = buf[...].astype(F32)
        mine = wide_s[pl.ds(pl.multiple_of(shift, 8), per), 0:width]
        inner = inner + jnp.sum(mine * outs[which][...], axis=-1, keepdims=True)
    lane = lax.broadcasted_iota(jnp.int32, (per, gains_ref.shape[1]), 1)
    row = lax.broadcasted_iota(jnp.int32, (per, gains_ref.shape[1]), 0)
    gain = jnp.sum(jnp.where(lane == row + start, gains_ref[gain_row[0]:gain_row[0] + 1, :], 0.0), axis=-1, keepdims=True)
    lane, row = lane[:, 0:LANE], row[:, 0:LANE]
    gain_ref[...] = jnp.sum(jnp.where(lane == row, inner / gain, 0.0), axis=0, keepdims=True)
    if with_table:
        table_ref, loss_ref = extra
        buckets, heads = table_ref.shape
        spare = sum_s[sum_s.shape[0] - 8:, :]
        table = jnp.concatenate([spare[:, 0:buckets], spare[:, buckets:2 * buckets]], axis=0)
        table = jnp.concatenate([table, jnp.zeros((16, LANE - buckets), F32)], axis=1)
        table = jnp.concatenate([table, jnp.zeros((LANE - 16, LANE), F32)], axis=0).T
        table_ref[...] = table[0:buckets, 0:heads]
        loss_ref[...] = spare[0:1, LANE:2 * LANE]


def finish(batch, places, shapes, gain_row, gains, weights, table=None):
    outs = [(shape, F32, "v") for shape in shapes] + [((1, LANE), F32, "v")]
    if table is not None:
        outs += [(table, F32, "v"), ((1, LANE), F32, "v")]
    width = max(w.shape[1] for w in weights)
    return call(
        functools.partial(finish_kernel, len(batch.parts), places, gain_row, table is not None),
        batch.name + "_finish",
        [(one, "v" if one.dtype == F32 else "h") for one in batch.parts] + [(gains, "v")] + [(w, "r") for w in weights],
        outs,
        [pltpu.VMEM((batch.rows, batch.cols), F32), pltpu.VMEM((32, width), F32)]
        + [pltpu.VMEM((32, w.shape[1]), BF16) for w in weights]
        + [pltpu.SemaphoreType.DMA((len(weights),))],
        16,
        0,
        0,
    )


def on_device(
    n_dp, n_grp, doc_tokens, doc_lengths, query_tokens, query_lengths, candidates, labels, gain_attn, w_query, w_key,
    w_value, w_out, bias_table, gain_ffn, w_gate, w_up, w_down, gain_final, w_proj,
):
    doc_rows, doc_len, width = doc_tokens.shape
    query_rows, query_len = query_tokens.shape[:2]
    hidden = w_gate.shape[1]
    bucket_total, heads = bias_table.shape
    devices = n_dp * n_grp
    axes = ("dp", "grp")
    x_doc = doc_tokens.reshape(doc_len, width)
    x_qry = query_tokens.reshape(query_rows * query_len, width)
    which = lax.broadcasted_iota(jnp.int32, (8 + bucket_total, width), 0)
    gains = jnp.where(which == 0, gain_attn[None], jnp.where(which == 1, gain_ffn[None], gain_final[None]))
    table = jnp.pad(bias_table, ((8, 0), (0, width - heads)))
    gains = jnp.where(which < 8, gains, table).astype(F32)
    weights = (w_query, w_key, w_value, w_out, w_gate, w_up, w_down, w_proj)
    hot = jnp.asarray(strip_onehot(), BF16)
    (q_q, q_k, q_v, q_e, q_il, q_mixt, q_mid, q_n1, q_n2, q_hid, q_a, q_b, q_out, q_n3, q_proj, packed, base) = forward(
        x_qry, query_lengths[None], gains, (hot, candidates, labels[None]), weights, False, heads
    )
    got = lax.all_to_all(jnp.broadcast_to(packed[None], (n_dp, *packed.shape)), "dp", 0, 0, tiled=True)
    (d_q, d_k, d_v, d_e, d_il, d_mixt, d_mid, d_n1, d_n2, d_hid, d_a, d_b, d_out, d_n3, d_proj, emb) = forward(
        x_doc, doc_lengths, gains, base, weights, True, heads
    )
    sums, lse = scores(got, emb, query_len)
    sums = lax.all_to_all(sums, "dp", 0, 0, tiled=True)
    demb_doc, demb_part, loss_group = retrieval_back(
        got, sums, emb, lse, query_len
    )
    demb_qry = lax.all_to_all(demb_part, "dp", 0, 0, tiled=True)
    back = (w_proj, w_down, w_gate, w_up, w_out)
    d_dpj, d_dbr, d_dg, d_du, d_datt, d_dmid, d_dmix, d_dmixt = chain(
        demb_doc, d_proj, d_out, d_mid, d_a, d_b, gains, *back, "doc_ff_back"
    )
    q_chain = (demb_qry, q_proj, q_out, q_mid, q_a, q_b, gains, *back)
    d_attention = lambda il: (d_q, d_k, d_v, d_e, il, d_mixt, d_dmix, d_dmixt)
    q_attention = lambda il, dmix, dmixt: (q_q, q_k, q_v, q_e, il, q_mixt, dmix, dmixt)
    qkv_weights = (w_query, w_key, w_value)
    fast = (n_dp, n_grp) == (8, 4)
    if fast:
        pairs = devices // 2
        q_dg, q_du, q_dmid, q_dmix, q_dmixt, own, send = down_grads(
            (q_chain, (q_hid, q_mixt, q_n3)), (d_hid, d_dbr, d_mixt, d_datt, d_n3, d_dpj), pairs
        )
        down = Batch(own, send, n_dp, n_grp, "down")
        own, send = gate_grads(d_n2, q_n2, d_dg, q_dg, d_du, q_du, pairs)
        gate = Batch(own, send, n_dp, n_grp, "gate")
        down.got = after(down.got, send)
        d_il = after(d_il, down.cross(), send)
        d_dqkv, d_diag, d_far = attention_back(*d_attention(d_il), "doc_attention_back")
        gate.got = after(gate.got, d_diag)
        q_il = after(q_il, gate.cross())
        q_dqkv, q_diag, q_far, own, send = qkv_grads(
            q_attention(q_il, q_dmix, q_dmixt), d_n1, q_n1, d_dqkv, d_diag, d_far, hot, loss_group, pairs
        )
        qkv = Batch(own, send, n_dp, n_grp, "qkv")
        (doc_grad,) = input_back(after(gains, send), ((d_dqkv, x_doc, d_dmid),), qkv_weights, "doc_input_back")
        down.back2 = after(down.back2, doc_grad)
        qkv.got = after(qkv.got, down.line(True))
        last_gains = after(gains, qkv.cross())
    else:
        q_dpj, q_dbr, q_dg, q_du, q_datt, q_dmid, q_dmix, q_dmixt = chain(*q_chain, "query_ff_back")
        d_dqkv, d_diag, d_far = attention_back(*d_attention(d_il), "doc_attention_back")
        q_dqkv, q_diag, q_far = attention_back(*q_attention(q_il, q_dmix, q_dmixt), "query_attention_back")
        last_gains = gains
        (doc_grad,) = input_back(gains, ((d_dqkv, x_doc, d_dmid),), qkv_weights, "doc_input_back")
    (query_grad,) = input_back(last_gains, ((q_dqkv, x_qry, q_dmid),), qkv_weights, "query_input_back")

    query_total = query_rows * devices
    per, per_down = width // devices, hidden // devices
    if fast:
        gate.back2 = after(gate.back2, query_grad)
        qkv.back2 = after(qkv.back2, gate.line())
        sent = qkv.line()
        down.parts, gate.parts = after((down.parts, gate.parts), sent)
        at = (width // 256) * per_down
        shard_down, shard_out, shard_proj, gain3 = finish(
            down, (0, at, at + 3 * per), ((per_down, width), (per, width), (per, w_proj.shape[1])), (2, (2,)), gains, [w_proj]
        )
        shard_gate, shard_up, gain2 = finish(
            gate, (0, (hidden // 256) * per), ((per, hidden),) * 2, (1, (0, 1)), gains, [w_gate, w_up]
        )
        shard_query, shard_key, shard_value, gain1, table_grad, loss = finish(
            qkv, (0, 3 * per, 6 * per), ((per, width),) * 3, (0, (0, 1, 2)), gains, qkv_weights, (bucket_total, heads)
        )
        shard_gains = [g[0, :per] for g in (gain1, gain2, gain3)]
        loss = loss[0, 0] / query_total
    else:

        def grad(left, right):
            product = tn(jnp.concatenate(left), jnp.concatenate(right))
            return lax.psum_scatter(product, axes, scatter_dimension=0, tiled=True)

        n1s = (d_n1, q_n1)
        shard_query, shard_key, shard_value = (
            grad(n1s, (d_dqkv[:, i * width:(i + 1) * width], q_dqkv[:, i * width:(i + 1) * width])) for i in range(3)
        )
        shard_out = grad((d_mixt.T, q_mixt.T), (d_datt, q_datt))
        shard_gate = grad((d_n2, q_n2), (d_dg, q_dg))
        shard_up = grad((d_n2, q_n2), (d_du, q_du))
        shard_down = grad((d_hid, q_hid), (d_dbr, q_dbr))
        shard_proj = grad((d_n3, q_n3), (d_dpj, q_dpj))
        start = (lax.axis_index("dp") * n_grp + lax.axis_index("grp")) * per
        mine = lambda a: lax.dynamic_slice_in_dim(a.astype(F32), start, per, 0)
        shard_gains = [
            sum(jnp.sum(mine(w) * g, axis=1) for w, g in pairs) / mine(gain)
            for gain, pairs in (
                (gain_attn, ((w_query, shard_query), (w_key, shard_key), (w_value, shard_value))),
                (gain_ffn, ((w_gate, shard_gate), (w_up, shard_up))),
                (gain_final, ((w_proj, shard_proj),)),
            )
        ]
        far = jnp.sum((d_far + q_far).reshape(heads, 2, -1), axis=-1)
        table = lax.dot_general(
            hot.astype(F32), (d_diag + q_diag).reshape(heads, -1), (((1,), (1,)), ((), ())),
            precision=highest, preferred_element_type=F32,
        )
        table = table.at[bucket_total // 2 - 1].add(far[:, 0]).at[bucket_total - 1].add(far[:, 1])
        table_grad, loss = lax.psum((table, loss_group[0, 0] / n_dp), axes)
        loss = loss / query_total
    return (
        loss,
        doc_grad.reshape(doc_rows, doc_len, width),
        query_grad.reshape(query_rows, query_len, width),
        shard_gains[0],
        shard_query,
        shard_key,
        shard_value,
        shard_out,
        table_grad,
        shard_gains[1],
        shard_gate,
        shard_up,
        shard_down,
        shard_gains[2],
        shard_proj,
    )


def solution(mesh):
    both = ("dp", "grp")
    rows3, rows2, rows1 = P(both, None, None), P(both, None), P(both)
    in_specs = (rows3, rows2, rows3, rows1, rows2, rows1) + (P(),) * 12
    out_specs = (
        P(), rows3, rows3, rows1, rows2, rows2, rows2, rows2, P(), rows1, rows2, rows2, rows2, rows1, rows2,
    )
    body = functools.partial(on_device, mesh.shape["dp"], mesh.shape["grp"])
    return jax.shard_map(body, mesh=mesh, in_specs=in_specs, out_specs=out_specs, check_vma=False)
```

```python
import functools
import itertools
import math

import jax
import jax.numpy as jnp
import numpy as np
from jax import lax
from jax.experimental import pallas as pl
from jax.experimental.pallas import tpu as pltpu
from jax.sharding import PartitionSpec as P

F32, BF16 = jnp.float32, jnp.bfloat16
BUCKETS = 32
DIST = 128
BLK = 128
MOST_DOC = 256
ROW_FILL = 480
EPS = 1e-6
SHARP = 0.25
SCALE = 16.0
NEG = -1e30
GELU_A = math.sqrt(2.0 / math.pi)
GELU_B = 0.044715
SPAN = 512
CH = 1024
LANE = 128
COST = 20
AHEAD = 1 << 30
PACK_INT = 48
highest = lax.Precision.HIGHEST


def nn(a, b):
    return jnp.dot(a, b, preferred_element_type=F32)


def nt(a, b):
    return lax.dot_general(a, b, (((1,), (1,)), ((), ())), preferred_element_type=F32)


def tn(a, b):
    return lax.dot_general(a, b, (((0,), (0,)), ((), ())), preferred_element_type=F32)


def bucket_of(offsets):
    half = BUCKETS // 2
    exact = half // 2
    dist = np.abs(offsets)
    scaled = np.log(np.maximum(dist, 1) / exact) / np.log(DIST / exact) * (half - exact)
    far = np.minimum(exact + np.maximum(scaled, 0).astype(np.int64), half - 1)
    return (offsets > 0) * half + np.where(dist < exact, dist, far)


def strip_onehot():
    j = np.arange(SPAN)
    offset = np.where(j < 384, 128 - j, 640 - j)
    index = np.stack([bucket_of(offset[(j - r) % SPAN]) for r in range(8)]).reshape(-1)
    return (index[None, :] == np.arange(BUCKETS)[:, None]).astype(np.float32)


VM = pl.BlockSpec(memory_space=pltpu.VMEM)
HB = pl.BlockSpec(memory_space=pl.ANY)


def by_part(run):
    return run if run[0][3] == 1 else sorted(run, key=lambda entry: entry[1])


class Io:
    def __init__(self, ins, outs, sems):
        self.ins, self.outs, self.sems, self.used = {}, {}, sems, 0
        self.going, self.queue, self.flying = [], [], 0
        for src, buf, parts in ins:
            self.ins[id(buf)] = (src, buf, parts, self.used)
            size = math.prod(buf.shape) * buf.dtype.itemsize // abs(parts)
            self.queue += [(id(buf), p, size, abs(parts)) for p in range(abs(parts))]
            self.used += abs(parts)
        for buf, dst in outs:
            self.outs[id(buf)] = (buf, dst)
        self.queue = [entry for _, run in itertools.groupby(self.queue, lambda e: e[3]) for entry in by_part(list(run))]
        self.feed()

    def feed(self, upto=()):
        upto = {id(buf) for buf in upto}
        while self.queue and (self.flying < AHEAD or any(entry[0] in upto for entry in self.queue)):
            key, p, size, _ = self.queue.pop(0)
            self.chunk(*self.ins[key], p).start()
            self.flying += size

    def landed(self, buf):
        self.flying -= math.prod(buf.shape) * buf.dtype.itemsize
        self.feed()

    def chunk(self, src, buf, parts, first, p):
        if parts == 1:
            return pltpu.make_async_copy(src, buf, self.sems.at[first])
        if parts > 0:
            size = buf.shape[0] // parts
            cut = (pl.ds(p * size if isinstance(p, int) else pl.multiple_of(p * size, 2), size),)
        else:
            size = buf.shape[1] // -parts
            cut = (slice(None), pl.ds(p * size if isinstance(p, int) else pl.multiple_of(p * size, LANE), size))
        return pltpu.make_async_copy(src.at[cut], buf.at[cut], self.sems.at[first + p])

    def need(self, *bufs):
        for buf in bufs:
            entry = self.ins.get(id(buf))
            if entry is not None:
                self.feed((buf,))
                for p in range(abs(entry[2])):
                    self.chunk(*entry, p).wait()
                del self.ins[id(buf)]
                self.landed(buf)

    def need_part(self, p, *bufs):
        for buf in bufs:
            if id(buf) in self.ins:
                self.chunk(*self.ins[id(buf)], p).wait()

    def had(self, *bufs):
        for buf in bufs:
            if self.ins.pop(id(buf), None) is not None:
                self.landed(buf)

    def done(self, *bufs):
        for buf in bufs:
            if id(buf) in self.outs:
                src, dst = self.outs.pop(id(buf))
                self.push(src, dst)

    def done_rows(self, buf, start, size):
        src, dst = self.outs[id(buf)]
        rows = (slice(None), pl.ds(start, size))
        self.push(src.at[rows], dst.at[rows])

    def gone(self, buf):
        self.outs.pop(id(buf))

    def push(self, src, dst):
        copy = pltpu.make_async_copy(src, dst, self.sems.at[self.used])
        self.used += 1
        copy.start()
        self.going.append(copy)

    def close(self):
        self.need(*[entry[1] for entry in list(self.ins.values())])
        self.done(*[entry[0] for entry in list(self.outs.values())])
        for copy in self.going:
            copy.wait()


def call(kernel, name, ins, outs, scratch, mib, flops, moved=8 << 20):
    args, in_specs, out_specs, out_shape, buffers, sems = [], [], [], [], [], 0
    for array, kind in ins:
        if kind == "r":
            args.append(array)
            in_specs.append(HB)
        elif kind[0] == "h":
            args.append(pltpu.with_memory_space_constraint(array, pltpu.HBM))
            in_specs.append(HB)
            buffers.append(pltpu.VMEM(array.shape, array.dtype))
            sems += abs(int(kind[1:] or 1))
        else:
            args.append(array)
            in_specs.append(VM)
    for shape, dtype, kind in outs:
        if kind == "a":
            out_shape.append(pltpu.HBM(shape, dtype))
            out_specs.append(HB)
            sems += 8
        elif kind == "h":
            out_shape.append(pltpu.HBM(shape, dtype))
            out_specs.append(HB)
            buffers.append(pltpu.VMEM(shape, dtype))
            sems += 4
        else:
            out_shape.append(jax.ShapeDtypeStruct(shape, dtype))
            out_specs.append(VM)

    def body(*refs):
        n_in, n_out, n_buf = len(ins), len(outs), len(buffers)
        given, made = list(refs[:n_in]), list(refs[n_in:n_in + n_out])
        bufs = iter(refs[n_in + n_out:n_in + n_out + n_buf])
        rest = refs[n_in + n_out + n_buf:]
        reads, writes = [], []
        for i, (_, kind) in enumerate(ins):
            if kind[0] == "h":
                buf = next(bufs)
                reads.append((given[i], buf, int(kind[1:] or 1)))
                given[i] = buf
        for i, (_, _, kind) in enumerate(outs):
            if kind == "h":
                buf = next(bufs)
                writes.append((buf, made[i]))
                made[i] = buf
        io = Io(reads, writes, rest[-1])
        kernel(io, *given, *made, *rest[:-1])
        io.close()

    return pl.pallas_call(
        body,
        name=name,
        out_shape=out_shape,
        in_specs=in_specs,
        out_specs=out_specs,
        scratch_shapes=buffers + scratch + [pltpu.SemaphoreType.DMA((max(sems, 1),))],
        compiler_params=pltpu.CompilerParams(vmem_limit_bytes=mib << 20),
        cost_estimate=pl.CostEstimate(flops=int(flops) * COST, bytes_accessed=int(moved) * COST, transcendentals=0),
    )(*args)


def reachable(d, tile):
    return (abs(d) - 1) * tile + 1 < MOST_DOC


def half_lanes(values, side):
    lane = lax.broadcasted_iota(jnp.int32, (1, LANE), 1)
    return jnp.where((lane // 64) == side, values.astype(F32), 0.0).astype(BF16)


def norm_back(values, gain, dn):
    s = lax.rsqrt(jnp.mean(values * values, axis=-1, keepdims=True) + EPS)
    unit = values * s
    t = dn * gain
    return s * (t - unit * jnp.mean(t * unit, axis=-1, keepdims=True))


def forward_kernel(
    is_doc, io, x_ref, lens_ref, gains_ref, extra_ref, wq_s, wk_s, wv_s, wo_s, wg_s, wu_s, wd_s, wp_s,
    q_ref, k_ref, v_ref, e_ref, il_ref, mixt_ref, mid_ref, n1_ref, n2_ref, hid_ref, a_ref, b_ref,
    out_ref, n3_ref, proj_ref, emb_ref, *rest,
):
    if is_doc:
        base_ref, tail = extra_ref, rest
    else:
        hot_ref, cand_ref, label_ref = extra_ref
        base_ref, tail = rest[0], rest[1:]
    mask_s, strip_s, s_s, e_s, vt_s = tail
    tokens, width = x_ref.shape
    hidden = wg_s.shape[1]
    heads = e_ref.shape[0]
    io.need(lens_ref)
    if not is_doc:
        io.need(hot_ref)
        tab = gains_ref[8:24, 0:hot_ref.shape[0]].astype(BF16)
        for r in range(8):
            rows = nn(tab, hot_ref[:, r * SPAN:(r + 1) * SPAN])
            for h in range(heads):
                base_ref[h, r:r + 1, :] = rows[h:h + 1, :]
    io.need(x_ref)
    x = x_ref[...].astype(F32)
    s1 = lax.rsqrt(jnp.mean(x * x, axis=-1, keepdims=True) + EPS)
    n1_ref[...] = (x * s1 * gains_ref[0:1, :]).astype(BF16)
    io.done(n1_ref)
    tile = min(tokens, 128)
    blocks = tokens // tile
    row_id = lax.broadcasted_iota(jnp.int32, (tokens, 1), 0)
    col_id = lax.broadcasted_iota(jnp.int32, (1, tokens), 1)
    if is_doc:
        seg_k = jnp.zeros((tokens, 1), jnp.int32)
        seg_q = jnp.zeros((1, tokens), jnp.int32)
        end = jnp.zeros((1, 1), jnp.int32)
        for i in range(lens_ref.shape[1]):
            end = end + lens_ref[0:1, i:i + 1]
            seg_k = seg_k + (row_id >= end).astype(jnp.int32)
            seg_q = seg_q + (col_id >= end).astype(jnp.int32)
    else:
        count = lens_ref.shape[1]
        length = tokens // count
        seg_q = col_id // length
        seg_k = jnp.full((tokens, 1), -1, jnp.int32)
        for i in range(count):
            inside = (row_id >= i * length) & (row_id < i * length + lens_ref[0:1, i:i + 1])
            seg_k = jnp.where(inside, i, seg_k)
    mask_s[...] = jnp.where(seg_k == seg_q, 0.0, NEG)
    for i, (w, o) in enumerate(((wq_s, q_ref), (wk_s, k_ref), (wv_s, v_ref))):
        io.need(w)
        o[...] = nn(n1_ref[...], w[...]).astype(BF16)
        io.done(o)
    vt_s[...] = v_ref[...].T
    if is_doc:
        io.need(base_ref)
    else:
        io.done(base_ref)

    def softmax_pair(p, slot):
        col = pl.ds(pl.multiple_of(p * LANE, LANE), LANE)
        for s in range(2):
            h = 2 * p + s
            first = base_ref[h]
            for g in range(tile // 8):
                strip_s[s, 8 * g:8 * g + 8, :] = pltpu.roll(first, 8 * g, 1) if g else first
            low_far, high_far = first[0:1, 256:256 + tile], first[0:1, 384:384 + tile]
            scores = nt(half_lanes(k_ref[:, col], s), q_ref[:, col])
            for qb in range(blocks):
                cols = slice(qb * tile, (qb + 1) * tile)
                tops = []
                near = [kb for kb in range(blocks) if reachable(kb - qb, tile)]
                for kb in near:
                    ks = slice(kb * tile, (kb + 1) * tile)
                    d = kb - qb
                    t = scores[ks, cols]
                    if abs(d) <= 1:
                        lo = (1 - d) * 128
                        t = t + strip_s[s, :, lo:lo + tile]
                    else:
                        t = t + (high_far if d > 0 else low_far)
                    t = t + mask_s[ks, cols]
                    s_s[s, ks, cols] = t
                    tops.append(jnp.max(t, axis=0, keepdims=True))
                top = functools.reduce(jnp.maximum, tops)
                total = None
                for kb in near:
                    ks = slice(kb * tile, (kb + 1) * tile)
                    e = jnp.exp(s_s[s, ks, cols] - top)
                    part = jnp.sum(e, axis=0, keepdims=True)
                    total = part if total is None else total + part
                    kept = e.astype(BF16)
                    e_ref[h, ks, cols] = kept
                    e_s[slot, s, ks, cols] = kept
                il_ref[h, :, cols] = 1.0 / total

    def mix_pair(p, slot):
        for s in range(2):
            rows = pl.ds(pl.multiple_of(p * LANE + 64 * s, 64), 64)
            mixt_ref[rows, :] = (nn(vt_s[rows, :], e_s[slot, s]) * il_ref[2 * p + s]).astype(BF16)

    def pair_step(i, carry):
        mix_pair(2 * i, 0)
        softmax_pair(2 * i + 1, 1)
        mix_pair(2 * i + 1, 1)
        softmax_pair(2 * i + 2, 0)
        return carry

    pairs = width // LANE
    for kb, qb in itertools.product(range(blocks), repeat=2):
        if not reachable(kb - qb, tile):
            far = (slice(kb * tile, (kb + 1) * tile), slice(qb * tile, (qb + 1) * tile))
            e_s[(slice(None), slice(None), *far)] = jnp.zeros((2, 2, tile, tile), BF16)
            e_ref[(slice(None), *far)] = jnp.zeros((heads, tile, tile), BF16)
    softmax_pair(0, 0)
    lax.fori_loop(0, pairs // 2 - 1, pair_step, 0)
    mix_pair(pairs - 2, 0)
    softmax_pair(pairs - 1, 1)
    mix_pair(pairs - 1, 1)
    io.done(e_ref, mixt_ref)
    io.need(wo_s)
    mid_ref[...] = x_ref[...].astype(F32) + nn(mixt_ref[...].T, wo_s[...])
    mid = mid_ref[...]
    s2 = lax.rsqrt(jnp.mean(mid * mid, axis=-1, keepdims=True) + EPS)
    n2_ref[...] = (mid * s2 * gains_ref[1:2, :]).astype(BF16)
    io.done(mid_ref, n2_ref)

    io.feed((wg_s, wu_s))

    def ff_body(j, carry):
        io.need_part(j, wg_s, wu_s)
        col = pl.ds(pl.multiple_of(j * CH, CH), CH)
        g = nn(n2_ref[...], wg_s[:, col])
        u = nn(n2_ref[...], wu_s[:, col])
        sq = g * g
        t = jnp.tanh(GELU_A * g * (1.0 + GELU_B * sq))
        half = 0.5 + 0.5 * t
        gel = g * half
        slope = half + (0.5 * GELU_A) * g * (1.0 - t * t) * (1.0 + 3.0 * GELU_B * sq)
        hid_ref[:, col] = (gel * u).astype(BF16)
        a_ref[:, col] = (u * slope).astype(BF16)
        b_ref[:, col] = gel.astype(BF16)
        return carry

    lax.fori_loop(0, hidden // CH, ff_body, 0)
    io.had(wg_s, wu_s)
    io.done(hid_ref, a_ref, b_ref)
    io.need(wd_s)
    out_ref[...] = mid_ref[...] + nn(hid_ref[...], wd_s[...])
    o = out_ref[...]
    s3 = lax.rsqrt(jnp.mean(o * o, axis=-1, keepdims=True) + EPS)
    n3_ref[...] = (o * s3 * gains_ref[2:3, :]).astype(BF16)
    io.done(out_ref, n3_ref)
    io.need(wp_s)
    pr = nn(n3_ref[...], wp_s[...])
    proj_ref[...] = pr
    emb = (pr * lax.rsqrt(jnp.sum(pr * pr, axis=-1, keepdims=True) + EPS)).astype(BF16)
    if is_doc:
        emb_ref[...] = emb
    else:
        io.need(cand_ref, label_ref)
        ints = pack_ints(cand_ref, label_ref, lens_ref)
        for i in range(emb_ref.shape[0]):
            emb_ref[i, 0:tokens, :] = emb
            emb_ref[i, tokens:, :] = ints


def pack_ints(cand_ref, label_ref, lens_ref):
    count = cand_ref.shape[1]
    eye = lax.broadcasted_iota(jnp.int32, (count, count), 0) == lax.broadcasted_iota(jnp.int32, (count, count), 1)
    lane = lax.broadcasted_iota(jnp.int32, (1, LANE), 1)
    row = lax.broadcasted_iota(jnp.int32, (PACK_INT, 1), 0)
    packed = jnp.zeros((PACK_INT, LANE), F32)
    for a in range(cand_ref.shape[0]):
        values = jnp.where(eye, cand_ref[a:a + 1, :].astype(F32), 0.0)
        column = jnp.sum(values, axis=1, keepdims=True)
        column = jnp.concatenate([column, jnp.zeros((PACK_INT - count, 1), F32)], axis=0)
        column = jnp.where(row == count, label_ref[0:1, a:a + 1].astype(F32), column)
        column = jnp.where(row == count + 1, lens_ref[0:1, a:a + 1].astype(F32), column)
        packed = jnp.where(lane == a, column, packed)
    return packed.astype(BF16)


def forward(x, lens, gains, extra, weights, is_doc, heads, copies=1):
    tokens, width = x.shape
    hidden = weights[4].shape[1]
    proj = weights[7].shape[1]
    outs = [((tokens, width), BF16, "h")] * 3 + [
        ((heads, tokens, tokens), BF16, "h"),
        ((heads, 1, tokens), F32, "v"),
        ((width, tokens), BF16, "h"),
        ((tokens, width), F32, "h"),
        ((tokens, width), BF16, "h"),
        ((tokens, width), BF16, "h"),
        ((tokens, hidden), BF16, "h"),
        ((tokens, hidden), BF16, "h"),
        ((tokens, hidden), BF16, "h"),
        ((tokens, width), F32, "h"),
        ((tokens, width), BF16, "h"),
        ((tokens, proj), F32, "h"),
        ((tokens, proj) if is_doc else (copies, tokens + PACK_INT, proj), BF16, "v"),
    ]
    tile = min(tokens, 128)
    scratch = [
        pltpu.VMEM((tokens, tokens), F32),
        pltpu.VMEM((2, tile, SPAN), F32),
        pltpu.VMEM((2, tokens, tokens), F32),
        pltpu.VMEM((2, 2, tokens, tokens), BF16),
        pltpu.VMEM((width, tokens), BF16),
    ]
    steps = weights[4].shape[1] // CH
    streams = [(w, f"h-{steps}" if w.shape == weights[4].shape else "h") for w in weights]
    ins = [(x, "h"), (lens, "h"), (gains, "v")]
    if is_doc:
        kernel = functools.partial(forward_kernel, True)
        ins = ins + [(extra, "h")] + streams
    else:
        outs.append(((heads, 8, SPAN), F32, "h"))

        def kernel(io, x_ref, lens_ref, gains_ref, hot_ref, cand_ref, label_ref, *rest):
            forward_kernel(False, io, x_ref, lens_ref, gains_ref, (hot_ref, cand_ref, label_ref), *rest)

        ins = ins + [(item, "h") for item in extra] + streams
    flops = 2 * tokens * (4 * width * width + 3 * width * hidden + width * proj) + 4 * tokens * tokens * width
    return call(kernel, "doc_forward" if is_doc else "query_forward", ins, outs, scratch, 50, flops, 30 << 20)


def unpack(got_ref, tokens):
    parts = got_ref.shape[0]
    own = 2
    lane = lax.broadcasted_iota(jnp.int32, (1, LANE), 1)
    ints = None
    for i in range(parts):
        block = got_ref[i, tokens:, :].astype(F32)
        if i:
            block = pltpu.roll(block, own * i, 1)
        block = jnp.where((lane // own) == i, block, 0.0)
        ints = block if ints is None else ints + block
    return ints[0:32, :], ints[32:33, :], ints[33:34, :]


def expand_onehot(queries, length):
    col = lax.broadcasted_iota(jnp.int32, (LANE, queries * length), 1)
    row = lax.broadcasted_iota(jnp.int32, (LANE, queries * length), 0)
    return ((col // length) == row).astype(F32)


def token_valid(lens, queries, length):
    hot = expand_onehot(queries, length)
    spread = jnp.dot(jnp.broadcast_to(lens, (8, LANE)), hot, precision=highest, preferred_element_type=F32)[0:1]
    place = lax.broadcasted_iota(jnp.int32, (1, queries * length), 1) % length
    return place.astype(F32) < spread, hot


def block_scores(emb_ref, q_s, b):
    t = nt(emb_ref[b * BLK:(b + 1) * BLK, :], q_s[...]) * (1.0 / SHARP)
    row = lax.broadcasted_iota(jnp.int32, (BLK, 1), 0) + b * BLK
    return jnp.where(row < ROW_FILL, t, NEG) if (b + 1) * BLK > ROW_FILL else t


def score_kernel(length, io, got_ref, emb_ref, sums_ref, lse_ref, q_s):
    parts = got_ref.shape[0]
    tokens = q_s.shape[0] // parts
    queries = q_s.shape[0] // length
    for i in range(parts):
        q_s[i * tokens:(i + 1) * tokens, :] = got_ref[i, 0:tokens, :]
    _, _, lens = unpack(got_ref, tokens)
    valid, hot = token_valid(lens, queries, length)
    blocks = emb_ref.shape[0] // BLK
    rows = []
    for b in range(blocks):
        t = block_scores(emb_ref, q_s, b)
        top = jnp.max(t, axis=0, keepdims=True)
        lse = top + jnp.log(jnp.sum(jnp.exp(t - top), axis=0, keepdims=True))
        lse_ref[b:b + 1, :] = lse
        rows.append(jnp.where(valid, SHARP * lse, 0.0))
    rows.append(jnp.zeros((8 - blocks, rows[0].shape[1]), F32))
    sums = lax.dot_general(
        jnp.concatenate(rows, axis=0), hot, (((1,), (1,)), ((), ())), precision=highest, preferred_element_type=F32
    )
    for i in range(parts):
        sums_ref[i] = sums


def scores(got, emb, length):
    parts = got.shape[0]
    tokens = got.shape[1] - PACK_INT
    total = parts * tokens
    return call(
        functools.partial(score_kernel, length),
        "block_sums",
        [(got, "v"), (emb, "v")],
        [((parts, 8, LANE), F32, "v"), ((8, total), F32, "v")],
        [pltpu.VMEM((total, emb.shape[1]), BF16)],
        24,
        2 * emb.shape[0] * total * 128,
        1 << 20,
    )


def loss_kernel(length, io, got_ref, sums_ref, emb_ref, lse_ref, doc_ref, qry_ref, loss_ref, q_s, d_s, s_s):
    parts = got_ref.shape[0]
    tokens = q_s.shape[0] // parts
    queries = q_s.shape[0] // length
    for i in range(parts):
        q_s[i * tokens:(i + 1) * tokens, :] = got_ref[i, 0:tokens, :]
    cand, label, lens = unpack(got_ref, tokens)
    valid, hot = token_valid(lens, queries, length)
    blocks = emb_ref.shape[0] // BLK
    logits = jnp.zeros(cand.shape, F32)
    for i in range(parts):
        for b in range(blocks):
            logits = logits + jnp.where(cand == float(i * blocks + b), sums_ref[i, b:b + 1, :], 0.0)
    logits = SCALE * logits
    top = jnp.max(logits, axis=0, keepdims=True)
    lse = top + jnp.log(jnp.sum(jnp.exp(logits - top), axis=0, keepdims=True))
    choice = lax.broadcasted_iota(jnp.int32, cand.shape, 0).astype(F32) == label
    lane = lax.broadcasted_iota(jnp.int32, (1, LANE), 1)
    picked = jnp.sum(jnp.where(choice, logits, 0.0), axis=0, keepdims=True)
    each = jnp.where(lane < queries, lse - picked, 0.0)
    loss_ref[...] = jnp.broadcast_to(jnp.sum(each, axis=1, keepdims=True), (1, LANE))
    dlogits = SCALE * (jnp.exp(logits - lse) - jnp.where(choice, 1.0, 0.0))
    me = lax.axis_index("dp").astype(jnp.int32)
    rows = []
    for b in range(blocks):
        mine = (me * blocks + b).astype(F32)
        rows.append(jnp.sum(jnp.where(cand == mine, dlogits, 0.0), axis=0, keepdims=True))
    rows.append(jnp.zeros((8 - blocks, LANE), F32))
    spread = jnp.dot(jnp.concatenate(rows, axis=0), hot, precision=highest, preferred_element_type=F32)
    for b in range(blocks):
        t = block_scores(emb_ref, q_s, b)
        weight = jnp.where(valid, spread[b:b + 1, :], 0.0)
        d_s[b * BLK:(b + 1) * BLK, :] = (weight * jnp.exp(t - lse_ref[b:b + 1, :])).astype(BF16)
    doc_ref[...] = nn(d_s[...], q_s[...])
    s_s[...] = d_s[...].T
    qry_ref[...] = nn(s_s[...], emb_ref[...]).reshape(qry_ref.shape)


def retrieval_back(got, sums, emb, lse, length):
    parts = got.shape[0]
    tokens = got.shape[1] - PACK_INT
    total = parts * tokens
    docs, proj = emb.shape
    return call(
        functools.partial(loss_kernel, length),
        "retrieval_back",
        [(got, "v"), (sums, "v"), (emb, "v"), (lse, "v")],
        [((docs, proj), F32, "v"), ((parts, tokens, proj), F32, "v"), ((1, LANE), F32, "v")],
        [pltpu.VMEM((total, proj), BF16), pltpu.VMEM((docs, total), BF16), pltpu.VMEM((total, docs), BF16)],
        32,
        6 * docs * total * proj,
        2 << 20,
    )


def chain_kernel(
    io, demb_ref, gains_ref, proj_ref, wp_s, out_ref, wd_s, a_ref, b_ref, wg_s, wu_s, mid_ref, wo_s,
    dpj_ref, dbr_ref, dg_ref, du_ref, datt_ref, dmid_ref, dmix_ref, dmixt_ref, acc_s,
):
    hidden = a_ref.shape[1]
    if len(demb_ref.shape) == 3:
        dy = demb_ref[0]
        for i in range(1, demb_ref.shape[0]):
            dy = dy + demb_ref[i]
    else:
        dy = demb_ref[...]
    io.need(proj_ref)
    pr = proj_ref[...]
    r = lax.rsqrt(jnp.sum(pr * pr, axis=-1, keepdims=True) + EPS)
    unit = pr * r
    dpj_ref[...] = (r * (dy - unit * jnp.sum(dy * unit, axis=-1, keepdims=True))).astype(BF16)
    io.done(dpj_ref)
    io.need(wp_s, out_ref)
    dn3 = nt(dpj_ref[...], wp_s[...])
    dout = norm_back(out_ref[...], gains_ref[2:3, :], dn3)
    dmid_ref[...] = dout
    dbr_ref[...] = dout.astype(BF16)
    io.done(dbr_ref)

    io.feed((wd_s, a_ref, b_ref, wg_s, wu_s))

    def body(j, carry):
        io.need_part(j, wd_s, a_ref, b_ref)
        col = pl.ds(pl.multiple_of(j * CH, CH), CH)
        dh = nt(dbr_ref[...], wd_s[col, :])
        dg_ref[:, col] = (dh * a_ref[:, col].astype(F32)).astype(BF16)
        du_ref[:, col] = (dh * b_ref[:, col].astype(F32)).astype(BF16)
        return carry

    lax.fori_loop(0, hidden // CH, body, 0)
    io.had(wd_s, a_ref, b_ref)
    io.done(dg_ref, du_ref)
    io.need(wg_s, wu_s)
    acc_s[...] = nt(dg_ref[...], wg_s[...]) + nt(du_ref[...], wu_s[...])
    io.need(mid_ref)
    dmid = dmid_ref[...] + norm_back(mid_ref[...], gains_ref[1:2, :], acc_s[...])
    dmid_ref[...] = dmid
    datt_ref[...] = dmid.astype(BF16)
    io.done(dmid_ref, datt_ref)
    io.need(wo_s)
    dmix = nt(datt_ref[...], wo_s[...]).astype(BF16)
    dmix_ref[...] = dmix
    dmixt_ref[...] = dmix.T


def chain_ins(demb, gains, proj, wp, out, wd, a, b, wg, wu, mid, wo):
    steps = a.shape[1] // CH
    plain = lambda *items: [(item, "h") for item in items]
    parts = [(wd, f"h{steps}")] + [(item, f"h-{steps}") for item in (a, b)]
    return [(demb, "v"), (gains, "v")] + plain(proj, wp, out) + parts + plain(wg, wu, mid, wo)


def chain(demb, proj, out, mid, a, b, gains, wp, wd, wg, wu, wo, name):
    tokens, width = out.shape
    hidden = a.shape[1]
    return call(
        chain_kernel,
        name,
        chain_ins(demb, gains, proj, wp, out, wd, a, b, wg, wu, mid, wo),
        [
            (proj.shape, BF16, "h"),
            ((tokens, width), BF16, "h"),
            ((tokens, hidden), BF16, "h"),
            ((tokens, hidden), BF16, "h"),
            ((tokens, width), BF16, "h"),
            ((tokens, width), F32, "h"),
            ((tokens, width), BF16, "h"),
            ((width, tokens), BF16, "h"),
        ],
        [pltpu.VMEM((tokens, width), F32)],
        44,
        2 * tokens * (width * width + 3 * width * hidden + width * 128),
        30 << 20,
    )


def attention_back_kernel(
    io, k_ref, v_ref, q_ref, dmix_ref, dmixt_ref, mixt_ref, il_ref, e_ref, dqkv_ref, diag_ref, far_ref,
    dqt_s, p_s, ds_s, strip_s, dk_s, dv_s,
):
    tokens, width = q_ref.shape
    tile = min(tokens, 128)
    wide = min(tokens, 256)
    blocks = tokens // tile
    io.feed((k_ref, v_ref, q_ref, dmix_ref, dmixt_ref, mixt_ref, e_ref))

    def pair_body(p, carry):
        io.need_part(p, k_ref, v_ref, q_ref, dmix_ref, dmixt_ref, mixt_ref, e_ref)
        col = pl.ds(pl.multiple_of(p * LANE, LANE), LANE)
        kt = k_ref[:, col].T
        for s in range(2):
            h = 2 * p + s
            vp = half_lanes(v_ref[:, col], s)
            dm = half_lanes(dmix_ref[:, col], s)
            qm = half_lanes(q_ref[:, col], s)
            rows = pl.ds(pl.multiple_of(p * LANE + 64 * s, 64), 64)
            strip_s[...] = jnp.zeros_like(strip_s)
            far_low = jnp.zeros((8, LANE), F32)
            far_high = jnp.zeros((8, LANE), F32)
            for qc in range(tokens // wide):
                cols = slice(qc * wide, (qc + 1) * wide)
                dt = dmixt_ref[col, cols]
                delta = jnp.sum(
                    dmixt_ref[rows, cols].astype(F32) * mixt_ref[rows, cols].astype(F32), axis=0, keepdims=True
                )
                inverse = il_ref[h, :, cols]
                for kb in range(blocks):
                    ks = slice(kb * tile, (kb + 1) * tile)
                    dp = nn(vp[ks], dt)
                    prob = e_ref[h, ks, cols].astype(F32) * inverse
                    p_s[ks, :] = prob.astype(BF16)
                    ds = (prob * (dp - delta)).astype(BF16)
                    ds_s[ks, :] = ds
                    kept = ds.astype(F32)
                    for qs in range(wide // tile):
                        d = kb - (qc * (wide // tile) + qs)
                        t = kept[:, qs * tile:(qs + 1) * tile]
                        if abs(d) <= 1:
                            lo = (1 - d) * 128
                            strip_s[0:tile, lo:lo + tile] += t
                        else:
                            part = t[0:8]
                            for g in range(1, tile // 8):
                                part = part + t[8 * g:8 * g + 8]
                            if d > 0:
                                far_high = far_high + part
                            else:
                                far_low = far_low + part
                dv = nn(p_s[...], dm[cols])
                dk = nn(ds_s[...], qm[cols])
                if s == 0 and qc == 0:
                    dv_s[...] = dv
                    dk_s[...] = dk
                else:
                    dv_s[...] += dv
                    dk_s[...] += dk
                dqt_s[rows, cols] = nn(kt[64 * s:64 * s + 64], ds_s[...]).astype(BF16)
            fold = strip_s[...]
            size = strip_s.shape[0]
            while size > 8:
                size //= 2
                fold = fold[:size] + pltpu.roll(fold[size:], SPAN - size, 1)
            diag_ref[h] = fold
            far_ref[h, 0:8, :] = far_low
            far_ref[h, 8:16, :] = far_high
        kcol = pl.ds(pl.multiple_of(width + p * LANE, LANE), LANE)
        vcol = pl.ds(pl.multiple_of(2 * width + p * LANE, LANE), LANE)
        dqkv_ref[:, kcol] = dk_s[...].astype(BF16)
        dqkv_ref[:, vcol] = dv_s[...].astype(BF16)
        return carry

    lax.fori_loop(0, width // LANE, pair_body, 0)
    io.had(k_ref, v_ref, q_ref, dmix_ref, dmixt_ref, mixt_ref, e_ref)
    dqkv_ref[:, 0:width] = dqt_s[...].T


def attention_ins(q, k, v, e, il, mixt, dmix, dmixt):
    pairs = q.shape[1] // LANE
    return [(item, "v") for item in (k, v, q, dmix, dmixt, mixt, il, e)]


def attention_outs(q, heads):
    tokens, width = q.shape
    return [((tokens, 3 * width), BF16, "v"), ((heads, 8, SPAN), F32, "v"), ((heads, 16, LANE), F32, "v")]


def attention_scratch(q):
    tokens, width = q.shape
    tile, wide = min(tokens, 128), min(tokens, 256)
    return [
        pltpu.VMEM((width, tokens), BF16),
        pltpu.VMEM((tokens, wide), BF16),
        pltpu.VMEM((tokens, wide), BF16),
        pltpu.VMEM((tile, SPAN), F32),
        pltpu.VMEM((tokens, LANE), F32),
        pltpu.VMEM((tokens, LANE), F32),
    ]


def attention_back(q, k, v, e, il, mixt, dmix, dmixt, name):
    tokens, width = q.shape
    return call(
        attention_back_kernel,
        name,
        attention_ins(q, k, v, e, il, mixt, dmix, dmixt),
        attention_outs(q, e.shape[0]),
        attention_scratch(q),
        9,
        10 * tokens * tokens * width,
        16 << 20,
    )


def input_kernel(io, gains_ref, *refs):
    kinds = (len(refs) - 3) // 4
    reads, weights, writes = refs[:3 * kinds], refs[3 * kinds:3 * kinds + 3], refs[3 * kinds + 3:]
    for kind in range(kinds):
        dqkv_ref, x_ref, dmid_ref = reads[3 * kind:3 * kind + 3]
        width = x_ref.shape[1]
        io.need(dqkv_ref)
        total = None
        for i, w in enumerate(weights):
            io.need(w)
            part = nt(dqkv_ref[:, i * width:(i + 1) * width], w[...])
            total = part if total is None else total + part
        io.need(x_ref, dmid_ref)
        writes[kind][...] = dmid_ref[...] + norm_back(x_ref[...].astype(F32), gains_ref[0:1, :], total)
        io.done(writes[kind])


def input_back(gains, kinds, weights, name):
    width = weights[0].shape[0]
    tokens = sum(x.shape[0] for _, x, _ in kinds)
    return call(
        input_kernel,
        name,
        [(gains, "v")] + [(item, "h") for kind in kinds for item in kind] + [(w, "h") for w in weights],
        [(x.shape, F32, "h") for _, x, _ in kinds],
        [],
        32,
        6 * tokens * width * width,
        8 << 20,
    )


def put_rows(buf, value, per, offset, lanes, extra=None):
    for j in range(buf.shape[1]):
        for core in range(2):
            rows = slice((2 * j + core) * per, (2 * j + core + 1) * per)
            pieces = [value[rows, lo:lo + 256] for lo in lanes]
            if extra is not None:
                pieces.append(extra(rows))
            block = jnp.concatenate(pieces, axis=0) if len(pieces) > 1 else pieces[0]
            buf[core, j, pl.ds(offset, block.shape[0]), :] = block.astype(BF16)


def push_rows(io, buf, own_ref, send_ref, start, size):
    core = core_index()
    rows = pl.ds(start, size)
    for ref, side in ((send_ref, 1 - core), (own_ref, core)):
        io.push(buf.at[side, :, rows], ref.at[:, rows])


def halves_buffer(count, rows):
    return pltpu.VMEM((2, count, rows, 256), BF16)


def core_index():
    return (lax.axis_index("grp") % 2).astype(jnp.int32)


def halves(count, rows):
    return [((count, rows, 256), BF16, "a")] * 2


def down_grad_kernel(
    io, demb_ref, gains_ref, proj_ref, wp_s, out_ref, wd_s, a_ref, b_ref, wg_s, wu_s, mid_ref, wo_s,
    hid_ref, hidq_ref, dbr_ref, mixt_ref, mixtq_ref, datt_ref, n3_ref, n3q_ref, dpj_ref,
    dg_ref, du_ref, dmid_ref, dmix_ref, dmixt_ref, own_ref, send_ref,
    acc1_s, dpjq_s, dbrq_s, dattq_s, hidt_s, hidtq_s, buf_s,
):
    chain_kernel(
        io, demb_ref, gains_ref, proj_ref, wp_s, out_ref, wd_s, a_ref, b_ref, wg_s, wu_s, mid_ref, wo_s,
        dpjq_s, dbrq_s, dg_ref, du_ref, dattq_s, dmid_ref, dmix_ref, dmixt_ref, acc1_s,
    )
    io.done(dmix_ref, dmixt_ref)
    hidden, width = hid_ref.shape[1], dbr_ref.shape[1]
    count = own_ref.shape[0]
    per, per_down = width // (2 * count), hidden // (2 * count)
    io.need(hid_ref, hidq_ref)
    hidt_s[...] = hid_ref[...].T
    hidtq_s[...] = hidq_ref[...].T
    io.need(dbr_ref)
    for i in range(width // 256):
        col = slice(i * 256, (i + 1) * 256)
        value = nn(hidt_s[...], dbr_ref[:, col]) + nn(hidtq_s[...], dbrq_s[:, col])
        put_rows(buf_s, value, per_down, i * per_down, (0,))
        push_rows(io, buf_s, own_ref, send_ref, i * per_down, per_down)
    base = (width // 256) * per_down
    io.need(mixt_ref, mixtq_ref, datt_ref, n3_ref, n3q_ref, dpj_ref)
    value = nn(mixt_ref[...], datt_ref[...]) + nn(mixtq_ref[...], dattq_s[...])
    put_rows(buf_s, value, per, base, (0, 256))
    push_rows(io, buf_s, own_ref, send_ref, base, 2 * per)
    base = base + 2 * per
    proj = nn(n3_ref[...].T, dpj_ref[...]) + nn(n3q_ref[...].T, dpjq_s[...])

    def proj_rows(rows):
        return jnp.concatenate([proj[rows], jnp.zeros((per, LANE), F32)], axis=1)

    put_rows(buf_s, value, per, base, (512,), extra=proj_rows)
    push_rows(io, buf_s, own_ref, send_ref, base, 2 * per)


def down_grads(query, doc, count):
    (demb, proj, out, mid, a, b, gains, wp, wd, wg, wu, wo), (hidq, mixtq, n3q) = query
    hid, dbr, mixt, datt, n3, dpj = doc
    tokens, hidden = hid.shape
    qtokens, width = out.shape
    per, per_down = width // (2 * count), hidden // (2 * count)
    plain = [(item, "h") for item in (hid, hidq, dbr, mixt, mixtq, datt, n3, n3q, dpj)]
    return call(
        down_grad_kernel,
        "query_ff_back_down_grads",
        chain_ins(demb, gains, proj, wp, out, wd, a, b, wg, wu, mid, wo) + plain,
        [
            ((qtokens, hidden), BF16, "h"),
            ((qtokens, hidden), BF16, "h"),
            ((qtokens, width), F32, "h"),
            ((qtokens, width), BF16, "h"),
            ((width, qtokens), BF16, "h"),
        ]
        + halves(count, (width // 256) * per_down + 4 * per),
        [
            pltpu.VMEM((qtokens, width), F32),
            pltpu.VMEM(proj.shape, BF16),
            pltpu.VMEM((qtokens, width), BF16),
            pltpu.VMEM((qtokens, width), BF16),
            pltpu.VMEM((hidden, tokens), BF16),
            pltpu.VMEM((hidden, qtokens), BF16),
            halves_buffer(count, (width // 256) * per_down + 4 * per),
        ],
        40,
        2 * (tokens + 256) * (width * width + width * hidden),
        24 << 20,
    )


def gate_grad_kernel(io, n2_ref, n2q_ref, dg_ref, dgq_ref, du_ref, duq_ref, own_ref, send_ref, n2t_s, n2tq_s, buf_s):
    width, hidden = n2_ref.shape[1], dg_ref.shape[1]
    count = own_ref.shape[0]
    per = width // (2 * count)
    io.need(n2_ref, n2q_ref)
    n2t_s[...] = n2_ref[...].T
    n2tq_s[...] = n2q_ref[...].T
    steps = hidden // CH
    for which, (d, dq) in enumerate(((dg_ref, dgq_ref), (du_ref, duq_ref))):
        io.need(dq)
        io.feed((d,))
        for i in range(steps):
            io.need_part(i, d)
            col = slice(i * CH, (i + 1) * CH)
            value = nn(n2t_s[...], d[:, col]) + nn(n2tq_s[...], dq[:, col])
            start = (which * steps + i) * (CH // 256) * per
            for lo in range(0, CH, 512):
                at = start + (lo // 256) * per
                put_rows(buf_s, value, per, at, (lo, lo + 256))
                push_rows(io, buf_s, own_ref, send_ref, at, 2 * per)
        io.had(d)


def gate_grads(n2, n2q, dg, dgq, du, duq, count):
    tokens, width = n2.shape
    qtokens, hidden = dgq.shape
    per = width // (2 * count)
    return call(
        gate_grad_kernel,
        "gate_up_grads",
        [(n2, "h"), (n2q, "h"), (dg, f"h-{hidden // CH}"), (dgq, "h"), (du, f"h-{hidden // CH}"), (duq, "h")],
        halves(count, 2 * (hidden // 256) * per),
        [
            pltpu.VMEM((width, tokens), BF16),
            pltpu.VMEM((width, qtokens), BF16),
            halves_buffer(count, 2 * (hidden // 256) * per),
        ],
        22,
        4 * (tokens + 256) * width * hidden,
        16 << 20,
    )


def qkv_grad_kernel(
    io, k_ref, v_ref, q_ref, dmix_ref, dmixt_ref, mixt_ref, il_ref, e_ref, n1_ref, n1q_ref, d_ref,
    diagd_ref, fard_ref, hot_ref, loss_ref, dq_ref, diag_ref, far_ref, own_ref, send_ref, *rest,
):
    own_parts = lax.axis_size("dp")
    n1t_s, n1tq_s, buf_s = rest[-3:]
    attention_back_kernel(
        io, k_ref, v_ref, q_ref, dmix_ref, dmixt_ref, mixt_ref, il_ref, e_ref, dq_ref, diag_ref, far_ref, *rest[:-3]
    )
    io.done(dq_ref)
    width = n1_ref.shape[1]
    count = own_ref.shape[0]
    per = width // (2 * count)
    io.need(n1_ref, n1q_ref)
    n1t_s[...] = n1_ref[...].T
    n1tq_s[...] = n1q_ref[...].T
    io.need(d_ref)
    steps = (3 * width) // 512
    value = nn(n1t_s[...], d_ref[...]) + nn(n1tq_s[...], dq_ref[...])
    for i in range(steps):
        put_rows(buf_s, value, per, i * 2 * per, (i * 512, i * 512 + 256))
        push_rows(io, buf_s, own_ref, send_ref, i * 2 * per, 2 * per)
    io.need(hot_ref)
    heads = diag_ref.shape[0]
    buckets = hot_ref.shape[0]
    table = jnp.zeros((heads, buckets), F32)
    for r in range(8):
        both = diagd_ref[:, r, :] + diag_ref[:, r, :]
        table = table + lax.dot_general(
            both, hot_ref[:, r * SPAN:(r + 1) * SPAN].astype(F32), (((1,), (1,)), ((), ())),
            precision=highest, preferred_element_type=F32,
        )
    far = fard_ref[...] + far_ref[...]
    low = jnp.sum(jnp.sum(far[:, 0:8, :], axis=1), axis=-1, keepdims=True)
    high = jnp.sum(jnp.sum(far[:, 8:16, :], axis=1), axis=-1, keepdims=True)
    column = lax.broadcasted_iota(jnp.int32, (1, buckets), 1)
    table = table + jnp.where(column == buckets // 2 - 1, low, 0.0) + jnp.where(column == buckets - 1, high, 0.0)
    table = jnp.concatenate([table, jnp.zeros((16 - heads, buckets), F32)], axis=0)
    loss = jnp.broadcast_to(loss_ref[...] * (1.0 / own_parts), (8, LANE))
    spare = jnp.concatenate([table[0:8], table[8:16], jnp.zeros((8, LANE - 2 * buckets), F32), loss], axis=1)
    put_rows(buf_s, value, per, steps * 2 * per, (steps * 512,), extra=lambda rows: spare)
    push_rows(io, buf_s, own_ref, send_ref, steps * 2 * per, per + 8)


def qkv_grads(query, n1, n1q, d, diag, far, hot, loss, count):
    tokens, width = n1.shape
    per = width // (2 * count)
    return call(
        qkv_grad_kernel,
        "query_attention_back_qkv_grads",
        attention_ins(*query)
        + [(item, "h") for item in (n1, n1q, d)]
        + [(diag, "v"), (far, "v"), (hot, "h"), (loss, "v")],
        attention_outs(query[0], query[3].shape[0]) + halves(count, 9 * per + 8),
        attention_scratch(query[0])
        + [
            pltpu.VMEM((width, tokens), BF16),
            pltpu.VMEM((width, n1q.shape[0]), BF16),
            halves_buffer(count, 9 * per + 8),
        ],
        24,
        2 * (tokens + 256) * 3 * width * width,
        10 << 20,
    )


def after(values, *deps):
    return lax.optimization_barrier((values, deps))[0]


def position(n_dp):
    dp, grp = lax.axis_index("dp").astype(jnp.int32), lax.axis_index("grp").astype(jnp.int32)
    return dp // 2, dp % 2, grp // 2


def slices(io_sems, moves):
    copies = [pltpu.make_async_copy(src, dst, io_sems.at[i]) for i, (src, dst) in enumerate(moves)]
    for copy in copies:
        copy.start()
    return copies


class Halves:
    def __init__(self, rows):
        self.rows, self.cut = rows, (rows // 32) * 16

    def sizes(self):
        return self.cut, self.rows - self.cut

    def spans(self):
        return pl.ds(0, self.cut), pl.ds(self.cut, self.rows - self.cut)


def first_kernel(n_dp, halves, io, own_ref, got_ref, x_ref, y_ref, ox_s, gx_s, oy_s, gy_s, sems):
    _, x, y = position(n_dp)
    top, low = halves.spans()
    moves = []
    for ref, a, b in ((own_ref, ox_s, oy_s), (got_ref, gx_s, gy_s)):
        moves += [(ref.at[:, 1 - x, :, top], a), (ref.at[:, :, 1 - y, low], b)]
    copies = slices(sems, moves)
    for i, (a, b, out) in enumerate(((ox_s, gx_s, x_ref), (oy_s, gy_s, y_ref))):
        copies[i].wait()
        copies[i + 2].wait()
        out[...] = (a[...].astype(F32) + b[...].astype(F32)).astype(BF16)
        io.done(out)


def pair_rows(n_dp, halves, flip, own_ref, got_ref, gx_ref, gy_ref, bufs, sems):
    _, x, y = position(n_dp)
    top, low = halves.spans()
    yt, xl = (1 - y, 1 - x) if flip else (y, x)
    ot_s, gt_s, rt_s, ol_s, gl_s, rl_s = bufs
    copies = slices(sems, [
        (own_ref.at[:, x, yt, top], ot_s), (got_ref.at[:, x, yt, top], gt_s), (gx_ref.at[:, yt], rt_s),
        (own_ref.at[:, xl, y, low], ol_s), (got_ref.at[:, xl, y, low], gl_s), (gy_ref.at[:, xl], rl_s),
    ])
    out = []
    for i in (0, 3):
        for copy in copies[i:i + 3]:
            copy.wait()
        a, b, c = bufs[i:i + 3]
        out.append(a[...].astype(F32) + b[...].astype(F32) + c[...].astype(F32))
    return out


def second_kernel(n_dp, halves, io, own_ref, got_ref, gx_ref, gy_ref, y_ref, x_ref, *refs):
    for out, value in zip((y_ref, x_ref), pair_rows(n_dp, halves, True, own_ref, got_ref, gx_ref, gy_ref, refs[:-1], refs[-1])):
        out[...] = value.astype(BF16)
        io.done(out)


def cross_kernel(n_dp, halves, io, own_ref, got_ref, xy_ref, x_ref, y_ref, own_s, got_s, sems):
    _, x, y = position(n_dp)
    moves = []
    for i, (xx, yy) in enumerate(((1 - x, 1 - y), (1 - x, y), (x, 1 - y))):
        moves += [(own_ref.at[:, xx, yy], own_s.at[i]), (got_ref.at[:, xx, yy], got_s.at[i])]
    copies = slices(sems, moves)
    for i, out in enumerate((xy_ref, x_ref, y_ref)):
        copies[2 * i].wait()
        copies[2 * i + 1].wait()
        out[...] = (own_s[i].astype(F32) + got_s[i].astype(F32)).astype(BF16)
        io.done(out)


def leave(z, line_s, outs, total_ref, io):
    nz = line_s.shape[0]
    if not outs:
        total_ref[...] = line_s[...].astype(BF16)
        return
    for k, out in enumerate(outs, 1):
        out[...] = line_s[(z + k) % nz].astype(BF16)
        io.done(out)
    total_ref[...] = line_s[z]


def cross_line_kernel(n_dp, halves, io, own_ref, got_ref, xy_ref, x_ref, y_ref, *refs):
    outs, total_ref, (line_s, own_s, got_s, sems) = refs[:-5], refs[-5], refs[-4:]
    z, x, y = position(n_dp)
    copies = slices(sems, [(own_ref.at[:, x, y], own_s), (got_ref.at[:, x, y], got_s)])
    for copy in copies:
        copy.wait()
    io.need(xy_ref, x_ref, y_ref)
    line_s[...] = own_s[...].astype(F32) + got_s[...].astype(F32) + xy_ref[...].astype(F32)
    line_s[...] += x_ref[...].astype(F32) + y_ref[...].astype(F32)
    leave(z, line_s, outs, total_ref, io)


def line_kernel(n_dp, halves, io, own_ref, got_ref, gx_ref, gy_ref, y_ref, x_ref, *refs):
    outs, total_ref, line_s, bufs, sems = refs[:-9], refs[-9], refs[-8], refs[-7:-1], refs[-1]
    z, _, _ = position(n_dp)
    top, low = pair_rows(n_dp, halves, False, own_ref, got_ref, gx_ref, gy_ref, bufs, sems)
    io.need(x_ref, y_ref)
    line_s[:, 0:halves.cut] = top + y_ref[...].astype(F32)
    line_s[:, halves.cut:] = low + x_ref[...].astype(F32)
    leave(z, line_s, outs, total_ref, io)


class Batch:
    def __init__(self, own, send, n_dp, n_grp, name):
        self.n_dp, self.n_grp, self.nz, self.name = n_dp, n_grp, n_dp // 2, name
        self.rows, self.cols = own.shape[1:]
        self.halves = Halves(self.rows)
        self.own = own
        self.got = lax.ppermute(send, "grp", [(i, i ^ 1) for i in range(n_grp)])

    def both(self):
        grid = lambda a: (a.reshape(self.nz, 2, 2, self.rows, self.cols), "r")
        own, kind = grid(self.own)
        return [(pltpu.with_memory_space_constraint(own, pltpu.HBM), kind), grid(self.got)]

    def along_x(self, array):
        return lax.ppermute(array, "dp", [(d, d ^ 1) for d in range(self.n_dp)])

    def along_y(self, array):
        return lax.ppermute(array, "grp", [(g, g ^ 2) for g in range(self.n_grp)])

    def run(self, kernel, step, ins, outs, scratch):
        body = functools.partial(kernel, self.n_dp, self.halves)
        return call(body, self.name + step, ins, outs, scratch, 24, 0, 0)

    def first(self):
        sizes = [(self.nz, 2, n, self.cols) for n in self.halves.sizes()]
        bufs = [pltpu.VMEM(size, BF16) for size in sizes for _ in range(2)]
        outs = [(size, BF16, "h") for size in sizes]
        sent = self.run(first_kernel, "_first", self.both(), outs, bufs + [pltpu.SemaphoreType.DMA((4,))])
        self.back1 = self.along_x(sent[0]), self.along_y(sent[1])
        return tuple(sent)

    def second_bufs(self):
        return [pltpu.VMEM((self.nz, n, self.cols), BF16) for n in self.halves.sizes() for _ in range(3)] + [
            pltpu.SemaphoreType.DMA((6,))
        ]

    def second(self):
        outs = [((self.nz, n, self.cols), BF16, "h") for n in self.halves.sizes()]
        ins = self.both() + [(a, "r") for a in self.back1]
        sent = self.run(second_kernel, "_second", ins, outs, self.second_bufs())
        self.back2 = self.along_y(sent[0]), self.along_x(sent[1])
        return tuple(sent)

    def cross(self):
        n_dp, n_grp = self.n_dp, self.n_grp
        piece = (self.nz, self.rows, self.cols)
        bufs = [pltpu.VMEM((3, *piece), BF16)] * 2 + [pltpu.SemaphoreType.DMA((6,))]
        sent = self.run(cross_kernel, "_cross", self.both(), [(piece, BF16, "h")] * 3, bufs)
        across = [(d * n_grp + g, (d ^ 1) * n_grp + (g ^ 2)) for d in range(n_dp) for g in range(n_grp)]
        self.back1 = ()
        self.back2 = lax.ppermute(sent[0], ("dp", "grp"), across), self.along_x(sent[1]), self.along_y(sent[2])
        return tuple(sent)

    def line(self, together=False):
        n_dp, nz = self.n_dp, self.nz
        piece, part = (nz, self.rows, self.cols), (self.rows, self.cols)
        outs = [(piece, BF16, "h")] if together else [(part, BF16, "h")] * (nz - 1) + [(part, F32, "v")]
        ins = self.both() + [(a, "r") for a in self.back1] + [(a, "v") for a in self.back2]
        if self.back1:
            kernel, bufs = line_kernel, self.second_bufs()
        else:
            kernel, bufs = cross_line_kernel, [pltpu.VMEM(piece, BF16)] * 2 + [pltpu.SemaphoreType.DMA((2,))]
        *sent, total = self.run(kernel, "_line", ins, outs, [pltpu.VMEM(piece, F32)] + bufs)
        if together:
            groups = [[2 * z + x for z in range(nz)] for x in range(2)]
            self.parts = [lax.all_to_all(total, "dp", 0, 0, tiled=True, axis_index_groups=groups)]
            return (total,)
        self.parts = [total] + [
            lax.ppermute(one, "dp", [(d, (d + 2 * k) % n_dp) for d in range(n_dp)]) for k, one in enumerate(sent, 1)
        ]
        return tuple(sent)


def weight_rows(weights, start):
    aligned = (start // 16) * 16
    return start - aligned, [w.at[pl.ds(pl.multiple_of(aligned, 16), 32)] for w in weights]


def finish_kernel(n_parts, places, gain_row, scale, io, *refs):
    total, gains_ref, rest = refs[:n_parts], refs[n_parts], refs[n_parts + 1:]
    n_out, n_weights = len(places), len(gain_row[1])
    weights, rest = rest[:n_weights], rest[n_weights:]
    outs, rest = rest[:n_out], rest[n_out:]
    gain_ref, rest = rest[0], rest[1:]
    extra, rest = (rest[:2], rest[2:]) if scale else ((), rest)
    sum_s, wide_s, bufs, sems = rest[0], rest[1], rest[2:-1], rest[-1]
    device = lax.axis_index("dp") * lax.axis_size("grp") + lax.axis_index("grp")
    per = outs[gain_row[1][0]].shape[0]
    start = device.astype(jnp.int32) * per
    shift, sources = weight_rows(weights, start)
    copies = slices(sems, list(zip(sources, bufs)))
    io.need(*total)
    if len(total) == 1:
        value = total[0][0].astype(F32)
        for i in range(1, total[0].shape[0]):
            value = value + total[0][i].astype(F32)
    else:
        value = total[0][...].astype(F32)
        for one in total[1:]:
            value = value + one[...].astype(F32)
    sum_s[...] = value
    for out, at in zip(outs, places):
        rows, width = out.shape
        for i in range(-(-width // 256)):
            cols = min(256, width - i * 256)
            out[:, i * 256:i * 256 + cols] = sum_s[at + i * rows:at + (i + 1) * rows, 0:cols]
    inner = jnp.zeros((per, 1), F32)
    for which, copy, buf in zip(gain_row[1], copies, bufs):
        copy.wait()
        width = buf.shape[1]
        wide_s[:, 0:width] = buf[...].astype(F32)
        mine = wide_s[pl.ds(pl.multiple_of(shift, 8), per), 0:width]
        inner = inner + jnp.sum(mine * outs[which][...], axis=-1, keepdims=True)
    lane = lax.broadcasted_iota(jnp.int32, (per, gains_ref.shape[1]), 1)
    row = lax.broadcasted_iota(jnp.int32, (per, gains_ref.shape[1]), 0)
    gain = jnp.sum(jnp.where(lane == row + start, gains_ref[gain_row[0]:gain_row[0] + 1, :], 0.0), axis=-1, keepdims=True)
    lane, row = lane[:, 0:LANE], row[:, 0:LANE]
    gain_ref[...] = jnp.sum(jnp.where(lane == row, inner / gain, 0.0), axis=0, keepdims=True)[:, 0:per]
    if scale:
        table_ref, loss_ref = extra
        heads, buckets = table_ref.shape
        spare = sum_s[sum_s.shape[0] - 8:, :]
        table = jnp.concatenate([spare[:, 0:buckets], spare[:, buckets:2 * buckets]], axis=0)
        table_ref[...] = table[0:heads]
        loss_ref[...] = spare[0:1, LANE:LANE + 1] * scale


def finish(batch, places, shapes, gain_row, gains, weights, table=None, scale=0.0):
    per = shapes[gain_row[1][0]][0]
    outs = [(shape, F32, "h") for shape in shapes] + [((1, per), F32, "v")]
    if table is not None:
        outs += [(table, F32, "v"), ((1, 1), F32, "v")]
    width = max(w.shape[1] for w in weights)
    return call(
        functools.partial(finish_kernel, len(batch.parts), places, gain_row, scale),
        batch.name + "_finish",
        [(one, "v") for one in batch.parts] + [(gains, "v")] + [(pltpu.with_memory_space_constraint(w, pltpu.HBM), "r") for w in weights],
        outs,
        [pltpu.VMEM((batch.rows, batch.cols), F32), pltpu.VMEM((32, width), F32)]
        + [pltpu.VMEM((32, w.shape[1]), BF16) for w in weights]
        + [pltpu.SemaphoreType.DMA((len(weights),))],
        16,
        0,
        0,
    )


def on_device(
    n_dp, n_grp, doc_tokens, doc_lengths, query_tokens, query_lengths, candidates, labels, gain_attn, w_query, w_key,
    w_value, w_out, bias_table, gain_ffn, w_gate, w_up, w_down, gain_final, w_proj,
):
    doc_rows, doc_len, width = doc_tokens.shape
    query_rows, query_len = query_tokens.shape[:2]
    hidden = w_gate.shape[1]
    bucket_total, heads = bias_table.shape
    devices = n_dp * n_grp
    axes = ("dp", "grp")
    x_doc = doc_tokens.reshape(doc_len, width)
    x_qry = query_tokens.reshape(query_rows * query_len, width)
    which = lax.broadcasted_iota(jnp.int32, (24, width), 0)
    gains = jnp.where(which == 0, gain_attn[None], jnp.where(which == 1, gain_ffn[None], gain_final[None]))
    table = jnp.pad(bias_table.T, ((8, 16 - heads), (0, width - bucket_total)))
    gains = jnp.where(which < 8, gains, table).astype(F32)
    weights = (w_query, w_key, w_value, w_out, w_gate, w_up, w_down, w_proj)
    hot = jnp.asarray(strip_onehot(), BF16)
    (q_q, q_k, q_v, q_e, q_il, q_mixt, q_mid, q_n1, q_n2, q_hid, q_a, q_b, q_out, q_n3, q_proj, packed, base) = forward(
        x_qry, query_lengths[None], gains, (hot, candidates, labels[None]), weights, False, heads, n_dp
    )
    got = lax.all_to_all(packed, "dp", 0, 0, tiled=True)
    (d_q, d_k, d_v, d_e, d_il, d_mixt, d_mid, d_n1, d_n2, d_hid, d_a, d_b, d_out, d_n3, d_proj, emb) = forward(
        x_doc, doc_lengths, gains, base, weights, True, heads
    )
    sums, lse = scores(got, emb, query_len)
    sums = lax.all_to_all(sums, "dp", 0, 0, tiled=True)
    demb_doc, demb_part, loss_group = retrieval_back(
        got, sums, emb, lse, query_len
    )
    demb_qry = lax.all_to_all(demb_part, "dp", 0, 0, tiled=True)
    back = (w_proj, w_down, w_gate, w_up, w_out)
    d_dpj, d_dbr, d_dg, d_du, d_datt, d_dmid, d_dmix, d_dmixt = chain(
        demb_doc, d_proj, d_out, d_mid, d_a, d_b, gains, *back, "doc_ff_back"
    )
    q_chain = (demb_qry, q_proj, q_out, q_mid, q_a, q_b, gains, *back)
    d_attention = lambda il: (d_q, d_k, d_v, d_e, il, d_mixt, d_dmix, d_dmixt)
    q_attention = lambda il, dmix, dmixt: (q_q, q_k, q_v, q_e, il, q_mixt, dmix, dmixt)
    qkv_weights = (w_query, w_key, w_value)
    fast = (n_dp, n_grp) == (8, 4)
    if fast:
        pairs = devices // 2
        q_dg, q_du, q_dmid, q_dmix, q_dmixt, own, send = down_grads(
            (q_chain, (q_hid, q_mixt, q_n3)), (d_hid, d_dbr, d_mixt, d_datt, d_n3, d_dpj), pairs
        )
        down = Batch(own, send, n_dp, n_grp, "down")
        own, send = gate_grads(d_n2, q_n2, d_dg, q_dg, d_du, q_du, pairs)
        gate = Batch(own, send, n_dp, n_grp, "gate")
        down.got = after(down.got, send)
        d_il = after(d_il, down.first(), send)
        d_dqkv, d_diag, d_far = attention_back(*d_attention(d_il), "doc_attention_back")
        gate.got, down.back1 = after((gate.got, down.back1), d_diag)
        q_il = after(q_il, gate.cross(), down.second())
        q_dqkv, q_diag, q_far, own, send = qkv_grads(
            q_attention(q_il, q_dmix, q_dmixt), d_n1, q_n1, d_dqkv, d_diag, d_far, hot, loss_group, pairs
        )
        qkv = Batch(own, send, n_dp, n_grp, "qkv")
        (doc_grad,) = input_back(after(gains, send), ((d_dqkv, x_doc, d_dmid),), qkv_weights, "doc_input_back")
        down.back2 = after(down.back2, doc_grad)
        qkv.got = after(qkv.got, down.line(True))
        last_gains = after(gains, qkv.cross())
    else:
        q_dpj, q_dbr, q_dg, q_du, q_datt, q_dmid, q_dmix, q_dmixt = chain(*q_chain, "query_ff_back")
        d_dqkv, d_diag, d_far = attention_back(*d_attention(d_il), "doc_attention_back")
        q_dqkv, q_diag, q_far = attention_back(*q_attention(q_il, q_dmix, q_dmixt), "query_attention_back")
        last_gains = gains
        (doc_grad,) = input_back(gains, ((d_dqkv, x_doc, d_dmid),), qkv_weights, "doc_input_back")
    (query_grad,) = input_back(last_gains, ((q_dqkv, x_qry, q_dmid),), qkv_weights, "query_input_back")

    query_total = query_rows * devices
    per, per_down = width // devices, hidden // devices
    if fast:
        gate.back2 = after(gate.back2, query_grad)
        qkv.back2 = after(qkv.back2, gate.line())
        sent = qkv.line()
        down.parts, gate.parts = after((down.parts, gate.parts), sent)
        at = (width // 256) * per_down
        shard_down, shard_out, shard_proj, gain3 = finish(
            down, (0, at, at + 3 * per), ((per_down, width), (per, width), (per, w_proj.shape[1])), (2, (2,)), gains, [w_proj]
        )
        shard_gate, shard_up, gain2 = finish(
            gate, (0, (hidden // 256) * per), ((per, hidden),) * 2, (1, (0, 1)), gains, [w_gate, w_up]
        )
        shard_query, shard_key, shard_value, gain1, table_grad, loss = finish(
            qkv, (0, 3 * per, 6 * per), ((per, width),) * 3, (0, (0, 1, 2)), gains, qkv_weights, (heads, bucket_total), 1.0 / query_total
        )
        shard_gains = [g.reshape(per) for g in (gain1, gain2, gain3)]
        table_grad, loss = table_grad.T, loss.reshape(())
    else:

        def grad(left, right):
            product = tn(jnp.concatenate(left), jnp.concatenate(right))
            return lax.psum_scatter(product, axes, scatter_dimension=0, tiled=True)

        n1s = (d_n1, q_n1)
        shard_query, shard_key, shard_value = (
            grad(n1s, (d_dqkv[:, i * width:(i + 1) * width], q_dqkv[:, i * width:(i + 1) * width])) for i in range(3)
        )
        shard_out = grad((d_mixt.T, q_mixt.T), (d_datt, q_datt))
        shard_gate = grad((d_n2, q_n2), (d_dg, q_dg))
        shard_up = grad((d_n2, q_n2), (d_du, q_du))
        shard_down = grad((d_hid, q_hid), (d_dbr, q_dbr))
        shard_proj = grad((d_n3, q_n3), (d_dpj, q_dpj))
        start = (lax.axis_index("dp") * n_grp + lax.axis_index("grp")) * per
        mine = lambda a: lax.dynamic_slice_in_dim(a.astype(F32), start, per, 0)
        shard_gains = [
            sum(jnp.sum(mine(w) * g, axis=1) for w, g in pairs) / mine(gain)
            for gain, pairs in (
                (gain_attn, ((w_query, shard_query), (w_key, shard_key), (w_value, shard_value))),
                (gain_ffn, ((w_gate, shard_gate), (w_up, shard_up))),
                (gain_final, ((w_proj, shard_proj),)),
            )
        ]
        far = jnp.sum((d_far + q_far).reshape(heads, 2, -1), axis=-1)
        table = lax.dot_general(
            hot.astype(F32), (d_diag + q_diag).reshape(heads, -1), (((1,), (1,)), ((), ())),
            precision=highest, preferred_element_type=F32,
        )
        table = table.at[bucket_total // 2 - 1].add(far[:, 0]).at[bucket_total - 1].add(far[:, 1])
        table_grad, loss = lax.psum((table, loss_group[0, 0] / n_dp), axes)
        loss = loss / query_total
    return (
        loss,
        doc_grad.reshape(doc_rows, doc_len, width),
        query_grad.reshape(query_rows, query_len, width),
        shard_gains[0],
        shard_query,
        shard_key,
        shard_value,
        shard_out,
        table_grad,
        shard_gains[1],
        shard_gate,
        shard_up,
        shard_down,
        shard_gains[2],
        shard_proj,
    )


def solution(mesh):
    both = ("dp", "grp")
    rows3, rows2, rows1 = P(both, None, None), P(both, None), P(both)
    in_specs = (rows3, rows2, rows3, rows1, rows2, rows1) + (P(),) * 12
    out_specs = (
        P(), rows3, rows3, rows1, rows2, rows2, rows2, rows2, P(), rows1, rows2, rows2, rows2, rows1, rows2,
    )
    body = functools.partial(on_device, mesh.shape["dp"], mesh.shape["grp"])
    return jax.shard_map(body, mesh=mesh, in_specs=in_specs, out_specs=out_specs, check_vma=False)
```

```python
import functools
import itertools
import math

import jax
import jax.numpy as jnp
import numpy as np
from jax import lax
from jax.experimental import pallas as pl
from jax.experimental.pallas import tpu as pltpu
from jax.sharding import PartitionSpec as P

F32, BF16 = jnp.float32, jnp.bfloat16
BUCKETS = 32
DIST = 128
BLK = 128
MOST_DOC = 256
ROW_FILL = 480
EPS = 1e-6
SHARP = 0.25
SCALE = 16.0
NEG = -1e30
GELU_A = math.sqrt(2.0 / math.pi)
GELU_B = 0.044715
SPAN = 512
CH = 1024
LANE = 128
COST = 20
AHEAD = 1 << 30
PACK_INT = 48
highest = lax.Precision.HIGHEST


def nn(a, b):
    return jnp.dot(a, b, preferred_element_type=F32)


def nt(a, b):
    return lax.dot_general(a, b, (((1,), (1,)), ((), ())), preferred_element_type=F32)


def tn(a, b):
    return lax.dot_general(a, b, (((0,), (0,)), ((), ())), preferred_element_type=F32)


def bucket_of(offsets):
    half = BUCKETS // 2
    exact = half // 2
    dist = np.abs(offsets)
    scaled = np.log(np.maximum(dist, 1) / exact) / np.log(DIST / exact) * (half - exact)
    far = np.minimum(exact + np.maximum(scaled, 0).astype(np.int64), half - 1)
    return (offsets > 0) * half + np.where(dist < exact, dist, far)


def strip_onehot():
    j = np.arange(SPAN)
    offset = np.where(j < 384, 128 - j, 640 - j)
    index = np.stack([bucket_of(offset[(j - r) % SPAN]) for r in range(8)]).reshape(-1)
    return (index[None, :] == np.arange(BUCKETS)[:, None]).astype(np.float32)


VM = pl.BlockSpec(memory_space=pltpu.VMEM)
HB = pl.BlockSpec(memory_space=pl.ANY)


def by_part(run):
    return run if run[0][3] == 1 else sorted(run, key=lambda entry: entry[1])


class Io:
    def __init__(self, ins, outs, sems):
        self.ins, self.outs, self.sems, self.used = {}, {}, sems, 0
        self.going, self.queue, self.flying = [], [], 0
        for src, buf, parts in ins:
            self.ins[id(buf)] = (src, buf, parts, self.used)
            size = math.prod(buf.shape) * buf.dtype.itemsize // abs(parts)
            self.queue += [(id(buf), p, size, abs(parts)) for p in range(abs(parts))]
            self.used += abs(parts)
        for buf, dst in outs:
            self.outs[id(buf)] = (buf, dst)
        self.queue = [entry for _, run in itertools.groupby(self.queue, lambda e: e[3]) for entry in by_part(list(run))]
        self.feed()

    def feed(self, upto=()):
        upto = {id(buf) for buf in upto}
        while self.queue and (self.flying < AHEAD or any(entry[0] in upto for entry in self.queue)):
            key, p, size, _ = self.queue.pop(0)
            self.chunk(*self.ins[key], p).start()
            self.flying += size

    def landed(self, buf):
        self.flying -= math.prod(buf.shape) * buf.dtype.itemsize
        self.feed()

    def chunk(self, src, buf, parts, first, p):
        if parts == 1:
            return pltpu.make_async_copy(src, buf, self.sems.at[first])
        if parts > 0:
            size = buf.shape[0] // parts
            cut = (pl.ds(p * size if isinstance(p, int) else pl.multiple_of(p * size, 2), size),)
        else:
            size = buf.shape[1] // -parts
            cut = (slice(None), pl.ds(p * size if isinstance(p, int) else pl.multiple_of(p * size, LANE), size))
        return pltpu.make_async_copy(src.at[cut], buf.at[cut], self.sems.at[first + p])

    def need(self, *bufs):
        for buf in bufs:
            entry = self.ins.get(id(buf))
            if entry is not None:
                self.feed((buf,))
                for p in range(abs(entry[2])):
                    self.chunk(*entry, p).wait()
                del self.ins[id(buf)]
                self.landed(buf)

    def need_part(self, p, *bufs):
        for buf in bufs:
            if id(buf) in self.ins:
                self.chunk(*self.ins[id(buf)], p).wait()

    def had(self, *bufs):
        for buf in bufs:
            if self.ins.pop(id(buf), None) is not None:
                self.landed(buf)

    def done(self, *bufs):
        for buf in bufs:
            if id(buf) in self.outs:
                src, dst = self.outs.pop(id(buf))
                self.push(src, dst)

    def done_rows(self, buf, start, size):
        src, dst = self.outs[id(buf)]
        rows = (slice(None), pl.ds(start, size))
        self.push(src.at[rows], dst.at[rows])

    def gone(self, buf):
        self.outs.pop(id(buf))

    def push(self, src, dst):
        copy = pltpu.make_async_copy(src, dst, self.sems.at[self.used])
        self.used += 1
        copy.start()
        self.going.append(copy)

    def close(self):
        self.need(*[entry[1] for entry in list(self.ins.values())])
        self.done(*[entry[0] for entry in list(self.outs.values())])
        for copy in self.going:
            copy.wait()


def call(kernel, name, ins, outs, scratch, mib, flops, moved=8 << 20, aliases=None):
    args, in_specs, out_specs, out_shape, buffers, sems = [], [], [], [], [], 0
    for array, kind in ins:
        if kind in ("r", "b"):
            args.append(array if kind == "r" else pltpu.with_memory_space_constraint(array, pltpu.HBM))
            in_specs.append(HB)
        elif kind[0] == "h":
            args.append(pltpu.with_memory_space_constraint(array, pltpu.HBM))
            in_specs.append(HB)
            buffers.append(pltpu.VMEM(array.shape, array.dtype))
            sems += abs(int(kind[1:] or 1))
        else:
            args.append(array)
            in_specs.append(VM)
    for shape, dtype, kind in outs:
        if kind == "a":
            out_shape.append(pltpu.HBM(shape, dtype))
            out_specs.append(HB)
            sems += 8
        elif kind == "h":
            out_shape.append(pltpu.HBM(shape, dtype))
            out_specs.append(HB)
            buffers.append(pltpu.VMEM(shape, dtype))
            sems += 4
        else:
            out_shape.append(jax.ShapeDtypeStruct(shape, dtype))
            out_specs.append(VM)

    def body(*refs):
        n_in, n_out, n_buf = len(ins), len(outs), len(buffers)
        given, made = list(refs[:n_in]), list(refs[n_in:n_in + n_out])
        bufs = iter(refs[n_in + n_out:n_in + n_out + n_buf])
        rest = refs[n_in + n_out + n_buf:]
        reads, writes = [], []
        for i, (_, kind) in enumerate(ins):
            if kind[0] == "h":
                buf = next(bufs)
                reads.append((given[i], buf, int(kind[1:] or 1)))
                given[i] = buf
        for i, (_, _, kind) in enumerate(outs):
            if kind == "h":
                buf = next(bufs)
                writes.append((buf, made[i]))
                made[i] = buf
        io = Io(reads, writes, rest[-1])
        kernel(io, *given, *made, *rest[:-1])
        io.close()

    return pl.pallas_call(
        body,
        name=name,
        out_shape=out_shape,
        in_specs=in_specs,
        out_specs=out_specs,
        scratch_shapes=buffers + scratch + [pltpu.SemaphoreType.DMA((max(sems, 1),))],
        compiler_params=pltpu.CompilerParams(vmem_limit_bytes=mib << 20),
        input_output_aliases=aliases or {},
        cost_estimate=pl.CostEstimate(flops=int(flops) * COST, bytes_accessed=int(moved) * COST, transcendentals=0),
    )(*args)


def reachable(d, tile):
    return (abs(d) - 1) * tile + 1 < MOST_DOC


def half_lanes(values, side):
    lane = lax.broadcasted_iota(jnp.int32, (1, LANE), 1)
    return jnp.where((lane // 64) == side, values.astype(F32), 0.0).astype(BF16)


def norm_back(values, gain, dn):
    s = lax.rsqrt(jnp.mean(values * values, axis=-1, keepdims=True) + EPS)
    unit = values * s
    t = dn * gain
    return s * (t - unit * jnp.mean(t * unit, axis=-1, keepdims=True))


def forward_kernel(
    is_doc, io, x_ref, lens_ref, gains_ref, extra_ref, wq_s, wk_s, wv_s, wo_s, wg_s, wu_s, wd_s, wp_s,
    q_ref, k_ref, v_ref, e_ref, il_ref, mixt_ref, mid_ref, n1_ref, n2_ref, hid_ref, a_ref, b_ref,
    out_ref, n3_ref, proj_ref, emb_ref, *rest,
):
    if is_doc:
        base_ref, tail = extra_ref, rest
    else:
        hot_ref, cand_ref, label_ref = extra_ref
        base_ref, tail = rest[0], rest[1:]
    mask_s, strip_s, s_s, e_s, vt_s, mid_s = tail
    tokens, width = x_ref.shape
    hidden = wg_s.shape[1]
    heads = e_ref.shape[0]
    io.need(lens_ref)
    if not is_doc:
        io.need(hot_ref)
        tab = gains_ref[8:24, 0:hot_ref.shape[0]].astype(BF16)
        for r in range(8):
            rows = nn(tab, hot_ref[:, r * SPAN:(r + 1) * SPAN])
            for h in range(heads):
                base_ref[h, r:r + 1, :] = rows[h:h + 1, :]
    io.need(x_ref)
    x = x_ref[...].astype(F32)
    s1 = lax.rsqrt(jnp.mean(x * x, axis=-1, keepdims=True) + EPS)
    n1_ref[...] = (x * s1 * gains_ref[0:1, :]).astype(BF16)
    io.done(n1_ref)
    tile = min(tokens, 128)
    blocks = tokens // tile
    row_id = lax.broadcasted_iota(jnp.int32, (tokens, 1), 0)
    col_id = lax.broadcasted_iota(jnp.int32, (1, tokens), 1)
    if is_doc:
        seg_k = jnp.zeros((tokens, 1), jnp.int32)
        seg_q = jnp.zeros((1, tokens), jnp.int32)
        end = jnp.zeros((1, 1), jnp.int32)
        for i in range(lens_ref.shape[1]):
            end = end + lens_ref[0:1, i:i + 1]
            seg_k = seg_k + (row_id >= end).astype(jnp.int32)
            seg_q = seg_q + (col_id >= end).astype(jnp.int32)
    else:
        count = lens_ref.shape[1]
        length = tokens // count
        seg_q = col_id // length
        seg_k = jnp.full((tokens, 1), -1, jnp.int32)
        for i in range(count):
            inside = (row_id >= i * length) & (row_id < i * length + lens_ref[0:1, i:i + 1])
            seg_k = jnp.where(inside, i, seg_k)
    mask_s[...] = jnp.where(seg_k == seg_q, 0.0, NEG)
    for i, (w, o) in enumerate(((wq_s, q_ref), (wk_s, k_ref), (wv_s, v_ref))):
        io.need(w)
        o[...] = nn(n1_ref[...], w[...]).astype(BF16)
        io.done(o)
    vt_s[...] = v_ref[...].T
    if is_doc:
        io.need(base_ref)
    else:
        io.done(base_ref)

    def softmax_pair(p, slot):
        col = pl.ds(pl.multiple_of(p * LANE, LANE), LANE)
        for s in range(2):
            h = 2 * p + s
            first = base_ref[h]
            for g in range(tile // 8):
                strip_s[s, 8 * g:8 * g + 8, :] = pltpu.roll(first, 8 * g, 1) if g else first
            low_far, high_far = first[0:1, 256:256 + tile], first[0:1, 384:384 + tile]
            scores = nt(half_lanes(k_ref[:, col], s), q_ref[:, col])
            for qb in range(blocks):
                cols = slice(qb * tile, (qb + 1) * tile)
                tops = []
                near = [kb for kb in range(blocks) if reachable(kb - qb, tile)]
                for kb in near:
                    ks = slice(kb * tile, (kb + 1) * tile)
                    d = kb - qb
                    t = scores[ks, cols]
                    if abs(d) <= 1:
                        lo = (1 - d) * 128
                        t = t + strip_s[s, :, lo:lo + tile]
                    else:
                        t = t + (high_far if d > 0 else low_far)
                    t = t + mask_s[ks, cols]
                    s_s[s, ks, cols] = t
                    tops.append(jnp.max(t, axis=0, keepdims=True))
                top = functools.reduce(jnp.maximum, tops)
                total = None
                for kb in near:
                    ks = slice(kb * tile, (kb + 1) * tile)
                    e = jnp.exp(s_s[s, ks, cols] - top)
                    part = jnp.sum(e, axis=0, keepdims=True)
                    total = part if total is None else total + part
                    kept = e.astype(BF16)
                    e_ref[h, ks, cols] = kept
                    e_s[slot, s, ks, cols] = kept
                il_ref[h, :, cols] = 1.0 / total

    def mix_pair(p, slot):
        for s in range(2):
            rows = pl.ds(pl.multiple_of(p * LANE + 64 * s, 64), 64)
            mixt_ref[rows, :] = (nn(vt_s[rows, :], e_s[slot, s]) * il_ref[2 * p + s]).astype(BF16)

    def pair_step(i, carry):
        mix_pair(2 * i, 0)
        softmax_pair(2 * i + 1, 1)
        mix_pair(2 * i + 1, 1)
        softmax_pair(2 * i + 2, 0)
        return carry

    pairs = width // LANE
    for kb, qb in itertools.product(range(blocks), repeat=2):
        if not reachable(kb - qb, tile):
            far = (slice(kb * tile, (kb + 1) * tile), slice(qb * tile, (qb + 1) * tile))
            e_s[(slice(None), slice(None), *far)] = jnp.zeros((2, 2, tile, tile), BF16)
            e_ref[(slice(None), *far)] = jnp.zeros((heads, tile, tile), BF16)
    softmax_pair(0, 0)
    lax.fori_loop(0, pairs // 2 - 1, pair_step, 0)
    mix_pair(pairs - 2, 0)
    softmax_pair(pairs - 1, 1)
    mix_pair(pairs - 1, 1)
    io.done(e_ref, mixt_ref)
    io.need(wo_s)
    mid_s[...] = x_ref[...].astype(F32) + nn(mixt_ref[...].T, wo_s[...])
    mid = mid_s[...]
    mid_ref[...] = mid.astype(BF16)
    s2 = lax.rsqrt(jnp.mean(mid * mid, axis=-1, keepdims=True) + EPS)
    n2_ref[...] = (mid * s2 * gains_ref[1:2, :]).astype(BF16)
    io.done(mid_ref, n2_ref)

    io.feed((wg_s, wu_s))

    def ff_body(j, carry):
        io.need_part(j, wg_s, wu_s)
        col = pl.ds(pl.multiple_of(j * CH, CH), CH)
        g = nn(n2_ref[...], wg_s[:, col])
        u = nn(n2_ref[...], wu_s[:, col])
        sq = g * g
        t = jnp.tanh(GELU_A * g * (1.0 + GELU_B * sq))
        half = 0.5 + 0.5 * t
        gel = g * half
        slope = half + (0.5 * GELU_A) * g * (1.0 - t * t) * (1.0 + 3.0 * GELU_B * sq)
        hid_ref[:, col] = (gel * u).astype(BF16)
        a_ref[:, col] = (u * slope).astype(BF16)
        b_ref[:, col] = gel.astype(BF16)
        return carry

    lax.fori_loop(0, hidden // CH, ff_body, 0)
    io.had(wg_s, wu_s)
    io.done(hid_ref, a_ref, b_ref)
    io.need(wd_s)
    mid_s[...] += nn(hid_ref[...], wd_s[...])
    o = mid_s[...]
    out_ref[...] = o.astype(BF16)
    s3 = lax.rsqrt(jnp.mean(o * o, axis=-1, keepdims=True) + EPS)
    n3_ref[...] = (o * s3 * gains_ref[2:3, :]).astype(BF16)
    io.done(out_ref, n3_ref)
    io.need(wp_s)
    pr = nn(n3_ref[...], wp_s[...])
    proj_ref[...] = pr
    emb = (pr * lax.rsqrt(jnp.sum(pr * pr, axis=-1, keepdims=True) + EPS)).astype(BF16)
    if is_doc:
        emb_ref[...] = emb
    else:
        io.need(cand_ref, label_ref)
        ints = pack_ints(cand_ref, label_ref, lens_ref)
        for i in range(emb_ref.shape[0]):
            emb_ref[i, 0:tokens, :] = emb
            emb_ref[i, tokens:, :] = ints


def pack_ints(cand_ref, label_ref, lens_ref):
    count = cand_ref.shape[1]
    eye = lax.broadcasted_iota(jnp.int32, (count, count), 0) == lax.broadcasted_iota(jnp.int32, (count, count), 1)
    lane = lax.broadcasted_iota(jnp.int32, (1, LANE), 1)
    row = lax.broadcasted_iota(jnp.int32, (PACK_INT, 1), 0)
    packed = jnp.zeros((PACK_INT, LANE), F32)
    for a in range(cand_ref.shape[0]):
        values = jnp.where(eye, cand_ref[a:a + 1, :].astype(F32), 0.0)
        column = jnp.sum(values, axis=1, keepdims=True)
        column = jnp.concatenate([column, jnp.zeros((PACK_INT - count, 1), F32)], axis=0)
        column = jnp.where(row == count, label_ref[0:1, a:a + 1].astype(F32), column)
        column = jnp.where(row == count + 1, lens_ref[0:1, a:a + 1].astype(F32), column)
        packed = jnp.where(lane == a, column, packed)
    return packed.astype(BF16)


def forward(x, lens, gains, extra, weights, is_doc, heads, copies=1):
    tokens, width = x.shape
    hidden = weights[4].shape[1]
    proj = weights[7].shape[1]
    outs = [((tokens, width), BF16, "h")] * 3 + [
        ((heads, tokens, tokens), BF16, "h"),
        ((heads, 1, tokens), F32, "v"),
        ((width, tokens), BF16, "h"),
        ((tokens, width), BF16, "h"),
        ((tokens, width), BF16, "h"),
        ((tokens, width), BF16, "h"),
        ((tokens, hidden), BF16, "h"),
        ((tokens, hidden), BF16, "h"),
        ((tokens, hidden), BF16, "h"),
        ((tokens, width), BF16, "h"),
        ((tokens, width), BF16, "h"),
        ((tokens, proj), F32, "h"),
        ((tokens, proj) if is_doc else (copies, tokens + PACK_INT, proj), BF16, "v"),
    ]
    tile = min(tokens, 128)
    scratch = [
        pltpu.VMEM((tokens, tokens), F32),
        pltpu.VMEM((2, tile, SPAN), F32),
        pltpu.VMEM((2, tokens, tokens), F32),
        pltpu.VMEM((2, 2, tokens, tokens), BF16),
        pltpu.VMEM((width, tokens), BF16),
        pltpu.VMEM((tokens, width), F32),
    ]
    steps = weights[4].shape[1] // CH
    streams = [(w, f"h-{steps}" if w.shape == weights[4].shape else "h") for w in weights]
    ins = [(x, "h"), (lens, "h"), (gains, "v")]
    if is_doc:
        kernel = functools.partial(forward_kernel, True)
        ins = ins + [(extra, "h")] + streams
    else:
        outs.append(((heads, 8, SPAN), F32, "h"))

        def kernel(io, x_ref, lens_ref, gains_ref, hot_ref, cand_ref, label_ref, *rest):
            forward_kernel(False, io, x_ref, lens_ref, gains_ref, (hot_ref, cand_ref, label_ref), *rest)

        ins = ins + [(item, "h") for item in extra] + streams
    flops = 2 * tokens * (4 * width * width + 3 * width * hidden + width * proj) + 4 * tokens * tokens * width
    return call(kernel, "doc_forward" if is_doc else "query_forward", ins, outs, scratch, 50, flops, 30 << 20)


def unpack(got_ref, tokens):
    parts = got_ref.shape[0]
    own = 2
    lane = lax.broadcasted_iota(jnp.int32, (1, LANE), 1)
    ints = None
    for i in range(parts):
        block = got_ref[i, tokens:, :].astype(F32)
        if i:
            block = pltpu.roll(block, own * i, 1)
        block = jnp.where((lane // own) == i, block, 0.0)
        ints = block if ints is None else ints + block
    return ints[0:32, :], ints[32:33, :], ints[33:34, :]


def expand_onehot(queries, length):
    col = lax.broadcasted_iota(jnp.int32, (LANE, queries * length), 1)
    row = lax.broadcasted_iota(jnp.int32, (LANE, queries * length), 0)
    return ((col // length) == row).astype(F32)


def token_valid(lens, queries, length):
    hot = expand_onehot(queries, length)
    spread = jnp.dot(jnp.broadcast_to(lens, (8, LANE)), hot, precision=highest, preferred_element_type=F32)[0:1]
    place = lax.broadcasted_iota(jnp.int32, (1, queries * length), 1) % length
    return place.astype(F32) < spread, hot


def block_scores(emb_ref, q_s, b):
    t = nt(emb_ref[b * BLK:(b + 1) * BLK, :], q_s[...]) * (1.0 / SHARP)
    row = lax.broadcasted_iota(jnp.int32, (BLK, 1), 0) + b * BLK
    return jnp.where(row < ROW_FILL, t, NEG) if (b + 1) * BLK > ROW_FILL else t


def score_kernel(length, io, got_ref, emb_ref, sums_ref, lse_ref, q_s):
    parts = got_ref.shape[0]
    tokens = q_s.shape[0] // parts
    queries = q_s.shape[0] // length
    for i in range(parts):
        q_s[i * tokens:(i + 1) * tokens, :] = got_ref[i, 0:tokens, :]
    _, _, lens = unpack(got_ref, tokens)
    valid, hot = token_valid(lens, queries, length)
    blocks = emb_ref.shape[0] // BLK
    rows = []
    for b in range(blocks):
        t = block_scores(emb_ref, q_s, b)
        top = jnp.max(t, axis=0, keepdims=True)
        lse = top + jnp.log(jnp.sum(jnp.exp(t - top), axis=0, keepdims=True))
        lse_ref[b:b + 1, :] = lse
        rows.append(jnp.where(valid, SHARP * lse, 0.0))
    rows.append(jnp.zeros((8 - blocks, rows[0].shape[1]), F32))
    sums = lax.dot_general(
        jnp.concatenate(rows, axis=0), hot, (((1,), (1,)), ((), ())), precision=highest, preferred_element_type=F32
    )
    for i in range(parts):
        sums_ref[i] = sums


def scores(got, emb, length):
    parts = got.shape[0]
    tokens = got.shape[1] - PACK_INT
    total = parts * tokens
    return call(
        functools.partial(score_kernel, length),
        "block_sums",
        [(got, "v"), (emb, "v")],
        [((parts, 8, LANE), F32, "v"), ((8, total), F32, "v")],
        [pltpu.VMEM((total, emb.shape[1]), BF16)],
        24,
        2 * emb.shape[0] * total * 128,
        1 << 20,
    )


def loss_kernel(length, io, got_ref, sums_ref, emb_ref, lse_ref, doc_ref, qry_ref, loss_ref, q_s, d_s, s_s):
    parts = got_ref.shape[0]
    tokens = q_s.shape[0] // parts
    queries = q_s.shape[0] // length
    for i in range(parts):
        q_s[i * tokens:(i + 1) * tokens, :] = got_ref[i, 0:tokens, :]
    cand, label, lens = unpack(got_ref, tokens)
    valid, hot = token_valid(lens, queries, length)
    blocks = emb_ref.shape[0] // BLK
    logits = jnp.zeros(cand.shape, F32)
    for i in range(parts):
        for b in range(blocks):
            logits = logits + jnp.where(cand == float(i * blocks + b), sums_ref[i, b:b + 1, :], 0.0)
    logits = SCALE * logits
    top = jnp.max(logits, axis=0, keepdims=True)
    lse = top + jnp.log(jnp.sum(jnp.exp(logits - top), axis=0, keepdims=True))
    choice = lax.broadcasted_iota(jnp.int32, cand.shape, 0).astype(F32) == label
    lane = lax.broadcasted_iota(jnp.int32, (1, LANE), 1)
    picked = jnp.sum(jnp.where(choice, logits, 0.0), axis=0, keepdims=True)
    each = jnp.where(lane < queries, lse - picked, 0.0)
    loss_ref[...] = jnp.broadcast_to(jnp.sum(each, axis=1, keepdims=True), (1, LANE))
    dlogits = SCALE * (jnp.exp(logits - lse) - jnp.where(choice, 1.0, 0.0))
    me = lax.axis_index("dp").astype(jnp.int32)
    rows = []
    for b in range(blocks):
        mine = (me * blocks + b).astype(F32)
        rows.append(jnp.sum(jnp.where(cand == mine, dlogits, 0.0), axis=0, keepdims=True))
    rows.append(jnp.zeros((8 - blocks, LANE), F32))
    spread = jnp.dot(jnp.concatenate(rows, axis=0), hot, precision=highest, preferred_element_type=F32)
    for b in range(blocks):
        t = block_scores(emb_ref, q_s, b)
        weight = jnp.where(valid, spread[b:b + 1, :], 0.0)
        d_s[b * BLK:(b + 1) * BLK, :] = (weight * jnp.exp(t - lse_ref[b:b + 1, :])).astype(BF16)
    doc_ref[...] = nn(d_s[...], q_s[...])
    s_s[...] = d_s[...].T
    qry_ref[...] = nn(s_s[...], emb_ref[...]).reshape(qry_ref.shape)


def retrieval_back(got, sums, emb, lse, length):
    parts = got.shape[0]
    tokens = got.shape[1] - PACK_INT
    total = parts * tokens
    docs, proj = emb.shape
    return call(
        functools.partial(loss_kernel, length),
        "retrieval_back",
        [(got, "v"), (sums, "v"), (emb, "v"), (lse, "v")],
        [((docs, proj), F32, "v"), ((parts, tokens, proj), F32, "v"), ((1, LANE), F32, "v")],
        [pltpu.VMEM((total, proj), BF16), pltpu.VMEM((docs, total), BF16), pltpu.VMEM((total, docs), BF16)],
        32,
        6 * docs * total * proj,
        2 << 20,
    )


def chain_kernel(
    io, demb_ref, gains_ref, proj_ref, wp_s, out_ref, wd_s, a_ref, b_ref, wg_s, wu_s, mid_ref, wo_s,
    dpj_ref, dbr_ref, dg_ref, du_ref, datt_ref, dmid_ref, dmix_ref, acc_s,
):
    hidden = a_ref.shape[1]
    if len(demb_ref.shape) == 3:
        dy = demb_ref[0]
        for i in range(1, demb_ref.shape[0]):
            dy = dy + demb_ref[i]
    else:
        dy = demb_ref[...]
    io.need(proj_ref)
    pr = proj_ref[...]
    r = lax.rsqrt(jnp.sum(pr * pr, axis=-1, keepdims=True) + EPS)
    unit = pr * r
    dpj_ref[...] = (r * (dy - unit * jnp.sum(dy * unit, axis=-1, keepdims=True))).astype(BF16)
    io.done(dpj_ref)
    io.need(wp_s, out_ref)
    dn3 = nt(dpj_ref[...], wp_s[...])
    dout = norm_back(out_ref[...].astype(F32), gains_ref[2:3, :], dn3)
    dmid_ref[...] = dout
    dbr_ref[...] = dout.astype(BF16)
    io.done(dbr_ref)

    io.feed((wd_s, a_ref, b_ref, wg_s, wu_s))

    def body(j, carry):
        io.need_part(j, wd_s, a_ref, b_ref)
        col = pl.ds(pl.multiple_of(j * CH, CH), CH)
        dh = nt(dbr_ref[...], wd_s[col, :])
        dg_ref[:, col] = (dh * a_ref[:, col].astype(F32)).astype(BF16)
        du_ref[:, col] = (dh * b_ref[:, col].astype(F32)).astype(BF16)
        return carry

    lax.fori_loop(0, hidden // CH, body, 0)
    io.had(wd_s, a_ref, b_ref)
    io.done(dg_ref, du_ref)
    io.need(wg_s, wu_s)
    acc_s[...] = nt(dg_ref[...], wg_s[...]) + nt(du_ref[...], wu_s[...])
    io.need(mid_ref)
    dmid = dmid_ref[...] + norm_back(mid_ref[...].astype(F32), gains_ref[1:2, :], acc_s[...])
    dmid_ref[...] = dmid
    datt_ref[...] = dmid.astype(BF16)
    io.done(dmid_ref, datt_ref)
    io.need(wo_s)
    dmix_ref[...] = nt(datt_ref[...], wo_s[...]).astype(BF16)


def chain_ins(demb, gains, proj, wp, out, wd, a, b, wg, wu, mid, wo):
    steps = a.shape[1] // CH
    plain = lambda *items: [(item, "h") for item in items]
    parts = [(wd, f"h{steps}")] + [(item, f"h-{steps}") for item in (a, b)]
    return [(demb, "v"), (gains, "v")] + plain(proj, wp, out) + parts + plain(wg, wu, mid, wo)


def chain(demb, proj, out, mid, a, b, gains, wp, wd, wg, wu, wo, name):
    tokens, width = out.shape
    hidden = a.shape[1]
    return call(
        chain_kernel,
        name,
        chain_ins(demb, gains, proj, wp, out, wd, a, b, wg, wu, mid, wo),
        [
            (proj.shape, BF16, "h"),
            ((tokens, width), BF16, "h"),
            ((tokens, hidden), BF16, "h"),
            ((tokens, hidden), BF16, "h"),
            ((tokens, width), BF16, "h"),
            ((tokens, width), F32, "h"),
            ((tokens, width), BF16, "h"),
        ],
        [pltpu.VMEM((tokens, width), F32)],
        44,
        2 * tokens * (width * width + 3 * width * hidden + width * 128),
        30 << 20,
    )


def attention_back_kernel(
    io, k_ref, v_ref, q_ref, dmix_ref, mixt_ref, il_ref, e_ref, dqkv_ref, diag_ref, far_ref,
    dqt_s, p_s, ds_s, strip_s, dk_s, dv_s,
):
    tokens, width = q_ref.shape
    tile = min(tokens, 128)
    wide = min(tokens, 256)
    blocks = tokens // tile
    io.feed((k_ref, v_ref, q_ref, dmix_ref, mixt_ref, e_ref))

    def pair_body(p, carry):
        io.need_part(p, k_ref, v_ref, q_ref, dmix_ref, mixt_ref, e_ref)
        col = pl.ds(pl.multiple_of(p * LANE, LANE), LANE)
        kt = k_ref[:, col].T
        dmixt = dmix_ref[:, col].T
        for s in range(2):
            h = 2 * p + s
            vp = half_lanes(v_ref[:, col], s)
            dm = half_lanes(dmix_ref[:, col], s)
            qm = half_lanes(q_ref[:, col], s)
            rows = pl.ds(pl.multiple_of(p * LANE + 64 * s, 64), 64)
            strip_s[...] = jnp.zeros_like(strip_s)
            far_low = jnp.zeros((8, LANE), F32)
            far_high = jnp.zeros((8, LANE), F32)
            for qc in range(tokens // wide):
                cols = slice(qc * wide, (qc + 1) * wide)
                dt = dmixt[:, cols]
                delta = jnp.sum(
                    dmixt[64 * s:64 * s + 64, cols].astype(F32) * mixt_ref[rows, cols].astype(F32), axis=0, keepdims=True
                )
                inverse = il_ref[h, :, cols]
                for kb in range(blocks):
                    ks = slice(kb * tile, (kb + 1) * tile)
                    dp = nn(vp[ks], dt)
                    prob = e_ref[h, ks, cols].astype(F32) * inverse
                    p_s[ks, :] = prob.astype(BF16)
                    ds = (prob * (dp - delta)).astype(BF16)
                    ds_s[ks, :] = ds
                    kept = ds.astype(F32)
                    for qs in range(wide // tile):
                        d = kb - (qc * (wide // tile) + qs)
                        t = kept[:, qs * tile:(qs + 1) * tile]
                        if abs(d) <= 1:
                            lo = (1 - d) * 128
                            strip_s[0:tile, lo:lo + tile] += t
                        else:
                            part = t[0:8]
                            for g in range(1, tile // 8):
                                part = part + t[8 * g:8 * g + 8]
                            if d > 0:
                                far_high = far_high + part
                            else:
                                far_low = far_low + part
                dv = nn(p_s[...], dm[cols])
                dk = nn(ds_s[...], qm[cols])
                if s == 0 and qc == 0:
                    dv_s[...] = dv
                    dk_s[...] = dk
                else:
                    dv_s[...] += dv
                    dk_s[...] += dk
                dqt_s[rows, cols] = nn(kt[64 * s:64 * s + 64], ds_s[...]).astype(BF16)
            fold = strip_s[...]
            size = strip_s.shape[0]
            while size > 8:
                size //= 2
                fold = fold[:size] + pltpu.roll(fold[size:], SPAN - size, 1)
            diag_ref[h] = fold
            far_ref[h, 0:8, :] = far_low
            far_ref[h, 8:16, :] = far_high
        kcol = pl.ds(pl.multiple_of(width + p * LANE, LANE), LANE)
        vcol = pl.ds(pl.multiple_of(2 * width + p * LANE, LANE), LANE)
        dqkv_ref[:, kcol] = dk_s[...].astype(BF16)
        dqkv_ref[:, vcol] = dv_s[...].astype(BF16)
        return carry

    lax.fori_loop(0, width // LANE, pair_body, 0)
    io.had(k_ref, v_ref, q_ref, dmix_ref, mixt_ref, e_ref)
    dqkv_ref[:, 0:width] = dqt_s[...].T


def attention_ins(q, k, v, e, il, mixt, dmix):
    pairs = q.shape[1] // LANE
    return [(item, "v") for item in (k, v, q, dmix, mixt, il, e)]


def attention_outs(q, heads):
    tokens, width = q.shape
    return [((tokens, 3 * width), BF16, "v"), ((heads, 8, SPAN), F32, "v"), ((heads, 16, LANE), F32, "v")]


def attention_scratch(q):
    tokens, width = q.shape
    tile, wide = min(tokens, 128), min(tokens, 256)
    return [
        pltpu.VMEM((width, tokens), BF16),
        pltpu.VMEM((tokens, wide), BF16),
        pltpu.VMEM((tokens, wide), BF16),
        pltpu.VMEM((tile, SPAN), F32),
        pltpu.VMEM((tokens, LANE), F32),
        pltpu.VMEM((tokens, LANE), F32),
    ]


def attention_back(q, k, v, e, il, mixt, dmix, name):
    tokens, width = q.shape
    return call(
        attention_back_kernel,
        name,
        attention_ins(q, k, v, e, il, mixt, dmix),
        attention_outs(q, e.shape[0]),
        attention_scratch(q),
        9,
        10 * tokens * tokens * width,
        16 << 20,
    )


def input_kernel(io, gains_ref, *refs):
    kinds = (len(refs) - 3) // 4
    reads, weights, writes = refs[:3 * kinds], refs[3 * kinds:3 * kinds + 3], refs[3 * kinds + 3:]
    for kind in range(kinds):
        dqkv_ref, x_ref, dmid_ref = reads[3 * kind:3 * kind + 3]
        width = x_ref.shape[1]
        io.need(dqkv_ref)
        total = None
        for i, w in enumerate(weights):
            io.need(w)
            part = nt(dqkv_ref[:, i * width:(i + 1) * width], w[...])
            total = part if total is None else total + part
        io.need(x_ref, dmid_ref)
        writes[kind][...] = dmid_ref[...] + norm_back(x_ref[...].astype(F32), gains_ref[0:1, :], total)
        io.done(writes[kind])


def input_back(gains, kinds, weights, name):
    width = weights[0].shape[0]
    tokens = sum(x.shape[0] for _, x, _ in kinds)
    return call(
        input_kernel,
        name,
        [(gains, "v")]
        + [(item, kind) for dqkv, x, dmid in kinds for item, kind in ((dqkv, "v"), (x, "h"), (dmid, "h"))]
        + [(w, "h") for w in weights],
        [(x.shape, F32, "h") for _, x, _ in kinds],
        [],
        32,
        6 * tokens * width * width,
        8 << 20,
    )


def put_rows(buf, value, per, offset, lanes, extra=None):
    for j in range(buf.shape[1]):
        for core in range(2):
            rows = slice((2 * j + core) * per, (2 * j + core + 1) * per)
            pieces = [value[rows, lo:lo + 256] for lo in lanes]
            if extra is not None:
                pieces.append(extra(rows))
            block = jnp.concatenate(pieces, axis=0) if len(pieces) > 1 else pieces[0]
            buf[core, j, pl.ds(offset, block.shape[0]), :] = block.astype(BF16)


def push_rows(io, buf, own_ref, send_ref, start, size, shift=0):
    core = core_index()
    rows, there = pl.ds(start, size), pl.ds(start + shift, size)
    for ref, side in ((send_ref, 1 - core), (own_ref, core)):
        io.push(buf.at[side, :, rows], ref.at[:, there])


def halves_buffer(count, rows):
    return pltpu.VMEM((2, count, rows, 256), BF16)


def core_index():
    return (lax.axis_index("grp") % 2).astype(jnp.int32)


def halves(count, rows):
    return [((count, rows, 256), BF16, "a")] * 2


def down_grad_kernel(
    io, demb_ref, gains_ref, proj_ref, wp_s, out_ref, wd_s, a_ref, b_ref, wg_s, wu_s, mid_ref, wo_s,
    hid_ref, hidq_ref, dbr_ref, mixt_ref, mixtq_ref, datt_ref, n3_ref, n3q_ref, dpj_ref,
    dg_ref, du_ref, dmid_ref, dmix_ref, own_ref, send_ref,
    acc1_s, dpjq_s, dbrq_s, dattq_s, hidt_s, hidtq_s, buf_s,
):
    chain_kernel(
        io, demb_ref, gains_ref, proj_ref, wp_s, out_ref, wd_s, a_ref, b_ref, wg_s, wu_s, mid_ref, wo_s,
        dpjq_s, dbrq_s, dg_ref, du_ref, dattq_s, dmid_ref, dmix_ref, acc1_s,
    )
    io.done(dmix_ref)
    hidden, width = hid_ref.shape[1], dbr_ref.shape[1]
    count = own_ref.shape[0]
    per, per_down = width // (2 * count), hidden // (2 * count)
    io.need(hid_ref, hidq_ref)
    hidt_s[...] = hid_ref[...].T
    hidtq_s[...] = hidq_ref[...].T
    io.need(dbr_ref)
    for i in range(width // 256):
        col = slice(i * 256, (i + 1) * 256)
        value = nn(hidt_s[...], dbr_ref[:, col]) + nn(hidtq_s[...], dbrq_s[:, col])
        put_rows(buf_s, value, per_down, i * per_down, (0,))
        push_rows(io, buf_s, own_ref, send_ref, i * per_down, per_down)
    base = (width // 256) * per_down
    io.need(mixt_ref, mixtq_ref, datt_ref, n3_ref, n3q_ref, dpj_ref)
    value = nn(mixt_ref[...], datt_ref[...]) + nn(mixtq_ref[...], dattq_s[...])
    put_rows(buf_s, value, per, base, (0, 256))
    push_rows(io, buf_s, own_ref, send_ref, base, 2 * per)
    base = base + 2 * per
    proj = nn(n3_ref[...].T, dpj_ref[...]) + nn(n3q_ref[...].T, dpjq_s[...])

    def proj_rows(rows):
        return jnp.concatenate([proj[rows], jnp.zeros((per, LANE), F32)], axis=1)

    put_rows(buf_s, value, per, base, (512,), extra=proj_rows)
    push_rows(io, buf_s, own_ref, send_ref, base, 2 * per)


def down_grads(query, doc, count):
    (demb, proj, out, mid, a, b, gains, wp, wd, wg, wu, wo), (hidq, mixtq, n3q) = query
    hid, dbr, mixt, datt, n3, dpj = doc
    tokens, hidden = hid.shape
    qtokens, width = out.shape
    per, per_down = width // (2 * count), hidden // (2 * count)
    plain = [(item, "h") for item in (hid, hidq, dbr, mixt, mixtq, datt, n3, n3q, dpj)]
    return call(
        down_grad_kernel,
        "query_ff_back_down_grads",
        chain_ins(demb, gains, proj, wp, out, wd, a, b, wg, wu, mid, wo) + plain,
        [
            ((qtokens, hidden), BF16, "h"),
            ((qtokens, hidden), BF16, "h"),
            ((qtokens, width), F32, "h"),
            ((qtokens, width), BF16, "h"),
        ]
        + halves(count, (width // 256) * per_down + 4 * per),
        [
            pltpu.VMEM((qtokens, width), F32),
            pltpu.VMEM(proj.shape, BF16),
            pltpu.VMEM((qtokens, width), BF16),
            pltpu.VMEM((qtokens, width), BF16),
            pltpu.VMEM((hidden, tokens), BF16),
            pltpu.VMEM((hidden, qtokens), BF16),
            halves_buffer(count, (width // 256) * per_down + 4 * per),
        ],
        40,
        2 * (tokens + 256) * (width * width + width * hidden),
        24 << 20,
    )


def gate_grad_kernel(which, io, n2_ref, n2q_ref, d, dq, *refs):
    own_ref, send_ref, n2t_s, n2tq_s, buf_s = refs[-5:]
    width, hidden = n2_ref.shape[1], d.shape[1]
    count, rows = own_ref.shape[:2]
    per = width // (2 * count)
    io.need(n2_ref, n2q_ref)
    n2t_s[...] = n2_ref[...].T
    n2tq_s[...] = n2q_ref[...].T
    io.need(dq)
    io.feed((d,))
    for i in range(hidden // CH):
        io.need_part(i, d)
        col = slice(i * CH, (i + 1) * CH)
        value = nn(n2t_s[...], d[:, col]) + nn(n2tq_s[...], dq[:, col])
        for lo in range(0, CH, 512):
            at = (i * CH + lo) // 256 * per
            put_rows(buf_s, value, per, at, (lo, lo + 256))
            push_rows(io, buf_s, own_ref, send_ref, at, 2 * per, which * (rows // 2))
    io.had(d)


def gate_grads(which, n2, n2q, d, dq, count, begun=()):
    tokens, width = n2.shape
    qtokens, hidden = dq.shape
    per = width // (2 * count)
    rows = 2 * (hidden // 256) * per
    return call(
        functools.partial(gate_grad_kernel, which),
        ("gate_grads", "up_grads")[which],
        [(n2, "h"), (n2q, "h"), (d, f"h-{hidden // CH}"), (dq, "h")] + [(item, "b") for item in begun],
        halves(count, rows),
        [
            pltpu.VMEM((width, tokens), BF16),
            pltpu.VMEM((width, qtokens), BF16),
            halves_buffer(count, rows // 2),
        ],
        18,
        2 * (tokens + 256) * width * hidden,
        16 << 20,
        {4: 0, 5: 1} if begun else None,
    )


def qkv_grad_kernel(
    io, k_ref, v_ref, q_ref, dmix_ref, mixt_ref, il_ref, e_ref, n1_ref, n1q_ref, d_ref,
    diagd_ref, fard_ref, hot_ref, loss_ref, dq_ref, diag_ref, far_ref, own_ref, send_ref, *rest,
):
    own_parts = lax.axis_size("dp")
    n1t_s, n1tq_s, buf_s = rest[-3:]
    attention_back_kernel(
        io, k_ref, v_ref, q_ref, dmix_ref, mixt_ref, il_ref, e_ref, dq_ref, diag_ref, far_ref, *rest[:-3]
    )
    io.done(dq_ref)
    width = n1_ref.shape[1]
    count = own_ref.shape[0]
    per = width // (2 * count)
    io.need(n1_ref, n1q_ref)
    n1t_s[...] = n1_ref[...].T
    n1tq_s[...] = n1q_ref[...].T
    io.need(d_ref)
    steps = (3 * width) // 512
    value = nn(n1t_s[...], d_ref[...]) + nn(n1tq_s[...], dq_ref[...])
    for i in range(steps):
        put_rows(buf_s, value, per, i * 2 * per, (i * 512, i * 512 + 256))
        push_rows(io, buf_s, own_ref, send_ref, i * 2 * per, 2 * per)
    io.need(hot_ref)
    heads = diag_ref.shape[0]
    buckets = hot_ref.shape[0]
    table = jnp.zeros((heads, buckets), F32)
    for r in range(8):
        both = diagd_ref[:, r, :] + diag_ref[:, r, :]
        table = table + lax.dot_general(
            both, hot_ref[:, r * SPAN:(r + 1) * SPAN].astype(F32), (((1,), (1,)), ((), ())),
            precision=highest, preferred_element_type=F32,
        )
    far = fard_ref[...] + far_ref[...]
    low = jnp.sum(jnp.sum(far[:, 0:8, :], axis=1), axis=-1, keepdims=True)
    high = jnp.sum(jnp.sum(far[:, 8:16, :], axis=1), axis=-1, keepdims=True)
    column = lax.broadcasted_iota(jnp.int32, (1, buckets), 1)
    table = table + jnp.where(column == buckets // 2 - 1, low, 0.0) + jnp.where(column == buckets - 1, high, 0.0)
    table = jnp.concatenate([table, jnp.zeros((16 - heads, buckets), F32)], axis=0)
    loss = jnp.broadcast_to(loss_ref[...] * (1.0 / own_parts), (8, LANE))
    spare = jnp.concatenate([table[0:8], table[8:16], jnp.zeros((8, LANE - 2 * buckets), F32), loss], axis=1)
    put_rows(buf_s, value, per, steps * 2 * per, (steps * 512,), extra=lambda rows: spare)
    push_rows(io, buf_s, own_ref, send_ref, steps * 2 * per, per + 8)


def qkv_grads(query, n1, n1q, d, diag, far, hot, loss, count):
    tokens, width = n1.shape
    per = width // (2 * count)
    return call(
        qkv_grad_kernel,
        "query_attention_back_qkv_grads",
        attention_ins(*query)
        + [(n1, "h"), (n1q, "h"), (d, "v")]
        + [(diag, "v"), (far, "v"), (hot, "h"), (loss, "v")],
        attention_outs(query[0], query[3].shape[0]) + halves(count, 9 * per + 8),
        attention_scratch(query[0])
        + [
            pltpu.VMEM((width, tokens), BF16),
            pltpu.VMEM((width, n1q.shape[0]), BF16),
            halves_buffer(count, 9 * per + 8),
        ],
        24,
        2 * (tokens + 256) * 3 * width * width,
        10 << 20,
    )


def after(values, *deps):
    return lax.optimization_barrier((values, deps))[0]


def position(n_dp):
    dp, grp = lax.axis_index("dp").astype(jnp.int32), lax.axis_index("grp").astype(jnp.int32)
    return dp // 2, dp % 2, grp // 2


def slices(io_sems, moves):
    copies = [pltpu.make_async_copy(src, dst, io_sems.at[i]) for i, (src, dst) in enumerate(moves)]
    for copy in copies:
        copy.start()
    return copies


class Halves:
    def __init__(self, rows):
        self.rows, self.cut = rows, (rows // 32) * 16

    def sizes(self):
        return self.cut, self.rows - self.cut

    def spans(self):
        return pl.ds(0, self.cut), pl.ds(self.cut, self.rows - self.cut)


def first_kernel(n_dp, halves, io, own_ref, got_ref, x_ref, y_ref, ox_s, gx_s, oy_s, gy_s, sems):
    _, x, y = position(n_dp)
    top, low = halves.spans()
    moves = []
    for ref, a, b in ((own_ref, ox_s, oy_s), (got_ref, gx_s, gy_s)):
        moves += [(ref.at[:, 1 - x, :, top], a), (ref.at[:, :, 1 - y, low], b)]
    copies = slices(sems, moves)
    for i, (a, b, out) in enumerate(((ox_s, gx_s, x_ref), (oy_s, gy_s, y_ref))):
        copies[i].wait()
        copies[i + 2].wait()
        out[...] = (a[...].astype(F32) + b[...].astype(F32)).astype(BF16)
        io.done(out)


def pair_rows(n_dp, halves, flip, own_ref, got_ref, gx_ref, gy_ref, bufs, sems):
    _, x, y = position(n_dp)
    top, low = halves.spans()
    yt, xl = (1 - y, 1 - x) if flip else (y, x)
    ot_s, gt_s, rt_s, ol_s, gl_s, rl_s = bufs
    copies = slices(sems, [
        (own_ref.at[:, x, yt, top], ot_s), (got_ref.at[:, x, yt, top], gt_s), (gx_ref.at[:, yt], rt_s),
        (own_ref.at[:, xl, y, low], ol_s), (got_ref.at[:, xl, y, low], gl_s), (gy_ref.at[:, xl], rl_s),
    ])
    out = []
    for i in (0, 3):
        for copy in copies[i:i + 3]:
            copy.wait()
        a, b, c = bufs[i:i + 3]
        out.append(a[...].astype(F32) + b[...].astype(F32) + c[...].astype(F32))
    return out


def second_kernel(n_dp, halves, io, own_ref, got_ref, gx_ref, gy_ref, y_ref, x_ref, *refs):
    for out, value in zip((y_ref, x_ref), pair_rows(n_dp, halves, True, own_ref, got_ref, gx_ref, gy_ref, refs[:-1], refs[-1])):
        out[...] = value.astype(BF16)
        io.done(out)


def cross_kernel(n_dp, halves, io, own_ref, got_ref, xy_ref, x_ref, y_ref, own_s, got_s, sems):
    _, x, y = position(n_dp)
    moves = []
    for i, (xx, yy) in enumerate(((1 - x, 1 - y), (1 - x, y), (x, 1 - y))):
        moves += [(own_ref.at[:, xx, yy], own_s.at[i]), (got_ref.at[:, xx, yy], got_s.at[i])]
    copies = slices(sems, moves)
    for i, out in enumerate((xy_ref, x_ref, y_ref)):
        copies[2 * i].wait()
        copies[2 * i + 1].wait()
        out[...] = (own_s[i].astype(F32) + got_s[i].astype(F32)).astype(BF16)
        io.done(out)


def leave(z, line_s, outs, total_ref, io):
    nz = line_s.shape[0]
    if not outs:
        total_ref[...] = line_s[...].astype(BF16)
        return
    for k, out in enumerate(outs, 1):
        out[...] = line_s[(z + k) % nz].astype(BF16)
        io.done(out)
    total_ref[...] = line_s[z]


def cross_line_kernel(n_dp, halves, io, own_ref, got_ref, xy_ref, x_ref, y_ref, *refs):
    outs, total_ref, (line_s, own_s, got_s, sems) = refs[:-5], refs[-5], refs[-4:]
    z, x, y = position(n_dp)
    copies = slices(sems, [(own_ref.at[:, x, y], own_s), (got_ref.at[:, x, y], got_s)])
    for copy in copies:
        copy.wait()
    io.need(xy_ref, x_ref, y_ref)
    line_s[...] = own_s[...].astype(F32) + got_s[...].astype(F32) + xy_ref[...].astype(F32)
    line_s[...] += x_ref[...].astype(F32) + y_ref[...].astype(F32)
    leave(z, line_s, outs, total_ref, io)


def line_kernel(n_dp, halves, io, own_ref, got_ref, gx_ref, gy_ref, y_ref, x_ref, *refs):
    outs, total_ref, line_s, bufs, sems = refs[:-9], refs[-9], refs[-8], refs[-7:-1], refs[-1]
    z, _, _ = position(n_dp)
    top, low = pair_rows(n_dp, halves, False, own_ref, got_ref, gx_ref, gy_ref, bufs, sems)
    io.need(x_ref, y_ref)
    line_s[:, 0:halves.cut] = top + y_ref[...].astype(F32)
    line_s[:, halves.cut:] = low + x_ref[...].astype(F32)
    leave(z, line_s, outs, total_ref, io)


class Batch:
    def __init__(self, own, send, n_dp, n_grp, name):
        self.n_dp, self.n_grp, self.nz, self.name = n_dp, n_grp, n_dp // 2, name
        self.rows, self.cols = own.shape[1:]
        self.halves = Halves(self.rows)
        self.own = own
        self.got = lax.ppermute(send, "grp", [(i, i ^ 1) for i in range(n_grp)])

    def both(self):
        grid = lambda a: (a.reshape(self.nz, 2, 2, self.rows, self.cols), "r")
        own, kind = grid(self.own)
        return [(pltpu.with_memory_space_constraint(own, pltpu.HBM), kind), grid(self.got)]

    def along_x(self, array):
        return lax.ppermute(array, "dp", [(d, d ^ 1) for d in range(self.n_dp)])

    def along_y(self, array):
        return lax.ppermute(array, "grp", [(g, g ^ 2) for g in range(self.n_grp)])

    def run(self, kernel, step, ins, outs, scratch):
        body = functools.partial(kernel, self.n_dp, self.halves)
        return call(body, self.name + step, ins, outs, scratch, 24, 0, 0)

    def first(self):
        sizes = [(self.nz, 2, n, self.cols) for n in self.halves.sizes()]
        bufs = [pltpu.VMEM(size, BF16) for size in sizes for _ in range(2)]
        outs = [(size, BF16, "h") for size in sizes]
        sent = self.run(first_kernel, "_first", self.both(), outs, bufs + [pltpu.SemaphoreType.DMA((4,))])
        self.back1 = self.along_x(sent[0]), self.along_y(sent[1])
        return tuple(sent)

    def second_bufs(self):
        return [pltpu.VMEM((self.nz, n, self.cols), BF16) for n in self.halves.sizes() for _ in range(3)] + [
            pltpu.SemaphoreType.DMA((6,))
        ]

    def second(self):
        outs = [((self.nz, n, self.cols), BF16, "h") for n in self.halves.sizes()]
        ins = self.both() + [(a, "r") for a in self.back1]
        sent = self.run(second_kernel, "_second", ins, outs, self.second_bufs())
        self.back2 = self.along_y(sent[0]), self.along_x(sent[1])
        return tuple(sent)

    def cross(self):
        n_dp, n_grp = self.n_dp, self.n_grp
        piece = (self.nz, self.rows, self.cols)
        bufs = [pltpu.VMEM((3, *piece), BF16)] * 2 + [pltpu.SemaphoreType.DMA((6,))]
        sent = self.run(cross_kernel, "_cross", self.both(), [(piece, BF16, "h")] * 3, bufs)
        across = [(d * n_grp + g, (d ^ 1) * n_grp + (g ^ 2)) for d in range(n_dp) for g in range(n_grp)]
        self.back1 = ()
        self.back2 = lax.ppermute(sent[0], ("dp", "grp"), across), self.along_x(sent[1]), self.along_y(sent[2])
        return tuple(sent)

    def line(self, together=False):
        n_dp, nz = self.n_dp, self.nz
        piece, part = (nz, self.rows, self.cols), (self.rows, self.cols)
        outs = [(piece, BF16, "h")] if together else [(part, BF16, "h")] * (nz - 1) + [(part, F32, "v")]
        ins = self.both() + [(a, "r") for a in self.back1] + [(a, "v") for a in self.back2]
        if self.back1:
            kernel, bufs = line_kernel, self.second_bufs()
        else:
            kernel, bufs = cross_line_kernel, [pltpu.VMEM(piece, BF16)] * 2 + [pltpu.SemaphoreType.DMA((2,))]
        *sent, total = self.run(kernel, "_line", ins, outs, [pltpu.VMEM(piece, F32)] + bufs)
        if together:
            groups = [[2 * z + x for z in range(nz)] for x in range(2)]
            self.parts = [lax.all_to_all(total, "dp", 0, 0, tiled=True, axis_index_groups=groups)]
            return (total,)
        self.parts = [total] + [
            lax.ppermute(one, "dp", [(d, (d + 2 * k) % n_dp) for d in range(n_dp)]) for k, one in enumerate(sent, 1)
        ]
        return tuple(sent)


def weight_rows(weights, start):
    aligned = (start // 16) * 16
    return start - aligned, [w.at[pl.ds(pl.multiple_of(aligned, 16), 32)] for w in weights]


def finish_kernel(n_parts, places, gain_row, scale, io, *refs):
    total, gains_ref, rest = refs[:n_parts], refs[n_parts], refs[n_parts + 1:]
    n_out, n_weights = len(places), len(gain_row[1])
    weights, rest = rest[:n_weights], rest[n_weights:]
    outs, rest = rest[:n_out], rest[n_out:]
    gain_ref, rest = rest[0], rest[1:]
    extra, rest = (rest[:2], rest[2:]) if scale else ((), rest)
    sum_s, wide_s, bufs, sems = rest[0], rest[1], rest[2:-1], rest[-1]
    device = lax.axis_index("dp") * lax.axis_size("grp") + lax.axis_index("grp")
    per = outs[gain_row[1][0]].shape[0]
    start = device.astype(jnp.int32) * per
    shift, sources = weight_rows(weights, start)
    copies = slices(sems, list(zip(sources, bufs)))
    io.need(*total)
    if len(total) == 1:
        value = total[0][0].astype(F32)
        for i in range(1, total[0].shape[0]):
            value = value + total[0][i].astype(F32)
    else:
        value = total[0][...].astype(F32)
        for one in total[1:]:
            value = value + one[...].astype(F32)
    sum_s[...] = value
    for out, at in zip(outs, places):
        rows, width = out.shape
        for i in range(-(-width // 256)):
            cols = min(256, width - i * 256)
            out[:, i * 256:i * 256 + cols] = sum_s[at + i * rows:at + (i + 1) * rows, 0:cols]
    inner = jnp.zeros((per, 1), F32)
    for which, copy, buf in zip(gain_row[1], copies, bufs):
        copy.wait()
        width = buf.shape[1]
        wide_s[:, 0:width] = buf[...].astype(F32)
        mine = wide_s[pl.ds(pl.multiple_of(shift, 8), per), 0:width]
        inner = inner + jnp.sum(mine * outs[which][...], axis=-1, keepdims=True)
    lane = lax.broadcasted_iota(jnp.int32, (per, gains_ref.shape[1]), 1)
    row = lax.broadcasted_iota(jnp.int32, (per, gains_ref.shape[1]), 0)
    gain = jnp.sum(jnp.where(lane == row + start, gains_ref[gain_row[0]:gain_row[0] + 1, :], 0.0), axis=-1, keepdims=True)
    lane, row = lane[:, 0:LANE], row[:, 0:LANE]
    gain_ref[...] = jnp.sum(jnp.where(lane == row, inner / gain, 0.0), axis=0, keepdims=True)[:, 0:per]
    if scale:
        table_ref, loss_ref = extra
        heads, buckets = table_ref.shape
        spare = sum_s[sum_s.shape[0] - 8:, :]
        table = jnp.concatenate([spare[:, 0:buckets], spare[:, buckets:2 * buckets]], axis=0)
        table_ref[...] = table[0:heads]
        loss_ref[...] = spare[0:1, LANE:LANE + 1] * scale


def finish(batch, places, shapes, gain_row, gains, weights, table=None, scale=0.0):
    per = shapes[gain_row[1][0]][0]
    outs = [(shape, F32, "h") for shape in shapes] + [((1, per), F32, "v")]
    if table is not None:
        outs += [(table, F32, "v"), ((1, 1), F32, "v")]
    width = max(w.shape[1] for w in weights)
    return call(
        functools.partial(finish_kernel, len(batch.parts), places, gain_row, scale),
        batch.name + "_finish",
        [(one, "v") for one in batch.parts] + [(gains, "v")] + [(pltpu.with_memory_space_constraint(w, pltpu.HBM), "r") for w in weights],
        outs,
        [pltpu.VMEM((batch.rows, batch.cols), F32), pltpu.VMEM((32, width), F32)]
        + [pltpu.VMEM((32, w.shape[1]), BF16) for w in weights]
        + [pltpu.SemaphoreType.DMA((len(weights),))],
        16,
        0,
        0,
    )


def on_device(
    n_dp, n_grp, doc_tokens, doc_lengths, query_tokens, query_lengths, candidates, labels, gain_attn, w_query, w_key,
    w_value, w_out, bias_table, gain_ffn, w_gate, w_up, w_down, gain_final, w_proj,
):
    doc_rows, doc_len, width = doc_tokens.shape
    query_rows, query_len = query_tokens.shape[:2]
    hidden = w_gate.shape[1]
    bucket_total, heads = bias_table.shape
    devices = n_dp * n_grp
    axes = ("dp", "grp")
    x_doc = doc_tokens.reshape(doc_len, width)
    x_qry = query_tokens.reshape(query_rows * query_len, width)
    which = lax.broadcasted_iota(jnp.int32, (24, width), 0)
    gains = jnp.where(which == 0, gain_attn[None], jnp.where(which == 1, gain_ffn[None], gain_final[None]))
    table = jnp.pad(bias_table.T, ((8, 16 - heads), (0, width - bucket_total)))
    gains = jnp.where(which < 8, gains, table).astype(F32)
    weights = (w_query, w_key, w_value, w_out, w_gate, w_up, w_down, w_proj)
    hot = jnp.asarray(strip_onehot(), BF16)
    (q_q, q_k, q_v, q_e, q_il, q_mixt, q_mid, q_n1, q_n2, q_hid, q_a, q_b, q_out, q_n3, q_proj, packed, base) = forward(
        x_qry, query_lengths[None], gains, (hot, candidates, labels[None]), weights, False, heads, n_dp
    )
    got = lax.all_to_all(packed, "dp", 0, 0, tiled=True)
    (d_q, d_k, d_v, d_e, d_il, d_mixt, d_mid, d_n1, d_n2, d_hid, d_a, d_b, d_out, d_n3, d_proj, emb) = forward(
        x_doc, doc_lengths, gains, base, weights, True, heads
    )
    sums, lse = scores(got, emb, query_len)
    sums = lax.all_to_all(sums, "dp", 0, 0, tiled=True)
    demb_doc, demb_part, loss_group = retrieval_back(
        got, sums, emb, lse, query_len
    )
    demb_qry = lax.all_to_all(demb_part, "dp", 0, 0, tiled=True)
    back = (w_proj, w_down, w_gate, w_up, w_out)
    d_dpj, d_dbr, d_dg, d_du, d_datt, d_dmid, d_dmix = chain(
        demb_doc, d_proj, d_out, d_mid, d_a, d_b, gains, *back, "doc_ff_back"
    )
    q_chain = (demb_qry, q_proj, q_out, q_mid, q_a, q_b, gains, *back)
    d_attention = lambda il: (d_q, d_k, d_v, d_e, il, d_mixt, d_dmix)
    q_attention = lambda il, dmix: (q_q, q_k, q_v, q_e, il, q_mixt, dmix)
    qkv_weights = (w_query, w_key, w_value)
    fast = (n_dp, n_grp) == (8, 4)
    if fast:
        pairs = devices // 2
        q_dg, q_du, q_dmid, q_dmix, own, send = down_grads(
            (q_chain, (q_hid, q_mixt, q_n3)), (d_hid, d_dbr, d_mixt, d_datt, d_n3, d_dpj), pairs
        )
        down = Batch(own, send, n_dp, n_grp, "down")
        begun = gate_grads(0, d_n2, q_n2, d_dg, q_dg, pairs)
        down.got = after(down.got, begun)
        q_du = after(q_du, down.cross())
        own, send = gate_grads(1, d_n2, q_n2, d_du, q_du, pairs, begun)
        gate = Batch(own, send, n_dp, n_grp, "gate")
        d_il = after(d_il, send)
        d_dqkv, d_diag, d_far = attention_back(*d_attention(d_il), "doc_attention_back")
        gate.got = after(gate.got, d_diag)
        q_il = after(q_il, gate.cross())
        q_dqkv, q_diag, q_far, own, send = qkv_grads(
            q_attention(q_il, q_dmix), d_n1, q_n1, d_dqkv, d_diag, d_far, hot, loss_group, pairs
        )
        qkv = Batch(own, send, n_dp, n_grp, "qkv")
        (doc_grad,) = input_back(after(gains, send), ((d_dqkv, x_doc, d_dmid),), qkv_weights, "doc_input_back")
        down.back2 = after(down.back2, doc_grad)
        qkv.got = after(qkv.got, down.line(True))
        last_gains = after(gains, qkv.cross())
    else:
        q_dpj, q_dbr, q_dg, q_du, q_datt, q_dmid, q_dmix = chain(*q_chain, "query_ff_back")
        d_dqkv, d_diag, d_far = attention_back(*d_attention(d_il), "doc_attention_back")
        q_dqkv, q_diag, q_far = attention_back(*q_attention(q_il, q_dmix), "query_attention_back")
        last_gains = gains
        (doc_grad,) = input_back(gains, ((d_dqkv, x_doc, d_dmid),), qkv_weights, "doc_input_back")
    (query_grad,) = input_back(last_gains, ((q_dqkv, x_qry, q_dmid),), qkv_weights, "query_input_back")

    query_total = query_rows * devices
    per, per_down = width // devices, hidden // devices
    if fast:
        gate.back2 = after(gate.back2, query_grad)
        qkv.back2 = after(qkv.back2, gate.line())
        sent = qkv.line()
        down.parts, gate.parts = after((down.parts, gate.parts), sent)
        at = (width // 256) * per_down
        shard_down, shard_out, shard_proj, gain3 = finish(
            down, (0, at, at + 3 * per), ((per_down, width), (per, width), (per, w_proj.shape[1])), (2, (2,)), gains, [w_proj]
        )
        shard_gate, shard_up, gain2 = finish(
            gate, (0, (hidden // 256) * per), ((per, hidden),) * 2, (1, (0, 1)), gains, [w_gate, w_up]
        )
        shard_query, shard_key, shard_value, gain1, table_grad, loss = finish(
            qkv, (0, 3 * per, 6 * per), ((per, width),) * 3, (0, (0, 1, 2)), gains, qkv_weights, (heads, bucket_total), 1.0 / query_total
        )
        shard_gains = [g.reshape(per) for g in (gain1, gain2, gain3)]
        table_grad, loss = table_grad.T, loss.reshape(())
    else:

        def grad(left, right):
            product = tn(jnp.concatenate(left), jnp.concatenate(right))
            return lax.psum_scatter(product, axes, scatter_dimension=0, tiled=True)

        n1s = (d_n1, q_n1)
        shard_query, shard_key, shard_value = (
            grad(n1s, (d_dqkv[:, i * width:(i + 1) * width], q_dqkv[:, i * width:(i + 1) * width])) for i in range(3)
        )
        shard_out = grad((d_mixt.T, q_mixt.T), (d_datt, q_datt))
        shard_gate = grad((d_n2, q_n2), (d_dg, q_dg))
        shard_up = grad((d_n2, q_n2), (d_du, q_du))
        shard_down = grad((d_hid, q_hid), (d_dbr, q_dbr))
        shard_proj = grad((d_n3, q_n3), (d_dpj, q_dpj))
        start = (lax.axis_index("dp") * n_grp + lax.axis_index("grp")) * per
        mine = lambda a: lax.dynamic_slice_in_dim(a.astype(F32), start, per, 0)
        shard_gains = [
            sum(jnp.sum(mine(w) * g, axis=1) for w, g in pairs) / mine(gain)
            for gain, pairs in (
                (gain_attn, ((w_query, shard_query), (w_key, shard_key), (w_value, shard_value))),
                (gain_ffn, ((w_gate, shard_gate), (w_up, shard_up))),
                (gain_final, ((w_proj, shard_proj),)),
            )
        ]
        far = jnp.sum((d_far + q_far).reshape(heads, 2, -1), axis=-1)
        table = lax.dot_general(
            hot.astype(F32), (d_diag + q_diag).reshape(heads, -1), (((1,), (1,)), ((), ())),
            precision=highest, preferred_element_type=F32,
        )
        table = table.at[bucket_total // 2 - 1].add(far[:, 0]).at[bucket_total - 1].add(far[:, 1])
        table_grad, loss = lax.psum((table, loss_group[0, 0] / n_dp), axes)
        loss = loss / query_total
    return (
        loss,
        doc_grad.reshape(doc_rows, doc_len, width),
        query_grad.reshape(query_rows, query_len, width),
        shard_gains[0],
        shard_query,
        shard_key,
        shard_value,
        shard_out,
        table_grad,
        shard_gains[1],
        shard_gate,
        shard_up,
        shard_down,
        shard_gains[2],
        shard_proj,
    )


def solution(mesh):
    both = ("dp", "grp")
    rows3, rows2, rows1 = P(both, None, None), P(both, None), P(both)
    in_specs = (rows3, rows2, rows3, rows1, rows2, rows1) + (P(),) * 12
    out_specs = (
        P(), rows3, rows3, rows1, rows2, rows2, rows2, rows2, P(), rows1, rows2, rows2, rows2, rows1, rows2,
    )
    body = functools.partial(on_device, mesh.shape["dp"], mesh.shape["grp"])
    return jax.shard_map(body, mesh=mesh, in_specs=in_specs, out_specs=out_specs, check_vma=False)
```

```python
import functools
import itertools
import math

import jax
import jax.numpy as jnp
import numpy as np
from jax import lax
from jax.experimental import pallas as pl
from jax.experimental.pallas import tpu as pltpu
from jax.sharding import PartitionSpec as P

F32, BF16 = jnp.float32, jnp.bfloat16
BUCKETS = 32
DIST = 128
BLK = 128
MOST_DOC = 256
ROW_FILL = 480
EPS = 1e-6
SHARP = 0.25
SCALE = 16.0
NEG = -1e30
GELU_A = math.sqrt(2.0 / math.pi)
GELU_B = 0.044715
SPAN = 512
CH = 1024
LANE = 128
COST = 20
AHEAD = 1 << 30
PACK_INT = 48
highest = lax.Precision.HIGHEST


def nn(a, b):
    return jnp.dot(a, b, preferred_element_type=F32)


def nt(a, b):
    return lax.dot_general(a, b, (((1,), (1,)), ((), ())), preferred_element_type=F32)


def tn(a, b):
    return lax.dot_general(a, b, (((0,), (0,)), ((), ())), preferred_element_type=F32)


def bucket_of(offsets):
    half = BUCKETS // 2
    exact = half // 2
    dist = np.abs(offsets)
    scaled = np.log(np.maximum(dist, 1) / exact) / np.log(DIST / exact) * (half - exact)
    far = np.minimum(exact + np.maximum(scaled, 0).astype(np.int64), half - 1)
    return (offsets > 0) * half + np.where(dist < exact, dist, far)


def strip_onehot():
    j = np.arange(SPAN)
    offset = np.where(j < 384, 128 - j, 640 - j)
    index = np.stack([bucket_of(offset[(j - r) % SPAN]) for r in range(8)]).reshape(-1)
    return (index[None, :] == np.arange(BUCKETS)[:, None]).astype(np.float32)


VM = pl.BlockSpec(memory_space=pltpu.VMEM)
HB = pl.BlockSpec(memory_space=pl.ANY)


def by_part(run):
    return run if run[0][3] == 1 else sorted(run, key=lambda entry: entry[1])


class Io:
    def __init__(self, ins, outs, sems):
        self.ins, self.outs, self.sems, self.used = {}, {}, sems, 0
        self.going, self.queue, self.flying = [], [], 0
        for src, buf, parts in ins:
            self.ins[id(buf)] = (src, buf, parts, self.used)
            size = math.prod(buf.shape) * buf.dtype.itemsize // abs(parts)
            self.queue += [(id(buf), p, size, abs(parts)) for p in range(abs(parts))]
            self.used += abs(parts)
        for buf, dst in outs:
            self.outs[id(buf)] = (buf, dst)
        self.queue = [entry for _, run in itertools.groupby(self.queue, lambda e: e[3]) for entry in by_part(list(run))]
        self.feed()

    def feed(self, upto=()):
        upto = {id(buf) for buf in upto}
        while self.queue and (self.flying < AHEAD or any(entry[0] in upto for entry in self.queue)):
            key, p, size, _ = self.queue.pop(0)
            self.chunk(*self.ins[key], p).start()
            self.flying += size

    def landed(self, buf):
        self.flying -= math.prod(buf.shape) * buf.dtype.itemsize
        self.feed()

    def chunk(self, src, buf, parts, first, p):
        if parts == 1:
            return pltpu.make_async_copy(src, buf, self.sems.at[first])
        if parts > 0:
            size = buf.shape[0] // parts
            cut = (pl.ds(p * size if isinstance(p, int) else pl.multiple_of(p * size, 2), size),)
        else:
            size = buf.shape[1] // -parts
            cut = (slice(None), pl.ds(p * size if isinstance(p, int) else pl.multiple_of(p * size, LANE), size))
        return pltpu.make_async_copy(src.at[cut], buf.at[cut], self.sems.at[first + p])

    def need(self, *bufs):
        for buf in bufs:
            entry = self.ins.get(id(buf))
            if entry is not None:
                self.feed((buf,))
                for p in range(abs(entry[2])):
                    self.chunk(*entry, p).wait()
                del self.ins[id(buf)]
                self.landed(buf)

    def need_part(self, p, *bufs):
        for buf in bufs:
            if id(buf) in self.ins:
                self.chunk(*self.ins[id(buf)], p).wait()

    def had(self, *bufs):
        for buf in bufs:
            if self.ins.pop(id(buf), None) is not None:
                self.landed(buf)

    def done(self, *bufs):
        for buf in bufs:
            if id(buf) in self.outs:
                src, dst = self.outs.pop(id(buf))
                self.push(src, dst)

    def done_rows(self, buf, start, size):
        src, dst = self.outs[id(buf)]
        rows = (slice(None), pl.ds(start, size))
        self.push(src.at[rows], dst.at[rows])

    def gone(self, buf):
        self.outs.pop(id(buf))

    def push(self, src, dst):
        copy = pltpu.make_async_copy(src, dst, self.sems.at[self.used])
        self.used += 1
        copy.start()
        self.going.append(copy)

    def close(self):
        self.need(*[entry[1] for entry in list(self.ins.values())])
        self.done(*[entry[0] for entry in list(self.outs.values())])
        for copy in self.going:
            copy.wait()


def call(kernel, name, ins, outs, scratch, mib, flops, moved=8 << 20, aliases=None):
    args, in_specs, out_specs, out_shape, buffers, sems = [], [], [], [], [], 0
    for array, kind in ins:
        if kind in ("r", "b"):
            args.append(array if kind == "r" else pltpu.with_memory_space_constraint(array, pltpu.HBM))
            in_specs.append(HB)
        elif kind[0] == "h":
            args.append(pltpu.with_memory_space_constraint(array, pltpu.HBM))
            in_specs.append(HB)
            buffers.append(pltpu.VMEM(array.shape, array.dtype))
            sems += abs(int(kind[1:] or 1))
        else:
            args.append(array)
            in_specs.append(VM)
    for shape, dtype, kind in outs:
        if kind == "a":
            out_shape.append(pltpu.HBM(shape, dtype))
            out_specs.append(HB)
            sems += 8
        elif kind == "h":
            out_shape.append(pltpu.HBM(shape, dtype))
            out_specs.append(HB)
            buffers.append(pltpu.VMEM(shape, dtype))
            sems += 4
        else:
            out_shape.append(jax.ShapeDtypeStruct(shape, dtype))
            out_specs.append(VM)

    def body(*refs):
        n_in, n_out, n_buf = len(ins), len(outs), len(buffers)
        given, made = list(refs[:n_in]), list(refs[n_in:n_in + n_out])
        bufs = iter(refs[n_in + n_out:n_in + n_out + n_buf])
        rest = refs[n_in + n_out + n_buf:]
        reads, writes = [], []
        for i, (_, kind) in enumerate(ins):
            if kind[0] == "h":
                buf = next(bufs)
                reads.append((given[i], buf, int(kind[1:] or 1)))
                given[i] = buf
        for i, (_, _, kind) in enumerate(outs):
            if kind == "h":
                buf = next(bufs)
                writes.append((buf, made[i]))
                made[i] = buf
        io = Io(reads, writes, rest[-1])
        kernel(io, *given, *made, *rest[:-1])
        io.close()

    return pl.pallas_call(
        body,
        name=name,
        out_shape=out_shape,
        in_specs=in_specs,
        out_specs=out_specs,
        scratch_shapes=buffers + scratch + [pltpu.SemaphoreType.DMA((max(sems, 1),))],
        compiler_params=pltpu.CompilerParams(vmem_limit_bytes=mib << 20),
        input_output_aliases=aliases or {},
        cost_estimate=pl.CostEstimate(flops=int(flops) * COST, bytes_accessed=int(moved) * COST, transcendentals=0),
    )(*args)


def reachable(d, tile):
    return (abs(d) - 1) * tile + 1 < MOST_DOC


def half_lanes(values, side):
    lane = lax.broadcasted_iota(jnp.int32, (1, LANE), 1)
    return jnp.where((lane // 64) == side, values.astype(F32), 0.0).astype(BF16)


def norm_back(values, gain, dn):
    s = lax.rsqrt(jnp.mean(values * values, axis=-1, keepdims=True) + EPS)
    unit = values * s
    t = dn * gain
    return s * (t - unit * jnp.mean(t * unit, axis=-1, keepdims=True))


def forward_kernel(
    is_doc, io, x_ref, lens_ref, gains_ref, extra_ref, wq_s, wk_s, wv_s, wo_s, wg_s, wu_s, wd_s, wp_s,
    q_ref, k_ref, v_ref, e_ref, il_ref, mixt_ref, mid_ref, n1_ref, n2_ref, hid_ref, a_ref, b_ref,
    out_ref, n3_ref, proj_ref, emb_ref, *rest,
):
    if is_doc:
        base_ref, tail = extra_ref, rest
    else:
        hot_ref, cand_ref, label_ref = extra_ref
        base_ref, tail = rest[0], rest[1:]
    mask_s, strip_s, s_s, e_s, vt_s, mid_s = tail
    tokens, width = x_ref.shape
    hidden = wg_s.shape[1]
    heads = e_ref.shape[0]
    io.need(lens_ref)
    if not is_doc:
        io.need(hot_ref)
        tab = gains_ref[8:24, 0:hot_ref.shape[0]].astype(BF16)
        for r in range(8):
            rows = nn(tab, hot_ref[:, r * SPAN:(r + 1) * SPAN])
            for h in range(heads):
                base_ref[h, r:r + 1, :] = rows[h:h + 1, :]
    io.need(x_ref)
    x = x_ref[...].astype(F32)
    s1 = lax.rsqrt(jnp.mean(x * x, axis=-1, keepdims=True) + EPS)
    n1_ref[...] = (x * s1 * gains_ref[0:1, :]).astype(BF16)
    io.done(n1_ref)
    tile = min(tokens, 128)
    blocks = tokens // tile
    row_id = lax.broadcasted_iota(jnp.int32, (tokens, 1), 0)
    col_id = lax.broadcasted_iota(jnp.int32, (1, tokens), 1)
    if is_doc:
        seg_k = jnp.zeros((tokens, 1), jnp.int32)
        seg_q = jnp.zeros((1, tokens), jnp.int32)
        end = jnp.zeros((1, 1), jnp.int32)
        for i in range(lens_ref.shape[1]):
            end = end + lens_ref[0:1, i:i + 1]
            seg_k = seg_k + (row_id >= end).astype(jnp.int32)
            seg_q = seg_q + (col_id >= end).astype(jnp.int32)
    else:
        count = lens_ref.shape[1]
        length = tokens // count
        seg_q = col_id // length
        seg_k = jnp.full((tokens, 1), -1, jnp.int32)
        for i in range(count):
            inside = (row_id >= i * length) & (row_id < i * length + lens_ref[0:1, i:i + 1])
            seg_k = jnp.where(inside, i, seg_k)
    mask_s[...] = jnp.where(seg_k == seg_q, 0.0, NEG)
    for i, (w, o) in enumerate(((wq_s, q_ref), (wk_s, k_ref), (wv_s, v_ref))):
        io.need(w)
        o[...] = nn(n1_ref[...], w[...]).astype(BF16)
        io.done(o)
    vt_s[...] = v_ref[...].T
    if is_doc:
        io.need(base_ref)
    else:
        io.done(base_ref)

    def softmax_pair(p, slot):
        col = pl.ds(pl.multiple_of(p * LANE, LANE), LANE)
        for s in range(2):
            h = 2 * p + s
            first = base_ref[h]
            for g in range(tile // 8):
                strip_s[s, 8 * g:8 * g + 8, :] = pltpu.roll(first, 8 * g, 1) if g else first
            low_far, high_far = first[0:1, 256:256 + tile], first[0:1, 384:384 + tile]
            scores = nt(half_lanes(k_ref[:, col], s), q_ref[:, col])
            for qb in range(blocks):
                cols = slice(qb * tile, (qb + 1) * tile)
                tops = []
                near = [kb for kb in range(blocks) if reachable(kb - qb, tile)]
                for kb in near:
                    ks = slice(kb * tile, (kb + 1) * tile)
                    d = kb - qb
                    t = scores[ks, cols]
                    if abs(d) <= 1:
                        lo = (1 - d) * 128
                        t = t + strip_s[s, :, lo:lo + tile]
                    else:
                        t = t + (high_far if d > 0 else low_far)
                    t = t + mask_s[ks, cols]
                    s_s[s, ks, cols] = t
                    tops.append(jnp.max(t, axis=0, keepdims=True))
                top = functools.reduce(jnp.maximum, tops)
                total = None
                for kb in near:
                    ks = slice(kb * tile, (kb + 1) * tile)
                    e = jnp.exp(s_s[s, ks, cols] - top)
                    part = jnp.sum(e, axis=0, keepdims=True)
                    total = part if total is None else total + part
                    kept = e.astype(BF16)
                    e_ref[h, ks, cols] = kept
                    e_s[slot, s, ks, cols] = kept
                il_ref[h, :, cols] = 1.0 / total

    def mix_pair(p, slot):
        for s in range(2):
            rows = pl.ds(pl.multiple_of(p * LANE + 64 * s, 64), 64)
            mixt_ref[rows, :] = (nn(vt_s[rows, :], e_s[slot, s]) * il_ref[2 * p + s]).astype(BF16)

    def pair_step(i, carry):
        mix_pair(2 * i, 0)
        softmax_pair(2 * i + 1, 1)
        mix_pair(2 * i + 1, 1)
        softmax_pair(2 * i + 2, 0)
        return carry

    pairs = width // LANE
    for kb, qb in itertools.product(range(blocks), repeat=2):
        if not reachable(kb - qb, tile):
            far = (slice(kb * tile, (kb + 1) * tile), slice(qb * tile, (qb + 1) * tile))
            e_s[(slice(None), slice(None), *far)] = jnp.zeros((2, 2, tile, tile), BF16)
            e_ref[(slice(None), *far)] = jnp.zeros((heads, tile, tile), BF16)
    softmax_pair(0, 0)
    lax.fori_loop(0, pairs // 2 - 1, pair_step, 0)
    mix_pair(pairs - 2, 0)
    softmax_pair(pairs - 1, 1)
    mix_pair(pairs - 1, 1)
    io.done(e_ref, mixt_ref)
    io.need(wo_s)
    mid_s[...] = x_ref[...].astype(F32) + nn(mixt_ref[...].T, wo_s[...])
    mid = mid_s[...]
    mid_ref[...] = mid.astype(BF16)
    s2 = lax.rsqrt(jnp.mean(mid * mid, axis=-1, keepdims=True) + EPS)
    n2_ref[...] = (mid * s2 * gains_ref[1:2, :]).astype(BF16)
    io.done(mid_ref, n2_ref)

    io.feed((wg_s, wu_s))

    def ff_body(j, carry):
        io.need_part(j, wg_s, wu_s)
        col = pl.ds(pl.multiple_of(j * CH, CH), CH)
        g = nn(n2_ref[...], wg_s[:, col])
        u = nn(n2_ref[...], wu_s[:, col])
        sq = g * g
        t = jnp.tanh(GELU_A * g * (1.0 + GELU_B * sq))
        half = 0.5 + 0.5 * t
        gel = g * half
        slope = half + (0.5 * GELU_A) * g * (1.0 - t * t) * (1.0 + 3.0 * GELU_B * sq)
        hid_ref[:, col] = (gel * u).astype(BF16)
        a_ref[:, col] = (u * slope).astype(BF16)
        b_ref[:, col] = gel.astype(BF16)
        return carry

    lax.fori_loop(0, hidden // CH, ff_body, 0)
    io.had(wg_s, wu_s)
    io.done(hid_ref, a_ref, b_ref)
    io.need(wd_s)
    mid_s[...] += nn(hid_ref[...], wd_s[...])
    o = mid_s[...]
    out_ref[...] = o.astype(BF16)
    s3 = lax.rsqrt(jnp.mean(o * o, axis=-1, keepdims=True) + EPS)
    n3_ref[...] = (o * s3 * gains_ref[2:3, :]).astype(BF16)
    io.done(out_ref, n3_ref)
    io.need(wp_s)
    pr = nn(n3_ref[...], wp_s[...])
    proj_ref[...] = pr
    emb = (pr * lax.rsqrt(jnp.sum(pr * pr, axis=-1, keepdims=True) + EPS)).astype(BF16)
    if is_doc:
        emb_ref[...] = emb
    else:
        io.need(cand_ref, label_ref)
        ints = pack_ints(cand_ref, label_ref, lens_ref)
        for i in range(emb_ref.shape[0]):
            emb_ref[i, 0:tokens, :] = emb
            emb_ref[i, tokens:, :] = ints


def pack_ints(cand_ref, label_ref, lens_ref):
    count = cand_ref.shape[1]
    eye = lax.broadcasted_iota(jnp.int32, (count, count), 0) == lax.broadcasted_iota(jnp.int32, (count, count), 1)
    lane = lax.broadcasted_iota(jnp.int32, (1, LANE), 1)
    row = lax.broadcasted_iota(jnp.int32, (PACK_INT, 1), 0)
    packed = jnp.zeros((PACK_INT, LANE), F32)
    for a in range(cand_ref.shape[0]):
        values = jnp.where(eye, cand_ref[a:a + 1, :].astype(F32), 0.0)
        column = jnp.sum(values, axis=1, keepdims=True)
        column = jnp.concatenate([column, jnp.zeros((PACK_INT - count, 1), F32)], axis=0)
        column = jnp.where(row == count, label_ref[0:1, a:a + 1].astype(F32), column)
        column = jnp.where(row == count + 1, lens_ref[0:1, a:a + 1].astype(F32), column)
        packed = jnp.where(lane == a, column, packed)
    return packed.astype(BF16)


def forward(x, lens, gains, extra, weights, is_doc, heads, copies=1):
    tokens, width = x.shape
    hidden = weights[4].shape[1]
    proj = weights[7].shape[1]
    outs = [((tokens, width), BF16, "h")] * 3 + [
        ((heads, tokens, tokens), BF16, "h"),
        ((heads, 1, tokens), F32, "v"),
        ((width, tokens), BF16, "h"),
        ((tokens, width), BF16, "h"),
        ((tokens, width), BF16, "h"),
        ((tokens, width), BF16, "h"),
        ((tokens, hidden), BF16, "h"),
        ((tokens, hidden), BF16, "h"),
        ((tokens, hidden), BF16, "h"),
        ((tokens, width), BF16, "h"),
        ((tokens, width), BF16, "h"),
        ((tokens, proj), F32, "h"),
        ((tokens, proj) if is_doc else (copies, tokens + PACK_INT, proj), BF16, "v"),
    ]
    tile = min(tokens, 128)
    scratch = [
        pltpu.VMEM((tokens, tokens), F32),
        pltpu.VMEM((2, tile, SPAN), F32),
        pltpu.VMEM((2, tokens, tokens), F32),
        pltpu.VMEM((2, 2, tokens, tokens), BF16),
        pltpu.VMEM((width, tokens), BF16),
        pltpu.VMEM((tokens, width), F32),
    ]
    steps = weights[4].shape[1] // CH
    streams = [(w, f"h-{steps}" if w.shape == weights[4].shape else "h") for w in weights]
    ins = [(x, "h"), (lens, "h"), (gains, "v")]
    if is_doc:
        kernel = functools.partial(forward_kernel, True)
        ins = ins + [(extra, "h")] + streams
    else:
        outs.append(((heads, 8, SPAN), F32, "h"))

        def kernel(io, x_ref, lens_ref, gains_ref, hot_ref, cand_ref, label_ref, *rest):
            forward_kernel(False, io, x_ref, lens_ref, gains_ref, (hot_ref, cand_ref, label_ref), *rest)

        ins = ins + [(item, "h") for item in extra] + streams
    flops = 2 * tokens * (4 * width * width + 3 * width * hidden + width * proj) + 4 * tokens * tokens * width
    return call(kernel, "doc_forward" if is_doc else "query_forward", ins, outs, scratch, 50, flops, 30 << 20)


def unpack(got_ref, tokens):
    parts = got_ref.shape[0]
    own = 2
    lane = lax.broadcasted_iota(jnp.int32, (1, LANE), 1)
    ints = None
    for i in range(parts):
        block = got_ref[i, tokens:, :].astype(F32)
        if i:
            block = pltpu.roll(block, own * i, 1)
        block = jnp.where((lane // own) == i, block, 0.0)
        ints = block if ints is None else ints + block
    return ints[0:32, :], ints[32:33, :], ints[33:34, :]


def expand_onehot(queries, length):
    col = lax.broadcasted_iota(jnp.int32, (LANE, queries * length), 1)
    row = lax.broadcasted_iota(jnp.int32, (LANE, queries * length), 0)
    return ((col // length) == row).astype(F32)


def token_valid(lens, queries, length):
    hot = expand_onehot(queries, length)
    spread = nn(jnp.broadcast_to(lens, (8, LANE)).astype(BF16), hot.astype(BF16))[0:1]
    place = lax.broadcasted_iota(jnp.int32, (1, queries * length), 1) % length
    return place.astype(F32) < spread, hot


def block_scores(emb_ref, q_s, b):
    t = nt(emb_ref[b * BLK:(b + 1) * BLK, :], q_s[...]) * (1.0 / SHARP)
    row = lax.broadcasted_iota(jnp.int32, (BLK, 1), 0) + b * BLK
    return jnp.where(row < ROW_FILL, t, NEG) if (b + 1) * BLK > ROW_FILL else t


def score_kernel(length, io, got_ref, emb_ref, sums_ref, lse_ref, q_s):
    parts = got_ref.shape[0]
    tokens = q_s.shape[0] // parts
    queries = q_s.shape[0] // length
    for i in range(parts):
        q_s[i * tokens:(i + 1) * tokens, :] = got_ref[i, 0:tokens, :]
    _, _, lens = unpack(got_ref, tokens)
    valid, hot = token_valid(lens, queries, length)
    blocks = emb_ref.shape[0] // BLK
    rows = []
    for b in range(blocks):
        t = block_scores(emb_ref, q_s, b)
        top = jnp.max(t, axis=0, keepdims=True)
        lse = top + jnp.log(jnp.sum(jnp.exp(t - top), axis=0, keepdims=True))
        lse_ref[b:b + 1, :] = lse
        rows.append(jnp.where(valid, SHARP * lse, 0.0))
    rows.append(jnp.zeros((8 - blocks, rows[0].shape[1]), F32))
    sums = lax.dot_general(
        jnp.concatenate(rows, axis=0), hot, (((1,), (1,)), ((), ())), precision=highest, preferred_element_type=F32
    )
    for i in range(parts):
        sums_ref[i] = sums


def scores(got, emb, length):
    parts = got.shape[0]
    tokens = got.shape[1] - PACK_INT
    total = parts * tokens
    return call(
        functools.partial(score_kernel, length),
        "block_sums",
        [(got, "v"), (emb, "v")],
        [((parts, 8, LANE), F32, "v"), ((8, total), F32, "v")],
        [pltpu.VMEM((total, emb.shape[1]), BF16)],
        24,
        2 * emb.shape[0] * total * 128,
        1 << 20,
    )


def loss_kernel(length, io, got_ref, sums_ref, emb_ref, lse_ref, doc_ref, qry_ref, loss_ref, q_s, d_s, s_s):
    parts = got_ref.shape[0]
    tokens = q_s.shape[0] // parts
    queries = q_s.shape[0] // length
    for i in range(parts):
        q_s[i * tokens:(i + 1) * tokens, :] = got_ref[i, 0:tokens, :]
    cand, label, lens = unpack(got_ref, tokens)
    valid, hot = token_valid(lens, queries, length)
    blocks = emb_ref.shape[0] // BLK
    logits = jnp.zeros(cand.shape, F32)
    for i in range(parts):
        for b in range(blocks):
            logits = logits + jnp.where(cand == float(i * blocks + b), sums_ref[i, b:b + 1, :], 0.0)
    logits = SCALE * logits
    top = jnp.max(logits, axis=0, keepdims=True)
    lse = top + jnp.log(jnp.sum(jnp.exp(logits - top), axis=0, keepdims=True))
    choice = lax.broadcasted_iota(jnp.int32, cand.shape, 0).astype(F32) == label
    lane = lax.broadcasted_iota(jnp.int32, (1, LANE), 1)
    picked = jnp.sum(jnp.where(choice, logits, 0.0), axis=0, keepdims=True)
    each = jnp.where(lane < queries, lse - picked, 0.0)
    loss_ref[...] = jnp.broadcast_to(jnp.sum(each, axis=1, keepdims=True), (1, LANE))
    dlogits = SCALE * (jnp.exp(logits - lse) - jnp.where(choice, 1.0, 0.0))
    me = lax.axis_index("dp").astype(jnp.int32)
    rows = []
    for b in range(blocks):
        mine = (me * blocks + b).astype(F32)
        rows.append(jnp.sum(jnp.where(cand == mine, dlogits, 0.0), axis=0, keepdims=True))
    rows.append(jnp.zeros((8 - blocks, LANE), F32))
    spread = jnp.dot(jnp.concatenate(rows, axis=0), hot, precision=highest, preferred_element_type=F32)
    for b in range(blocks):
        t = block_scores(emb_ref, q_s, b)
        weight = jnp.where(valid, spread[b:b + 1, :], 0.0)
        d_s[b * BLK:(b + 1) * BLK, :] = (weight * jnp.exp(t - lse_ref[b:b + 1, :])).astype(BF16)
    doc_ref[...] = nn(d_s[...], q_s[...])
    s_s[...] = d_s[...].T
    qry_ref[...] = nn(s_s[...], emb_ref[...]).reshape(qry_ref.shape)


def retrieval_back(got, sums, emb, lse, length):
    parts = got.shape[0]
    tokens = got.shape[1] - PACK_INT
    total = parts * tokens
    docs, proj = emb.shape
    return call(
        functools.partial(loss_kernel, length),
        "retrieval_back",
        [(got, "v"), (sums, "v"), (emb, "v"), (lse, "v")],
        [((docs, proj), F32, "v"), ((parts, tokens, proj), F32, "v"), ((1, LANE), F32, "v")],
        [pltpu.VMEM((total, proj), BF16), pltpu.VMEM((docs, total), BF16), pltpu.VMEM((total, docs), BF16)],
        32,
        6 * docs * total * proj,
        2 << 20,
    )


def chain_kernel(
    io, demb_ref, gains_ref, proj_ref, wp_s, out_ref, wd_s, a_ref, b_ref, wg_s, wu_s, mid_ref, wo_s,
    dpj_ref, dbr_ref, dg_ref, du_ref, datt_ref, dmid_ref, dmix_ref, acc_s,
):
    hidden = a_ref.shape[1]
    if len(demb_ref.shape) == 3:
        dy = demb_ref[0]
        for i in range(1, demb_ref.shape[0]):
            dy = dy + demb_ref[i]
    else:
        dy = demb_ref[...]
    io.need(proj_ref)
    pr = proj_ref[...]
    r = lax.rsqrt(jnp.sum(pr * pr, axis=-1, keepdims=True) + EPS)
    unit = pr * r
    dpj_ref[...] = (r * (dy - unit * jnp.sum(dy * unit, axis=-1, keepdims=True))).astype(BF16)
    io.done(dpj_ref)
    io.need(wp_s, out_ref)
    dn3 = nt(dpj_ref[...], wp_s[...])
    dout = norm_back(out_ref[...].astype(F32), gains_ref[2:3, :], dn3)
    dmid_ref[...] = dout
    dbr_ref[...] = dout.astype(BF16)
    io.done(dbr_ref)

    io.feed((wd_s, a_ref, b_ref, wg_s, wu_s))

    def body(j, carry):
        io.need_part(j, wd_s, a_ref, b_ref)
        col = pl.ds(pl.multiple_of(j * CH, CH), CH)
        dh = nt(dbr_ref[...], wd_s[col, :])
        dg_ref[:, col] = (dh * a_ref[:, col].astype(F32)).astype(BF16)
        du_ref[:, col] = (dh * b_ref[:, col].astype(F32)).astype(BF16)
        return carry

    lax.fori_loop(0, hidden // CH, body, 0)
    io.had(wd_s, a_ref, b_ref)
    io.done(dg_ref, du_ref)
    io.need(wg_s, wu_s)
    acc_s[...] = nt(dg_ref[...], wg_s[...]) + nt(du_ref[...], wu_s[...])
    io.need(mid_ref)
    dmid = dmid_ref[...] + norm_back(mid_ref[...].astype(F32), gains_ref[1:2, :], acc_s[...])
    dmid_ref[...] = dmid
    datt_ref[...] = dmid.astype(BF16)
    io.done(dmid_ref, datt_ref)
    io.need(wo_s)
    dmix_ref[...] = nt(datt_ref[...], wo_s[...]).astype(BF16)


def chain_ins(demb, gains, proj, wp, out, wd, a, b, wg, wu, mid, wo):
    steps = a.shape[1] // CH
    plain = lambda *items: [(item, "h") for item in items]
    parts = [(wd, f"h{steps}")] + [(item, f"h-{steps}") for item in (a, b)]
    return [(demb, "v"), (gains, "v")] + plain(proj, wp, out) + parts + plain(wg, wu, mid, wo)


def chain(demb, proj, out, mid, a, b, gains, wp, wd, wg, wu, wo, name):
    tokens, width = out.shape
    hidden = a.shape[1]
    return call(
        chain_kernel,
        name,
        chain_ins(demb, gains, proj, wp, out, wd, a, b, wg, wu, mid, wo),
        [
            (proj.shape, BF16, "h"),
            ((tokens, width), BF16, "h"),
            ((tokens, hidden), BF16, "h"),
            ((tokens, hidden), BF16, "h"),
            ((tokens, width), BF16, "h"),
            ((tokens, width), F32, "h"),
            ((tokens, width), BF16, "h"),
        ],
        [pltpu.VMEM((tokens, width), F32)],
        44,
        2 * tokens * (width * width + 3 * width * hidden + width * 128),
        30 << 20,
    )


def attention_back_kernel(
    io, k_ref, v_ref, q_ref, dmix_ref, mixt_ref, il_ref, e_ref, dqkv_ref, diag_ref, far_ref,
    dqt_s, p_s, ds_s, strip_s, dk_s, dv_s,
):
    tokens, width = q_ref.shape
    tile = min(tokens, 128)
    wide = min(tokens, 256)
    blocks = tokens // tile
    io.feed((k_ref, v_ref, q_ref, dmix_ref, mixt_ref, e_ref))

    def pair_body(p, carry):
        io.need_part(p, k_ref, v_ref, q_ref, dmix_ref, mixt_ref, e_ref)
        col = pl.ds(pl.multiple_of(p * LANE, LANE), LANE)
        kt = k_ref[:, col].T
        dmixt = dmix_ref[:, col].T
        for s in range(2):
            h = 2 * p + s
            vp = half_lanes(v_ref[:, col], s)
            dm = half_lanes(dmix_ref[:, col], s)
            qm = half_lanes(q_ref[:, col], s)
            rows = pl.ds(pl.multiple_of(p * LANE + 64 * s, 64), 64)
            strip_s[...] = jnp.zeros_like(strip_s)
            far_low = jnp.zeros((8, LANE), F32)
            far_high = jnp.zeros((8, LANE), F32)
            for qc in range(tokens // wide):
                cols = slice(qc * wide, (qc + 1) * wide)
                dt = dmixt[:, cols]
                delta = jnp.sum(
                    dmixt[64 * s:64 * s + 64, cols].astype(F32) * mixt_ref[rows, cols].astype(F32), axis=0, keepdims=True
                )
                inverse = il_ref[h, :, cols]
                for kb in range(blocks):
                    ks = slice(kb * tile, (kb + 1) * tile)
                    dp = nn(vp[ks], dt)
                    prob = e_ref[h, ks, cols].astype(F32) * inverse
                    p_s[ks, :] = prob.astype(BF16)
                    ds = (prob * (dp - delta)).astype(BF16)
                    ds_s[ks, :] = ds
                    kept = ds.astype(F32)
                    for qs in range(wide // tile):
                        d = kb - (qc * (wide // tile) + qs)
                        t = kept[:, qs * tile:(qs + 1) * tile]
                        if abs(d) <= 1:
                            lo = (1 - d) * 128
                            strip_s[0:tile, lo:lo + tile] += t
                        else:
                            part = t[0:8]
                            for g in range(1, tile // 8):
                                part = part + t[8 * g:8 * g + 8]
                            if d > 0:
                                far_high = far_high + part
                            else:
                                far_low = far_low + part
                dv = nn(p_s[...], dm[cols])
                dk = nn(ds_s[...], qm[cols])
                if s == 0 and qc == 0:
                    dv_s[...] = dv
                    dk_s[...] = dk
                else:
                    dv_s[...] += dv
                    dk_s[...] += dk
                dqt_s[rows, cols] = nn(kt[64 * s:64 * s + 64], ds_s[...]).astype(BF16)
            fold = strip_s[...]
            size = strip_s.shape[0]
            while size > 8:
                size //= 2
                fold = fold[:size] + pltpu.roll(fold[size:], SPAN - size, 1)
            diag_ref[h] = fold
            far_ref[h, 0:8, :] = far_low
            far_ref[h, 8:16, :] = far_high
        kcol = pl.ds(pl.multiple_of(width + p * LANE, LANE), LANE)
        vcol = pl.ds(pl.multiple_of(2 * width + p * LANE, LANE), LANE)
        dqkv_ref[:, kcol] = dk_s[...].astype(BF16)
        dqkv_ref[:, vcol] = dv_s[...].astype(BF16)
        return carry

    lax.fori_loop(0, width // LANE, pair_body, 0)
    io.had(k_ref, v_ref, q_ref, dmix_ref, mixt_ref, e_ref)
    dqkv_ref[:, 0:width] = dqt_s[...].T


def attention_ins(q, k, v, e, il, mixt, dmix):
    pairs = q.shape[1] // LANE
    return [(item, "v") for item in (k, v, q, dmix, mixt, il, e)]


def attention_outs(q, heads):
    tokens, width = q.shape
    return [((tokens, 3 * width), BF16, "v"), ((heads, 8, SPAN), F32, "v"), ((heads, 16, LANE), F32, "v")]


def attention_scratch(q):
    tokens, width = q.shape
    tile, wide = min(tokens, 128), min(tokens, 256)
    return [
        pltpu.VMEM((width, tokens), BF16),
        pltpu.VMEM((tokens, wide), BF16),
        pltpu.VMEM((tokens, wide), BF16),
        pltpu.VMEM((tile, SPAN), F32),
        pltpu.VMEM((tokens, LANE), F32),
        pltpu.VMEM((tokens, LANE), F32),
    ]


def attention_back(q, k, v, e, il, mixt, dmix, name):
    tokens, width = q.shape
    return call(
        attention_back_kernel,
        name,
        attention_ins(q, k, v, e, il, mixt, dmix),
        attention_outs(q, e.shape[0]),
        attention_scratch(q),
        9,
        10 * tokens * tokens * width,
        16 << 20,
    )


def input_kernel(io, gains_ref, *refs):
    kinds = (len(refs) - 3) // 4
    reads, weights, writes = refs[:3 * kinds], refs[3 * kinds:3 * kinds + 3], refs[3 * kinds + 3:]
    for kind in range(kinds):
        dqkv_ref, x_ref, dmid_ref = reads[3 * kind:3 * kind + 3]
        width = x_ref.shape[1]
        io.need(dqkv_ref)
        total = None
        for i, w in enumerate(weights):
            io.need(w)
            part = nt(dqkv_ref[:, i * width:(i + 1) * width], w[...])
            total = part if total is None else total + part
        io.need(x_ref, dmid_ref)
        writes[kind][...] = dmid_ref[...] + norm_back(x_ref[...].astype(F32), gains_ref[0:1, :], total)
        io.done(writes[kind])


def input_back(gains, kinds, weights, name):
    width = weights[0].shape[0]
    tokens = sum(x.shape[0] for _, x, _ in kinds)
    return call(
        input_kernel,
        name,
        [(gains, "v")]
        + [(item, kind) for dqkv, x, dmid in kinds for item, kind in ((dqkv, "v"), (x, "h"), (dmid, "h"))]
        + [(w, "h") for w in weights],
        [(x.shape, F32, "h") for _, x, _ in kinds],
        [],
        32,
        6 * tokens * width * width,
        8 << 20,
    )


def put_rows(buf, value, per, offset, lanes, extra=None):
    for j in range(buf.shape[1]):
        for core in range(2):
            rows = slice((2 * j + core) * per, (2 * j + core + 1) * per)
            pieces = [value[rows, lo:lo + 256] for lo in lanes]
            if extra is not None:
                pieces.append(extra(rows))
            block = jnp.concatenate(pieces, axis=0) if len(pieces) > 1 else pieces[0]
            buf[core, j, pl.ds(offset, block.shape[0]), :] = block.astype(BF16)


def push_rows(io, buf, own_ref, send_ref, start, size, shift=0):
    core = core_index()
    rows, there = pl.ds(start, size), pl.ds(start + shift, size)
    for ref, side in ((send_ref, 1 - core), (own_ref, core)):
        io.push(buf.at[side, :, rows], ref.at[:, there])


def halves_buffer(count, rows):
    return pltpu.VMEM((2, count, rows, 256), BF16)


def core_index():
    return (lax.axis_index("grp") % 2).astype(jnp.int32)


def halves(count, rows):
    return [((count, rows, 256), BF16, "a")] * 2


def down_grad_kernel(
    io, demb_ref, gains_ref, proj_ref, wp_s, out_ref, wd_s, a_ref, b_ref, wg_s, wu_s, mid_ref, wo_s,
    hid_ref, hidq_ref, dbr_ref, mixt_ref, mixtq_ref, datt_ref, n3_ref, n3q_ref, dpj_ref,
    dg_ref, du_ref, dmid_ref, dmix_ref, own_ref, send_ref,
    acc1_s, dpjq_s, dbrq_s, dattq_s, hidt_s, hidtq_s, buf_s,
):
    chain_kernel(
        io, demb_ref, gains_ref, proj_ref, wp_s, out_ref, wd_s, a_ref, b_ref, wg_s, wu_s, mid_ref, wo_s,
        dpjq_s, dbrq_s, dg_ref, du_ref, dattq_s, dmid_ref, dmix_ref, acc1_s,
    )
    io.done(dmix_ref)
    hidden, width = hid_ref.shape[1], dbr_ref.shape[1]
    count = own_ref.shape[0]
    per, per_down = width // (2 * count), hidden // (2 * count)
    io.need(hid_ref, hidq_ref)
    hidt_s[...] = hid_ref[...].T
    hidtq_s[...] = hidq_ref[...].T
    io.need(dbr_ref)
    for i in range(width // 256):
        col = slice(i * 256, (i + 1) * 256)
        value = nn(hidt_s[...], dbr_ref[:, col]) + nn(hidtq_s[...], dbrq_s[:, col])
        put_rows(buf_s, value, per_down, i * per_down, (0,))
        push_rows(io, buf_s, own_ref, send_ref, i * per_down, per_down)
    base = (width // 256) * per_down
    io.need(mixt_ref, mixtq_ref, datt_ref, n3_ref, n3q_ref, dpj_ref)
    value = nn(mixt_ref[...], datt_ref[...]) + nn(mixtq_ref[...], dattq_s[...])
    put_rows(buf_s, value, per, base, (0, 256))
    push_rows(io, buf_s, own_ref, send_ref, base, 2 * per)
    base = base + 2 * per
    proj = nn(n3_ref[...].T, dpj_ref[...]) + nn(n3q_ref[...].T, dpjq_s[...])

    def proj_rows(rows):
        return jnp.concatenate([proj[rows], jnp.zeros((per, LANE), F32)], axis=1)

    put_rows(buf_s, value, per, base, (512,), extra=proj_rows)
    push_rows(io, buf_s, own_ref, send_ref, base, 2 * per)


def down_grads(query, doc, count):
    (demb, proj, out, mid, a, b, gains, wp, wd, wg, wu, wo), (hidq, mixtq, n3q) = query
    hid, dbr, mixt, datt, n3, dpj = doc
    tokens, hidden = hid.shape
    qtokens, width = out.shape
    per, per_down = width // (2 * count), hidden // (2 * count)
    plain = [(item, "h") for item in (hid, hidq, dbr, mixt, mixtq, datt, n3, n3q, dpj)]
    return call(
        down_grad_kernel,
        "query_ff_back_down_grads",
        chain_ins(demb, gains, proj, wp, out, wd, a, b, wg, wu, mid, wo) + plain,
        [
            ((qtokens, hidden), BF16, "h"),
            ((qtokens, hidden), BF16, "h"),
            ((qtokens, width), F32, "h"),
            ((qtokens, width), BF16, "h"),
        ]
        + halves(count, (width // 256) * per_down + 4 * per),
        [
            pltpu.VMEM((qtokens, width), F32),
            pltpu.VMEM(proj.shape, BF16),
            pltpu.VMEM((qtokens, width), BF16),
            pltpu.VMEM((qtokens, width), BF16),
            pltpu.VMEM((hidden, tokens), BF16),
            pltpu.VMEM((hidden, qtokens), BF16),
            halves_buffer(count, (width // 256) * per_down + 4 * per),
        ],
        40,
        2 * (tokens + 256) * (width * width + width * hidden),
        24 << 20,
    )


def gate_grad_kernel(which, io, n2_ref, n2q_ref, d, dq, *refs):
    own_ref, send_ref, n2t_s, n2tq_s, buf_s = refs[-5:]
    width, hidden = n2_ref.shape[1], d.shape[1]
    count, rows = own_ref.shape[:2]
    per = width // (2 * count)
    io.need(n2_ref, n2q_ref)
    n2t_s[...] = n2_ref[...].T
    n2tq_s[...] = n2q_ref[...].T
    io.need(dq)
    io.feed((d,))
    for i in range(hidden // CH):
        io.need_part(i, d)
        col = slice(i * CH, (i + 1) * CH)
        value = nn(n2t_s[...], d[:, col]) + nn(n2tq_s[...], dq[:, col])
        for lo in range(0, CH, 512):
            at = (i * CH + lo) // 256 * per
            put_rows(buf_s, value, per, at, (lo, lo + 256))
            push_rows(io, buf_s, own_ref, send_ref, at, 2 * per, which * (rows // 2))
    io.had(d)


def gate_grads(which, n2, n2q, d, dq, count, begun=()):
    tokens, width = n2.shape
    qtokens, hidden = dq.shape
    per = width // (2 * count)
    rows = 2 * (hidden // 256) * per
    return call(
        functools.partial(gate_grad_kernel, which),
        ("gate_grads", "up_grads")[which],
        [(n2, "h"), (n2q, "h"), (d, f"h-{hidden // CH}"), (dq, "h")] + [(item, "b") for item in begun],
        halves(count, rows),
        [
            pltpu.VMEM((width, tokens), BF16),
            pltpu.VMEM((width, qtokens), BF16),
            halves_buffer(count, rows // 2),
        ],
        18,
        2 * (tokens + 256) * width * hidden,
        16 << 20,
        {4: 0, 5: 1} if begun else None,
    )


def qkv_grad_kernel(
    io, k_ref, v_ref, q_ref, dmix_ref, mixt_ref, il_ref, e_ref, n1_ref, n1q_ref, d_ref,
    diagd_ref, fard_ref, hot_ref, loss_ref, dq_ref, diag_ref, far_ref, own_ref, send_ref, *rest,
):
    own_parts = lax.axis_size("dp")
    n1t_s, n1tq_s, buf_s = rest[-3:]
    attention_back_kernel(
        io, k_ref, v_ref, q_ref, dmix_ref, mixt_ref, il_ref, e_ref, dq_ref, diag_ref, far_ref, *rest[:-3]
    )
    io.done(dq_ref)
    width = n1_ref.shape[1]
    count = own_ref.shape[0]
    per = width // (2 * count)
    io.need(n1_ref, n1q_ref)
    n1t_s[...] = n1_ref[...].T
    n1tq_s[...] = n1q_ref[...].T
    io.need(d_ref)
    steps = (3 * width) // 512
    value = nn(n1t_s[...], d_ref[...]) + nn(n1tq_s[...], dq_ref[...])
    for i in range(steps):
        put_rows(buf_s, value, per, i * 2 * per, (i * 512, i * 512 + 256))
        push_rows(io, buf_s, own_ref, send_ref, i * 2 * per, 2 * per)
    io.need(hot_ref)
    heads = diag_ref.shape[0]
    buckets = hot_ref.shape[0]
    table = jnp.zeros((heads, buckets), F32)
    for r in range(8):
        both = diagd_ref[:, r, :] + diag_ref[:, r, :]
        table = table + lax.dot_general(
            both, hot_ref[:, r * SPAN:(r + 1) * SPAN].astype(F32), (((1,), (1,)), ((), ())),
            precision=highest, preferred_element_type=F32,
        )
    far = fard_ref[...] + far_ref[...]
    low = jnp.sum(jnp.sum(far[:, 0:8, :], axis=1), axis=-1, keepdims=True)
    high = jnp.sum(jnp.sum(far[:, 8:16, :], axis=1), axis=-1, keepdims=True)
    column = lax.broadcasted_iota(jnp.int32, (1, buckets), 1)
    table = table + jnp.where(column == buckets // 2 - 1, low, 0.0) + jnp.where(column == buckets - 1, high, 0.0)
    table = jnp.concatenate([table, jnp.zeros((16 - heads, buckets), F32)], axis=0)
    loss = jnp.broadcast_to(loss_ref[...] * (1.0 / own_parts), (8, LANE))
    spare = jnp.concatenate([table[0:8], table[8:16], jnp.zeros((8, LANE - 2 * buckets), F32), loss], axis=1)
    put_rows(buf_s, value, per, steps * 2 * per, (steps * 512,), extra=lambda rows: spare)
    push_rows(io, buf_s, own_ref, send_ref, steps * 2 * per, per + 8)


def qkv_grads(query, n1, n1q, d, diag, far, hot, loss, count):
    tokens, width = n1.shape
    per = width // (2 * count)
    return call(
        qkv_grad_kernel,
        "query_attention_back_qkv_grads",
        attention_ins(*query)
        + [(n1, "h"), (n1q, "h"), (d, "v")]
        + [(diag, "v"), (far, "v"), (hot, "h"), (loss, "v")],
        attention_outs(query[0], query[3].shape[0]) + halves(count, 9 * per + 8),
        attention_scratch(query[0])
        + [
            pltpu.VMEM((width, tokens), BF16),
            pltpu.VMEM((width, n1q.shape[0]), BF16),
            halves_buffer(count, 9 * per + 8),
        ],
        24,
        2 * (tokens + 256) * 3 * width * width,
        10 << 20,
    )


def after(values, *deps):
    return lax.optimization_barrier((values, deps))[0]


def position(n_dp):
    dp, grp = lax.axis_index("dp").astype(jnp.int32), lax.axis_index("grp").astype(jnp.int32)
    return dp // 2, dp % 2, grp // 2


def slices(io_sems, moves):
    copies = [pltpu.make_async_copy(src, dst, io_sems.at[i]) for i, (src, dst) in enumerate(moves)]
    for copy in copies:
        copy.start()
    return copies


class Halves:
    def __init__(self, rows):
        self.rows, self.cut = rows, (rows // 32) * 16

    def sizes(self):
        return self.cut, self.rows - self.cut

    def spans(self):
        return pl.ds(0, self.cut), pl.ds(self.cut, self.rows - self.cut)


def first_kernel(n_dp, halves, io, own_ref, got_ref, x_ref, y_ref, ox_s, gx_s, oy_s, gy_s, sems):
    _, x, y = position(n_dp)
    top, low = halves.spans()
    moves = []
    for ref, a, b in ((own_ref, ox_s, oy_s), (got_ref, gx_s, gy_s)):
        moves += [(ref.at[:, 1 - x, :, top], a), (ref.at[:, :, 1 - y, low], b)]
    copies = slices(sems, moves)
    for i, (a, b, out) in enumerate(((ox_s, gx_s, x_ref), (oy_s, gy_s, y_ref))):
        copies[i].wait()
        copies[i + 2].wait()
        out[...] = (a[...].astype(F32) + b[...].astype(F32)).astype(BF16)
        io.done(out)


def pair_rows(n_dp, halves, flip, own_ref, got_ref, gx_ref, gy_ref, bufs, sems):
    _, x, y = position(n_dp)
    top, low = halves.spans()
    yt, xl = (1 - y, 1 - x) if flip else (y, x)
    ot_s, gt_s, rt_s, ol_s, gl_s, rl_s = bufs
    copies = slices(sems, [
        (own_ref.at[:, x, yt, top], ot_s), (got_ref.at[:, x, yt, top], gt_s), (gx_ref.at[:, yt], rt_s),
        (own_ref.at[:, xl, y, low], ol_s), (got_ref.at[:, xl, y, low], gl_s), (gy_ref.at[:, xl], rl_s),
    ])
    out = []
    for i in (0, 3):
        for copy in copies[i:i + 3]:
            copy.wait()
        a, b, c = bufs[i:i + 3]
        out.append(a[...].astype(F32) + b[...].astype(F32) + c[...].astype(F32))
    return out


def second_kernel(n_dp, halves, io, own_ref, got_ref, gx_ref, gy_ref, y_ref, x_ref, *refs):
    for out, value in zip((y_ref, x_ref), pair_rows(n_dp, halves, True, own_ref, got_ref, gx_ref, gy_ref, refs[:-1], refs[-1])):
        out[...] = value.astype(BF16)
        io.done(out)


def cross_kernel(n_dp, halves, io, own_ref, got_ref, xy_ref, x_ref, y_ref, own_s, got_s, sems):
    _, x, y = position(n_dp)
    moves = []
    for i, (xx, yy) in enumerate(((1 - x, 1 - y), (1 - x, y), (x, 1 - y))):
        moves += [(own_ref.at[:, xx, yy], own_s.at[i]), (got_ref.at[:, xx, yy], got_s.at[i])]
    copies = slices(sems, moves)
    for i, out in enumerate((xy_ref, x_ref, y_ref)):
        copies[2 * i].wait()
        copies[2 * i + 1].wait()
        out[...] = (own_s[i].astype(F32) + got_s[i].astype(F32)).astype(BF16)
        io.done(out)


def leave(z, line_s, outs, total_ref, io):
    nz = line_s.shape[0]
    if not outs:
        total_ref[...] = line_s[...].astype(BF16)
        return
    for k, out in enumerate(outs, 1):
        out[...] = line_s[(z + k) % nz].astype(BF16)
        io.done(out)
    total_ref[...] = line_s[z]


def cross_line_kernel(n_dp, halves, io, own_ref, got_ref, xy_ref, x_ref, y_ref, *refs):
    outs, total_ref, (line_s, own_s, got_s, sems) = refs[:-5], refs[-5], refs[-4:]
    z, x, y = position(n_dp)
    copies = slices(sems, [(own_ref.at[:, x, y], own_s), (got_ref.at[:, x, y], got_s)])
    for copy in copies:
        copy.wait()
    io.need(xy_ref, x_ref, y_ref)
    line_s[...] = own_s[...].astype(F32) + got_s[...].astype(F32) + xy_ref[...].astype(F32)
    line_s[...] += x_ref[...].astype(F32) + y_ref[...].astype(F32)
    leave(z, line_s, outs, total_ref, io)


def line_kernel(n_dp, halves, io, own_ref, got_ref, gx_ref, gy_ref, y_ref, x_ref, *refs):
    outs, total_ref, line_s, bufs, sems = refs[:-9], refs[-9], refs[-8], refs[-7:-1], refs[-1]
    z, _, _ = position(n_dp)
    top, low = pair_rows(n_dp, halves, False, own_ref, got_ref, gx_ref, gy_ref, bufs, sems)
    io.need(x_ref, y_ref)
    line_s[:, 0:halves.cut] = top + y_ref[...].astype(F32)
    line_s[:, halves.cut:] = low + x_ref[...].astype(F32)
    leave(z, line_s, outs, total_ref, io)


class Batch:
    def __init__(self, own, send, n_dp, n_grp, name):
        self.n_dp, self.n_grp, self.nz, self.name = n_dp, n_grp, n_dp // 2, name
        self.rows, self.cols = own.shape[1:]
        self.halves = Halves(self.rows)
        self.own = own
        self.got = lax.ppermute(send, "grp", [(i, i ^ 1) for i in range(n_grp)])

    def both(self):
        grid = lambda a: (a.reshape(self.nz, 2, 2, self.rows, self.cols), "r")
        own, kind = grid(self.own)
        return [(pltpu.with_memory_space_constraint(own, pltpu.HBM), kind), grid(self.got)]

    def along_x(self, array):
        return lax.ppermute(array, "dp", [(d, d ^ 1) for d in range(self.n_dp)])

    def along_y(self, array):
        return lax.ppermute(array, "grp", [(g, g ^ 2) for g in range(self.n_grp)])

    def run(self, kernel, step, ins, outs, scratch):
        body = functools.partial(kernel, self.n_dp, self.halves)
        return call(body, self.name + step, ins, outs, scratch, 24, 0, 0)

    def first(self):
        sizes = [(self.nz, 2, n, self.cols) for n in self.halves.sizes()]
        bufs = [pltpu.VMEM(size, BF16) for size in sizes for _ in range(2)]
        outs = [(size, BF16, "h") for size in sizes]
        sent = self.run(first_kernel, "_first", self.both(), outs, bufs + [pltpu.SemaphoreType.DMA((4,))])
        self.back1 = self.along_x(sent[0]), self.along_y(sent[1])
        return tuple(sent)

    def second_bufs(self):
        return [pltpu.VMEM((self.nz, n, self.cols), BF16) for n in self.halves.sizes() for _ in range(3)] + [
            pltpu.SemaphoreType.DMA((6,))
        ]

    def second(self):
        outs = [((self.nz, n, self.cols), BF16, "h") for n in self.halves.sizes()]
        ins = self.both() + [(a, "r") for a in self.back1]
        sent = self.run(second_kernel, "_second", ins, outs, self.second_bufs())
        self.back2 = self.along_y(sent[0]), self.along_x(sent[1])
        return tuple(sent)

    def cross(self):
        n_dp, n_grp = self.n_dp, self.n_grp
        piece = (self.nz, self.rows, self.cols)
        bufs = [pltpu.VMEM((3, *piece), BF16)] * 2 + [pltpu.SemaphoreType.DMA((6,))]
        sent = self.run(cross_kernel, "_cross", self.both(), [(piece, BF16, "h")] * 3, bufs)
        across = [(d * n_grp + g, (d ^ 1) * n_grp + (g ^ 2)) for d in range(n_dp) for g in range(n_grp)]
        self.back1 = ()
        self.back2 = lax.ppermute(sent[0], ("dp", "grp"), across), self.along_x(sent[1]), self.along_y(sent[2])
        return tuple(sent)

    def line(self, together=False):
        n_dp, nz = self.n_dp, self.nz
        piece, part = (nz, self.rows, self.cols), (self.rows, self.cols)
        outs = [(piece, BF16, "h")] if together else [(part, BF16, "h")] * (nz - 1) + [(part, F32, "v")]
        ins = self.both() + [(a, "r") for a in self.back1] + [(a, "v") for a in self.back2]
        if self.back1:
            kernel, bufs = line_kernel, self.second_bufs()
        else:
            kernel, bufs = cross_line_kernel, [pltpu.VMEM(piece, BF16)] * 2 + [pltpu.SemaphoreType.DMA((2,))]
        *sent, total = self.run(kernel, "_line", ins, outs, [pltpu.VMEM(piece, F32)] + bufs)
        if together:
            groups = [[2 * z + x for z in range(nz)] for x in range(2)]
            self.parts = [lax.all_to_all(total, "dp", 0, 0, tiled=True, axis_index_groups=groups)]
            return (total,)
        self.parts = [total] + [
            lax.ppermute(one, "dp", [(d, (d + 2 * k) % n_dp) for d in range(n_dp)]) for k, one in enumerate(sent, 1)
        ]
        return tuple(sent)


def weight_rows(weights, start):
    aligned = (start // 16) * 16
    return start - aligned, [w.at[pl.ds(pl.multiple_of(aligned, 16), 32)] for w in weights]


def finish_kernel(n_parts, places, gain_row, scale, io, *refs):
    total, gains_ref, rest = refs[:n_parts], refs[n_parts], refs[n_parts + 1:]
    n_out, n_weights = len(places), len(gain_row[1])
    weights, rest = rest[:n_weights], rest[n_weights:]
    outs, rest = rest[:n_out], rest[n_out:]
    gain_ref, rest = rest[0], rest[1:]
    extra, rest = (rest[:2], rest[2:]) if scale else ((), rest)
    sum_s, wide_s, bufs, sems = rest[0], rest[1], rest[2:-1], rest[-1]
    device = lax.axis_index("dp") * lax.axis_size("grp") + lax.axis_index("grp")
    per = outs[gain_row[1][0]].shape[0]
    start = device.astype(jnp.int32) * per
    shift, sources = weight_rows(weights, start)
    copies = slices(sems, list(zip(sources, bufs)))
    io.need(*total)
    if len(total) == 1:
        value = total[0][0].astype(F32)
        for i in range(1, total[0].shape[0]):
            value = value + total[0][i].astype(F32)
    else:
        value = total[0][...].astype(F32)
        for one in total[1:]:
            value = value + one[...].astype(F32)
    sum_s[...] = value
    for out, at in zip(outs, places):
        rows, width = out.shape
        for i in range(-(-width // 256)):
            cols = min(256, width - i * 256)
            out[:, i * 256:i * 256 + cols] = sum_s[at + i * rows:at + (i + 1) * rows, 0:cols]
    inner = jnp.zeros((per, 1), F32)
    for which, copy, buf in zip(gain_row[1], copies, bufs):
        copy.wait()
        width = buf.shape[1]
        wide_s[:, 0:width] = buf[...].astype(F32)
        mine = wide_s[pl.ds(pl.multiple_of(shift, 8), per), 0:width]
        inner = inner + jnp.sum(mine * outs[which][...], axis=-1, keepdims=True)
    lane = lax.broadcasted_iota(jnp.int32, (per, gains_ref.shape[1]), 1)
    row = lax.broadcasted_iota(jnp.int32, (per, gains_ref.shape[1]), 0)
    gain = jnp.sum(jnp.where(lane == row + start, gains_ref[gain_row[0]:gain_row[0] + 1, :], 0.0), axis=-1, keepdims=True)
    lane, row = lane[:, 0:LANE], row[:, 0:LANE]
    gain_ref[...] = jnp.sum(jnp.where(lane == row, inner / gain, 0.0), axis=0, keepdims=True)[:, 0:per]
    if scale:
        table_ref, loss_ref = extra
        heads, buckets = table_ref.shape
        spare = sum_s[sum_s.shape[0] - 8:, :]
        table = jnp.concatenate([spare[:, 0:buckets], spare[:, buckets:2 * buckets]], axis=0)
        table_ref[...] = table[0:heads]
        loss_ref[...] = spare[0:1, LANE:LANE + 1] * scale


def finish(batch, places, shapes, gain_row, gains, weights, table=None, scale=0.0):
    per = shapes[gain_row[1][0]][0]
    outs = [(shape, F32, "h") for shape in shapes] + [((1, per), F32, "v")]
    if table is not None:
        outs += [(table, F32, "v"), ((1, 1), F32, "v")]
    width = max(w.shape[1] for w in weights)
    return call(
        functools.partial(finish_kernel, len(batch.parts), places, gain_row, scale),
        batch.name + "_finish",
        [(one, "v") for one in batch.parts] + [(gains, "v")] + [(pltpu.with_memory_space_constraint(w, pltpu.HBM), "r") for w in weights],
        outs,
        [pltpu.VMEM((batch.rows, batch.cols), F32), pltpu.VMEM((32, width), F32)]
        + [pltpu.VMEM((32, w.shape[1]), BF16) for w in weights]
        + [pltpu.SemaphoreType.DMA((len(weights),))],
        16,
        0,
        0,
    )


def on_device(
    n_dp, n_grp, doc_tokens, doc_lengths, query_tokens, query_lengths, candidates, labels, gain_attn, w_query, w_key,
    w_value, w_out, bias_table, gain_ffn, w_gate, w_up, w_down, gain_final, w_proj,
):
    doc_rows, doc_len, width = doc_tokens.shape
    query_rows, query_len = query_tokens.shape[:2]
    hidden = w_gate.shape[1]
    bucket_total, heads = bias_table.shape
    devices = n_dp * n_grp
    axes = ("dp", "grp")
    x_doc = doc_tokens.reshape(doc_len, width)
    x_qry = query_tokens.reshape(query_rows * query_len, width)
    which = lax.broadcasted_iota(jnp.int32, (24, width), 0)
    gains = jnp.where(which == 0, gain_attn[None], jnp.where(which == 1, gain_ffn[None], gain_final[None]))
    table = jnp.pad(bias_table.T, ((8, 16 - heads), (0, width - bucket_total)))
    gains = jnp.where(which < 8, gains, table).astype(F32)
    weights = (w_query, w_key, w_value, w_out, w_gate, w_up, w_down, w_proj)
    hot = jnp.asarray(strip_onehot(), BF16)
    (q_q, q_k, q_v, q_e, q_il, q_mixt, q_mid, q_n1, q_n2, q_hid, q_a, q_b, q_out, q_n3, q_proj, packed, base) = forward(
        x_qry, query_lengths[None], gains, (hot, candidates, labels[None]), weights, False, heads, n_dp
    )
    got = lax.all_to_all(packed, "dp", 0, 0, tiled=True)
    (d_q, d_k, d_v, d_e, d_il, d_mixt, d_mid, d_n1, d_n2, d_hid, d_a, d_b, d_out, d_n3, d_proj, emb) = forward(
        x_doc, doc_lengths, gains, base, weights, True, heads
    )
    sums, lse = scores(got, emb, query_len)
    sums = lax.all_to_all(sums, "dp", 0, 0, tiled=True)
    demb_doc, demb_part, loss_group = retrieval_back(
        got, sums, emb, lse, query_len
    )
    demb_qry = lax.all_to_all(demb_part, "dp", 0, 0, tiled=True)
    back = (w_proj, w_down, w_gate, w_up, w_out)
    d_dpj, d_dbr, d_dg, d_du, d_datt, d_dmid, d_dmix = chain(
        demb_doc, d_proj, d_out, d_mid, d_a, d_b, gains, *back, "doc_ff_back"
    )
    q_chain = (demb_qry, q_proj, q_out, q_mid, q_a, q_b, gains, *back)
    d_attention = lambda il: (d_q, d_k, d_v, d_e, il, d_mixt, d_dmix)
    q_attention = lambda il, dmix: (q_q, q_k, q_v, q_e, il, q_mixt, dmix)
    qkv_weights = (w_query, w_key, w_value)
    fast = (n_dp, n_grp) == (8, 4)
    if fast:
        pairs = devices // 2
        q_dg, q_du, q_dmid, q_dmix, own, send = down_grads(
            (q_chain, (q_hid, q_mixt, q_n3)), (d_hid, d_dbr, d_mixt, d_datt, d_n3, d_dpj), pairs
        )
        down = Batch(own, send, n_dp, n_grp, "down")
        begun = gate_grads(0, d_n2, q_n2, d_dg, q_dg, pairs)
        down.got = after(down.got, begun)
        q_du = after(q_du, down.cross())
        own, send = gate_grads(1, d_n2, q_n2, d_du, q_du, pairs, begun)
        gate = Batch(own, send, n_dp, n_grp, "gate")
        d_il = after(d_il, send)
        d_dqkv, d_diag, d_far = attention_back(*d_attention(d_il), "doc_attention_back")
        gate.got = after(gate.got, d_diag)
        q_il = after(q_il, gate.cross())
        q_dqkv, q_diag, q_far, own, send = qkv_grads(
            q_attention(q_il, q_dmix), d_n1, q_n1, d_dqkv, d_diag, d_far, hot, loss_group, pairs
        )
        qkv = Batch(own, send, n_dp, n_grp, "qkv")
        (doc_grad,) = input_back(after(gains, send), ((d_dqkv, x_doc, d_dmid),), qkv_weights, "doc_input_back")
        down.back2 = after(down.back2, doc_grad)
        last_gains = after(gains, down.line(True))
    else:
        q_dpj, q_dbr, q_dg, q_du, q_datt, q_dmid, q_dmix = chain(*q_chain, "query_ff_back")
        d_dqkv, d_diag, d_far = attention_back(*d_attention(d_il), "doc_attention_back")
        q_dqkv, q_diag, q_far = attention_back(*q_attention(q_il, q_dmix), "query_attention_back")
        last_gains = gains
        (doc_grad,) = input_back(gains, ((d_dqkv, x_doc, d_dmid),), qkv_weights, "doc_input_back")
    (query_grad,) = input_back(last_gains, ((q_dqkv, x_qry, q_dmid),), qkv_weights, "query_input_back")

    query_total = query_rows * devices
    per, per_down = width // devices, hidden // devices
    if fast:
        qkv.got = after(qkv.got, query_grad)
        gate.back2 = after(gate.back2, qkv.cross())
        qkv.back2 = after(qkv.back2, gate.line())
        sent = qkv.line()
        down.parts, gate.parts = after((down.parts, gate.parts), sent)
        at = (width // 256) * per_down
        shard_down, shard_out, shard_proj, gain3 = finish(
            down, (0, at, at + 3 * per), ((per_down, width), (per, width), (per, w_proj.shape[1])), (2, (2,)), gains, [w_proj]
        )
        shard_gate, shard_up, gain2 = finish(
            gate, (0, (hidden // 256) * per), ((per, hidden),) * 2, (1, (0, 1)), gains, [w_gate, w_up]
        )
        shard_query, shard_key, shard_value, gain1, table_grad, loss = finish(
            qkv, (0, 3 * per, 6 * per), ((per, width),) * 3, (0, (0, 1, 2)), gains, qkv_weights, (heads, bucket_total), 1.0 / query_total
        )
        shard_gains = [g.reshape(per) for g in (gain1, gain2, gain3)]
        table_grad, loss = table_grad.T, loss.reshape(())
    else:

        def grad(left, right):
            product = tn(jnp.concatenate(left), jnp.concatenate(right))
            return lax.psum_scatter(product, axes, scatter_dimension=0, tiled=True)

        n1s = (d_n1, q_n1)
        shard_query, shard_key, shard_value = (
            grad(n1s, (d_dqkv[:, i * width:(i + 1) * width], q_dqkv[:, i * width:(i + 1) * width])) for i in range(3)
        )
        shard_out = grad((d_mixt.T, q_mixt.T), (d_datt, q_datt))
        shard_gate = grad((d_n2, q_n2), (d_dg, q_dg))
        shard_up = grad((d_n2, q_n2), (d_du, q_du))
        shard_down = grad((d_hid, q_hid), (d_dbr, q_dbr))
        shard_proj = grad((d_n3, q_n3), (d_dpj, q_dpj))
        start = (lax.axis_index("dp") * n_grp + lax.axis_index("grp")) * per
        mine = lambda a: lax.dynamic_slice_in_dim(a.astype(F32), start, per, 0)
        shard_gains = [
            sum(jnp.sum(mine(w) * g, axis=1) for w, g in pairs) / mine(gain)
            for gain, pairs in (
                (gain_attn, ((w_query, shard_query), (w_key, shard_key), (w_value, shard_value))),
                (gain_ffn, ((w_gate, shard_gate), (w_up, shard_up))),
                (gain_final, ((w_proj, shard_proj),)),
            )
        ]
        far = jnp.sum((d_far + q_far).reshape(heads, 2, -1), axis=-1)
        table = lax.dot_general(
            hot.astype(F32), (d_diag + q_diag).reshape(heads, -1), (((1,), (1,)), ((), ())),
            precision=highest, preferred_element_type=F32,
        )
        table = table.at[bucket_total // 2 - 1].add(far[:, 0]).at[bucket_total - 1].add(far[:, 1])
        table_grad, loss = lax.psum((table, loss_group[0, 0] / n_dp), axes)
        loss = loss / query_total
    return (
        loss,
        doc_grad.reshape(doc_rows, doc_len, width),
        query_grad.reshape(query_rows, query_len, width),
        shard_gains[0],
        shard_query,
        shard_key,
        shard_value,
        shard_out,
        table_grad,
        shard_gains[1],
        shard_gate,
        shard_up,
        shard_down,
        shard_gains[2],
        shard_proj,
    )


def solution(mesh):
    both = ("dp", "grp")
    rows3, rows2, rows1 = P(both, None, None), P(both, None), P(both)
    in_specs = (rows3, rows2, rows3, rows1, rows2, rows1) + (P(),) * 12
    out_specs = (
        P(), rows3, rows3, rows1, rows2, rows2, rows2, rows2, P(), rows1, rows2, rows2, rows2, rows1, rows2,
    )
    body = functools.partial(on_device, mesh.shape["dp"], mesh.shape["grp"])
    return jax.shard_map(body, mesh=mesh, in_specs=in_specs, out_specs=out_specs, check_vma=False)
```

```python
import functools
import itertools
import math

import jax
import jax.numpy as jnp
import numpy as np
from jax import lax
from jax.experimental import pallas as pl
from jax.experimental.pallas import tpu as pltpu
from jax.sharding import PartitionSpec as P

F32, BF16 = jnp.float32, jnp.bfloat16
BUCKETS = 32
DIST = 128
BLK = 128
MOST_DOC = 256
ROW_FILL = 480
EPS = 1e-6
SHARP = 0.25
SCALE = 16.0
NEG = -1e30
GELU_A = math.sqrt(2.0 / math.pi)
GELU_B = 0.044715
SPAN = 512
CH = 1024
LANE = 128
COST = 20
AHEAD = 1 << 30
PACK_INT = 48
highest = lax.Precision.HIGHEST


def nn(a, b):
    return jnp.dot(a, b, preferred_element_type=F32)


def nt(a, b):
    return lax.dot_general(a, b, (((1,), (1,)), ((), ())), preferred_element_type=F32)


def tn(a, b):
    return lax.dot_general(a, b, (((0,), (0,)), ((), ())), preferred_element_type=F32)


def bucket_of(offsets):
    half = BUCKETS // 2
    exact = half // 2
    dist = np.abs(offsets)
    scaled = np.log(np.maximum(dist, 1) / exact) / np.log(DIST / exact) * (half - exact)
    far = np.minimum(exact + np.maximum(scaled, 0).astype(np.int64), half - 1)
    return (offsets > 0) * half + np.where(dist < exact, dist, far)


def strip_onehot():
    j = np.arange(SPAN)
    offset = np.where(j < 384, 128 - j, 640 - j)
    index = np.stack([bucket_of(offset[(j - r) % SPAN]) for r in range(8)]).reshape(-1)
    return (index[None, :] == np.arange(BUCKETS)[:, None]).astype(np.float32)


VM = pl.BlockSpec(memory_space=pltpu.VMEM)
HB = pl.BlockSpec(memory_space=pl.ANY)


def by_part(run):
    return run if run[0][3] == 1 else sorted(run, key=lambda entry: entry[1])


class Io:
    def __init__(self, ins, outs, sems):
        self.ins, self.outs, self.sems, self.used = {}, {}, sems, 0
        self.going, self.queue, self.flying = [], [], 0
        for src, buf, parts in ins:
            self.ins[id(buf)] = (src, buf, parts, self.used)
            size = math.prod(buf.shape) * buf.dtype.itemsize // abs(parts)
            self.queue += [(id(buf), p, size, abs(parts)) for p in range(abs(parts))]
            self.used += abs(parts)
        for buf, dst in outs:
            self.outs[id(buf)] = (buf, dst)
        self.queue = [entry for _, run in itertools.groupby(self.queue, lambda e: e[3]) for entry in by_part(list(run))]
        self.feed()

    def feed(self, upto=()):
        upto = {id(buf) for buf in upto}
        while self.queue and (self.flying < AHEAD or any(entry[0] in upto for entry in self.queue)):
            key, p, size, _ = self.queue.pop(0)
            self.chunk(*self.ins[key], p).start()
            self.flying += size

    def landed(self, buf):
        self.flying -= math.prod(buf.shape) * buf.dtype.itemsize
        self.feed()

    def chunk(self, src, buf, parts, first, p):
        if parts == 1:
            return pltpu.make_async_copy(src, buf, self.sems.at[first])
        if parts > 0:
            size = buf.shape[0] // parts
            cut = (pl.ds(p * size if isinstance(p, int) else pl.multiple_of(p * size, 2), size),)
        else:
            size = buf.shape[1] // -parts
            cut = (slice(None), pl.ds(p * size if isinstance(p, int) else pl.multiple_of(p * size, LANE), size))
        return pltpu.make_async_copy(src.at[cut], buf.at[cut], self.sems.at[first + p])

    def need(self, *bufs):
        for buf in bufs:
            entry = self.ins.get(id(buf))
            if entry is not None:
                self.feed((buf,))
                for p in range(abs(entry[2])):
                    self.chunk(*entry, p).wait()
                del self.ins[id(buf)]
                self.landed(buf)

    def need_part(self, p, *bufs):
        for buf in bufs:
            if id(buf) in self.ins:
                self.chunk(*self.ins[id(buf)], p).wait()

    def had(self, *bufs):
        for buf in bufs:
            if self.ins.pop(id(buf), None) is not None:
                self.landed(buf)

    def done(self, *bufs):
        for buf in bufs:
            if id(buf) in self.outs:
                src, dst = self.outs.pop(id(buf))
                self.push(src, dst)

    def done_rows(self, buf, start, size):
        src, dst = self.outs[id(buf)]
        rows = (slice(None), pl.ds(start, size))
        self.push(src.at[rows], dst.at[rows])

    def gone(self, buf):
        self.outs.pop(id(buf))

    def push(self, src, dst):
        copy = pltpu.make_async_copy(src, dst, self.sems.at[self.used])
        self.used += 1
        copy.start()
        self.going.append(copy)

    def close(self):
        self.need(*[entry[1] for entry in list(self.ins.values())])
        self.done(*[entry[0] for entry in list(self.outs.values())])
        for copy in self.going:
            copy.wait()


def call(kernel, name, ins, outs, scratch, mib, flops, moved=8 << 20, aliases=None):
    args, in_specs, out_specs, out_shape, buffers, sems = [], [], [], [], [], 0
    for array, kind in ins:
        if kind in ("r", "b"):
            args.append(array if kind == "r" else pltpu.with_memory_space_constraint(array, pltpu.HBM))
            in_specs.append(HB)
        elif kind[0] == "h":
            args.append(pltpu.with_memory_space_constraint(array, pltpu.HBM))
            in_specs.append(HB)
            buffers.append(pltpu.VMEM(array.shape, array.dtype))
            sems += abs(int(kind[1:] or 1))
        else:
            args.append(array)
            in_specs.append(VM)
    for shape, dtype, kind in outs:
        if kind == "a":
            out_shape.append(pltpu.HBM(shape, dtype))
            out_specs.append(HB)
            sems += 8
        elif kind == "h":
            out_shape.append(pltpu.HBM(shape, dtype))
            out_specs.append(HB)
            buffers.append(pltpu.VMEM(shape, dtype))
            sems += 4
        else:
            out_shape.append(jax.ShapeDtypeStruct(shape, dtype))
            out_specs.append(VM)

    def body(*refs):
        n_in, n_out, n_buf = len(ins), len(outs), len(buffers)
        given, made = list(refs[:n_in]), list(refs[n_in:n_in + n_out])
        bufs = iter(refs[n_in + n_out:n_in + n_out + n_buf])
        rest = refs[n_in + n_out + n_buf:]
        reads, writes = [], []
        for i, (_, kind) in enumerate(ins):
            if kind[0] == "h":
                buf = next(bufs)
                reads.append((given[i], buf, int(kind[1:] or 1)))
                given[i] = buf
        for i, (_, _, kind) in enumerate(outs):
            if kind == "h":
                buf = next(bufs)
                writes.append((buf, made[i]))
                made[i] = buf
        io = Io(reads, writes, rest[-1])
        kernel(io, *given, *made, *rest[:-1])
        io.close()

    return pl.pallas_call(
        body,
        name=name,
        out_shape=out_shape,
        in_specs=in_specs,
        out_specs=out_specs,
        scratch_shapes=buffers + scratch + [pltpu.SemaphoreType.DMA((max(sems, 1),))],
        compiler_params=pltpu.CompilerParams(vmem_limit_bytes=mib << 20),
        input_output_aliases=aliases or {},
        cost_estimate=pl.CostEstimate(flops=int(flops) * COST, bytes_accessed=int(moved) * COST, transcendentals=0),
    )(*args)


def reachable(d, tile):
    return (abs(d) - 1) * tile + 1 < MOST_DOC


def half_lanes(values, side):
    lane = lax.broadcasted_iota(jnp.int32, (1, LANE), 1)
    return jnp.where((lane // 64) == side, values.astype(F32), 0.0).astype(BF16)


def norm_back(values, gain, dn):
    s = lax.rsqrt(jnp.mean(values * values, axis=-1, keepdims=True) + EPS)
    unit = values * s
    t = dn * gain
    return s * (t - unit * jnp.mean(t * unit, axis=-1, keepdims=True))


def forward_kernel(
    is_doc, io, x_ref, lens_ref, gains_ref, extra_ref, wq_s, wk_s, wv_s, wo_s, wg_s, wu_s, wd_s, wp_s,
    q_ref, k_ref, v_ref, e_ref, il_ref, mixt_ref, mid_ref, n1_ref, n2_ref, hid_ref, a_ref, b_ref,
    out_ref, n3_ref, proj_ref, emb_ref, *rest,
):
    if is_doc:
        base_ref, tail = extra_ref, rest
    else:
        hot_ref, cand_ref, label_ref = extra_ref
        base_ref, tail = rest[0], rest[1:]
    mask_s, strip_s, s_s, e_s, vt_s, mid_s = tail
    tokens, width = x_ref.shape
    hidden = wg_s.shape[1]
    heads = e_ref.shape[0]
    io.need(lens_ref)
    if not is_doc:
        io.need(hot_ref)
        tab = gains_ref[8:24, 0:hot_ref.shape[0]].astype(BF16)
        for r in range(8):
            rows = nn(tab, hot_ref[:, r * SPAN:(r + 1) * SPAN])
            for h in range(heads):
                base_ref[h, r:r + 1, :] = rows[h:h + 1, :]
    io.need(x_ref)
    x = x_ref[...].astype(F32)
    s1 = lax.rsqrt(jnp.mean(x * x, axis=-1, keepdims=True) + EPS)
    n1_ref[...] = (x * s1 * gains_ref[0:1, :]).astype(BF16)
    io.done(n1_ref)
    tile = min(tokens, 128)
    blocks = tokens // tile
    row_id = lax.broadcasted_iota(jnp.int32, (tokens, 1), 0)
    col_id = lax.broadcasted_iota(jnp.int32, (1, tokens), 1)
    if is_doc:
        seg_k = jnp.zeros((tokens, 1), jnp.int32)
        seg_q = jnp.zeros((1, tokens), jnp.int32)
        end = jnp.zeros((1, 1), jnp.int32)
        for i in range(lens_ref.shape[1]):
            end = end + lens_ref[0:1, i:i + 1]
            seg_k = seg_k + (row_id >= end).astype(jnp.int32)
            seg_q = seg_q + (col_id >= end).astype(jnp.int32)
    else:
        count = lens_ref.shape[1]
        length = tokens // count
        seg_q = col_id // length
        seg_k = jnp.full((tokens, 1), -1, jnp.int32)
        for i in range(count):
            inside = (row_id >= i * length) & (row_id < i * length + lens_ref[0:1, i:i + 1])
            seg_k = jnp.where(inside, i, seg_k)
    mask_s[...] = jnp.where(seg_k == seg_q, 0.0, NEG)
    for i, (w, o) in enumerate(((wq_s, q_ref), (wk_s, k_ref), (wv_s, v_ref))):
        io.need(w)
        o[...] = nn(n1_ref[...], w[...]).astype(BF16)
        io.done(o)
    vt_s[...] = v_ref[...].T
    if is_doc:
        io.need(base_ref)
    else:
        io.done(base_ref)

    def softmax_pair(p, slot):
        col = pl.ds(pl.multiple_of(p * LANE, LANE), LANE)
        for s in range(2):
            h = 2 * p + s
            first = base_ref[h]
            for g in range(tile // 8):
                strip_s[s, 8 * g:8 * g + 8, :] = pltpu.roll(first, 8 * g, 1) if g else first
            low_far, high_far = first[0:1, 256:256 + tile], first[0:1, 384:384 + tile]
            scores = nt(half_lanes(k_ref[:, col], s), q_ref[:, col])
            for qb in range(blocks):
                cols = slice(qb * tile, (qb + 1) * tile)
                tops = []
                near = [kb for kb in range(blocks) if reachable(kb - qb, tile)]
                for kb in near:
                    ks = slice(kb * tile, (kb + 1) * tile)
                    d = kb - qb
                    t = scores[ks, cols]
                    if abs(d) <= 1:
                        lo = (1 - d) * 128
                        t = t + strip_s[s, :, lo:lo + tile]
                    else:
                        t = t + (high_far if d > 0 else low_far)
                    t = t + mask_s[ks, cols]
                    s_s[s, ks, cols] = t
                    tops.append(jnp.max(t, axis=0, keepdims=True))
                top = functools.reduce(jnp.maximum, tops)
                total = None
                for kb in near:
                    ks = slice(kb * tile, (kb + 1) * tile)
                    e = jnp.exp(s_s[s, ks, cols] - top)
                    part = jnp.sum(e, axis=0, keepdims=True)
                    total = part if total is None else total + part
                    kept = e.astype(BF16)
                    e_ref[h, ks, cols] = kept
                    e_s[slot, s, ks, cols] = kept
                il_ref[h, :, cols] = 1.0 / total

    def mix_pair(p, slot):
        for s in range(2):
            rows = pl.ds(pl.multiple_of(p * LANE + 64 * s, 64), 64)
            mixt_ref[rows, :] = (nn(vt_s[rows, :], e_s[slot, s]) * il_ref[2 * p + s]).astype(BF16)

    def pair_step(i, carry):
        mix_pair(2 * i, 0)
        softmax_pair(2 * i + 1, 1)
        mix_pair(2 * i + 1, 1)
        softmax_pair(2 * i + 2, 0)
        return carry

    pairs = width // LANE
    for kb, qb in itertools.product(range(blocks), repeat=2):
        if not reachable(kb - qb, tile):
            far = (slice(kb * tile, (kb + 1) * tile), slice(qb * tile, (qb + 1) * tile))
            e_s[(slice(None), slice(None), *far)] = jnp.zeros((2, 2, tile, tile), BF16)
            e_ref[(slice(None), *far)] = jnp.zeros((heads, tile, tile), BF16)
    softmax_pair(0, 0)
    lax.fori_loop(0, pairs // 2 - 1, pair_step, 0)
    mix_pair(pairs - 2, 0)
    softmax_pair(pairs - 1, 1)
    mix_pair(pairs - 1, 1)
    io.done(e_ref, mixt_ref)
    io.need(wo_s)
    mid_s[...] = x_ref[...].astype(F32) + nn(mixt_ref[...].T, wo_s[...])
    mid = mid_s[...]
    mid_ref[...] = mid.astype(BF16)
    s2 = lax.rsqrt(jnp.mean(mid * mid, axis=-1, keepdims=True) + EPS)
    n2_ref[...] = (mid * s2 * gains_ref[1:2, :]).astype(BF16)
    io.done(mid_ref, n2_ref)

    io.feed((wg_s, wu_s))

    def ff_body(j, carry):
        io.need_part(j, wg_s, wu_s)
        col = pl.ds(pl.multiple_of(j * CH, CH), CH)
        g = nn(n2_ref[...], wg_s[:, col])
        u = nn(n2_ref[...], wu_s[:, col])
        sq = g * g
        t = jnp.tanh(GELU_A * g * (1.0 + GELU_B * sq))
        half = 0.5 + 0.5 * t
        gel = g * half
        slope = half + (0.5 * GELU_A) * g * (1.0 - t * t) * (1.0 + 3.0 * GELU_B * sq)
        hid_ref[:, col] = (gel * u).astype(BF16)
        a_ref[:, col] = (u * slope).astype(BF16)
        b_ref[:, col] = gel.astype(BF16)
        return carry

    lax.fori_loop(0, hidden // CH, ff_body, 0)
    io.had(wg_s, wu_s)
    io.done(hid_ref, a_ref, b_ref)
    io.need(wd_s)
    mid_s[...] += nn(hid_ref[...], wd_s[...])
    o = mid_s[...]
    out_ref[...] = o.astype(BF16)
    s3 = lax.rsqrt(jnp.mean(o * o, axis=-1, keepdims=True) + EPS)
    n3_ref[...] = (o * s3 * gains_ref[2:3, :]).astype(BF16)
    io.done(out_ref, n3_ref)
    io.need(wp_s)
    pr = nn(n3_ref[...], wp_s[...])
    proj_ref[...] = pr
    emb = (pr * lax.rsqrt(jnp.sum(pr * pr, axis=-1, keepdims=True) + EPS)).astype(BF16)
    if is_doc:
        emb_ref[...] = emb
    else:
        io.need(cand_ref, label_ref)
        ints = pack_ints(cand_ref, label_ref, lens_ref)
        for i in range(emb_ref.shape[0]):
            emb_ref[i, 0:tokens, :] = emb
            emb_ref[i, tokens:, :] = ints


def pack_ints(cand_ref, label_ref, lens_ref):
    count = cand_ref.shape[1]
    eye = lax.broadcasted_iota(jnp.int32, (count, count), 0) == lax.broadcasted_iota(jnp.int32, (count, count), 1)
    lane = lax.broadcasted_iota(jnp.int32, (1, LANE), 1)
    row = lax.broadcasted_iota(jnp.int32, (PACK_INT, 1), 0)
    packed = jnp.zeros((PACK_INT, LANE), F32)
    for a in range(cand_ref.shape[0]):
        values = jnp.where(eye, cand_ref[a:a + 1, :].astype(F32), 0.0)
        column = jnp.sum(values, axis=1, keepdims=True)
        column = jnp.concatenate([column, jnp.zeros((PACK_INT - count, 1), F32)], axis=0)
        column = jnp.where(row == count, label_ref[0:1, a:a + 1].astype(F32), column)
        column = jnp.where(row == count + 1, lens_ref[0:1, a:a + 1].astype(F32), column)
        packed = jnp.where(lane == a, column, packed)
    return packed.astype(BF16)


def forward(x, lens, gains, extra, weights, is_doc, heads, copies=1):
    tokens, width = x.shape
    hidden = weights[4].shape[1]
    proj = weights[7].shape[1]
    outs = [((tokens, width), BF16, "h")] * 3 + [
        ((heads, tokens, tokens), BF16, "h"),
        ((heads, 1, tokens), F32, "v"),
        ((width, tokens), BF16, "h"),
        ((tokens, width), BF16, "h"),
        ((tokens, width), BF16, "h"),
        ((tokens, width), BF16, "h"),
        ((tokens, hidden), BF16, "h"),
        ((tokens, hidden), BF16, "h"),
        ((tokens, hidden), BF16, "h"),
        ((tokens, width), BF16, "h"),
        ((tokens, width), BF16, "h"),
        ((tokens, proj), F32, "h"),
        ((tokens, proj) if is_doc else (copies, tokens + PACK_INT, proj), BF16, "v"),
    ]
    tile = min(tokens, 128)
    scratch = [
        pltpu.VMEM((tokens, tokens), F32),
        pltpu.VMEM((2, tile, SPAN), F32),
        pltpu.VMEM((2, tokens, tokens), F32),
        pltpu.VMEM((2, 2, tokens, tokens), BF16),
        pltpu.VMEM((width, tokens), BF16),
        pltpu.VMEM((tokens, width), F32),
    ]
    steps = weights[4].shape[1] // CH
    streams = [(w, f"h-{steps}" if w.shape == weights[4].shape else "h") for w in weights]
    ins = [(x, "h"), (lens, "h"), (gains, "v")]
    if is_doc:
        kernel = functools.partial(forward_kernel, True)
        ins = ins + [(extra, "h")] + streams
    else:
        outs.append(((heads, 8, SPAN), F32, "h"))

        def kernel(io, x_ref, lens_ref, gains_ref, hot_ref, cand_ref, label_ref, *rest):
            forward_kernel(False, io, x_ref, lens_ref, gains_ref, (hot_ref, cand_ref, label_ref), *rest)

        ins = ins + [(item, "h") for item in extra] + streams
    flops = 2 * tokens * (4 * width * width + 3 * width * hidden + width * proj) + 4 * tokens * tokens * width
    return call(kernel, "doc_forward" if is_doc else "query_forward", ins, outs, scratch, 50, flops, 30 << 20)


def unpack(got_ref, tokens):
    parts = got_ref.shape[0]
    own = 2
    lane = lax.broadcasted_iota(jnp.int32, (1, LANE), 1)
    ints = None
    for i in range(parts):
        block = got_ref[i, tokens:, :].astype(F32)
        if i:
            block = pltpu.roll(block, own * i, 1)
        block = jnp.where((lane // own) == i, block, 0.0)
        ints = block if ints is None else ints + block
    return ints[0:32, :], ints[32:33, :], ints[33:34, :]


def expand_onehot(queries, length):
    col = lax.broadcasted_iota(jnp.int32, (LANE, queries * length), 1)
    row = lax.broadcasted_iota(jnp.int32, (LANE, queries * length), 0)
    return ((col // length) == row).astype(F32)


def token_valid(lens, queries, length):
    hot = expand_onehot(queries, length)
    spread = nn(jnp.broadcast_to(lens, (8, LANE)).astype(BF16), hot.astype(BF16))[0:1]
    place = lax.broadcasted_iota(jnp.int32, (1, queries * length), 1) % length
    return place.astype(F32) < spread, hot


def block_scores(emb_ref, q_s, b):
    t = nt(emb_ref[b * BLK:(b + 1) * BLK, :], q_s[...]) * (1.0 / SHARP)
    row = lax.broadcasted_iota(jnp.int32, (BLK, 1), 0) + b * BLK
    return jnp.where(row < ROW_FILL, t, NEG) if (b + 1) * BLK > ROW_FILL else t


def score_kernel(length, io, got_ref, emb_ref, sums_ref, lse_ref, q_s):
    parts = got_ref.shape[0]
    tokens = q_s.shape[0] // parts
    queries = q_s.shape[0] // length
    for i in range(parts):
        q_s[i * tokens:(i + 1) * tokens, :] = got_ref[i, 0:tokens, :]
    _, _, lens = unpack(got_ref, tokens)
    valid, hot = token_valid(lens, queries, length)
    blocks = emb_ref.shape[0] // BLK
    rows = []
    for b in range(blocks):
        t = block_scores(emb_ref, q_s, b)
        top = jnp.max(t, axis=0, keepdims=True)
        lse = top + jnp.log(jnp.sum(jnp.exp(t - top), axis=0, keepdims=True))
        lse_ref[b:b + 1, :] = lse
        rows.append(jnp.where(valid, SHARP * lse, 0.0))
    rows.append(jnp.zeros((8 - blocks, rows[0].shape[1]), F32))
    sums = lax.dot_general(
        jnp.concatenate(rows, axis=0), hot, (((1,), (1,)), ((), ())), precision=highest, preferred_element_type=F32
    )
    for i in range(parts):
        sums_ref[i] = sums


def scores(got, emb, length):
    parts = got.shape[0]
    tokens = got.shape[1] - PACK_INT
    total = parts * tokens
    return call(
        functools.partial(score_kernel, length),
        "block_sums",
        [(got, "v"), (emb, "v")],
        [((parts, 8, LANE), F32, "v"), ((8, total), F32, "v")],
        [pltpu.VMEM((total, emb.shape[1]), BF16)],
        24,
        2 * emb.shape[0] * total * 128,
        1 << 20,
    )


def loss_kernel(length, io, got_ref, sums_ref, emb_ref, lse_ref, doc_ref, qry_ref, loss_ref, q_s, d_s, s_s):
    parts = got_ref.shape[0]
    tokens = q_s.shape[0] // parts
    queries = q_s.shape[0] // length
    for i in range(parts):
        q_s[i * tokens:(i + 1) * tokens, :] = got_ref[i, 0:tokens, :]
    cand, label, lens = unpack(got_ref, tokens)
    valid, hot = token_valid(lens, queries, length)
    blocks = emb_ref.shape[0] // BLK
    logits = jnp.zeros(cand.shape, F32)
    for i in range(parts):
        for b in range(blocks):
            logits = logits + jnp.where(cand == float(i * blocks + b), sums_ref[i, b:b + 1, :], 0.0)
    logits = SCALE * logits
    top = jnp.max(logits, axis=0, keepdims=True)
    lse = top + jnp.log(jnp.sum(jnp.exp(logits - top), axis=0, keepdims=True))
    choice = lax.broadcasted_iota(jnp.int32, cand.shape, 0).astype(F32) == label
    lane = lax.broadcasted_iota(jnp.int32, (1, LANE), 1)
    picked = jnp.sum(jnp.where(choice, logits, 0.0), axis=0, keepdims=True)
    each = jnp.where(lane < queries, lse - picked, 0.0)
    loss_ref[...] = jnp.broadcast_to(jnp.sum(each, axis=1, keepdims=True), (1, LANE))
    dlogits = SCALE * (jnp.exp(logits - lse) - jnp.where(choice, 1.0, 0.0))
    me = lax.axis_index("dp").astype(jnp.int32)
    rows = []
    for b in range(blocks):
        mine = (me * blocks + b).astype(F32)
        rows.append(jnp.sum(jnp.where(cand == mine, dlogits, 0.0), axis=0, keepdims=True))
    rows.append(jnp.zeros((8 - blocks, LANE), F32))
    spread = jnp.dot(jnp.concatenate(rows, axis=0), hot, precision=highest, preferred_element_type=F32)
    for b in range(blocks):
        t = block_scores(emb_ref, q_s, b)
        weight = jnp.where(valid, spread[b:b + 1, :], 0.0)
        d_s[b * BLK:(b + 1) * BLK, :] = (weight * jnp.exp(t - lse_ref[b:b + 1, :])).astype(BF16)
    doc_ref[...] = nn(d_s[...], q_s[...])
    s_s[...] = d_s[...].T
    qry_ref[...] = nn(s_s[...], emb_ref[...]).reshape(qry_ref.shape)


def retrieval_back(got, sums, emb, lse, length):
    parts = got.shape[0]
    tokens = got.shape[1] - PACK_INT
    total = parts * tokens
    docs, proj = emb.shape
    return call(
        functools.partial(loss_kernel, length),
        "retrieval_back",
        [(got, "v"), (sums, "v"), (emb, "v"), (lse, "v")],
        [((docs, proj), F32, "v"), ((parts, tokens, proj), F32, "v"), ((1, LANE), F32, "v")],
        [pltpu.VMEM((total, proj), BF16), pltpu.VMEM((docs, total), BF16), pltpu.VMEM((total, docs), BF16)],
        32,
        6 * docs * total * proj,
        2 << 20,
    )


def chain_kernel(
    io, demb_ref, gains_ref, proj_ref, wp_s, out_ref, wd_s, a_ref, b_ref, wg_s, wu_s, mid_ref, wo_s,
    dpj_ref, dbr_ref, dg_ref, du_ref, datt_ref, dmid_ref, dmix_ref, acc_s,
):
    hidden = a_ref.shape[1]
    if len(demb_ref.shape) == 3:
        dy = demb_ref[0]
        for i in range(1, demb_ref.shape[0]):
            dy = dy + demb_ref[i]
    else:
        dy = demb_ref[...]
    io.need(proj_ref)
    pr = proj_ref[...]
    r = lax.rsqrt(jnp.sum(pr * pr, axis=-1, keepdims=True) + EPS)
    unit = pr * r
    dpj_ref[...] = (r * (dy - unit * jnp.sum(dy * unit, axis=-1, keepdims=True))).astype(BF16)
    io.done(dpj_ref)
    io.need(wp_s, out_ref)
    dn3 = nt(dpj_ref[...], wp_s[...])
    dout = norm_back(out_ref[...].astype(F32), gains_ref[2:3, :], dn3)
    dbr_ref[...] = dout.astype(BF16)
    io.done(dbr_ref)

    io.feed((wd_s, a_ref, b_ref, wg_s, wu_s))

    def body(j, carry):
        io.need_part(j, wd_s, a_ref, b_ref)
        col = pl.ds(pl.multiple_of(j * CH, CH), CH)
        dh = nt(dbr_ref[...], wd_s[col, :])
        dg_ref[:, col] = (dh * a_ref[:, col].astype(F32)).astype(BF16)
        du_ref[:, col] = (dh * b_ref[:, col].astype(F32)).astype(BF16)
        return carry

    lax.fori_loop(0, hidden // CH, body, 0)
    io.had(wd_s, a_ref, b_ref)
    io.done(dg_ref, du_ref)
    io.need(wg_s, wu_s)
    acc_s[...] = nt(dg_ref[...], wg_s[...]) + nt(du_ref[...], wu_s[...])
    io.need(mid_ref)
    dmid = dout + norm_back(mid_ref[...].astype(F32), gains_ref[1:2, :], acc_s[...])
    dmid_ref[...] = dmid.astype(BF16)
    datt_ref[...] = dmid.astype(BF16)
    io.done(dmid_ref, datt_ref)
    io.need(wo_s)
    dmix_ref[...] = nt(datt_ref[...], wo_s[...]).astype(BF16)


def chain_ins(demb, gains, proj, wp, out, wd, a, b, wg, wu, mid, wo):
    steps = a.shape[1] // CH
    plain = lambda *items: [(item, "h") for item in items]
    parts = [(wd, f"h{steps}")] + [(item, f"h-{steps}") for item in (a, b)]
    return [(demb, "v"), (gains, "v")] + plain(proj, wp, out) + parts + plain(wg, wu, mid, wo)


def chain(demb, proj, out, mid, a, b, gains, wp, wd, wg, wu, wo, name):
    tokens, width = out.shape
    hidden = a.shape[1]
    return call(
        chain_kernel,
        name,
        chain_ins(demb, gains, proj, wp, out, wd, a, b, wg, wu, mid, wo),
        [
            (proj.shape, BF16, "h"),
            ((tokens, width), BF16, "h"),
            ((tokens, hidden), BF16, "h"),
            ((tokens, hidden), BF16, "h"),
            ((tokens, width), BF16, "h"),
            ((tokens, width), BF16, "h"),
            ((tokens, width), BF16, "h"),
        ],
        [pltpu.VMEM((tokens, width), F32)],
        44,
        2 * tokens * (width * width + 3 * width * hidden + width * 128),
        30 << 20,
    )


def attention_back_kernel(
    io, k_ref, v_ref, q_ref, dmix_ref, mixt_ref, il_ref, e_ref, dqkv_ref, diag_ref, far_ref,
    dqt_s, p_s, ds_s, strip_s, dk_s, dv_s,
):
    tokens, width = q_ref.shape
    tile = min(tokens, 128)
    wide = min(tokens, 256)
    blocks = tokens // tile
    io.feed((k_ref, v_ref, q_ref, dmix_ref, mixt_ref, e_ref))

    def pair_body(p, carry):
        io.need_part(p, k_ref, v_ref, q_ref, dmix_ref, mixt_ref, e_ref)
        col = pl.ds(pl.multiple_of(p * LANE, LANE), LANE)
        kt = k_ref[:, col].T
        dmixt = dmix_ref[:, col].T
        for s in range(2):
            h = 2 * p + s
            vp = half_lanes(v_ref[:, col], s)
            dm = half_lanes(dmix_ref[:, col], s)
            qm = half_lanes(q_ref[:, col], s)
            rows = pl.ds(pl.multiple_of(p * LANE + 64 * s, 64), 64)
            strip_s[...] = jnp.zeros_like(strip_s)
            far_low = jnp.zeros((8, LANE), F32)
            far_high = jnp.zeros((8, LANE), F32)
            for qc in range(tokens // wide):
                cols = slice(qc * wide, (qc + 1) * wide)
                dt = dmixt[:, cols]
                delta = jnp.sum(
                    dmixt[64 * s:64 * s + 64, cols].astype(F32) * mixt_ref[rows, cols].astype(F32), axis=0, keepdims=True
                )
                inverse = il_ref[h, :, cols]
                for kb in range(blocks):
                    ks = slice(kb * tile, (kb + 1) * tile)
                    dp = nn(vp[ks], dt)
                    prob = e_ref[h, ks, cols].astype(F32) * inverse
                    p_s[ks, :] = prob.astype(BF16)
                    ds = (prob * (dp - delta)).astype(BF16)
                    ds_s[ks, :] = ds
                    kept = ds.astype(F32)
                    for qs in range(wide // tile):
                        d = kb - (qc * (wide // tile) + qs)
                        t = kept[:, qs * tile:(qs + 1) * tile]
                        if abs(d) <= 1:
                            lo = (1 - d) * 128
                            strip_s[0:tile, lo:lo + tile] += t
                        else:
                            part = t[0:8]
                            for g in range(1, tile // 8):
                                part = part + t[8 * g:8 * g + 8]
                            if d > 0:
                                far_high = far_high + part
                            else:
                                far_low = far_low + part
                dv = nn(p_s[...], dm[cols])
                dk = nn(ds_s[...], qm[cols])
                if s == 0 and qc == 0:
                    dv_s[...] = dv
                    dk_s[...] = dk
                else:
                    dv_s[...] += dv
                    dk_s[...] += dk
                dqt_s[rows, cols] = nn(kt[64 * s:64 * s + 64], ds_s[...]).astype(BF16)
            fold = strip_s[...]
            size = strip_s.shape[0]
            while size > 8:
                size //= 2
                fold = fold[:size] + pltpu.roll(fold[size:], SPAN - size, 1)
            diag_ref[h] = fold
            far_ref[h, 0:8, :] = far_low
            far_ref[h, 8:16, :] = far_high
        kcol = pl.ds(pl.multiple_of(width + p * LANE, LANE), LANE)
        vcol = pl.ds(pl.multiple_of(2 * width + p * LANE, LANE), LANE)
        dqkv_ref[:, kcol] = dk_s[...].astype(BF16)
        dqkv_ref[:, vcol] = dv_s[...].astype(BF16)
        return carry

    lax.fori_loop(0, width // LANE, pair_body, 0)
    io.had(k_ref, v_ref, q_ref, dmix_ref, mixt_ref, e_ref)
    dqkv_ref[:, 0:width] = dqt_s[...].T


def attention_ins(q, k, v, e, il, mixt, dmix):
    pairs = q.shape[1] // LANE
    return [(item, "v") for item in (k, v, q, dmix, mixt, il, e)]


def attention_outs(q, heads):
    tokens, width = q.shape
    return [((tokens, 3 * width), BF16, "v"), ((heads, 8, SPAN), F32, "v"), ((heads, 16, LANE), F32, "v")]


def attention_scratch(q):
    tokens, width = q.shape
    tile, wide = min(tokens, 128), min(tokens, 256)
    return [
        pltpu.VMEM((width, tokens), BF16),
        pltpu.VMEM((tokens, wide), BF16),
        pltpu.VMEM((tokens, wide), BF16),
        pltpu.VMEM((tile, SPAN), F32),
        pltpu.VMEM((tokens, LANE), F32),
        pltpu.VMEM((tokens, LANE), F32),
    ]


def attention_back(q, k, v, e, il, mixt, dmix, name):
    tokens, width = q.shape
    return call(
        attention_back_kernel,
        name,
        attention_ins(q, k, v, e, il, mixt, dmix),
        attention_outs(q, e.shape[0]),
        attention_scratch(q),
        9,
        10 * tokens * tokens * width,
        16 << 20,
    )


def input_kernel(io, gains_ref, *refs):
    kinds = (len(refs) - 3) // 4
    reads, weights, writes = refs[:3 * kinds], refs[3 * kinds:3 * kinds + 3], refs[3 * kinds + 3:]
    for kind in range(kinds):
        dqkv_ref, x_ref, dmid_ref = reads[3 * kind:3 * kind + 3]
        width = x_ref.shape[1]
        io.need(dqkv_ref)
        total = None
        for i, w in enumerate(weights):
            io.need(w)
            part = nt(dqkv_ref[:, i * width:(i + 1) * width], w[...])
            total = part if total is None else total + part
        io.need(x_ref, dmid_ref)
        writes[kind][...] = dmid_ref[...].astype(F32) + norm_back(x_ref[...].astype(F32), gains_ref[0:1, :], total)
        io.done(writes[kind])


def input_back(gains, kinds, weights, name):
    width = weights[0].shape[0]
    tokens = sum(x.shape[0] for _, x, _ in kinds)
    return call(
        input_kernel,
        name,
        [(gains, "v")]
        + [(item, kind) for dqkv, x, dmid in kinds for item, kind in ((dqkv, "v"), (x, "h"), (dmid, "h"))]
        + [(w, "h") for w in weights],
        [(x.shape, F32, "h") for _, x, _ in kinds],
        [],
        32,
        6 * tokens * width * width,
        8 << 20,
    )


def put_rows(buf, value, per, offset, lanes, extra=None):
    for j in range(buf.shape[1]):
        for core in range(2):
            rows = slice((2 * j + core) * per, (2 * j + core + 1) * per)
            pieces = [value[rows, lo:lo + 256] for lo in lanes]
            if extra is not None:
                pieces.append(extra(rows))
            block = jnp.concatenate(pieces, axis=0) if len(pieces) > 1 else pieces[0]
            buf[core, j, pl.ds(offset, block.shape[0]), :] = block.astype(BF16)


def push_rows(io, buf, own_ref, send_ref, start, size, shift=0):
    core = core_index()
    rows, there = pl.ds(start, size), pl.ds(start + shift, size)
    for ref, side in ((send_ref, 1 - core), (own_ref, core)):
        io.push(buf.at[side, :, rows], ref.at[:, there])


def halves_buffer(count, rows):
    return pltpu.VMEM((2, count, rows, 256), BF16)


def core_index():
    return (lax.axis_index("grp") % 2).astype(jnp.int32)


def halves(count, rows):
    return [((count, rows, 256), BF16, "a")] * 2


def down_grad_kernel(
    io, demb_ref, gains_ref, proj_ref, wp_s, out_ref, wd_s, a_ref, b_ref, wg_s, wu_s, mid_ref, wo_s,
    hid_ref, hidq_ref, dbr_ref, mixt_ref, mixtq_ref, datt_ref, n3_ref, n3q_ref, dpj_ref,
    dg_ref, du_ref, dmid_ref, dmix_ref, own_ref, send_ref,
    acc1_s, dpjq_s, dbrq_s, dattq_s, hidt_s, hidtq_s, buf_s,
):
    chain_kernel(
        io, demb_ref, gains_ref, proj_ref, wp_s, out_ref, wd_s, a_ref, b_ref, wg_s, wu_s, mid_ref, wo_s,
        dpjq_s, dbrq_s, dg_ref, du_ref, dattq_s, dmid_ref, dmix_ref, acc1_s,
    )
    io.done(dmix_ref)
    hidden, width = hid_ref.shape[1], dbr_ref.shape[1]
    count = own_ref.shape[0]
    per, per_down = width // (2 * count), hidden // (2 * count)
    io.need(hid_ref, hidq_ref)
    hidt_s[...] = hid_ref[...].T
    hidtq_s[...] = hidq_ref[...].T
    io.need(dbr_ref)
    for i in range(width // 256):
        col = slice(i * 256, (i + 1) * 256)
        value = nn(hidt_s[...], dbr_ref[:, col]) + nn(hidtq_s[...], dbrq_s[:, col])
        put_rows(buf_s, value, per_down, i * per_down, (0,))
        push_rows(io, buf_s, own_ref, send_ref, i * per_down, per_down)
    base = (width // 256) * per_down
    io.need(mixt_ref, mixtq_ref, datt_ref, n3_ref, n3q_ref, dpj_ref)
    value = nn(mixt_ref[...], datt_ref[...]) + nn(mixtq_ref[...], dattq_s[...])
    put_rows(buf_s, value, per, base, (0, 256))
    push_rows(io, buf_s, own_ref, send_ref, base, 2 * per)
    base = base + 2 * per
    proj = nn(n3_ref[...].T, dpj_ref[...]) + nn(n3q_ref[...].T, dpjq_s[...])

    def proj_rows(rows):
        return jnp.concatenate([proj[rows], jnp.zeros((per, LANE), F32)], axis=1)

    put_rows(buf_s, value, per, base, (512,), extra=proj_rows)
    push_rows(io, buf_s, own_ref, send_ref, base, 2 * per)


def down_grads(query, doc, count):
    (demb, proj, out, mid, a, b, gains, wp, wd, wg, wu, wo), (hidq, mixtq, n3q) = query
    hid, dbr, mixt, datt, n3, dpj = doc
    tokens, hidden = hid.shape
    qtokens, width = out.shape
    per, per_down = width // (2 * count), hidden // (2 * count)
    plain = [(item, "h") for item in (hid, hidq, dbr, mixt, mixtq, datt, n3, n3q, dpj)]
    return call(
        down_grad_kernel,
        "query_ff_back_down_grads",
        chain_ins(demb, gains, proj, wp, out, wd, a, b, wg, wu, mid, wo) + plain,
        [
            ((qtokens, hidden), BF16, "h"),
            ((qtokens, hidden), BF16, "h"),
            ((qtokens, width), BF16, "h"),
            ((qtokens, width), BF16, "h"),
        ]
        + halves(count, (width // 256) * per_down + 4 * per),
        [
            pltpu.VMEM((qtokens, width), F32),
            pltpu.VMEM(proj.shape, BF16),
            pltpu.VMEM((qtokens, width), BF16),
            pltpu.VMEM((qtokens, width), BF16),
            pltpu.VMEM((hidden, tokens), BF16),
            pltpu.VMEM((hidden, qtokens), BF16),
            halves_buffer(count, (width // 256) * per_down + 4 * per),
        ],
        40,
        2 * (tokens + 256) * (width * width + width * hidden),
        24 << 20,
    )


def gate_grad_kernel(which, io, n2_ref, n2q_ref, d, dq, *refs):
    own_ref, send_ref, n2t_s, n2tq_s, buf_s = refs[-5:]
    width, hidden = n2_ref.shape[1], d.shape[1]
    count, rows = own_ref.shape[:2]
    per = width // (2 * count)
    io.need(n2_ref, n2q_ref)
    n2t_s[...] = n2_ref[...].T
    n2tq_s[...] = n2q_ref[...].T
    io.need(dq)
    io.feed((d,))
    for i in range(hidden // CH):
        io.need_part(i, d)
        col = slice(i * CH, (i + 1) * CH)
        value = nn(n2t_s[...], d[:, col]) + nn(n2tq_s[...], dq[:, col])
        for lo in range(0, CH, 512):
            at = (i * CH + lo) // 256 * per
            put_rows(buf_s, value, per, at, (lo, lo + 256))
            push_rows(io, buf_s, own_ref, send_ref, at, 2 * per, which * (rows // 2))
    io.had(d)


def gate_grads(which, n2, n2q, d, dq, count, begun=()):
    tokens, width = n2.shape
    qtokens, hidden = dq.shape
    per = width // (2 * count)
    rows = 2 * (hidden // 256) * per
    return call(
        functools.partial(gate_grad_kernel, which),
        ("gate_grads", "up_grads")[which],
        [(n2, "h"), (n2q, "h"), (d, f"h-{hidden // CH}"), (dq, "h")] + [(item, "b") for item in begun],
        halves(count, rows),
        [
            pltpu.VMEM((width, tokens), BF16),
            pltpu.VMEM((width, qtokens), BF16),
            halves_buffer(count, rows // 2),
        ],
        18,
        2 * (tokens + 256) * width * hidden,
        16 << 20,
        {4: 0, 5: 1} if begun else None,
    )


def qkv_grad_kernel(
    io, k_ref, v_ref, q_ref, dmix_ref, mixt_ref, il_ref, e_ref, n1_ref, n1q_ref, d_ref,
    diagd_ref, fard_ref, hot_ref, loss_ref, dq_ref, diag_ref, far_ref, own_ref, send_ref, *rest,
):
    own_parts = lax.axis_size("dp")
    n1t_s, n1tq_s, buf_s = rest[-3:]
    attention_back_kernel(
        io, k_ref, v_ref, q_ref, dmix_ref, mixt_ref, il_ref, e_ref, dq_ref, diag_ref, far_ref, *rest[:-3]
    )
    io.done(dq_ref)
    width = n1_ref.shape[1]
    count = own_ref.shape[0]
    per = width // (2 * count)
    io.need(n1_ref, n1q_ref)
    n1t_s[...] = n1_ref[...].T
    n1tq_s[...] = n1q_ref[...].T
    io.need(d_ref)
    steps = (3 * width) // 512
    value = nn(n1t_s[...], d_ref[...]) + nn(n1tq_s[...], dq_ref[...])
    for i in range(steps):
        put_rows(buf_s, value, per, i * 2 * per, (i * 512, i * 512 + 256))
        push_rows(io, buf_s, own_ref, send_ref, i * 2 * per, 2 * per)
    io.need(hot_ref)
    heads = diag_ref.shape[0]
    buckets = hot_ref.shape[0]
    table = jnp.zeros((heads, buckets), F32)
    for r in range(8):
        both = diagd_ref[:, r, :] + diag_ref[:, r, :]
        table = table + lax.dot_general(
            both, hot_ref[:, r * SPAN:(r + 1) * SPAN].astype(F32), (((1,), (1,)), ((), ())),
            precision=highest, preferred_element_type=F32,
        )
    far = fard_ref[...] + far_ref[...]
    low = jnp.sum(jnp.sum(far[:, 0:8, :], axis=1), axis=-1, keepdims=True)
    high = jnp.sum(jnp.sum(far[:, 8:16, :], axis=1), axis=-1, keepdims=True)
    column = lax.broadcasted_iota(jnp.int32, (1, buckets), 1)
    table = table + jnp.where(column == buckets // 2 - 1, low, 0.0) + jnp.where(column == buckets - 1, high, 0.0)
    table = jnp.concatenate([table, jnp.zeros((16 - heads, buckets), F32)], axis=0)
    loss = jnp.broadcast_to(loss_ref[...] * (1.0 / own_parts), (8, LANE))
    spare = jnp.concatenate([table[0:8], table[8:16], jnp.zeros((8, LANE - 2 * buckets), F32), loss], axis=1)
    put_rows(buf_s, value, per, steps * 2 * per, (steps * 512,), extra=lambda rows: spare)
    push_rows(io, buf_s, own_ref, send_ref, steps * 2 * per, per + 8)


def qkv_grads(query, n1, n1q, d, diag, far, hot, loss, count):
    tokens, width = n1.shape
    per = width // (2 * count)
    return call(
        qkv_grad_kernel,
        "query_attention_back_qkv_grads",
        attention_ins(*query)
        + [(n1, "h"), (n1q, "h"), (d, "v")]
        + [(diag, "v"), (far, "v"), (hot, "h"), (loss, "v")],
        attention_outs(query[0], query[3].shape[0]) + halves(count, 9 * per + 8),
        attention_scratch(query[0])
        + [
            pltpu.VMEM((width, tokens), BF16),
            pltpu.VMEM((width, n1q.shape[0]), BF16),
            halves_buffer(count, 9 * per + 8),
        ],
        24,
        2 * (tokens + 256) * 3 * width * width,
        10 << 20,
    )


def after(values, *deps):
    return lax.optimization_barrier((values, deps))[0]


def position(n_dp):
    dp, grp = lax.axis_index("dp").astype(jnp.int32), lax.axis_index("grp").astype(jnp.int32)
    return dp // 2, dp % 2, grp // 2


def slices(io_sems, moves):
    copies = [pltpu.make_async_copy(src, dst, io_sems.at[i]) for i, (src, dst) in enumerate(moves)]
    for copy in copies:
        copy.start()
    return copies


class Halves:
    def __init__(self, rows):
        self.rows, self.cut = rows, (rows // 32) * 16

    def sizes(self):
        return self.cut, self.rows - self.cut

    def spans(self):
        return pl.ds(0, self.cut), pl.ds(self.cut, self.rows - self.cut)


def first_kernel(n_dp, halves, io, own_ref, got_ref, x_ref, y_ref, ox_s, gx_s, oy_s, gy_s, sems):
    _, x, y = position(n_dp)
    top, low = halves.spans()
    moves = []
    for ref, a, b in ((own_ref, ox_s, oy_s), (got_ref, gx_s, gy_s)):
        moves += [(ref.at[:, 1 - x, :, top], a), (ref.at[:, :, 1 - y, low], b)]
    copies = slices(sems, moves)
    for i, (a, b, out) in enumerate(((ox_s, gx_s, x_ref), (oy_s, gy_s, y_ref))):
        copies[i].wait()
        copies[i + 2].wait()
        out[...] = (a[...].astype(F32) + b[...].astype(F32)).astype(BF16)
        io.done(out)


def pair_rows(n_dp, halves, flip, own_ref, got_ref, gx_ref, gy_ref, bufs, sems):
    _, x, y = position(n_dp)
    top, low = halves.spans()
    yt, xl = (1 - y, 1 - x) if flip else (y, x)
    ot_s, gt_s, rt_s, ol_s, gl_s, rl_s = bufs
    copies = slices(sems, [
        (own_ref.at[:, x, yt, top], ot_s), (got_ref.at[:, x, yt, top], gt_s), (gx_ref.at[:, yt], rt_s),
        (own_ref.at[:, xl, y, low], ol_s), (got_ref.at[:, xl, y, low], gl_s), (gy_ref.at[:, xl], rl_s),
    ])
    out = []
    for i in (0, 3):
        for copy in copies[i:i + 3]:
            copy.wait()
        a, b, c = bufs[i:i + 3]
        out.append(a[...].astype(F32) + b[...].astype(F32) + c[...].astype(F32))
    return out


def second_kernel(n_dp, halves, io, own_ref, got_ref, gx_ref, gy_ref, y_ref, x_ref, *refs):
    for out, value in zip((y_ref, x_ref), pair_rows(n_dp, halves, True, own_ref, got_ref, gx_ref, gy_ref, refs[:-1], refs[-1])):
        out[...] = value.astype(BF16)
        io.done(out)


def cross_kernel(n_dp, halves, io, own_ref, got_ref, xy_ref, x_ref, y_ref, own_s, got_s, sems):
    _, x, y = position(n_dp)
    moves = []
    for i, (xx, yy) in enumerate(((1 - x, 1 - y), (1 - x, y), (x, 1 - y))):
        moves += [(own_ref.at[:, xx, yy], own_s.at[i]), (got_ref.at[:, xx, yy], got_s.at[i])]
    copies = slices(sems, moves)
    for i, out in enumerate((xy_ref, x_ref, y_ref)):
        copies[2 * i].wait()
        copies[2 * i + 1].wait()
        out[...] = (own_s[i].astype(F32) + got_s[i].astype(F32)).astype(BF16)
        io.done(out)


def leave(z, line_s, outs, total_ref, io):
    nz = line_s.shape[0]
    if not outs:
        total_ref[...] = line_s[...].astype(BF16)
        return
    for k, out in enumerate(outs, 1):
        out[...] = line_s[(z + k) % nz].astype(BF16)
        io.done(out)
    total_ref[...] = line_s[z]


def cross_line_kernel(n_dp, halves, io, own_ref, got_ref, xy_ref, x_ref, y_ref, *refs):
    outs, total_ref, (line_s, own_s, got_s, sems) = refs[:-5], refs[-5], refs[-4:]
    z, x, y = position(n_dp)
    copies = slices(sems, [(own_ref.at[:, x, y], own_s), (got_ref.at[:, x, y], got_s)])
    for copy in copies:
        copy.wait()
    io.need(xy_ref, x_ref, y_ref)
    line_s[...] = own_s[...].astype(F32) + got_s[...].astype(F32) + xy_ref[...].astype(F32)
    line_s[...] += x_ref[...].astype(F32) + y_ref[...].astype(F32)
    leave(z, line_s, outs, total_ref, io)


def line_kernel(n_dp, halves, io, own_ref, got_ref, gx_ref, gy_ref, y_ref, x_ref, *refs):
    outs, total_ref, line_s, bufs, sems = refs[:-9], refs[-9], refs[-8], refs[-7:-1], refs[-1]
    z, _, _ = position(n_dp)
    top, low = pair_rows(n_dp, halves, False, own_ref, got_ref, gx_ref, gy_ref, bufs, sems)
    io.need(x_ref, y_ref)
    line_s[:, 0:halves.cut] = top + y_ref[...].astype(F32)
    line_s[:, halves.cut:] = low + x_ref[...].astype(F32)
    leave(z, line_s, outs, total_ref, io)


class Batch:
    def __init__(self, own, send, n_dp, n_grp, name):
        self.n_dp, self.n_grp, self.nz, self.name = n_dp, n_grp, n_dp // 2, name
        self.rows, self.cols = own.shape[1:]
        self.halves = Halves(self.rows)
        self.own = own
        self.got = lax.ppermute(send, "grp", [(i, i ^ 1) for i in range(n_grp)])

    def both(self):
        grid = lambda a: (a.reshape(self.nz, 2, 2, self.rows, self.cols), "r")
        own, kind = grid(self.own)
        return [(pltpu.with_memory_space_constraint(own, pltpu.HBM), kind), grid(self.got)]

    def along_x(self, array):
        return lax.ppermute(array, "dp", [(d, d ^ 1) for d in range(self.n_dp)])

    def along_y(self, array):
        return lax.ppermute(array, "grp", [(g, g ^ 2) for g in range(self.n_grp)])

    def run(self, kernel, step, ins, outs, scratch):
        body = functools.partial(kernel, self.n_dp, self.halves)
        return call(body, self.name + step, ins, outs, scratch, 24, 0, 0)

    def first(self):
        sizes = [(self.nz, 2, n, self.cols) for n in self.halves.sizes()]
        bufs = [pltpu.VMEM(size, BF16) for size in sizes for _ in range(2)]
        outs = [(size, BF16, "h") for size in sizes]
        sent = self.run(first_kernel, "_first", self.both(), outs, bufs + [pltpu.SemaphoreType.DMA((4,))])
        self.back1 = self.along_x(sent[0]), self.along_y(sent[1])
        return tuple(sent)

    def second_bufs(self):
        return [pltpu.VMEM((self.nz, n, self.cols), BF16) for n in self.halves.sizes() for _ in range(3)] + [
            pltpu.SemaphoreType.DMA((6,))
        ]

    def second(self):
        outs = [((self.nz, n, self.cols), BF16, "h") for n in self.halves.sizes()]
        ins = self.both() + [(a, "r") for a in self.back1]
        sent = self.run(second_kernel, "_second", ins, outs, self.second_bufs())
        self.back2 = self.along_y(sent[0]), self.along_x(sent[1])
        return tuple(sent)

    def cross(self):
        n_dp, n_grp = self.n_dp, self.n_grp
        piece = (self.nz, self.rows, self.cols)
        bufs = [pltpu.VMEM((3, *piece), BF16)] * 2 + [pltpu.SemaphoreType.DMA((6,))]
        sent = self.run(cross_kernel, "_cross", self.both(), [(piece, BF16, "h")] * 3, bufs)
        across = [(d * n_grp + g, (d ^ 1) * n_grp + (g ^ 2)) for d in range(n_dp) for g in range(n_grp)]
        self.back1 = ()
        self.back2 = lax.ppermute(sent[0], ("dp", "grp"), across), self.along_x(sent[1]), self.along_y(sent[2])
        return tuple(sent)

    def line(self, together=False):
        n_dp, nz = self.n_dp, self.nz
        piece, part = (nz, self.rows, self.cols), (self.rows, self.cols)
        outs = [(piece, BF16, "h")] if together else [(part, BF16, "h")] * (nz - 1) + [(part, F32, "v")]
        ins = self.both() + [(a, "r") for a in self.back1] + [(a, "v") for a in self.back2]
        if self.back1:
            kernel, bufs = line_kernel, self.second_bufs()
        else:
            kernel, bufs = cross_line_kernel, [pltpu.VMEM(piece, BF16)] * 2 + [pltpu.SemaphoreType.DMA((2,))]
        *sent, total = self.run(kernel, "_line", ins, outs, [pltpu.VMEM(piece, F32)] + bufs)
        if together:
            groups = [[2 * z + x for z in range(nz)] for x in range(2)]
            self.parts = [lax.all_to_all(total, "dp", 0, 0, tiled=True, axis_index_groups=groups)]
            return (total,)
        self.parts = [total] + [
            lax.ppermute(one, "dp", [(d, (d + 2 * k) % n_dp) for d in range(n_dp)]) for k, one in enumerate(sent, 1)
        ]
        return tuple(sent)


def weight_rows(weights, start):
    aligned = (start // 16) * 16
    return start - aligned, [w.at[pl.ds(pl.multiple_of(aligned, 16), 32)] for w in weights]


def finish_kernel(n_parts, places, gain_row, scale, io, *refs):
    total, gains_ref, rest = refs[:n_parts], refs[n_parts], refs[n_parts + 1:]
    n_out, n_weights = len(places), len(gain_row[1])
    weights, rest = rest[:n_weights], rest[n_weights:]
    outs, rest = rest[:n_out], rest[n_out:]
    gain_ref, rest = rest[0], rest[1:]
    extra, rest = (rest[:2], rest[2:]) if scale else ((), rest)
    sum_s, wide_s, bufs, sems = rest[0], rest[1], rest[2:-1], rest[-1]
    device = lax.axis_index("dp") * lax.axis_size("grp") + lax.axis_index("grp")
    per = outs[gain_row[1][0]].shape[0]
    start = device.astype(jnp.int32) * per
    shift, sources = weight_rows(weights, start)
    copies = slices(sems, list(zip(sources, bufs)))
    io.need(*total)
    if len(total) == 1:
        value = total[0][0].astype(F32)
        for i in range(1, total[0].shape[0]):
            value = value + total[0][i].astype(F32)
    else:
        value = total[0][...].astype(F32)
        for one in total[1:]:
            value = value + one[...].astype(F32)
    sum_s[...] = value
    for out, at in zip(outs, places):
        rows, width = out.shape
        for i in range(-(-width // 256)):
            cols = min(256, width - i * 256)
            out[:, i * 256:i * 256 + cols] = sum_s[at + i * rows:at + (i + 1) * rows, 0:cols]
    inner = jnp.zeros((per, 1), F32)
    for which, copy, buf in zip(gain_row[1], copies, bufs):
        copy.wait()
        width = buf.shape[1]
        wide_s[:, 0:width] = buf[...].astype(F32)
        mine = wide_s[pl.ds(pl.multiple_of(shift, 8), per), 0:width]
        inner = inner + jnp.sum(mine * outs[which][...], axis=-1, keepdims=True)
    lane = lax.broadcasted_iota(jnp.int32, (per, gains_ref.shape[1]), 1)
    row = lax.broadcasted_iota(jnp.int32, (per, gains_ref.shape[1]), 0)
    gain = jnp.sum(jnp.where(lane == row + start, gains_ref[gain_row[0]:gain_row[0] + 1, :], 0.0), axis=-1, keepdims=True)
    lane, row = lane[:, 0:LANE], row[:, 0:LANE]
    gain_ref[...] = jnp.sum(jnp.where(lane == row, inner / gain, 0.0), axis=0, keepdims=True)[:, 0:per]
    if scale:
        table_ref, loss_ref = extra
        heads, buckets = table_ref.shape
        spare = sum_s[sum_s.shape[0] - 8:, :]
        table = jnp.concatenate([spare[:, 0:buckets], spare[:, buckets:2 * buckets]], axis=0)
        table_ref[...] = table[0:heads]
        loss_ref[...] = spare[0:1, LANE:LANE + 1] * scale


def finish(batch, places, shapes, gain_row, gains, weights, table=None, scale=0.0):
    per = shapes[gain_row[1][0]][0]
    outs = [(shape, F32, "h") for shape in shapes] + [((1, per), F32, "v")]
    if table is not None:
        outs += [(table, F32, "v"), ((1, 1), F32, "v")]
    width = max(w.shape[1] for w in weights)
    return call(
        functools.partial(finish_kernel, len(batch.parts), places, gain_row, scale),
        batch.name + "_finish",
        [(one, "v") for one in batch.parts] + [(gains, "v")] + [(pltpu.with_memory_space_constraint(w, pltpu.HBM), "r") for w in weights],
        outs,
        [pltpu.VMEM((batch.rows, batch.cols), F32), pltpu.VMEM((32, width), F32)]
        + [pltpu.VMEM((32, w.shape[1]), BF16) for w in weights]
        + [pltpu.SemaphoreType.DMA((len(weights),))],
        16,
        0,
        0,
    )


def on_device(
    n_dp, n_grp, doc_tokens, doc_lengths, query_tokens, query_lengths, candidates, labels, gain_attn, w_query, w_key,
    w_value, w_out, bias_table, gain_ffn, w_gate, w_up, w_down, gain_final, w_proj,
):
    doc_rows, doc_len, width = doc_tokens.shape
    query_rows, query_len = query_tokens.shape[:2]
    hidden = w_gate.shape[1]
    bucket_total, heads = bias_table.shape
    devices = n_dp * n_grp
    axes = ("dp", "grp")
    x_doc = doc_tokens.reshape(doc_len, width)
    x_qry = query_tokens.reshape(query_rows * query_len, width)
    which = lax.broadcasted_iota(jnp.int32, (24, width), 0)
    gains = jnp.where(which == 0, gain_attn[None], jnp.where(which == 1, gain_ffn[None], gain_final[None]))
    table = jnp.pad(bias_table.T, ((8, 16 - heads), (0, width - bucket_total)))
    gains = jnp.where(which < 8, gains, table).astype(F32)
    weights = (w_query, w_key, w_value, w_out, w_gate, w_up, w_down, w_proj)
    hot = jnp.asarray(strip_onehot(), BF16)
    (q_q, q_k, q_v, q_e, q_il, q_mixt, q_mid, q_n1, q_n2, q_hid, q_a, q_b, q_out, q_n3, q_proj, packed, base) = forward(
        x_qry, query_lengths[None], gains, (hot, candidates, labels[None]), weights, False, heads, n_dp
    )
    got = lax.all_to_all(packed, "dp", 0, 0, tiled=True)
    (d_q, d_k, d_v, d_e, d_il, d_mixt, d_mid, d_n1, d_n2, d_hid, d_a, d_b, d_out, d_n3, d_proj, emb) = forward(
        x_doc, doc_lengths, gains, base, weights, True, heads
    )
    sums, lse = scores(got, emb, query_len)
    sums = lax.all_to_all(sums, "dp", 0, 0, tiled=True)
    demb_doc, demb_part, loss_group = retrieval_back(
        got, sums, emb, lse, query_len
    )
    demb_qry = lax.all_to_all(demb_part, "dp", 0, 0, tiled=True)
    back = (w_proj, w_down, w_gate, w_up, w_out)
    d_dpj, d_dbr, d_dg, d_du, d_datt, d_dmid, d_dmix = chain(
        demb_doc, d_proj, d_out, d_mid, d_a, d_b, gains, *back, "doc_ff_back"
    )
    q_chain = (demb_qry, q_proj, q_out, q_mid, q_a, q_b, gains, *back)
    d_attention = lambda il: (d_q, d_k, d_v, d_e, il, d_mixt, d_dmix)
    q_attention = lambda il, dmix: (q_q, q_k, q_v, q_e, il, q_mixt, dmix)
    qkv_weights = (w_query, w_key, w_value)
    fast = (n_dp, n_grp) == (8, 4)
    if fast:
        pairs = devices // 2
        q_dg, q_du, q_dmid, q_dmix, own, send = down_grads(
            (q_chain, (q_hid, q_mixt, q_n3)), (d_hid, d_dbr, d_mixt, d_datt, d_n3, d_dpj), pairs
        )
        down = Batch(own, send, n_dp, n_grp, "down")
        begun = gate_grads(0, d_n2, q_n2, d_dg, q_dg, pairs)
        down.got = after(down.got, begun)
        q_du = after(q_du, down.cross())
        own, send = gate_grads(1, d_n2, q_n2, d_du, q_du, pairs, begun)
        gate = Batch(own, send, n_dp, n_grp, "gate")
        d_il = after(d_il, send)
        d_dqkv, d_diag, d_far = attention_back(*d_attention(d_il), "doc_attention_back")
        gate.got = after(gate.got, d_diag)
        q_il = after(q_il, gate.cross())
        q_dqkv, q_diag, q_far, own, send = qkv_grads(
            q_attention(q_il, q_dmix), d_n1, q_n1, d_dqkv, d_diag, d_far, hot, loss_group, pairs
        )
        qkv = Batch(own, send, n_dp, n_grp, "qkv")
        (doc_grad,) = input_back(after(gains, send), ((d_dqkv, x_doc, d_dmid),), qkv_weights, "doc_input_back")
        down.back2 = after(down.back2, doc_grad)
        last_gains = after(gains, down.line(True))
    else:
        q_dpj, q_dbr, q_dg, q_du, q_datt, q_dmid, q_dmix = chain(*q_chain, "query_ff_back")
        d_dqkv, d_diag, d_far = attention_back(*d_attention(d_il), "doc_attention_back")
        q_dqkv, q_diag, q_far = attention_back(*q_attention(q_il, q_dmix), "query_attention_back")
        last_gains = gains
        (doc_grad,) = input_back(gains, ((d_dqkv, x_doc, d_dmid),), qkv_weights, "doc_input_back")
    (query_grad,) = input_back(last_gains, ((q_dqkv, x_qry, q_dmid),), qkv_weights, "query_input_back")

    query_total = query_rows * devices
    per, per_down = width // devices, hidden // devices
    if fast:
        qkv.got = after(qkv.got, query_grad)
        gate.back2 = after(gate.back2, qkv.cross())
        qkv.back2 = after(qkv.back2, gate.line())
        sent = qkv.line()
        down.parts, gate.parts = after((down.parts, gate.parts), sent)
        at = (width // 256) * per_down
        shard_down, shard_out, shard_proj, gain3 = finish(
            down, (0, at, at + 3 * per), ((per_down, width), (per, width), (per, w_proj.shape[1])), (2, (2,)), gains, [w_proj]
        )
        shard_gate, shard_up, gain2 = finish(
            gate, (0, (hidden // 256) * per), ((per, hidden),) * 2, (1, (0, 1)), gains, [w_gate, w_up]
        )
        shard_query, shard_key, shard_value, gain1, table_grad, loss = finish(
            qkv, (0, 3 * per, 6 * per), ((per, width),) * 3, (0, (0, 1, 2)), gains, qkv_weights, (heads, bucket_total), 1.0 / query_total
        )
        shard_gains = [g.reshape(per) for g in (gain1, gain2, gain3)]
        table_grad, loss = table_grad.T, loss.reshape(())
    else:

        def grad(left, right):
            product = tn(jnp.concatenate(left), jnp.concatenate(right))
            return lax.psum_scatter(product, axes, scatter_dimension=0, tiled=True)

        n1s = (d_n1, q_n1)
        shard_query, shard_key, shard_value = (
            grad(n1s, (d_dqkv[:, i * width:(i + 1) * width], q_dqkv[:, i * width:(i + 1) * width])) for i in range(3)
        )
        shard_out = grad((d_mixt.T, q_mixt.T), (d_datt, q_datt))
        shard_gate = grad((d_n2, q_n2), (d_dg, q_dg))
        shard_up = grad((d_n2, q_n2), (d_du, q_du))
        shard_down = grad((d_hid, q_hid), (d_dbr, q_dbr))
        shard_proj = grad((d_n3, q_n3), (d_dpj, q_dpj))
        start = (lax.axis_index("dp") * n_grp + lax.axis_index("grp")) * per
        mine = lambda a: lax.dynamic_slice_in_dim(a.astype(F32), start, per, 0)
        shard_gains = [
            sum(jnp.sum(mine(w) * g, axis=1) for w, g in pairs) / mine(gain)
            for gain, pairs in (
                (gain_attn, ((w_query, shard_query), (w_key, shard_key), (w_value, shard_value))),
                (gain_ffn, ((w_gate, shard_gate), (w_up, shard_up))),
                (gain_final, ((w_proj, shard_proj),)),
            )
        ]
        far = jnp.sum((d_far + q_far).reshape(heads, 2, -1), axis=-1)
        table = lax.dot_general(
            hot.astype(F32), (d_diag + q_diag).reshape(heads, -1), (((1,), (1,)), ((), ())),
            precision=highest, preferred_element_type=F32,
        )
        table = table.at[bucket_total // 2 - 1].add(far[:, 0]).at[bucket_total - 1].add(far[:, 1])
        table_grad, loss = lax.psum((table, loss_group[0, 0] / n_dp), axes)
        loss = loss / query_total
    return (
        loss,
        doc_grad.reshape(doc_rows, doc_len, width),
        query_grad.reshape(query_rows, query_len, width),
        shard_gains[0],
        shard_query,
        shard_key,
        shard_value,
        shard_out,
        table_grad,
        shard_gains[1],
        shard_gate,
        shard_up,
        shard_down,
        shard_gains[2],
        shard_proj,
    )


def solution(mesh):
    both = ("dp", "grp")
    rows3, rows2, rows1 = P(both, None, None), P(both, None), P(both)
    in_specs = (rows3, rows2, rows3, rows1, rows2, rows1) + (P(),) * 12
    out_specs = (
        P(), rows3, rows3, rows1, rows2, rows2, rows2, rows2, P(), rows1, rows2, rows2, rows2, rows1, rows2,
    )
    body = functools.partial(on_device, mesh.shape["dp"], mesh.shape["grp"])
    return jax.shard_map(body, mesh=mesh, in_specs=in_specs, out_specs=out_specs, check_vma=False)
```
